32 devices in a mesh: section: 16 (over z, y, core), head: 2 (over x).
Axes of the slice: x: 2, y: 2, z: 4, core: 2. Of those that a mesh axis runs over, the one named last changes fastest.
Arguments:
- hidden: bfloat16 [2048, 3072], P('section', 'head'), may hold values from -6 to 6
- text_hidden: bfloat16 [256, 3072], P(None, 'head'), may hold values from -6 to 6
- text_mask: int32 [256], replicated, may hold values 0 or 1
- stale_cache: bfloat16 [2, 2048, 1536], P(None, 'section', 'head'), may hold values from -2.5 to 2.5
- qkv_weight: bfloat16 [3072, 4608], P('head'), may hold values from -0.109375 to 0.109375
- out_weight: bfloat16 [1536, 3072], P(None, 'head'), may hold values from -0.15625 to 0.15625
- query_gain: float32 [128], replicated, may hold values from 1 to 2
- key_gain: float32 [128], replicated, may hold values from 1 to 2
- norm_shift: float32 [3072], P('head'), may hold values from -3 to 3
- norm_scale: float32 [3072], P('head'), may hold values from -0.5 to 0.5
- branch_gate: float32 [3072], P('head'), may hold values from 0.5 to 2
Outputs:
- mixed: bfloat16 [2048, 3072], P('section', 'head')
- new_cache: bfloat16 [2, 2048, 1536], P(None, 'section', 'head')
The draws below stay inside these ranges and needn't reach their ends.
All inputs are finite; a program needn't handle non-finite values.
Results may differ from the reference program's by a relative error of at most 0.0066.
Values may be sent and summed in bfloat16 or wider, within the bound.
No kernel may reach another device: no remote copies, remote signals or barrier semaphores. Data moves between devices by JAX's collectives and lax.ppermute only.
A program may use at most 192 MiB of HBM per device.

```python
import math
import jax
import jax.numpy as jnp
from jax import lax

D = 3072
HEADS = 12
HEAD_DIM = 128
TXT = 256
TOK_DEV = 128
HD = 1536
PATCHES = 16
TOKENS = 2048


def touch_ends(entries, rng, low, top_value):
    spot = [jax.random.randint(jax.random.fold_in(rng, axis), (), 0, length) for axis, length in enumerate(entries.shape)]
    widest = entries.shape.index(max(entries.shape))
    neighbour = spot[:widest] + [(spot[widest] + 1) % entries.shape[widest]] + spot[widest + 1:]
    return entries.at[tuple(spot)].set(low).at[tuple(neighbour)].set(top_value)


def levels(own_key, extent, split, smallest, largest):
    factor_of, own = 1.0, jax.random.fold_in(own_key, 6)
    for dim, blocks in split:
        heights = jnp.exp(jax.random.uniform(jax.random.fold_in(own, dim), (blocks,), jnp.float32, smallest / len(split), largest / len(split)))
        factor_of = factor_of * jnp.repeat(heights, extent[dim] // blocks).reshape([-1 if axis == dim else 1 for axis in range(len(extent))])
    return factor_of


def scatter_about(own_key, dims, deviation, reach, shards=(), kind=jnp.bfloat16):
    factor_of = levels(own_key, dims, shards, -0.22, 0.18) if shards else 1.0
    array = jax.random.normal(own_key, dims, jnp.float32) * deviation * factor_of
    return jnp.minimum(jnp.maximum(array, -reach), reach).astype(kind)


def setup_inputs(seed: int = 0) -> dict:
    arg_keys = jax.random.split(jax.random.key(seed), 12)
    return {
        "hidden": scatter_about(arg_keys[0], (TOKENS, D), 1.0, 6.0, ((0, 16), (1, 2))),
        "text_hidden": scatter_about(arg_keys[1], (TXT, D), 1.0, 6.0, ((1, 2),)),
        "text_mask": touch_ends((jax.random.randint(arg_keys[2], (TXT,), 0, 4) < 3).astype(jnp.int32), jax.random.fold_in(arg_keys[2], 1), 0, 1),
        "stale_cache": scatter_about(arg_keys[3], (2, TOKENS, HD), 1.0, 2.5, ((1, 16), (2, 2))),
        "qkv_weight": scatter_about(arg_keys[4], (D, 3 * HD), D ** -0.5, 0.109375, ((0, 2),)),
        "out_weight": scatter_about(arg_keys[5], (HD, D), HD ** -0.5, 0.15625, ((1, 2),)),
        "query_gain": jnp.clip(jnp.exp(jax.random.uniform(arg_keys[6], (HEAD_DIM,), jnp.float32, math.log(1.0), math.log(2.0))), 1.0, 2.0),
        "key_gain": jnp.clip(jnp.exp(jax.random.uniform(arg_keys[7], (HEAD_DIM,), jnp.float32, math.log(1.0), math.log(2.0))), 1.0, 2.0),
        "norm_shift": scatter_about(arg_keys[8], (D,), 0.5, 3.0, ((0, 2),), jnp.float32),
        "norm_scale": jnp.clip(jax.random.uniform(arg_keys[9], (D,), jnp.float32, -0.5, 0.5) * levels(arg_keys[9], (D,), ((0, 2),), -0.4, 0.0), -0.5, 0.5),
        "branch_gate": jnp.clip(jnp.exp(math.log(2.0) - 1.3862944 * jax.random.uniform(arg_keys[10], (D,), jnp.float32) ** levels(arg_keys[10], (D,), ((0, 2),), -0.2, 0.2)), 0.5, 2.0),
    }


def head_norm(part_rows, gain_vec):
    return part_rows * lax.rsqrt(lax.optimization_barrier(jnp.mean(part_rows * part_rows, axis=-1, keepdims=True)) + 1e-06) * gain_vec

def context_terms(query_rows, key_rows, value_rows, keep_rows):
    factor = 1.0 / math.sqrt(HEAD_DIM)
    scores = jnp.einsum('qhc,khc->hqk', query_rows.astype(jnp.float32), key_rows.astype(jnp.float32)) * factor
    weights = jnp.exp(scores) * keep_rows[None, None, :]
    rounded = weights.astype(jnp.bfloat16).astype(jnp.float32)
    weighted = jnp.einsum('hqk,khc->qhc', rounded, value_rows.astype(jnp.float32))
    return (weighted, lax.optimization_barrier(jnp.sum(weights, axis=-1)).T)

def reference(hidden, text_hidden, text_mask, stale_cache, qkv_weight, out_weight, query_gain, key_gain, norm_shift, norm_scale, branch_gate):
    inputs_all = jnp.concatenate([hidden, text_hidden], 0).astype(jnp.float32)
    row_mean = lax.optimization_barrier(jnp.sum(inputs_all, axis=1)) / D
    row_var = lax.optimization_barrier(jnp.sum(inputs_all * inputs_all, axis=1)) / D - row_mean * row_mean
    normed = ((inputs_all - row_mean[:, None]) * lax.rsqrt(row_var + 1e-06)[:, None] * (1.0 + norm_scale) + norm_shift).astype(jnp.bfloat16)
    projected = jnp.dot(normed, qkv_weight, preferred_element_type=jnp.float32)
    projected = projected.reshape(TOKENS + TXT, HEADS, 3 * HEAD_DIM)
    queries_all = head_norm(projected[..., :HEAD_DIM], query_gain).astype(jnp.bfloat16)
    keys_all = head_norm(projected[..., HEAD_DIM:2 * HEAD_DIM], key_gain).astype(jnp.bfloat16)
    values_all = projected[..., 2 * HEAD_DIM:].astype(jnp.bfloat16)
    fresh_keys = keys_all[:TOKENS]
    fresh_values = values_all[:TOKENS]
    text_keys = keys_all[TOKENS:]
    text_values = values_all[TOKENS:]
    new_cache = jnp.stack([fresh_keys.reshape(TOKENS, HD), fresh_values.reshape(TOKENS, HD)])
    stale_keys = stale_cache[0].reshape(TOKENS, HEADS, HEAD_DIM)
    stale_values = stale_cache[1].reshape(TOKENS, HEADS, HEAD_DIM)
    text_keep = text_mask.astype(jnp.float32)
    video_keep = jnp.ones((TOKENS,), jnp.float32)

    def patch_rows(patch_index):
        first_row = (patch_index * TOK_DEV).astype(jnp.int32)
        query_rows = lax.dynamic_slice_in_dim(queries_all, first_row, TOK_DEV, 0)
        own_keys = lax.dynamic_slice_in_dim(fresh_keys, first_row, TOK_DEV, 0)
        own_values = lax.dynamic_slice_in_dim(fresh_values, first_row, TOK_DEV, 0)
        context_keys = lax.dynamic_update_slice_in_dim(stale_keys, own_keys, first_row, 0)
        context_values = lax.dynamic_update_slice_in_dim(stale_values, own_values, first_row, 0)
        video_num, video_den = context_terms(query_rows, context_keys, context_values, video_keep)
        text_num, text_den = context_terms(query_rows, text_keys, text_values, text_keep)
        return ((video_num + text_num) / (video_den + text_den)[..., None]).astype(jnp.bfloat16)
    attended = lax.map(patch_rows, jnp.arange(PATCHES, dtype=jnp.int32)).reshape(TOKENS, HD)
    projection_out = jnp.dot(attended, out_weight, preferred_element_type=jnp.float32)
    mixed = (hidden.astype(jnp.float32) + branch_gate * projection_out).astype(jnp.bfloat16)
    return (mixed, new_cache)
```

```python
import functools
import math

import jax
import jax.numpy as jnp
from jax import lax
from jax.experimental import pallas as pl
from jax.experimental.pallas import tpu as pltpu
from jax.sharding import PartitionSpec as P

HEAD_DIM = 128
TRIPLE = 3 * HEAD_DIM
EPS = 1e-06
F32 = jnp.float32
BF16 = jnp.bfloat16


def round_up(value, step):
    return -(-value // step) * step


def split_bf16(value, parts):
    pieces = []
    rest = value
    for _ in range(parts):
        piece = rest.astype(BF16)
        pieces.append(piece)
        rest = rest - piece.astype(F32)
    return pieces


def send_kernel(group_ref, x_ref, t_ref, scale_ref, shift_ref, w_ref, a_ref, msg_ref, stat_ref):
    step = pl.program_id(0)
    video, features = x_ref.shape
    text = t_ref.shape[0]
    columns = w_ref.shape[1]
    width = msg_ref.shape[1] - HEAD_DIM

    @pl.when(step == 0)
    def _():
        gain = 1.0 + scale_ref[...]

        def place(rows_ref, start):
            rows = rows_ref[...].astype(F32)
            count = rows.shape[0]
            mean = jnp.sum(rows, axis=1, keepdims=True) * (1.0 / features)
            centered = rows - mean
            second = jnp.sum(centered * centered, axis=1, keepdims=True)
            a_ref[start : start + count, :] = (centered * gain).astype(BF16)
            pieces = split_bf16(mean, 3) + split_bf16(second, 3)
            lane = lax.broadcasted_iota(jnp.int32, (count, HEAD_DIM), 1)
            packed = jnp.zeros((count, HEAD_DIM), F32)
            for index, piece in enumerate(pieces):
                packed = jnp.where(lane == index, piece.astype(F32), packed)
            msg_ref[start : start + count, width:] = packed.astype(BF16)
            own = jnp.where(lane == 0, mean, jnp.where(lane == 1, second, 0.0))
            stat_ref[start : start + count, :] = own

        place(x_ref, 0)
        place(t_ref, video)
        tail = a_ref.shape[0] - video - text
        pieces = split_bf16(gain, 2) + split_bf16(shift_ref[...], 2)
        row = lax.broadcasted_iota(jnp.int32, (tail, features), 0)
        extra = jnp.zeros((tail, features), F32)
        for index, piece in enumerate(pieces):
            extra = jnp.where(row == index, piece.astype(F32), extra)
        a_ref[video + text :, :] = extra.astype(BF16)
        msg_ref[video + text :, width:] = jnp.zeros((tail, HEAD_DIM), BF16)

    product = jnp.dot(a_ref[...], w_ref[...], preferred_element_type=F32)
    msg_ref[:, pl.ds(pl.multiple_of(step * columns, columns), columns)] = product.astype(BF16)


def own_kernel(group_ref, a_ref, w_ref, out_ref):
    out_ref[...] = jnp.dot(a_ref[...], w_ref[...], preferred_element_type=F32)


def norm_kernel(
    video, text, total_features, own_ref, msg_ref, stat_ref, mstat_ref, qg_ref, kg_ref,
    q_ref, cache_ref, text_ref,
):
    rows = video + text
    half = total_features // 2
    mean_own = stat_ref[:rows, 0:1]
    second_own = stat_ref[:rows, 1:2]
    received = mstat_ref[:rows, :].astype(F32)
    mean_other = received[:, 0:1] + received[:, 1:2] + received[:, 2:3]
    second_other = received[:, 3:4] + received[:, 4:5] + received[:, 5:6]
    gap = 0.5 * (mean_own - mean_other)
    var = (second_own + second_other) * (1.0 / total_features) + gap * gap
    inverse = lax.rsqrt(var + EPS)

    own = own_ref[...]
    other = msg_ref[...].astype(F32)
    scale_own = own[rows : rows + 1] + own[rows + 1 : rows + 2]
    scale_other = other[rows : rows + 1] + other[rows + 1 : rows + 2]
    shift = (own[rows + 2 : rows + 3] + own[rows + 3 : rows + 4]) + (
        other[rows + 2 : rows + 3] + other[rows + 3 : rows + 4]
    )
    total = (own[:rows] + other[:rows] + gap * (scale_own - scale_other)) * inverse + shift

    def head_norm(part, gain):
        square = jnp.sum(part * part, axis=1, keepdims=True) * (1.0 / HEAD_DIM)
        return part * lax.rsqrt(square + EPS) * gain

    q_ref[...] = head_norm(total[:video, :HEAD_DIM], qg_ref[...]).astype(BF16)
    keys = head_norm(total[:, HEAD_DIM : 2 * HEAD_DIM], kg_ref[...]).astype(BF16)
    values = total[:, 2 * HEAD_DIM :].astype(BF16)
    cache_ref[0] = keys[:video]
    cache_ref[1] = values[:video]
    text_ref[0] = keys[video:]
    text_ref[1] = values[video:]


def attention_kernel(
    chip_ref, qo_ref, qp_ref, stale_ref, cache_ref, text_ref, mask_ref, own_ref, msg_ref, own_den_ref,
):
    head = pl.program_id(0)
    blocks, _, video, depth = stale_ref.shape
    factor = math.log2(math.e) / math.sqrt(depth)
    contract = (((1,), (1,)), ((), ()))
    chip = chip_ref[0]

    queries = jnp.concatenate([qo_ref[...], qp_ref[...]], axis=0)
    lane = lax.broadcasted_iota(jnp.int32, (video, HEAD_DIM), 1)

    def weigh(rows, keys):
        scores = lax.dot_general(rows, keys, contract, preferred_element_type=F32)
        return jnp.exp2(scores * factor)

    def lanes(weights):
        total = weights[:, :HEAD_DIM]
        for start in range(HEAD_DIM, weights.shape[1], HEAD_DIM):
            total = total + weights[:, start : start + HEAD_DIM]
        return total

    def times(weights, values):
        return jnp.dot(weights.astype(BF16), values, preferred_element_type=F32)

    fresh = weigh(queries[:video], cache_ref[0])
    num_own = times(fresh, cache_ref[1])
    den_own = lanes(fresh)

    text_k = text_ref[:, 0].reshape(-1, depth)
    text_v = text_ref[:, 1].reshape(-1, depth)
    weights = weigh(queries, text_k) * mask_ref[...]
    num = times(weights, text_v)
    den = lanes(weights)

    keep_rows = lax.broadcasted_iota(jnp.int32, (2 * video, 1), 0) >= video
    for block in range(blocks):
        weights = weigh(queries, stale_ref[block, 0])
        keep = jnp.where(keep_rows | (chip != block), 1.0, 0.0)
        weights = weights * keep
        num = num + times(weights, stale_ref[block, 1])
        den = den + lanes(weights)

    den_own = jnp.sum(den_own + den[:video], axis=1, keepdims=True)
    den_other = jnp.sum(den[video:], axis=1, keepdims=True)
    columns = pl.ds(pl.multiple_of(head * depth, depth), depth)
    width = msg_ref.shape[1] - HEAD_DIM
    own_ref[:, columns] = num_own + num[:video]
    msg_ref[:, columns] = num[video:]

    @pl.when(head == 0)
    def _():
        own_den_ref[...] = jnp.zeros_like(own_den_ref)
        msg_ref[:, width:] = jnp.zeros((video, HEAD_DIM), F32)

    own_den_ref[...] = jnp.where(lane == head, den_own, own_den_ref[...])
    msg_ref[:, width:] = jnp.where(lane == head, den_other, msg_ref[:, width:])


def merge_kernel(group_ref, own_ref, den_ref, msg_ref, w_ref, att_ref, out_ref):
    width = att_ref.shape[1]
    for head in range(width // HEAD_DIM):
        columns = slice(head * HEAD_DIM, (head + 1) * HEAD_DIM)
        num = own_ref[:, columns] + msg_ref[:, columns]
        den = den_ref[:, head : head + 1] + msg_ref[:, width + head : width + head + 1]
        att_ref[:, columns] = (num / den).astype(BF16)
    out_ref[...] = jnp.dot(att_ref[...], w_ref[...], preferred_element_type=F32)


def final_kernel(group_ref, part_ref, att_ref, w_ref, hidden_ref, gate_ref, out_ref):
    total = part_ref[...] + jnp.dot(att_ref[...], w_ref[...], preferred_element_type=F32)
    out_ref[...] = (hidden_ref[...].astype(F32) + gate_ref[...] * total).astype(BF16)


def params(megabytes=48):
    return pltpu.CompilerParams(vmem_limit_bytes=megabytes * 1024 * 1024)


def cost(flops, nbytes, transcendentals=0):
    return pl.CostEstimate(flops=flops, bytes_accessed=nbytes, transcendentals=transcendentals)


def per_device(
    sections, hidden, text_hidden, text_mask, stale_cache, qkv_weight, out_weight, query_gain,
    key_gain, norm_shift, norm_scale, branch_gate,
):
    video, features = hidden.shape
    text_rows = text_hidden.shape[0]
    text = text_rows // sections
    text_pad = round_up(text, 16)
    width = stale_cache.shape[2]
    heads = width // HEAD_DIM
    group_columns = heads * TRIPLE
    chips = sections // 2
    out_features = out_weight.shape[1]
    rows = video + text_pad
    padded = rows + 16

    section = lax.axis_index("section")
    group = lax.axis_index("head").astype(jnp.int32).reshape(1)
    core = section % 2
    chip = (section // 2).astype(jnp.int32).reshape(1)
    same_core = [list(range(c, sections, 2)) for c in range(2)]
    swap_core = [(s, s ^ 1) for s in range(sections)]
    swap_head = [(0, 1), (1, 0)]

    stale = lax.all_gather(
        stale_cache.reshape(2 * video, width), "section", axis=0, tiled=True,
        axis_index_groups=same_core,
    ).reshape(chips, 2, video, width)

    own_text = lax.dynamic_slice_in_dim(text_hidden, section * text, text, 0)
    mask = lax.dynamic_index_in_dim(text_mask.reshape(chips, 2, text), core, 1, keepdims=False)
    if text_pad != text:
        own_text = jnp.pad(own_text, ((0, text_pad - text), (0, 0)))
        mask = jnp.pad(mask, ((0, 0), (0, text_pad - text)))
    mask = mask.astype(F32).reshape(1, chips * text_pad)

    vmem_full = lambda *shape: pl.BlockSpec(shape, lambda h, *_: (0,) * len(shape))
    weight_bytes = features * group_columns * 2
    project_flops = 2 * padded * features * group_columns
    a_rows, message, stats = pl.pallas_call(
        send_kernel,
        grid_spec=pltpu.PrefetchScalarGridSpec(
            num_scalar_prefetch=1,
            grid=(heads,),
            in_specs=[
                vmem_full(video, features),
                vmem_full(text_pad, features),
                vmem_full(1, features),
                vmem_full(1, features),
                pl.BlockSpec((features, TRIPLE), lambda h, g: (0, (1 - g[0]) * heads + h)),
            ],
            out_specs=[
                vmem_full(padded, features),
                vmem_full(padded, group_columns + HEAD_DIM),
                vmem_full(rows, HEAD_DIM),
            ],
        ),
        out_shape=[
            jax.ShapeDtypeStruct((padded, features), BF16),
            jax.ShapeDtypeStruct((padded, group_columns + HEAD_DIM), BF16),
            jax.ShapeDtypeStruct((rows, HEAD_DIM), F32),
        ],
        compiler_params=params(),
        cost_estimate=cost(project_flops, weight_bytes),
        name="project_send",
    )(group, hidden, own_text, norm_scale.reshape(1, -1), norm_shift.reshape(1, -1), qkv_weight)

    received = lax.ppermute(message, "head", swap_head)

    own = pl.pallas_call(
        own_kernel,
        grid_spec=pltpu.PrefetchScalarGridSpec(
            num_scalar_prefetch=1,
            grid=(heads,),
            in_specs=[
                vmem_full(padded, features),
                pl.BlockSpec((features, TRIPLE), lambda h, g: (0, g[0] * heads + h)),
            ],
            out_specs=pl.BlockSpec((padded, TRIPLE), lambda h, g: (0, h)),
        ),
        out_shape=jax.ShapeDtypeStruct((padded, group_columns), F32),
        compiler_params=params(),
        cost_estimate=cost(project_flops, weight_bytes),
        name="project_own",
    )(group, a_rows, qkv_weight)

    queries, new_cache, text_kv = pl.pallas_call(
        functools.partial(norm_kernel, video, text_pad, features * 2),
        grid=(heads,),
        in_specs=[
            pl.BlockSpec((padded, TRIPLE), lambda h: (0, h)),
            pl.BlockSpec((padded, TRIPLE), lambda h: (0, h)),
            vmem_full(rows, HEAD_DIM),
            pl.BlockSpec((padded, HEAD_DIM), lambda h: (0, 3 * heads)),
            vmem_full(1, HEAD_DIM),
            vmem_full(1, HEAD_DIM),
        ],
        out_specs=[
            pl.BlockSpec((video, HEAD_DIM), lambda h: (0, h)),
            pl.BlockSpec((2, video, HEAD_DIM), lambda h: (0, 0, h)),
            pl.BlockSpec((2, text_pad, HEAD_DIM), lambda h: (0, 0, h)),
        ],
        out_shape=[
            jax.ShapeDtypeStruct((video, width), BF16),
            jax.ShapeDtypeStruct((2, video, width), BF16),
            jax.ShapeDtypeStruct((2, text_pad, width), BF16),
        ],
        compiler_params=params(),
        cost_estimate=cost(20 * rows * group_columns, 6 * padded * group_columns),
        name="norm_heads",
    )(own, received, stats, received, query_gain.reshape(1, -1), key_gain.reshape(1, -1))

    other_queries = lax.ppermute(queries, "section", swap_core)
    text_all = lax.all_gather(
        text_kv.reshape(2 * text_pad, width), "section", axis=0, tiled=True,
        axis_index_groups=same_core,
    ).reshape(chips, 2, text_pad, width)

    context = chips * (video + text_pad) + video
    num_own, num_message, den_own = pl.pallas_call(
        attention_kernel,
        grid_spec=pltpu.PrefetchScalarGridSpec(
            num_scalar_prefetch=1,
            grid=(heads,),
            in_specs=[
                pl.BlockSpec((video, HEAD_DIM), lambda h, c: (0, h)),
                pl.BlockSpec((video, HEAD_DIM), lambda h, c: (0, h)),
                pl.BlockSpec((chips, 2, video, HEAD_DIM), lambda h, c: (0, 0, 0, h)),
                pl.BlockSpec((2, video, HEAD_DIM), lambda h, c: (0, 0, h)),
                pl.BlockSpec((chips, 2, text_pad, HEAD_DIM), lambda h, c: (0, 0, 0, h)),
                vmem_full(1, chips * text_pad),
            ],
            out_specs=[
                vmem_full(video, width),
                vmem_full(video, width + HEAD_DIM),
                vmem_full(video, HEAD_DIM),
            ],
        ),
        out_shape=[
            jax.ShapeDtypeStruct((video, width), F32),
            jax.ShapeDtypeStruct((video, width + HEAD_DIM), F32),
            jax.ShapeDtypeStruct((video, HEAD_DIM), F32),
        ],
        compiler_params=params(),
        cost_estimate=cost(8 * video * context * width, 4 * context * width, 2 * video * context * heads),
        name="attend",
    )(chip, queries, other_queries, stale, new_cache, text_all, mask)

    num_received = lax.ppermute(num_message, "section", swap_core)

    attended, part = pl.pallas_call(
        merge_kernel,
        grid_spec=pltpu.PrefetchScalarGridSpec(
            num_scalar_prefetch=1,
            grid=(1,),
            in_specs=[
                vmem_full(video, width),
                vmem_full(video, HEAD_DIM),
                vmem_full(video, width + HEAD_DIM),
                pl.BlockSpec((width, out_features), lambda h, g: (g[0], 0)),
            ],
            out_specs=[vmem_full(video, width), vmem_full(video, out_features)],
        ),
        out_shape=[
            jax.ShapeDtypeStruct((video, width), BF16),
            jax.ShapeDtypeStruct((video, out_features), F32),
        ],
        compiler_params=params(),
        cost_estimate=cost(2 * video * width * out_features, 2 * width * out_features),
        name="merge_out",
    )(group, num_own, den_own, num_received, out_weight)

    other_attended = lax.ppermute(attended, "head", swap_head)

    mixed = pl.pallas_call(
        final_kernel,
        grid_spec=pltpu.PrefetchScalarGridSpec(
            num_scalar_prefetch=1,
            grid=(1,),
            in_specs=[
                vmem_full(video, out_features),
                vmem_full(video, width),
                pl.BlockSpec((width, out_features), lambda h, g: (1 - g[0], 0)),
                vmem_full(video, features),
                vmem_full(1, features),
            ],
            out_specs=vmem_full(video, out_features),
        ),
        out_shape=jax.ShapeDtypeStruct((video, out_features), BF16),
        compiler_params=params(),
        cost_estimate=cost(2 * video * width * out_features, 2 * width * out_features),
        name="final_out",
    )(group, part, other_attended, out_weight, hidden, branch_gate.reshape(1, -1))
    return (mixed, new_cache)


def solution(mesh):
    in_specs = (
        P("section", "head"),
        P(None, "head"),
        P(),
        P(None, "section", "head"),
        P("head", None),
        P(None, "head"),
        P(),
        P(),
        P("head"),
        P("head"),
        P("head"),
    )
    out_specs = (P("section", "head"), P(None, "section", "head"))
    return jax.shard_map(
        functools.partial(per_device, mesh.shape["section"]),
        mesh=mesh, in_specs=in_specs, out_specs=out_specs, check_vma=False,
    )
```

```python
import functools
import math

import jax
import jax.numpy as jnp
from jax import lax
from jax.experimental import pallas as pl
from jax.experimental.pallas import tpu as pltpu
from jax.sharding import PartitionSpec as P

HEAD_DIM = 128
TRIPLE = 3 * HEAD_DIM
EXTRA = 16
EPS = 1e-06
F32 = jnp.float32
BF16 = jnp.bfloat16


def split_bf16(value, parts):
    pieces = []
    rest = value
    for _ in range(parts):
        piece = rest.astype(BF16)
        pieces.append(piece)
        rest = rest - piece.astype(F32)
    return pieces


def send_kernel(
    place_ref, x_ref, t_ref, scale_ref, shift_ref, w_ref, a_ref, msg_ref, tmsg_ref, stat_ref,
):
    step = pl.program_id(0)
    video, features = x_ref.shape
    text = t_ref.shape[0]
    top = video + EXTRA
    columns = w_ref.shape[1]
    width = msg_ref.shape[1] - HEAD_DIM
    twidth = tmsg_ref.shape[1] - HEAD_DIM

    @pl.when(step == 0)
    def _():
        gain = 1.0 + scale_ref[...]

        def place(rows_ref, start):
            rows = rows_ref[...].astype(F32)
            count = rows.shape[0]
            mean = jnp.sum(rows, axis=1, keepdims=True) * (1.0 / features)
            centered = rows - mean
            second = jnp.sum(centered * centered, axis=1, keepdims=True)
            a_ref[start : start + count, :] = (centered * gain).astype(BF16)
            pieces = split_bf16(mean, 3) + split_bf16(second, 3)
            lane = lax.broadcasted_iota(jnp.int32, (count, HEAD_DIM), 1)
            packed = jnp.zeros((count, HEAD_DIM), F32)
            for index, piece in enumerate(pieces):
                packed = jnp.where(lane == index, piece.astype(F32), packed)
            stat_ref[start : start + count, :] = jnp.where(
                lane == 0, mean, jnp.where(lane == 1, second, 0.0)
            )
            return packed.astype(BF16)

        msg_ref[:video, width:] = place(x_ref, 0)
        tmsg_ref[:, twidth:] = place(t_ref, top)
        pieces = split_bf16(gain, 2) + split_bf16(shift_ref[...], 2)
        row = lax.broadcasted_iota(jnp.int32, (EXTRA, features), 0)
        extra = jnp.zeros((EXTRA, features), F32)
        for index, piece in enumerate(pieces):
            extra = jnp.where(row == index, piece.astype(F32), extra)
        a_ref[video:top, :] = extra.astype(BF16)
        msg_ref[video:, width:] = jnp.zeros((EXTRA, HEAD_DIM), BF16)
        stat_ref[video:top, :] = jnp.zeros((EXTRA, HEAD_DIM), F32)

    product = jnp.dot(a_ref[...], w_ref[...], preferred_element_type=F32)
    msg_ref[:, pl.ds(pl.multiple_of(step * columns, columns), columns)] = product[:top].astype(BF16)
    heads = columns // TRIPLE
    for index in range(heads):
        start = pl.multiple_of((step * heads + index) * 2 * HEAD_DIM, 2 * HEAD_DIM)
        tmsg_ref[:, pl.ds(start, 2 * HEAD_DIM)] = product[
            top:, index * TRIPLE + HEAD_DIM : (index + 1) * TRIPLE
        ].astype(BF16)


def own_kernel(place_ref, a_ref, w_ref, out_ref, text_ref):
    top = out_ref.shape[0]
    product = jnp.dot(a_ref[...], w_ref[...], preferred_element_type=F32)
    out_ref[...] = product[:top]
    for index in range(w_ref.shape[1] // TRIPLE):
        text_ref[:, index * 2 * HEAD_DIM : (index + 1) * 2 * HEAD_DIM] = product[
            top:, index * TRIPLE + HEAD_DIM : (index + 1) * TRIPLE
        ]


def row_stats(total_features, own, received):
    received = received.astype(F32)
    mean_other = received[:, 0:1] + received[:, 1:2] + received[:, 2:3]
    second_other = received[:, 3:4] + received[:, 4:5] + received[:, 5:6]
    gap = 0.5 * (own[:, 0:1] - mean_other)
    var = (own[:, 1:2] + second_other) * (1.0 / total_features) + gap * gap
    return gap, lax.rsqrt(var + EPS)


def column_terms(own, other):
    other = other.astype(F32)
    scale = (own[0:1] + own[1:2]) - (other[0:1] + other[1:2])
    shift = (own[2:3] + own[3:4]) + (other[2:3] + other[3:4])
    return scale, shift


def head_norm(part, gain):
    square = jnp.sum(part * part, axis=1, keepdims=True) * (1.0 / HEAD_DIM)
    return part * lax.rsqrt(square + EPS) * gain


def norm_kernel(
    total_features, own_ref, msg_ref, stat_ref, qg_ref, kg_ref, q_ref, cache_ref, kv_ref,
):
    video = q_ref.shape[0]
    heads = q_ref.shape[1] // HEAD_DIM
    gap, inverse = row_stats(
        total_features, stat_ref[:video, :], msg_ref[:video, heads * TRIPLE :]
    )
    for head in range(heads):
        part = slice(head * TRIPLE, (head + 1) * TRIPLE)
        columns = slice(head * HEAD_DIM, (head + 1) * HEAD_DIM)
        scale, shift = column_terms(own_ref[video:, part], msg_ref[video:, part])
        total = own_ref[:video, part] + msg_ref[:video, part].astype(F32)
        total = (total + gap * scale) * inverse + shift
        q_ref[:, columns] = head_norm(total[:, :HEAD_DIM], qg_ref[...]).astype(BF16)
        keys = head_norm(total[:, HEAD_DIM : 2 * HEAD_DIM], kg_ref[...]).astype(BF16)
        values = total[:, 2 * HEAD_DIM :].astype(BF16)
        cache_ref[0, :, columns] = keys
        cache_ref[1, :, columns] = values
        kv_ref[0, :, columns] = keys
        kv_ref[1, :, columns] = values


def text_kernel(
    total_features, own_ref, msg_ref, stat_ref, top_ref, tmsg_ref, kg_ref, kv_ref,
):
    heads = kv_ref.shape[2] // HEAD_DIM
    top = top_ref.shape[0]
    video = top - EXTRA
    gap, inverse = row_stats(
        total_features, stat_ref[top:, :], tmsg_ref[:, heads * 2 * HEAD_DIM :]
    )
    for head in range(heads):
        part = slice(head * TRIPLE + HEAD_DIM, (head + 1) * TRIPLE)
        pair = slice(head * 2 * HEAD_DIM, (head + 1) * 2 * HEAD_DIM)
        columns = slice(head * HEAD_DIM, (head + 1) * HEAD_DIM)
        scale, shift = column_terms(top_ref[video:, part], msg_ref[video:, part])
        total = own_ref[:, pair] + tmsg_ref[:, pair].astype(F32)
        total = (total + gap * scale) * inverse + shift
        kv_ref[0, :, columns] = head_norm(total[:, :HEAD_DIM], kg_ref[...]).astype(BF16)
        kv_ref[1, :, columns] = total[:, HEAD_DIM:].astype(BF16)


FACTOR = math.log2(math.e) / math.sqrt(HEAD_DIM)


def weigh(rows, keys):
    scores = lax.dot_general(rows, keys, (((1,), (1,)), ((), ())), preferred_element_type=F32)
    return jnp.exp2(scores * FACTOR)


def lanes(weights):
    total = weights[:, :HEAD_DIM]
    for start in range(HEAD_DIM, weights.shape[1], HEAD_DIM):
        total = total + weights[:, start : start + HEAD_DIM]
    return total


def times(weights, values):
    return jnp.dot(weights.astype(BF16), values, preferred_element_type=F32)


def absorb(queries, blocks, num, den, columns):
    for first in range(0, len(blocks), 2):
        pair = blocks[first : first + 2]
        keys = jnp.concatenate([k(columns) for k, _ in pair], axis=0)
        values = jnp.concatenate([v(columns) for _, v in pair], axis=0)
        weights = weigh(queries, keys)
        num = num + times(weights, values)
        den = den + lanes(weights)
    return num, den


def loaders(ref):
    return (lambda columns: ref[0, :, columns]), (lambda columns: ref[1, :, columns])


def first_kernel(
    count, group_ref, weight_ref, qo_ref, qp_ref, fresh_ref, stale_ref, text_ref, mask_ref, *refs
):
    ring = refs[:count]
    num_ref, den_ref, w_own_ref, w_other_ref, sems = refs[count:]
    depth = w_own_ref.shape[0]
    group = group_ref[0]
    copies = []
    for index, (half, target) in enumerate(((group, w_own_ref), (1 - group, w_other_ref))):
        source = weight_ref.at[pl.ds(pl.multiple_of(half * depth, depth), depth)]
        copies.append(pltpu.make_async_copy(source, target, sems.at[index]))
    for copy in copies:
        copy.start()
    video, width = qo_ref.shape
    lane = lax.broadcasted_iota(jnp.int32, (2 * video, HEAD_DIM), 1)
    packed = jnp.zeros((2 * video, HEAD_DIM), F32)
    for head in range(width // HEAD_DIM):
        columns = slice(head * HEAD_DIM, (head + 1) * HEAD_DIM)
        own, other = qo_ref[:, columns], qp_ref[:, columns]
        queries = jnp.concatenate([own, other], axis=0)
        fresh = weigh(own, fresh_ref[0, :, columns])
        stale = weigh(other, stale_ref[0, :, columns])
        num = jnp.concatenate(
            [times(fresh, fresh_ref[1, :, columns]), times(stale, stale_ref[1, :, columns])], axis=0
        )
        den = jnp.concatenate([fresh, stale], axis=0)
        weights = weigh(queries, text_ref[0, :, columns]) * mask_ref[...]
        num = num + times(weights, text_ref[1, :, columns])
        den = den + lanes(weights)
        num, den = absorb(queries, [loaders(ref) for ref in ring], num, den, columns)
        num_ref[:, columns] = num
        packed = jnp.where(lane == head, jnp.sum(den, axis=1, keepdims=True), packed)
    den_ref[...] = packed
    for copy in copies:
        copy.wait()


def last_kernel(qo_ref, qp_ref, num_ref, den_ref, k_ref, v_ref, own_ref, own_den_ref, msg_ref):
    video, width = qo_ref.shape
    lane = lax.broadcasted_iota(jnp.int32, (2 * video, HEAD_DIM), 1)
    packed = den_ref[...]
    for head in range(width // HEAD_DIM):
        columns = slice(head * HEAD_DIM, (head + 1) * HEAD_DIM)
        queries = jnp.concatenate([qo_ref[:, columns], qp_ref[:, columns]], axis=0)
        weights = weigh(queries, k_ref[:, columns])
        num = num_ref[:, columns] + times(weights, v_ref[:, columns])
        own_ref[:, columns] = num[:video]
        msg_ref[:, columns] = num[video:]
        total = jnp.sum(lanes(weights), axis=1, keepdims=True)
        packed = packed + jnp.where(lane == head, total, 0.0)
    own_den_ref[...] = packed[:video]
    msg_ref[:, width:] = packed[video:]


def merge_kernel(own_ref, den_ref, msg_ref, att_ref):
    width = att_ref.shape[1]
    for head in range(width // HEAD_DIM):
        columns = slice(head * HEAD_DIM, (head + 1) * HEAD_DIM)
        num = own_ref[:, columns] + msg_ref[:, columns]
        den = den_ref[:, head : head + 1] + msg_ref[:, width + head : width + head + 1]
        att_ref[:, columns] = (num / den).astype(BF16)


def part_kernel(att_ref, w_ref, out_ref):
    out_ref[...] = jnp.dot(att_ref[...], w_ref[...], preferred_element_type=F32)


def final_kernel(part_ref, att_ref, w_ref, hidden_ref, gate_ref, out_ref):
    total = part_ref[...] + jnp.dot(att_ref[...], w_ref[...], preferred_element_type=F32)
    out_ref[...] = (hidden_ref[...].astype(F32) + gate_ref[...] * total).astype(BF16)


def params(megabytes):
    return pltpu.CompilerParams(vmem_limit_bytes=megabytes * 1024 * 1024)


def cost(flops, nbytes, transcendentals=0):
    return pl.CostEstimate(
        flops=int(flops), bytes_accessed=int(nbytes), transcendentals=int(transcendentals)
    )


def full(*shape):
    return pl.BlockSpec(shape, lambda *_: (0,) * len(shape))


def plain_call(kernel, outs, name, estimate, *operands):
    return pl.pallas_call(
        kernel,
        in_specs=[pl.BlockSpec(memory_space=pltpu.VMEM)] * len(operands),
        out_specs=[pl.BlockSpec(memory_space=pltpu.VMEM)] * len(outs),
        out_shape=[jax.ShapeDtypeStruct(shape, dtype) for shape, dtype in outs],
        compiler_params=params(24),
        cost_estimate=estimate,
        name=name,
    )(*operands)


def ring_moves(sections):
    chips = sections // 2
    order = list(range(0, chips, 2)) + list(range(chips - 1, 0, -2))
    onward = []
    for here, there in zip(order, order[1:] + order[:1]):
        onward += [(2 * here + core, 2 * there + core) for core in range(2)]
    return sorted(onward), sorted((there, here) for here, there in onward)


def per_device(
    sections, hidden, text_hidden, text_mask, stale_cache, qkv_weight, out_weight, query_gain,
    key_gain, norm_shift, norm_scale, branch_gate,
):
    video, features = hidden.shape
    text = text_hidden.shape[0] // 2
    width = stale_cache.shape[2]
    heads = width // HEAD_DIM
    group_columns = heads * TRIPLE
    chips = sections // 2
    out_features = out_weight.shape[1]
    top = video + EXTRA
    rows = top + text

    group = lax.axis_index("head")
    core = lax.axis_index("section") % 2
    place = jnp.stack([group, core]).astype(jnp.int32)
    swap_core = [(s, s ^ 1) for s in range(sections)]
    swap_head = [(0, 1), (1, 0)]
    onward, back = ring_moves(sections)
    half_way = chips // 2

    mask = lax.dynamic_slice_in_dim(text_mask, core * text, text, 0).astype(F32).reshape(1, text)
    query_gain, key_gain = query_gain.reshape(1, -1), key_gain.reshape(1, -1)

    def ring_step(up, down, *after):
        up, down = lax.optimization_barrier((up, down) + after)[:2]
        return lax.ppermute(up, "section", onward), lax.ppermute(down, "section", back)

    ring = [ring_step(stale_cache, stale_cache)]

    step_heads = 2 if heads % 2 == 0 else 1
    columns = step_heads * TRIPLE
    steps = heads // step_heads
    weight_bytes = features * group_columns * 2
    project_flops = 2 * rows * features * group_columns
    a_rows, message, text_message, stats = pl.pallas_call(
        send_kernel,
        grid_spec=pltpu.PrefetchScalarGridSpec(
            num_scalar_prefetch=1,
            grid=(steps,),
            in_specs=[
                full(video, features),
                pl.BlockSpec((text, features), lambda h, p: (p[1], 0)),
                full(1, features),
                full(1, features),
                pl.BlockSpec((features, columns), lambda h, p: (0, (1 - p[0]) * steps + h)),
            ],
            out_specs=[
                full(rows, features),
                full(top, group_columns + HEAD_DIM),
                full(text, 2 * width + HEAD_DIM),
                full(rows, HEAD_DIM),
            ],
        ),
        out_shape=[
            jax.ShapeDtypeStruct((rows, features), BF16),
            jax.ShapeDtypeStruct((top, group_columns + HEAD_DIM), BF16),
            jax.ShapeDtypeStruct((text, 2 * width + HEAD_DIM), BF16),
            jax.ShapeDtypeStruct((rows, HEAD_DIM), F32),
        ],
        compiler_params=params(50),
        cost_estimate=cost(project_flops, weight_bytes),
        name="project_send",
    )(place, hidden, text_hidden, norm_scale.reshape(1, -1), norm_shift.reshape(1, -1), qkv_weight)

    received = lax.ppermute(message, "head", swap_head)
    text_received = lax.ppermute(text_message, "head", swap_head)
    ring.append(ring_step(*ring[-1], message, text_message))

    own, own_text = pl.pallas_call(
        own_kernel,
        grid_spec=pltpu.PrefetchScalarGridSpec(
            num_scalar_prefetch=1,
            grid=(steps,),
            in_specs=[
                full(rows, features),
                pl.BlockSpec((features, columns), lambda h, p: (0, p[0] * steps + h)),
            ],
            out_specs=[
                pl.BlockSpec((top, columns), lambda h, p: (0, h)),
                pl.BlockSpec((text, step_heads * 2 * HEAD_DIM), lambda h, p: (0, h)),
            ],
        ),
        out_shape=[
            jax.ShapeDtypeStruct((top, group_columns), F32),
            jax.ShapeDtypeStruct((text, 2 * width), F32),
        ],
        compiler_params=params(50),
        cost_estimate=cost(project_flops, weight_bytes),
        name="project_own",
    )(place, a_rows, qkv_weight)

    for _ in range(half_way - 3):
        ring.append(ring_step(*ring[-1], own))
    arrived = [block for step in ring for block in step]
    far_keys = lax.ppermute(ring[-1][0][0], "section", onward)
    far_values = lax.ppermute(ring[-1][1][1], "section", back)

    queries, new_cache, fresh = plain_call(
        functools.partial(norm_kernel, features * 2),
        [((video, width), BF16), ((2, video, width), BF16), ((2, video, width), BF16)],
        "norm_video",
        cost(20 * top * group_columns, 8 * top * group_columns),
        own, received, stats, query_gain, key_gain,
    )
    other_queries = lax.ppermute(queries, "section", swap_core)
    (text_kv,) = plain_call(
        functools.partial(text_kernel, features * 2),
        [((2, text, width), BF16)],
        "norm_text",
        cost(20 * text * group_columns, 8 * text * group_columns),
        own_text, received, stats, own, text_received, key_gain,
    )

    context = (len(arrived) + 1) * video + text
    vmem = pl.BlockSpec(memory_space=pltpu.VMEM)
    num, den, w_own, w_other = pl.pallas_call(
        functools.partial(first_kernel, len(arrived)),
        in_specs=[pl.BlockSpec(memory_space=pltpu.SMEM), pl.BlockSpec(memory_space=pl.ANY)]
        + [vmem] * (6 + len(arrived)),
        out_specs=[vmem] * 4,
        out_shape=[
            jax.ShapeDtypeStruct((2 * video, width), F32),
            jax.ShapeDtypeStruct((2 * video, HEAD_DIM), F32),
            jax.ShapeDtypeStruct((width, out_features), BF16),
            jax.ShapeDtypeStruct((width, out_features), BF16),
        ],
        scratch_shapes=[pltpu.SemaphoreType.DMA((2,))],
        compiler_params=params(24),
        cost_estimate=cost(
            8 * video * context * width, 4 * context * width, 2 * video * context * heads
        ),
        name="attend_first",
    )(
        place[:1], out_weight, queries, other_queries, fresh, stale_cache, text_kv, mask, *arrived
    )
    num_own, den_own, num_message = plain_call(
        last_kernel,
        [((video, width), F32), ((video, HEAD_DIM), F32), ((video, width + HEAD_DIM), F32)],
        "attend_last",
        cost(8 * video * video * width, 12 * video * width, 2 * video * video * heads),
        queries, other_queries, num, den, far_keys, far_values,
    )

    num_received = lax.ppermute(num_message, "section", swap_core)
    (attended,) = plain_call(
        merge_kernel,
        [((video, width), BF16)],
        "merge",
        cost(4 * video * width, 10 * video * width),
        num_own, den_own, num_received,
    )
    other_attended = lax.ppermute(attended, "head", swap_head)

    out_cost = cost(2 * video * width * out_features, 2 * width * out_features)
    (part,) = plain_call(
        part_kernel, [((video, out_features), F32)], "part_out", out_cost, attended, w_own
    )
    (mixed,) = plain_call(
        final_kernel, [((video, out_features), BF16)], "final_out", out_cost,
        part, other_attended, w_other, hidden, branch_gate.reshape(1, -1),
    )
    return (mixed, new_cache)


def solution(mesh):
    in_specs = (
        P("section", "head"),
        P(None, "head"),
        P(),
        P(None, "section", "head"),
        P("head", None),
        P(None, "head"),
        P(),
        P(),
        P("head"),
        P("head"),
        P("head"),
    )
    out_specs = (P("section", "head"), P(None, "section", "head"))
    return jax.shard_map(
        functools.partial(per_device, mesh.shape["section"]),
        mesh=mesh, in_specs=in_specs, out_specs=out_specs, check_vma=False,
    )
```

```python
import functools
import math

import jax
import jax.numpy as jnp
from jax import lax
from jax.experimental import pallas as pl
from jax.experimental.pallas import tpu as pltpu
from jax.sharding import PartitionSpec as P

HEAD_DIM = 128
TRIPLE = 3 * HEAD_DIM
EXTRA = 16
STAT_ROW = 8
EPS = 1e-06
F32 = jnp.float32
BF16 = jnp.bfloat16


def split_bf16(value, parts):
    pieces = []
    rest = value
    for _ in range(parts):
        piece = rest.astype(BF16)
        pieces.append(piece)
        rest = rest - piece.astype(F32)
    return pieces


def start_weights(w_ref, buffer_ref, sems, first):
    count, _, columns = buffer_ref.shape
    copies = []
    for index in range(count):
        start = pl.multiple_of(first + index * columns, HEAD_DIM)
        copy = pltpu.make_async_copy(
            w_ref.at[:, pl.ds(start, columns)], buffer_ref.at[index], sems.at[index]
        )
        copy.start()
        copies.append(copy)
    return copies


def send_kernel(
    place_ref, x_ref, t_ref, scale_ref, shift_ref, w_ref,
    a_ref, msg_ref, stat_ref, x_buffer, t_buffer, w_buffer, in_sems, w_sems,
):
    video, features = x_buffer.shape
    text = t_buffer.shape[0]
    top = video + EXTRA
    blocks, _, columns = w_buffer.shape
    width = blocks * columns
    x_copy = pltpu.make_async_copy(x_ref, x_buffer, in_sems.at[0])
    t_copy = pltpu.make_async_copy(
        t_ref.at[pl.ds(pl.multiple_of(place_ref[1] * text, text), text)], t_buffer, in_sems.at[1]
    )
    x_copy.start()
    t_copy.start()
    w_copies = start_weights(w_ref, w_buffer, w_sems, (1 - place_ref[0]) * width)

    gain = 1.0 + scale_ref[...].reshape(1, features)
    pieces = split_bf16(gain, 2) + split_bf16(shift_ref[...].reshape(1, features), 2)
    row = lax.broadcasted_iota(jnp.int32, (EXTRA, features), 0)
    extra = jnp.zeros((EXTRA, features), F32)
    for index, piece in enumerate(pieces):
        extra = jnp.where(row == index, piece.astype(F32), extra)
    a_ref[video:top, :] = extra.astype(BF16)

    def prepare(rows_ref, start):
        rows = rows_ref[...].astype(F32)
        count = rows.shape[0]
        mean = jnp.sum(rows, axis=1, keepdims=True) * (1.0 / features)
        centered = rows - mean
        second = jnp.sum(centered * centered, axis=1, keepdims=True)
        a_ref[start : start + count, :] = (centered * gain).astype(BF16)
        lane = lax.broadcasted_iota(jnp.int32, (count, HEAD_DIM), 1)
        packed = jnp.zeros((count, HEAD_DIM), F32)
        for index, piece in enumerate(split_bf16(mean, 3) + split_bf16(second, 3)):
            packed = jnp.where(lane == STAT_ROW + index, piece.astype(F32), packed)
        stat_ref[start : start + count, :] = jnp.where(
            lane == 0, mean, jnp.where(lane == 1, second, 0.0)
        )
        return jnp.transpose(packed)[:EXTRA]

    x_copy.wait()
    video_stats = prepare(x_buffer, 0)
    t_copy.wait()
    text_stats = prepare(t_buffer, top)
    stat_ref[video:top, :] = jnp.zeros((EXTRA, HEAD_DIM), F32)

    heads = columns // TRIPLE
    for block in range(blocks):
        w_copies[block].wait()
        product = jnp.dot(a_ref[...], w_buffer[block], preferred_element_type=F32)
        start = block * columns
        msg_ref[:top, start : start + columns] = product[:top].astype(BF16)
        if block == 0:
            msg_ref[video:top, : video + text] = (
                product[video:top, : video + text]
                + jnp.concatenate([video_stats, text_stats], axis=1)
            ).astype(BF16)
        for head in range(heads):
            pair = product[top:, head * TRIPLE + HEAD_DIM : (head + 1) * TRIPLE].astype(BF16)
            for quarter in range(4):
                rows, cells = text_slot(text, width, block * heads + head, quarter)
                msg_ref[top + rows.start : top + rows.stop, cells] = pair[
                    quarter * text // 4 : (quarter + 1) * text // 4
                ]


def text_slot(text, width, head, quarter):
    slots = width // (2 * HEAD_DIM)
    band, slot = divmod(head * 4 + quarter, slots)
    depth = text // 4
    return (
        slice(band * depth, (band + 1) * depth),
        slice(slot * 2 * HEAD_DIM, (slot + 1) * 2 * HEAD_DIM),
    )


def own_kernel(place_ref, a_ref, w_ref, out_ref, text_ref, w_buffer, w_sems):
    top = out_ref.shape[0]
    blocks, _, columns = w_buffer.shape
    heads = columns // TRIPLE
    w_copies = start_weights(w_ref, w_buffer, w_sems, place_ref[0] * blocks * columns)
    for block in range(blocks):
        w_copies[block].wait()
        product = jnp.dot(a_ref[...], w_buffer[block], preferred_element_type=F32)
        out_ref[:, block * columns : (block + 1) * columns] = product[:top]
        for index in range(heads):
            start = (block * heads + index) * 2 * HEAD_DIM
            text_ref[:, start : start + 2 * HEAD_DIM] = product[
                top:, index * TRIPLE + HEAD_DIM : (index + 1) * TRIPLE
            ]


def row_stats(total_features, own, received):
    count = own.shape[0]
    received = received.astype(F32)
    padding = jnp.zeros((HEAD_DIM - received.shape[0], count), F32)
    received = jnp.transpose(jnp.concatenate([received, padding], axis=0))
    parts = [received[:, STAT_ROW + index : STAT_ROW + index + 1] for index in range(6)]
    gap = 0.5 * (own[:, 0:1] - (parts[0] + parts[1] + parts[2]))
    second = own[:, 1:2] + (parts[3] + parts[4] + parts[5])
    var = second * (1.0 / total_features) + gap * gap
    return gap, lax.rsqrt(var + EPS)


def column_terms(own, other):
    other = other.astype(F32)
    scale = (own[0:1] + own[1:2]) - (other[0:1] + other[1:2])
    shift = (own[2:3] + own[3:4]) + (other[2:3] + other[3:4])
    return scale, shift


def head_norm(part, gain):
    square = jnp.sum(part * part, axis=1, keepdims=True) * (1.0 / HEAD_DIM)
    return part * lax.rsqrt(square + EPS) * gain


def norm_kernel(
    total_features, own_ref, msg_ref, stat_ref, qg_ref, kg_ref, q_ref, cache_ref, kv_ref,
):
    video = q_ref.shape[0]
    top = video + EXTRA
    heads = q_ref.shape[1] // HEAD_DIM
    gap, inverse = row_stats(total_features, stat_ref[:video, :], msg_ref[video:top, :video])
    for head in range(heads):
        part = slice(head * TRIPLE, (head + 1) * TRIPLE)
        columns = slice(head * HEAD_DIM, (head + 1) * HEAD_DIM)
        scale, shift = column_terms(own_ref[video:, part], msg_ref[video:top, part])
        total = own_ref[:video, part] + msg_ref[:video, part].astype(F32)
        total = (total + gap * scale) * inverse + shift
        q_ref[:, columns] = head_norm(total[:, :HEAD_DIM], qg_ref[...]).astype(BF16)
        keys = head_norm(total[:, HEAD_DIM : 2 * HEAD_DIM], kg_ref[...]).astype(BF16)
        values = total[:, 2 * HEAD_DIM :].astype(BF16)
        cache_ref[0, :, columns] = keys
        cache_ref[1, :, columns] = values
        kv_ref[0, :, columns] = keys
        kv_ref[1, :, columns] = values


def text_kernel(total_features, own_ref, msg_ref, stat_ref, top_ref, kg_ref, kv_ref):
    text = kv_ref.shape[1]
    heads = kv_ref.shape[2] // HEAD_DIM
    top, width = top_ref.shape
    video = top - EXTRA
    gap, inverse = row_stats(
        total_features, stat_ref[top:, :], msg_ref[video:top, video : video + text]
    )
    for head in range(heads):
        part = slice(head * TRIPLE + HEAD_DIM, (head + 1) * TRIPLE)
        pair = slice(head * 2 * HEAD_DIM, (head + 1) * 2 * HEAD_DIM)
        columns = slice(head * HEAD_DIM, (head + 1) * HEAD_DIM)
        scale, shift = column_terms(top_ref[video:, part], msg_ref[video:top, part])
        other = []
        for quarter in range(4):
            rows, cells = text_slot(text, width, head, quarter)
            other.append(msg_ref[top + rows.start : top + rows.stop, cells])
        total = own_ref[:, pair] + jnp.concatenate(other, axis=0).astype(F32)
        total = (total + gap * scale) * inverse + shift
        kv_ref[0, :, columns] = head_norm(total[:, :HEAD_DIM], kg_ref[...]).astype(BF16)
        kv_ref[1, :, columns] = total[:, HEAD_DIM:].astype(BF16)


FACTOR = math.log2(math.e) / math.sqrt(HEAD_DIM)


def weigh(rows, keys):
    scores = lax.dot_general(rows, keys, (((1,), (1,)), ((), ())), preferred_element_type=F32)
    return jnp.exp2(scores * FACTOR)


def lanes(weights):
    total = weights[:, :HEAD_DIM]
    for start in range(HEAD_DIM, weights.shape[1], HEAD_DIM):
        total = total + weights[:, start : start + HEAD_DIM]
    return total


def times(weights, values):
    return jnp.dot(weights.astype(BF16), values, preferred_element_type=F32)


def absorb(queries, blocks, num, den, columns):
    for first in range(0, len(blocks), 2):
        pair = blocks[first : first + 2]
        keys = jnp.concatenate([k(columns) for k, _ in pair], axis=0)
        values = jnp.concatenate([v(columns) for _, v in pair], axis=0)
        weights = weigh(queries, keys)
        num = num + times(weights, values)
        den = den + lanes(weights)
    return num, den


def loaders(ref):
    return (lambda columns: ref[0, :, columns]), (lambda columns: ref[1, :, columns])


def first_kernel(
    count, group_ref, weight_ref, qo_ref, qp_ref, fresh_ref, stale_ref, text_ref, mask_ref, *refs
):
    ring = refs[:count]
    num_ref, den_ref, w_own_ref, w_other_ref, stale_buffer, sems = refs[count:]
    depth = w_own_ref.shape[0]
    group = group_ref[0]
    stale_copy = pltpu.make_async_copy(stale_ref, stale_buffer, sems.at[2])
    stale_copy.start()
    copies = []
    for index, (half, target) in enumerate(((group, w_own_ref), (1 - group, w_other_ref))):
        source = weight_ref.at[pl.ds(pl.multiple_of(half * depth, depth), depth)]
        copies.append(pltpu.make_async_copy(source, target, sems.at[index]))
    for copy in copies:
        copy.start()
    video, width = qo_ref.shape
    lane = lax.broadcasted_iota(jnp.int32, (2 * video, HEAD_DIM), 1)
    packed = jnp.zeros((2 * video, HEAD_DIM), F32)
    stale_copy.wait()
    for head in range(width // HEAD_DIM):
        columns = slice(head * HEAD_DIM, (head + 1) * HEAD_DIM)
        own, other = qo_ref[:, columns], qp_ref[:, columns]
        queries = jnp.concatenate([own, other], axis=0)
        fresh = weigh(own, fresh_ref[0, :, columns])
        stale = weigh(other, stale_buffer[0, :, columns])
        num = jnp.concatenate(
            [times(fresh, fresh_ref[1, :, columns]), times(stale, stale_buffer[1, :, columns])], axis=0
        )
        den = jnp.concatenate([fresh, stale], axis=0)
        weights = weigh(queries, text_ref[0, :, columns]) * mask_ref[...]
        num = num + times(weights, text_ref[1, :, columns])
        den = den + lanes(weights)
        num, den = absorb(queries, [loaders(ref) for ref in ring], num, den, columns)
        num_ref[:, columns] = num
        packed = jnp.where(lane == head, jnp.sum(den, axis=1, keepdims=True), packed)
    den_ref[...] = packed
    for copy in copies:
        copy.wait()


def last_kernel(qo_ref, qp_ref, num_ref, den_ref, kv_ref, own_ref, own_den_ref, msg_ref):
    video, width = qo_ref.shape
    lane = lax.broadcasted_iota(jnp.int32, (2 * video, HEAD_DIM), 1)
    packed = den_ref[...]
    for head in range(width // HEAD_DIM):
        columns = slice(head * HEAD_DIM, (head + 1) * HEAD_DIM)
        queries = jnp.concatenate([qo_ref[:, columns], qp_ref[:, columns]], axis=0)
        weights = weigh(queries, kv_ref[0, :, columns])
        num = num_ref[:, columns] + times(weights, kv_ref[1, :, columns])
        own_ref[:, columns] = num[:video]
        msg_ref[:, columns] = num[video:]
        total = jnp.sum(lanes(weights), axis=1, keepdims=True)
        packed = packed + jnp.where(lane == head, total, 0.0)
    own_den_ref[...] = packed[:video]
    msg_ref[:, width:] = packed[video:]


def merge_kernel(own_ref, den_ref, msg_ref, att_ref):
    width = att_ref.shape[1]
    for head in range(width // HEAD_DIM):
        columns = slice(head * HEAD_DIM, (head + 1) * HEAD_DIM)
        num = own_ref[:, columns] + msg_ref[:, columns]
        den = den_ref[:, head : head + 1] + msg_ref[:, width + head : width + head + 1]
        att_ref[:, columns] = (num / den).astype(BF16)


def part_kernel(att_ref, w_ref, out_ref):
    out_ref[...] = jnp.dot(att_ref[...], w_ref[...], preferred_element_type=F32)


def final_kernel(part_ref, att_ref, w_ref, hidden_ref, gate_ref, out_ref):
    total = part_ref[...] + jnp.dot(att_ref[...], w_ref[...], preferred_element_type=F32)
    out_ref[...] = (hidden_ref[...].astype(F32) + gate_ref[...] * total).astype(BF16)


def params(megabytes):
    return pltpu.CompilerParams(vmem_limit_bytes=megabytes * 1024 * 1024)


def cost(flops, nbytes, transcendentals=0):
    return pl.CostEstimate(
        flops=int(flops), bytes_accessed=int(nbytes), transcendentals=int(transcendentals)
    )


def plain_call(kernel, outs, name, estimate, *operands):
    return pl.pallas_call(
        kernel,
        in_specs=[pl.BlockSpec(memory_space=pltpu.VMEM)] * len(operands),
        out_specs=[pl.BlockSpec(memory_space=pltpu.VMEM)] * len(outs),
        out_shape=[jax.ShapeDtypeStruct(shape, dtype) for shape, dtype in outs],
        compiler_params=params(24),
        cost_estimate=estimate,
        name=name,
    )(*operands)


def ring_moves(sections):
    chips = sections // 2
    order = list(range(0, chips, 2)) + list(range(chips - 1, 0, -2))
    moves = [], []
    for here, there in zip(order, order[1:] + order[:1]):
        for core in range(2):
            moves[core].append((2 * here + core, 2 * there + core))
            moves[1 - core].append((2 * there + core, 2 * here + core))
    return sorted(moves[0]), sorted(moves[1])


def per_device(
    sections, hidden, text_hidden, text_mask, stale_cache, qkv_weight, out_weight, query_gain,
    key_gain, norm_shift, norm_scale, branch_gate,
):
    video, features = hidden.shape
    text = text_hidden.shape[0] // 2
    width = stale_cache.shape[2]
    heads = width // HEAD_DIM
    group_columns = heads * TRIPLE
    chips = sections // 2
    out_features = out_weight.shape[1]
    top = video + EXTRA
    rows = top + text

    group = lax.axis_index("head")
    core = lax.axis_index("section") % 2
    place = jnp.stack([group, core]).astype(jnp.int32)
    swap_core = [(s, s ^ 1) for s in range(sections)]
    swap_head = [(0, 1), (1, 0)]
    first_way, second_way = ring_moves(sections)
    half_way = chips // 2

    mask = lax.dynamic_slice_in_dim(text_mask, core * text, text, 0).astype(F32).reshape(1, text)
    query_gain, key_gain = query_gain.reshape(1, -1), key_gain.reshape(1, -1)

    def ring_step(up, down, *after):
        up, down = lax.optimization_barrier((up, down) + after)[:2]
        return lax.ppermute(up, "section", first_way), lax.ppermute(down, "section", second_way)

    ring = [ring_step(stale_cache, stale_cache)]

    block_heads = 2 if heads % 2 == 0 else 1
    columns = block_heads * TRIPLE
    blocks = heads // block_heads
    bands = -(-heads * 4 // (group_columns // (2 * HEAD_DIM)))
    message_rows = top + bands * text // 4
    project_cost = cost(2 * rows * features * group_columns, 2 * features * group_columns)
    vmem = pl.BlockSpec(memory_space=pltpu.VMEM)
    hbm = pl.BlockSpec(memory_space=pltpu.HBM)
    smem = pl.BlockSpec(memory_space=pltpu.SMEM)
    weight_scratch = [
        pltpu.VMEM((blocks, features, columns), BF16),
        pltpu.SemaphoreType.DMA((blocks,)),
    ]
    a_rows, message, stats = pl.pallas_call(
        send_kernel,
        in_specs=[smem, hbm, hbm, vmem, vmem, hbm],
        out_specs=[vmem] * 3,
        out_shape=[
            jax.ShapeDtypeStruct((rows, features), BF16),
            jax.ShapeDtypeStruct((message_rows, group_columns), BF16),
            jax.ShapeDtypeStruct((rows, HEAD_DIM), F32),
        ],
        scratch_shapes=[
            pltpu.VMEM((video, features), BF16),
            pltpu.VMEM((text, features), BF16),
            weight_scratch[0],
            pltpu.SemaphoreType.DMA((2,)),
            weight_scratch[1],
        ],
        compiler_params=params(40),
        cost_estimate=project_cost,
        name="project_send",
    )(place, hidden, text_hidden, norm_scale, norm_shift, qkv_weight)

    received = lax.ppermute(message, "head", swap_head)
    ring.append(ring_step(*ring[-1], message))

    own, own_text = pl.pallas_call(
        own_kernel,
        in_specs=[smem, vmem, hbm],
        out_specs=[vmem] * 2,
        out_shape=[
            jax.ShapeDtypeStruct((top, group_columns), F32),
            jax.ShapeDtypeStruct((text, 2 * width), F32),
        ],
        scratch_shapes=weight_scratch,
        compiler_params=params(40),
        cost_estimate=project_cost,
        name="project_own",
    )(place, a_rows, qkv_weight)

    for _ in range(half_way - 3):
        ring.append(ring_step(*ring[-1], own))
    arrived = [block for step in ring for block in step]
    far = lax.ppermute(ring[-1][0], "section", first_way)

    queries, new_cache, fresh = plain_call(
        functools.partial(norm_kernel, features * 2),
        [((video, width), BF16), ((2, video, width), BF16), ((2, video, width), BF16)],
        "norm_video",
        cost(20 * top * group_columns, 8 * top * group_columns),
        own, received, stats, query_gain, key_gain,
    )
    other_queries = lax.ppermute(queries, "section", swap_core)
    (text_kv,) = plain_call(
        functools.partial(text_kernel, features * 2),
        [((2, text, width), BF16)],
        "norm_text",
        cost(20 * text * group_columns, 8 * text * group_columns),
        own_text, received, stats, own, key_gain,
    )

    context = (len(arrived) + 1) * video + text
    num, den, w_own, w_other = pl.pallas_call(
        functools.partial(first_kernel, len(arrived)),
        in_specs=[smem, hbm] + [vmem] * 3 + [hbm] + [vmem] * (2 + len(arrived)),
        out_specs=[vmem] * 4,
        out_shape=[
            jax.ShapeDtypeStruct((2 * video, width), F32),
            jax.ShapeDtypeStruct((2 * video, HEAD_DIM), F32),
            jax.ShapeDtypeStruct((width, out_features), BF16),
            jax.ShapeDtypeStruct((width, out_features), BF16),
        ],
        scratch_shapes=[
            pltpu.VMEM(stale_cache.shape, BF16),
            pltpu.SemaphoreType.DMA((3,)),
        ],
        compiler_params=params(24),
        cost_estimate=cost(
            8 * video * context * width, 4 * context * width, 2 * video * context * heads
        ),
        name="attend_first",
    )(
        place[:1], out_weight, queries, other_queries, fresh, stale_cache, text_kv, mask, *arrived
    )
    num_own, den_own, num_message = plain_call(
        last_kernel,
        [((video, width), F32), ((video, HEAD_DIM), F32), ((video, width + HEAD_DIM), F32)],
        "attend_last",
        cost(8 * video * video * width, 12 * video * width, 2 * video * video * heads),
        queries, other_queries, num, den, far,
    )

    num_received = lax.ppermute(num_message, "section", swap_core)
    (attended,) = plain_call(
        merge_kernel,
        [((video, width), BF16)],
        "merge",
        cost(4 * video * width, 10 * video * width),
        num_own, den_own, num_received,
    )
    other_attended = lax.ppermute(attended, "head", swap_head)

    out_cost = cost(2 * video * width * out_features, 2 * width * out_features)
    (part,) = plain_call(
        part_kernel, [((video, out_features), F32)], "part_out", out_cost, attended, w_own
    )
    (mixed,) = plain_call(
        final_kernel, [((video, out_features), BF16)], "final_out", out_cost,
        part, other_attended, w_other, hidden, branch_gate.reshape(1, -1),
    )
    return (mixed, new_cache)


def solution(mesh):
    in_specs = (
        P("section", "head"),
        P(None, "head"),
        P(),
        P(None, "section", "head"),
        P("head", None),
        P(None, "head"),
        P(),
        P(),
        P("head"),
        P("head"),
        P("head"),
    )
    out_specs = (P("section", "head"), P(None, "section", "head"))
    return jax.shard_map(
        functools.partial(per_device, mesh.shape["section"]),
        mesh=mesh, in_specs=in_specs, out_specs=out_specs, check_vma=False,
    )
```

```python
import functools
import math

import jax
import jax.numpy as jnp
from jax import lax
from jax.experimental import pallas as pl
from jax.experimental.pallas import tpu as pltpu
from jax.sharding import PartitionSpec as P

HEAD_DIM = 128
TRIPLE = 3 * HEAD_DIM
EXTRA = 16
STAT_ROW = 8
EPS = 1e-06
F32 = jnp.float32
BF16 = jnp.bfloat16


def split_bf16(value, parts):
    pieces = []
    rest = value
    for _ in range(parts):
        piece = rest.astype(BF16)
        pieces.append(piece)
        rest = rest - piece.astype(F32)
    return pieces


def start_weights(w_ref, buffer_ref, sems, first):
    count, _, columns = buffer_ref.shape
    copies = []
    for index in range(count):
        start = pl.multiple_of(first + index * columns, HEAD_DIM)
        copy = pltpu.make_async_copy(
            w_ref.at[:, pl.ds(start, columns)], buffer_ref.at[index], sems.at[index]
        )
        copy.start()
        copies.append(copy)
    return copies


def send_kernel(
    place_ref, x_ref, t_ref, scale_ref, shift_ref, w_ref,
    a_ref, msg_ref, stat_ref, x_buffer, t_buffer, scale_buffer, shift_buffer, w_buffer,
    in_sems, w_sems,
):
    video, features = x_buffer.shape
    text = t_buffer.shape[0]
    top = video + EXTRA
    blocks, _, columns = w_buffer.shape
    width = blocks * columns
    x_copy = pltpu.make_async_copy(x_ref, x_buffer, in_sems.at[0])
    t_copy = pltpu.make_async_copy(
        t_ref.at[pl.ds(pl.multiple_of(place_ref[1] * text, text), text)], t_buffer, in_sems.at[1]
    )
    scale_copy = pltpu.make_async_copy(scale_ref, scale_buffer, in_sems.at[2])
    shift_copy = pltpu.make_async_copy(shift_ref, shift_buffer, in_sems.at[3])
    for copy in (scale_copy, shift_copy, x_copy, t_copy):
        copy.start()
    w_copies = start_weights(w_ref, w_buffer, w_sems, (1 - place_ref[0]) * width)

    scale_copy.wait()
    shift_copy.wait()
    gain = 1.0 + scale_buffer[...].reshape(1, features)
    pieces = split_bf16(gain, 2) + split_bf16(shift_buffer[...].reshape(1, features), 2)
    row = lax.broadcasted_iota(jnp.int32, (EXTRA, features), 0)
    extra = jnp.zeros((EXTRA, features), F32)
    for index, piece in enumerate(pieces):
        extra = jnp.where(row == index, piece.astype(F32), extra)
    a_ref[video:top, :] = extra.astype(BF16)

    def prepare(rows_ref, start):
        rows = rows_ref[...].astype(F32)
        count = rows.shape[0]
        mean = jnp.sum(rows, axis=1, keepdims=True) * (1.0 / features)
        centered = rows - mean
        second = jnp.sum(centered * centered, axis=1, keepdims=True)
        a_ref[start : start + count, :] = (centered * gain).astype(BF16)
        lane = lax.broadcasted_iota(jnp.int32, (count, HEAD_DIM), 1)
        packed = jnp.zeros((count, HEAD_DIM), F32)
        for index, piece in enumerate(split_bf16(mean, 3) + split_bf16(second, 3)):
            packed = jnp.where(lane == STAT_ROW + index, piece.astype(F32), packed)
        stat_ref[start : start + count, :] = jnp.where(
            lane == 0, mean, jnp.where(lane == 1, second, 0.0)
        )
        return jnp.transpose(packed)[:EXTRA]

    x_copy.wait()
    video_stats = prepare(x_buffer, 0)
    t_copy.wait()
    text_stats = prepare(t_buffer, top)
    stat_ref[video:top, :] = jnp.zeros((EXTRA, HEAD_DIM), F32)

    heads = columns // TRIPLE
    for block in range(blocks):
        w_copies[block].wait()
        product = jnp.dot(a_ref[...], w_buffer[block], preferred_element_type=F32)
        start = block * columns
        msg_ref[:top, start : start + columns] = product[:top].astype(BF16)
        if block == 0:
            msg_ref[video:top, : video + text] = (
                product[video:top, : video + text]
                + jnp.concatenate([video_stats, text_stats], axis=1)
            ).astype(BF16)
        for head in range(heads):
            pair = product[top:, head * TRIPLE + HEAD_DIM : (head + 1) * TRIPLE].astype(BF16)
            for quarter in range(4):
                rows, cells = text_slot(text, width, block * heads + head, quarter)
                msg_ref[top + rows.start : top + rows.stop, cells] = pair[
                    quarter * text // 4 : (quarter + 1) * text // 4
                ]


def text_slot(text, width, head, quarter):
    slots = width // (2 * HEAD_DIM)
    band, slot = divmod(head * 4 + quarter, slots)
    depth = text // 4
    return (
        slice(band * depth, (band + 1) * depth),
        slice(slot * 2 * HEAD_DIM, (slot + 1) * 2 * HEAD_DIM),
    )


def own_kernel(place_ref, a_ref, w_ref, *refs):
    small = (len(refs) - 5) // 2
    out_ref, text_ref = refs[small : small + 2]
    w_buffer, w_sems, sems = refs[-3:]
    top = out_ref.shape[0]
    blocks, _, columns = w_buffer.shape
    heads = columns // TRIPLE
    w_copies = start_weights(w_ref, w_buffer, w_sems, place_ref[0] * blocks * columns)
    copies = []
    for index, (source, target) in enumerate(zip(refs[:small], refs[small + 2 : -3])):
        copies.append(pltpu.make_async_copy(source, target, sems.at[index]))
        copies[-1].start()
    for block in range(blocks):
        w_copies[block].wait()
        product = jnp.dot(a_ref[...], w_buffer[block], preferred_element_type=F32)
        out_ref[:, block * columns : (block + 1) * columns] = product[:top]
        for index in range(heads):
            start = (block * heads + index) * 2 * HEAD_DIM
            text_ref[:, start : start + 2 * HEAD_DIM] = product[
                top:, index * TRIPLE + HEAD_DIM : (index + 1) * TRIPLE
            ]
    for copy in copies:
        copy.wait()


def row_stats(total_features, own, received):
    count = own.shape[0]
    received = received.astype(F32)
    padding = jnp.zeros((HEAD_DIM - received.shape[0], count), F32)
    received = jnp.transpose(jnp.concatenate([received, padding], axis=0))
    parts = [received[:, STAT_ROW + index : STAT_ROW + index + 1] for index in range(6)]
    gap = 0.5 * (own[:, 0:1] - (parts[0] + parts[1] + parts[2]))
    second = own[:, 1:2] + (parts[3] + parts[4] + parts[5])
    var = second * (1.0 / total_features) + gap * gap
    return gap, lax.rsqrt(var + EPS)


def column_terms(own, other):
    other = other.astype(F32)
    scale = (own[0:1] + own[1:2]) - (other[0:1] + other[1:2])
    shift = (own[2:3] + own[3:4]) + (other[2:3] + other[3:4])
    return scale, shift


def head_norm(part, gain):
    square = jnp.sum(part * part, axis=1, keepdims=True) * (1.0 / HEAD_DIM)
    return part * lax.rsqrt(square + EPS) * gain


def norm_kernel(
    total_features, own_ref, msg_ref, stat_ref, qg_ref, kg_ref, q_ref, cache_ref, kv_ref,
):
    video = q_ref.shape[0]
    top = video + EXTRA
    query_gain = qg_ref[...].reshape(1, HEAD_DIM)
    key_gain = kg_ref[...].reshape(1, HEAD_DIM)
    heads = q_ref.shape[1] // HEAD_DIM
    gap, inverse = row_stats(total_features, stat_ref[:video, :], msg_ref[video:top, :video])
    for head in range(heads):
        part = slice(head * TRIPLE, (head + 1) * TRIPLE)
        columns = slice(head * HEAD_DIM, (head + 1) * HEAD_DIM)
        scale, shift = column_terms(own_ref[video:, part], msg_ref[video:top, part])
        total = own_ref[:video, part] + msg_ref[:video, part].astype(F32)
        total = (total + gap * scale) * inverse + shift
        q_ref[:, columns] = head_norm(total[:, :HEAD_DIM], query_gain).astype(BF16)
        keys = head_norm(total[:, HEAD_DIM : 2 * HEAD_DIM], key_gain).astype(BF16)
        values = total[:, 2 * HEAD_DIM :].astype(BF16)
        cache_ref[0, :, columns] = keys
        cache_ref[1, :, columns] = values
        kv_ref[0, :, columns] = keys
        kv_ref[1, :, columns] = values


def text_kernel(total_features, own_ref, msg_ref, stat_ref, top_ref, kg_ref, kv_ref):
    text = kv_ref.shape[1]
    heads = kv_ref.shape[2] // HEAD_DIM
    top, width = top_ref.shape
    video = top - EXTRA
    key_gain = kg_ref[...].reshape(1, HEAD_DIM)
    gap, inverse = row_stats(
        total_features, stat_ref[top:, :], msg_ref[video:top, video : video + text]
    )
    for head in range(heads):
        part = slice(head * TRIPLE + HEAD_DIM, (head + 1) * TRIPLE)
        pair = slice(head * 2 * HEAD_DIM, (head + 1) * 2 * HEAD_DIM)
        columns = slice(head * HEAD_DIM, (head + 1) * HEAD_DIM)
        scale, shift = column_terms(top_ref[video:, part], msg_ref[video:top, part])
        other = []
        for quarter in range(4):
            rows, cells = text_slot(text, width, head, quarter)
            other.append(msg_ref[top + rows.start : top + rows.stop, cells])
        total = own_ref[:, pair] + jnp.concatenate(other, axis=0).astype(F32)
        total = (total + gap * scale) * inverse + shift
        kv_ref[0, :, columns] = head_norm(total[:, :HEAD_DIM], key_gain).astype(BF16)
        kv_ref[1, :, columns] = total[:, HEAD_DIM:].astype(BF16)


FACTOR = math.log2(math.e) / math.sqrt(HEAD_DIM)


def weigh(rows, keys):
    scores = lax.dot_general(rows, keys, (((1,), (1,)), ((), ())), preferred_element_type=F32)
    return jnp.exp2(scores * FACTOR)


def lanes(weights):
    total = weights[:, :HEAD_DIM]
    for start in range(HEAD_DIM, weights.shape[1], HEAD_DIM):
        total = total + weights[:, start : start + HEAD_DIM]
    return total


def times(weights, values):
    return jnp.dot(weights.astype(BF16), values, preferred_element_type=F32)


def absorb(queries, blocks, num, den, columns):
    for first in range(0, len(blocks), 2):
        pair = blocks[first : first + 2]
        keys = jnp.concatenate([k(columns) for k, _ in pair], axis=0)
        values = jnp.concatenate([v(columns) for _, v in pair], axis=0)
        weights = weigh(queries, keys)
        num = num + times(weights, values)
        den = den + lanes(weights)
    return num, den


def loaders(ref):
    return (lambda columns: ref[0, :, columns]), (lambda columns: ref[1, :, columns])


def first_kernel(
    count, place_ref, weight_ref, qo_ref, qp_ref, fresh_ref, stale_ref, text_ref, mask_ref, *refs
):
    ring = refs[:count]
    num_ref, den_ref, w_own_ref, w_other_ref, stale_buffer, sems = refs[count:]
    depth = w_own_ref.shape[0]
    group = place_ref[0]
    stale_copy = pltpu.make_async_copy(stale_ref, stale_buffer, sems.at[2])
    stale_copy.start()
    copies = []
    for index, (half, target) in enumerate(((group, w_own_ref), (1 - group, w_other_ref))):
        source = weight_ref.at[pl.ds(pl.multiple_of(half * depth, depth), depth)]
        copies.append(pltpu.make_async_copy(source, target, sems.at[index]))
    for copy in copies:
        copy.start()
    video, width = qo_ref.shape
    lane = lax.broadcasted_iota(jnp.int32, (2 * video, HEAD_DIM), 1)
    packed = jnp.zeros((2 * video, HEAD_DIM), F32)
    text = text_ref.shape[1]
    mask = mask_ref[...].reshape(1, 2 * text).astype(F32)
    mask = jnp.where(place_ref[1] == 0, mask[:, :text], mask[:, text:])
    for head in range(width // HEAD_DIM):
        columns = slice(head * HEAD_DIM, (head + 1) * HEAD_DIM)
        own = qo_ref[:, columns]
        queries = jnp.concatenate([own, qp_ref[:, columns]], axis=0)
        weights = weigh(queries, text_ref[0, :, columns]) * mask
        num = times(weights, text_ref[1, :, columns])
        den = lanes(weights)
        num, den = absorb(queries, [loaders(ref) for ref in ring], num, den, columns)
        fresh = weigh(own, fresh_ref[0, :, columns])
        num_ref[:video, columns] = num[:video] + times(fresh, fresh_ref[1, :, columns])
        num_ref[video:, columns] = num[video:]
        packed = jnp.where(
            lane == head,
            jnp.sum(jnp.concatenate([den[:video] + fresh, den[video:]], axis=0), axis=1, keepdims=True),
            packed,
        )
    stale_copy.wait()
    for head in range(width // HEAD_DIM):
        columns = slice(head * HEAD_DIM, (head + 1) * HEAD_DIM)
        stale = weigh(qp_ref[:, columns], stale_buffer[0, :, columns])
        num_ref[video:, columns] += times(stale, stale_buffer[1, :, columns])
        total = jnp.concatenate(
            [jnp.zeros((video, 1), F32), jnp.sum(stale, axis=1, keepdims=True)], axis=0
        )
        packed = packed + jnp.where(lane == head, total, 0.0)
    den_ref[...] = packed
    for copy in copies:
        copy.wait()


def last_kernel(qo_ref, qp_ref, num_ref, den_ref, kv_ref, own_ref, own_den_ref, msg_ref):
    video, width = qo_ref.shape
    lane = lax.broadcasted_iota(jnp.int32, (2 * video, HEAD_DIM), 1)
    packed = den_ref[...]
    for head in range(width // HEAD_DIM):
        columns = slice(head * HEAD_DIM, (head + 1) * HEAD_DIM)
        queries = jnp.concatenate([qo_ref[:, columns], qp_ref[:, columns]], axis=0)
        weights = weigh(queries, kv_ref[0, :, columns])
        num = num_ref[:, columns] + times(weights, kv_ref[1, :, columns])
        own_ref[:, columns] = num[:video]
        msg_ref[:, columns] = num[video:]
        total = jnp.sum(lanes(weights), axis=1, keepdims=True)
        packed = packed + jnp.where(lane == head, total, 0.0)
    own_den_ref[...] = packed[:video]
    msg_ref[:, width:] = packed[video:]


def merge_kernel(own_ref, den_ref, msg_ref, att_ref):
    width = att_ref.shape[1]
    for head in range(width // HEAD_DIM):
        columns = slice(head * HEAD_DIM, (head + 1) * HEAD_DIM)
        num = own_ref[:, columns] + msg_ref[:, columns]
        den = den_ref[:, head : head + 1] + msg_ref[:, width + head : width + head + 1]
        att_ref[:, columns] = (num / den).astype(BF16)


def part_kernel(att_ref, w_ref, out_ref):
    out_ref[...] = jnp.dot(att_ref[...], w_ref[...], preferred_element_type=F32)


def final_kernel(part_ref, att_ref, w_ref, hidden_ref, gate_ref, out_ref):
    total = part_ref[...] + jnp.dot(att_ref[...], w_ref[...], preferred_element_type=F32)
    gate = gate_ref[...].reshape(1, total.shape[1])
    out_ref[...] = (hidden_ref[...].astype(F32) + gate * total).astype(BF16)


def params(megabytes):
    return pltpu.CompilerParams(vmem_limit_bytes=megabytes * 1024 * 1024)


def in_hbm(array):
    return pltpu.with_memory_space_constraint(array, pltpu.HBM)


def cost(flops, nbytes, transcendentals=0):
    return pl.CostEstimate(
        flops=int(flops), bytes_accessed=int(nbytes), transcendentals=int(transcendentals)
    )


def plain_call(kernel, outs, name, estimate, *operands):
    return pl.pallas_call(
        kernel,
        in_specs=[pl.BlockSpec(memory_space=pltpu.VMEM)] * len(operands),
        out_specs=[pl.BlockSpec(memory_space=pltpu.VMEM)] * len(outs),
        out_shape=[jax.ShapeDtypeStruct(shape, dtype) for shape, dtype in outs],
        compiler_params=params(24),
        cost_estimate=estimate,
        name=name,
    )(*operands)


def ring_moves(sections):
    chips = sections // 2
    order = list(range(0, chips, 2)) + list(range(chips - 1, 0, -2))
    moves = [], []
    for here, there in zip(order, order[1:] + order[:1]):
        for core in range(2):
            moves[core].append((2 * here + core, 2 * there + core))
            moves[1 - core].append((2 * there + core, 2 * here + core))
    return sorted(moves[0]), sorted(moves[1])


def per_device(
    sections, hidden, text_hidden, text_mask, stale_cache, qkv_weight, out_weight, query_gain,
    key_gain, norm_shift, norm_scale, branch_gate,
):
    video, features = hidden.shape
    text = text_hidden.shape[0] // 2
    width = stale_cache.shape[2]
    heads = width // HEAD_DIM
    group_columns = heads * TRIPLE
    chips = sections // 2
    out_features = out_weight.shape[1]
    top = video + EXTRA
    rows = top + text

    group = lax.axis_index("head")
    core = lax.axis_index("section") % 2
    place = jnp.stack([group, core]).astype(jnp.int32)
    swap_core = [(s, s ^ 1) for s in range(sections)]
    swap_head = [(0, 1), (1, 0)]
    first_way, second_way = ring_moves(sections)
    half_way = chips // 2


    def ring_step(up, down, *after):
        up, down = lax.optimization_barrier((up, down) + after)[:2]
        return lax.ppermute(up, "section", first_way), lax.ppermute(down, "section", second_way)

    ring = [ring_step(stale_cache, stale_cache)]

    block_heads = 2 if heads % 2 == 0 else 1
    columns = block_heads * TRIPLE
    blocks = heads // block_heads
    bands = -(-heads * 4 // (group_columns // (2 * HEAD_DIM)))
    message_rows = top + bands * text // 4
    project_cost = cost(2 * rows * features * group_columns, 2 * features * group_columns)
    vmem = pl.BlockSpec(memory_space=pltpu.VMEM)
    hbm = pl.BlockSpec(memory_space=pltpu.HBM)
    smem = pl.BlockSpec(memory_space=pltpu.SMEM)
    weight_scratch = [
        pltpu.VMEM((blocks, features, columns), BF16),
        pltpu.SemaphoreType.DMA((blocks,)),
    ]
    a_rows, message, stats = pl.pallas_call(
        send_kernel,
        in_specs=[smem] + [hbm] * 5,
        out_specs=[vmem] * 3,
        out_shape=[
            jax.ShapeDtypeStruct((rows, features), BF16),
            jax.ShapeDtypeStruct((message_rows, group_columns), BF16),
            jax.ShapeDtypeStruct((rows, HEAD_DIM), F32),
        ],
        scratch_shapes=[
            pltpu.VMEM((video, features), BF16),
            pltpu.VMEM((text, features), BF16),
            pltpu.VMEM((features,), F32),
            pltpu.VMEM((features,), F32),
            weight_scratch[0],
            pltpu.SemaphoreType.DMA((4,)),
            weight_scratch[1],
        ],
        compiler_params=params(40),
        cost_estimate=project_cost,
        name="project_send",
    )(place, *map(in_hbm, (hidden, text_hidden, norm_scale, norm_shift, qkv_weight)))

    received = lax.ppermute(message, "head", swap_head)
    ring.append(ring_step(*ring[-1], message))

    small = (query_gain, key_gain, text_mask, branch_gate, hidden)
    own, own_text, query_gain, key_gain, text_mask, branch_gate, hidden = pl.pallas_call(
        own_kernel,
        in_specs=[smem, vmem, hbm] + [hbm] * len(small),
        out_specs=[vmem] * (2 + len(small)),
        out_shape=[
            jax.ShapeDtypeStruct((top, group_columns), F32),
            jax.ShapeDtypeStruct((text, 2 * width), F32),
        ]
        + [jax.ShapeDtypeStruct(array.shape, array.dtype) for array in small],
        scratch_shapes=weight_scratch + [pltpu.SemaphoreType.DMA((len(small),))],
        compiler_params=params(40),
        cost_estimate=project_cost,
        name="project_own",
    )(place, a_rows, *map(in_hbm, (qkv_weight,) + small))

    for _ in range(half_way - 3):
        ring.append(ring_step(*ring[-1], own))
    arrived = [block for step in ring for block in step]
    far = lax.ppermute(ring[-1][0], "section", first_way)

    queries, new_cache, fresh = plain_call(
        functools.partial(norm_kernel, features * 2),
        [((video, width), BF16), ((2, video, width), BF16), ((2, video, width), BF16)],
        "norm_video",
        cost(20 * top * group_columns, 8 * top * group_columns),
        own, received, stats, query_gain, key_gain,
    )
    other_queries = lax.ppermute(queries, "section", swap_core)
    (text_kv,) = plain_call(
        functools.partial(text_kernel, features * 2),
        [((2, text, width), BF16)],
        "norm_text",
        cost(20 * text * group_columns, 8 * text * group_columns),
        own_text, received, stats, own, key_gain,
    )

    context = (len(arrived) + 1) * video + text
    num, den, w_own, w_other = pl.pallas_call(
        functools.partial(first_kernel, len(arrived)),
        in_specs=[smem, hbm] + [vmem] * 3 + [hbm] + [vmem] * (2 + len(arrived)),
        out_specs=[vmem] * 4,
        out_shape=[
            jax.ShapeDtypeStruct((2 * video, width), F32),
            jax.ShapeDtypeStruct((2 * video, HEAD_DIM), F32),
            jax.ShapeDtypeStruct((width, out_features), BF16),
            jax.ShapeDtypeStruct((width, out_features), BF16),
        ],
        scratch_shapes=[
            pltpu.VMEM(stale_cache.shape, BF16),
            pltpu.SemaphoreType.DMA((3,)),
        ],
        compiler_params=params(24),
        cost_estimate=cost(
            8 * video * context * width, 4 * context * width, 2 * video * context * heads
        ),
        name="attend_first",
    )(
        place, in_hbm(out_weight), queries, other_queries, fresh, in_hbm(stale_cache), text_kv,
        text_mask, *arrived,
    )
    num_own, den_own, num_message = plain_call(
        last_kernel,
        [((video, width), F32), ((video, HEAD_DIM), F32), ((video, width + HEAD_DIM), F32)],
        "attend_last",
        cost(8 * video * video * width, 12 * video * width, 2 * video * video * heads),
        queries, other_queries, num, den, far,
    )

    num_received = lax.ppermute(num_message, "section", swap_core)
    (attended,) = plain_call(
        merge_kernel,
        [((video, width), BF16)],
        "merge",
        cost(4 * video * width, 10 * video * width),
        num_own, den_own, num_received,
    )
    other_attended = lax.ppermute(attended, "head", swap_head)

    out_cost = cost(2 * video * width * out_features, 2 * width * out_features)
    (part,) = plain_call(
        part_kernel, [((video, out_features), F32)], "part_out", out_cost, attended, w_own
    )
    (mixed,) = plain_call(
        final_kernel, [((video, out_features), BF16)], "final_out", out_cost,
        part, other_attended, w_other, hidden, branch_gate,
    )
    return (mixed, new_cache)


def solution(mesh):
    in_specs = (
        P("section", "head"),
        P(None, "head"),
        P(),
        P(None, "section", "head"),
        P("head", None),
        P(None, "head"),
        P(),
        P(),
        P("head"),
        P("head"),
        P("head"),
    )
    out_specs = (P("section", "head"), P(None, "section", "head"))
    return jax.shard_map(
        functools.partial(per_device, mesh.shape["section"]),
        mesh=mesh, in_specs=in_specs, out_specs=out_specs, check_vma=False,
    )
```

```python
import functools
import math

import jax
import jax.numpy as jnp
from jax import lax
from jax.experimental import pallas as pl
from jax.experimental.pallas import tpu as pltpu
from jax.sharding import PartitionSpec as P

HEAD_DIM = 128
TRIPLE = 3 * HEAD_DIM
EXTRA = 16
STAT_ROW = 8
EPS = 1e-06
F32 = jnp.float32
BF16 = jnp.bfloat16


def split_bf16(value, parts):
    pieces = []
    rest = value
    for _ in range(parts):
        piece = rest.astype(BF16)
        pieces.append(piece)
        rest = rest - piece.astype(F32)
    return pieces


def start_weights(w_ref, buffer_ref, sems, first):
    count, _, columns = buffer_ref.shape
    copies = []
    for index in range(count):
        start = pl.multiple_of(first + index * columns, HEAD_DIM)
        copy = pltpu.make_async_copy(
            w_ref.at[:, pl.ds(start, columns)], buffer_ref.at[index], sems.at[index]
        )
        copy.start()
        copies.append(copy)
    return copies


def send_kernel(
    place_ref, x_ref, t_ref, scale_ref, shift_ref, w_ref,
    a_ref, msg_ref, tmsg_ref, stat_ref, w_own_ref,
    x_buffer, t_buffer, scale_buffer, shift_buffer, w_buffer, in_sems, w_sems, own_sems,
):
    video, features = x_buffer.shape
    text = t_buffer.shape[0]
    top = video + EXTRA
    blocks, _, columns = w_buffer.shape
    width = blocks * columns
    copies = [
        pltpu.make_async_copy(scale_ref, scale_buffer, in_sems.at[0]),
        pltpu.make_async_copy(shift_ref, shift_buffer, in_sems.at[1]),
        pltpu.make_async_copy(x_ref, x_buffer, in_sems.at[2]),
        pltpu.make_async_copy(
            t_ref.at[pl.ds(pl.multiple_of(place_ref[1] * text, text), text)], t_buffer, in_sems.at[3]
        ),
    ]
    for copy in copies:
        copy.start()
    w_copies = start_weights(w_ref, w_buffer, w_sems, (1 - place_ref[0]) * width)
    own_copies = start_weights(w_ref, w_own_ref, own_sems, place_ref[0] * width)

    copies[0].wait()
    copies[1].wait()
    gain = 1.0 + scale_buffer[...].reshape(1, features)
    pieces = split_bf16(gain, 2) + split_bf16(shift_buffer[...].reshape(1, features), 2)
    row = lax.broadcasted_iota(jnp.int32, (EXTRA, features), 0)
    extra = jnp.zeros((EXTRA, features), F32)
    for index, piece in enumerate(pieces):
        extra = jnp.where(row == index, piece.astype(F32), extra)
    a_ref[video:top, :] = extra.astype(BF16)

    def prepare(rows_ref, start):
        rows = rows_ref[...].astype(F32)
        count = rows.shape[0]
        mean = jnp.sum(rows, axis=1, keepdims=True) * (1.0 / features)
        centered = rows - mean
        second = jnp.sum(centered * centered, axis=1, keepdims=True)
        a_ref[start : start + count, :] = (centered * gain).astype(BF16)
        lane = lax.broadcasted_iota(jnp.int32, (count, HEAD_DIM), 1)
        packed = jnp.zeros((count, HEAD_DIM), F32)
        for index, piece in enumerate(split_bf16(mean, 3) + split_bf16(second, 3)):
            packed = jnp.where(lane == STAT_ROW + index, piece.astype(F32), packed)
        stat_ref[start : start + count, :] = jnp.where(
            lane == 0, mean, jnp.where(lane == 1, second, 0.0)
        )
        return jnp.transpose(packed)[:EXTRA]

    copies[2].wait()
    video_stats = prepare(x_buffer, 0)
    copies[3].wait()
    text_stats = prepare(t_buffer, top)
    stat_ref[video:top, :] = jnp.zeros((EXTRA, HEAD_DIM), F32)

    def write(start, product):
        cells = slice(start, start + product.shape[1])
        msg_ref[:, cells] = product[:top].astype(BF16)
        if start == 0:
            stats = jnp.concatenate([video_stats, text_stats], axis=1)
            msg_ref[video:, : video + text] = (product[video:top] + stats).astype(BF16)
        for source, target in text_columns(start, product.shape[1]):
            tmsg_ref[:, target] = product[top:, source].astype(BF16)

    for block in range(blocks):
        w_copies[block].wait()
        multiply(a_ref, w_buffer.at[block], block * columns, write)
    for copy in own_copies:
        copy.wait()


PIECE = 2 * HEAD_DIM


def multiply(a_ref, w_ref, first, write):
    for start in range(0, w_ref.shape[1], PIECE):
        piece = jnp.dot(
            a_ref[...], w_ref[:, start : start + PIECE], preferred_element_type=F32
        )
        write(first + start, piece)


def text_columns(first, count):
    for start in range(0, count, HEAD_DIM):
        head, kind = divmod((first + start) // HEAD_DIM, 3)
        if kind:
            target = (2 * head + kind - 1) * HEAD_DIM
            yield slice(start, start + HEAD_DIM), slice(target, target + HEAD_DIM)


def own_kernel(place_ref, a_ref, w_ref, out_weight_ref, *refs):
    small = (len(refs) - 5) // 2
    out_ref, text_ref, w_own_ref, w_other_ref = refs[small : small + 4]
    sems = refs[-1]
    top = out_ref.shape[0]
    depth = w_own_ref.shape[0]
    group = place_ref[0]
    pairs = list(zip(refs[:small], refs[small + 4 : -1]))
    for half, target in ((group, w_own_ref), (1 - group, w_other_ref)):
        rows = pl.ds(pl.multiple_of(half * depth, depth), depth)
        pairs.append((out_weight_ref.at[rows], target))
    copies = []
    for index, (source, target) in enumerate(pairs):
        copies.append(pltpu.make_async_copy(source, target, sems.at[index]))
        copies[-1].start()

    def write(start, product):
        out_ref[:, start : start + product.shape[1]] = product[:top]
        for source, target in text_columns(start, product.shape[1]):
            text_ref[:, target] = product[top:, source]

    blocks, _, columns = w_ref.shape
    for block in range(blocks):
        multiply(a_ref, w_ref.at[block], block * columns, write)
    for copy in copies:
        copy.wait()


def split_kernel(block_ref, first_ref, second_ref, sems):
    width = first_ref.shape[2]
    copies = [
        pltpu.make_async_copy(
            block_ref.at[:, :, pl.ds(index * width, width)], target, sems.at[index]
        )
        for index, target in enumerate((first_ref, second_ref))
    ]
    for copy in copies:
        copy.start()
    for copy in copies:
        copy.wait()


def row_stats(total_features, own, received):
    count = own.shape[0]
    received = received.astype(F32)
    padding = jnp.zeros((HEAD_DIM - received.shape[0], count), F32)
    received = jnp.transpose(jnp.concatenate([received, padding], axis=0))
    parts = [received[:, STAT_ROW + index : STAT_ROW + index + 1] for index in range(6)]
    gap = 0.5 * (own[:, 0:1] - (parts[0] + parts[1] + parts[2]))
    second = own[:, 1:2] + (parts[3] + parts[4] + parts[5])
    var = second * (1.0 / total_features) + gap * gap
    return gap, lax.rsqrt(var + EPS)


def column_terms(own, other):
    other = other.astype(F32)
    scale = (own[0:1] + own[1:2]) - (other[0:1] + other[1:2])
    shift = (own[2:3] + own[3:4]) + (other[2:3] + other[3:4])
    return scale, shift


def head_norm(part, gain):
    square = jnp.sum(part * part, axis=1, keepdims=True) * (1.0 / HEAD_DIM)
    return part * lax.rsqrt(square + EPS) * gain


def norm_kernel(
    total_features, own_ref, msg_ref, stat_ref, qg_ref, kg_ref, q_ref, cache_ref, kv_ref,
):
    video = q_ref.shape[0]
    top = video + EXTRA
    query_gain = qg_ref[...].reshape(1, HEAD_DIM)
    key_gain = kg_ref[...].reshape(1, HEAD_DIM)
    heads = q_ref.shape[1] // HEAD_DIM
    gap, inverse = row_stats(total_features, stat_ref[:video, :], msg_ref[video:top, :video])
    for head in range(heads):
        part = slice(head * TRIPLE, (head + 1) * TRIPLE)
        columns = slice(head * HEAD_DIM, (head + 1) * HEAD_DIM)
        scale, shift = column_terms(own_ref[video:, part], msg_ref[video:top, part])
        total = own_ref[:video, part] + msg_ref[:video, part].astype(F32)
        total = (total + gap * scale) * inverse + shift
        q_ref[:, columns] = head_norm(total[:, :HEAD_DIM], query_gain).astype(BF16)
        keys = head_norm(total[:, HEAD_DIM : 2 * HEAD_DIM], key_gain).astype(BF16)
        values = total[:, 2 * HEAD_DIM :].astype(BF16)
        cache_ref[0, :, columns] = keys
        cache_ref[1, :, columns] = values
        kv_ref[0, :, columns] = keys
        kv_ref[1, :, columns] = values


def text_kernel(total_features, own_ref, tmsg_ref, stat_ref, top_ref, msg_ref, kg_ref, kv_ref):
    text = kv_ref.shape[1]
    heads = kv_ref.shape[2] // HEAD_DIM
    top = top_ref.shape[0]
    video = top - EXTRA
    key_gain = kg_ref[...].reshape(1, HEAD_DIM)
    gap, inverse = row_stats(
        total_features, stat_ref[top:, :], msg_ref[video:top, video : video + text]
    )
    for head in range(heads):
        part = slice(head * TRIPLE + HEAD_DIM, (head + 1) * TRIPLE)
        pair = slice(head * 2 * HEAD_DIM, (head + 1) * 2 * HEAD_DIM)
        columns = slice(head * HEAD_DIM, (head + 1) * HEAD_DIM)
        scale, shift = column_terms(top_ref[video:, part], msg_ref[video:top, part])
        total = own_ref[:, pair] + tmsg_ref[:, pair].astype(F32)
        total = (total + gap * scale) * inverse + shift
        kv_ref[0, :, columns] = head_norm(total[:, :HEAD_DIM], key_gain).astype(BF16)
        kv_ref[1, :, columns] = total[:, HEAD_DIM:].astype(BF16)


FACTOR = math.log2(math.e) / math.sqrt(HEAD_DIM)


def weigh(rows, keys):
    scores = lax.dot_general(rows, keys, (((1,), (1,)), ((), ())), preferred_element_type=F32)
    return jnp.exp2(scores * FACTOR)


def lanes(weights):
    total = weights[:, :HEAD_DIM]
    for start in range(HEAD_DIM, weights.shape[1], HEAD_DIM):
        total = total + weights[:, start : start + HEAD_DIM]
    return total


def times(weights, values):
    return jnp.dot(weights.astype(BF16), values, preferred_element_type=F32)


def absorb(queries, blocks, num, den):
    for first in range(0, len(blocks), 2):
        pair = blocks[first : first + 2]
        keys = jnp.concatenate([ref[0, :, columns] for ref, columns in pair], axis=0)
        values = jnp.concatenate([ref[1, :, columns] for ref, columns in pair], axis=0)
        weights = weigh(queries, keys)
        num = num + times(weights, values)
        den = den + lanes(weights)
    return num, den


def first_kernel(qo_ref, qp_ref, fresh_ref, *refs):
    num_ref, den_ref = refs[-2:]
    stales, halves = refs[:2], refs[2:-2]
    video, width = qo_ref.shape
    lane = lax.broadcasted_iota(jnp.int32, (2 * video, HEAD_DIM), 1)
    packed = jnp.zeros((2 * video, HEAD_DIM), F32)
    for head in range(width // HEAD_DIM):
        columns = slice(head * HEAD_DIM, (head + 1) * HEAD_DIM)
        second, start = divmod(head * HEAD_DIM, width // 2)
        cells = slice(start, start + HEAD_DIM)
        own, other = qo_ref[:, columns], qp_ref[:, columns]
        queries = jnp.concatenate([own, other], axis=0)
        fresh = weigh(own, fresh_ref[0, :, columns])
        stale_ref = stales[second]
        stale = weigh(other, stale_ref[0, :, cells])
        num = jnp.concatenate(
            [times(fresh, fresh_ref[1, :, columns]), times(stale, stale_ref[1, :, cells])], axis=0
        )
        den = jnp.concatenate([fresh, stale], axis=0)
        num, den = absorb(queries, [(ref, cells) for ref in halves[second::2]], num, den)
        num_ref[:, columns] = num
        packed = jnp.where(lane == head, jnp.sum(den, axis=1, keepdims=True), packed)
    den_ref[...] = packed


def last_kernel(
    first, place_ref, qo_ref, qp_ref, num_ref, den_ref, text_ref, mask_ref, far_ref,
    own_ref, own_den_ref, msg_ref,
):
    video = qo_ref.shape[0]
    text, width = text_ref.shape[1], far_ref.shape[2]
    lane = lax.broadcasted_iota(jnp.int32, (2 * video, HEAD_DIM), 1)
    mask = mask_ref[...].reshape(1, 2 * text).astype(F32)
    mask = jnp.where(place_ref[1] == 0, mask[:, :text], mask[:, text:])
    keep = jnp.concatenate([mask, jnp.ones((1, video), F32)], axis=1)
    packed = den_ref[...]
    for head in range(width // HEAD_DIM):
        cells = slice(head * HEAD_DIM, (head + 1) * HEAD_DIM)
        columns = slice((first + head) * HEAD_DIM, (first + head + 1) * HEAD_DIM)
        queries = jnp.concatenate([qo_ref[:, columns], qp_ref[:, columns]], axis=0)
        keys = jnp.concatenate([text_ref[0, :, columns], far_ref[0, :, cells]], axis=0)
        values = jnp.concatenate([text_ref[1, :, columns], far_ref[1, :, cells]], axis=0)
        weights = weigh(queries, keys) * keep
        num = num_ref[:, columns] + times(weights, values)
        own_ref[:, cells] = num[:video]
        msg_ref[:, cells] = num[video:]
        total = jnp.sum(lanes(weights), axis=1, keepdims=True)
        packed = packed + jnp.where(lane == first + head, total, 0.0)
    own_den_ref[...] = packed[:video]
    msg_ref[:, width:] = packed[video:]


def merge_kernel(first, own_ref, den_ref, msg_ref, att_ref):
    width = att_ref.shape[1]
    for head in range(width // HEAD_DIM):
        columns = slice(head * HEAD_DIM, (head + 1) * HEAD_DIM)
        lane = first + head
        num = own_ref[:, columns] + msg_ref[:, columns]
        den = den_ref[:, lane : lane + 1] + msg_ref[:, width + lane : width + lane + 1]
        att_ref[:, columns] = (num / den).astype(BF16)


def project_out(first_ref, second_ref, w_ref):
    half = first_ref.shape[1]
    return jnp.dot(first_ref[...], w_ref[:half, :], preferred_element_type=F32) + jnp.dot(
        second_ref[...], w_ref[half:, :], preferred_element_type=F32
    )


def part_kernel(first_ref, second_ref, w_ref, out_ref):
    out_ref[...] = project_out(first_ref, second_ref, w_ref)


def final_kernel(part_ref, first_ref, second_ref, w_ref, hidden_ref, gate_ref, out_ref):
    total = part_ref[...] + project_out(first_ref, second_ref, w_ref)
    gate = gate_ref[...].reshape(1, total.shape[1])
    out_ref[...] = (hidden_ref[...].astype(F32) + gate * total).astype(BF16)


def params(megabytes):
    return pltpu.CompilerParams(vmem_limit_bytes=megabytes * 1024 * 1024)


def in_hbm(array):
    return pltpu.with_memory_space_constraint(array, pltpu.HBM)


def cost(flops, nbytes, transcendentals=0):
    return pl.CostEstimate(
        flops=int(flops), bytes_accessed=int(nbytes), transcendentals=int(transcendentals)
    )


def plain_call(kernel, outs, name, estimate, *operands):
    return pl.pallas_call(
        kernel,
        in_specs=[pl.BlockSpec(memory_space=pltpu.VMEM)] * len(operands),
        out_specs=[pl.BlockSpec(memory_space=pltpu.VMEM)] * len(outs),
        out_shape=[jax.ShapeDtypeStruct(shape, dtype) for shape, dtype in outs],
        compiler_params=params(24),
        cost_estimate=estimate,
        name=name,
    )(*operands)


def ring_moves(sections):
    chips = sections // 2
    order = list(range(0, chips, 2)) + list(range(chips - 1, 0, -2))
    moves = [], []
    for here, there in zip(order, order[1:] + order[:1]):
        for core in range(2):
            moves[core].append((2 * here + core, 2 * there + core))
            moves[1 - core].append((2 * there + core, 2 * here + core))
    return sorted(moves[0]), sorted(moves[1])


def per_device(
    sections, hidden, text_hidden, text_mask, stale_cache, qkv_weight, out_weight, query_gain,
    key_gain, norm_shift, norm_scale, branch_gate,
):
    video, features = hidden.shape
    text = text_hidden.shape[0] // 2
    width = stale_cache.shape[2]
    heads = width // HEAD_DIM
    group_columns = heads * TRIPLE
    chips = sections // 2
    out_features = out_weight.shape[1]
    top = video + EXTRA
    rows = top + text

    group = lax.axis_index("head")
    core = lax.axis_index("section") % 2
    place = jnp.stack([group, core]).astype(jnp.int32)
    swap_core = [(s, s ^ 1) for s in range(sections)]
    swap_head = [(0, 1), (1, 0)]
    ways = ring_moves(sections)
    half_way = chips // 2

    def ring_step(blocks):
        return [lax.ppermute(block, "section", way) for block, way in zip(blocks, ways)]

    vmem = pl.BlockSpec(memory_space=pltpu.VMEM)
    hbm = pl.BlockSpec(memory_space=pltpu.HBM)
    smem = pl.BlockSpec(memory_space=pltpu.SMEM)
    half_block = jax.ShapeDtypeStruct((2, video, width // 2), BF16)
    stale = pl.pallas_call(
        split_kernel,
        in_specs=[hbm],
        out_specs=[vmem] * 2,
        out_shape=[half_block] * 2,
        scratch_shapes=[pltpu.SemaphoreType.DMA((2,))],
        compiler_params=params(16),
        cost_estimate=cost(0, 8 * video * width),
        name="split_heads",
    )(in_hbm(stale_cache))
    place = lax.optimization_barrier((place, *stale))[0]
    chains = [[ring_step((half, half))] for half in stale]

    block_heads = 2 if heads % 2 == 0 else 1
    columns = block_heads * TRIPLE
    blocks = heads // block_heads
    project_cost = cost(8 * rows * features * group_columns, 2 * features * group_columns)
    a_rows, message, text_message, stats, w_columns = pl.pallas_call(
        send_kernel,
        in_specs=[smem] + [hbm] * 5,
        out_specs=[vmem] * 5,
        out_shape=[
            jax.ShapeDtypeStruct((rows, features), BF16),
            jax.ShapeDtypeStruct((top, group_columns), BF16),
            jax.ShapeDtypeStruct((text, 2 * width), BF16),
            jax.ShapeDtypeStruct((rows, HEAD_DIM), F32),
            jax.ShapeDtypeStruct((blocks, features, columns), BF16),
        ],
        scratch_shapes=[
            pltpu.VMEM((video, features), BF16),
            pltpu.VMEM((text, features), BF16),
            pltpu.VMEM((features,), F32),
            pltpu.VMEM((features,), F32),
            pltpu.VMEM((blocks, features, columns), BF16),
            pltpu.SemaphoreType.DMA((4,)),
            pltpu.SemaphoreType.DMA((blocks,)),
            pltpu.SemaphoreType.DMA((blocks,)),
        ],
        compiler_params=params(28),
        cost_estimate=project_cost,
        name="project_send",
    )(
        place,
        *map(in_hbm, (hidden, text_hidden, norm_scale, norm_shift, qkv_weight)),
    )

    received = lax.ppermute(message, "head", swap_head)

    for chain in chains:
        chain.append(ring_step(lax.optimization_barrier((*chain[-1], message))[:2]))

    small = (query_gain, key_gain, text_mask, branch_gate, hidden)
    outs = pl.pallas_call(
        own_kernel,
        in_specs=[smem, vmem, vmem, hbm] + [hbm] * len(small),
        out_specs=[vmem] * (4 + len(small)),
        out_shape=[
            jax.ShapeDtypeStruct((top, group_columns), F32),
            jax.ShapeDtypeStruct((text, 2 * width), F32),
            jax.ShapeDtypeStruct((width, out_features), BF16),
            jax.ShapeDtypeStruct((width, out_features), BF16),
        ]
        + [jax.ShapeDtypeStruct(array.shape, array.dtype) for array in small],
        scratch_shapes=[pltpu.SemaphoreType.DMA((len(small) + 2,))],
        compiler_params=params(24),
        cost_estimate=project_cost,
        name="project_own",
    )(place, a_rows, w_columns, *map(in_hbm, (out_weight,) + small))
    own, own_text, w_own, w_other = outs[:4]
    query_gain, key_gain, text_mask, branch_gate, hidden = outs[4:]

    for step in range(half_way - 3):
        for chain in chains:
            last = chain[-1]
            if step == 0:
                last = lax.optimization_barrier((*last, own))[:2]
            chain.append(ring_step(last))

    received = lax.optimization_barrier((received, *chains[1][1]))[0]
    text_message = lax.optimization_barrier((text_message, received))[0]
    text_received = lax.ppermute(text_message, "head", swap_head)

    queries, new_cache, fresh = plain_call(
        functools.partial(norm_kernel, features * 2),
        [((video, width), BF16), ((2, video, width), BF16), ((2, video, width), BF16)],
        "norm_video",
        cost(20 * top * group_columns, 8 * top * group_columns),
        own, received, stats, query_gain, key_gain,
    )
    other_queries = lax.ppermute(queries, "section", swap_core)
    far = [
        lax.ppermute(lax.optimization_barrier((chain[-1][0], queries))[0], "section", ways[0])
        for chain in chains
    ]

    halves = [
        block
        for steps in zip(*chains)
        for way in range(2)
        for block in (steps[0][way], steps[1][way])
    ]
    context = (len(halves) // 2 + 1) * video
    num, den = plain_call(
        first_kernel,
        [((2 * video, width), F32), ((2 * video, HEAD_DIM), F32)],
        "attend_first",
        cost(8 * video * context * width, 4 * context * width, 2 * video * context * heads),
        queries, other_queries, fresh, *stale, *halves,
    )
    (text_kv,) = plain_call(
        functools.partial(text_kernel, features * 2),
        [((2, text, width), BF16)],
        "norm_text",
        cost(20 * text * group_columns, 8 * text * group_columns),
        own_text, text_received, stats, own, received, key_gain,
    )

    last_context = video + text
    attended, other_attended = [], []
    for index, block in enumerate(far):
        first = index * heads // 2
        num_own, den_own, num_message = pl.pallas_call(
            functools.partial(last_kernel, first),
            in_specs=[smem] + [vmem] * 7,
            out_specs=[vmem] * 3,
            out_shape=[
                jax.ShapeDtypeStruct((video, width // 2), F32),
                jax.ShapeDtypeStruct((video, HEAD_DIM), F32),
                jax.ShapeDtypeStruct((video, width // 2 + HEAD_DIM), F32),
            ],
            compiler_params=params(24),
            cost_estimate=cost(
                4 * video * last_context * width, 6 * video * width, video * last_context * heads
            ),
            name="attend_last",
        )(place, queries, other_queries, num, den, text_kv, text_mask, block)
        num_received = lax.ppermute(num_message, "section", swap_core)
        attended += plain_call(
            functools.partial(merge_kernel, first),
            [((video, width // 2), BF16)],
            "merge",
            cost(2 * video * width, 5 * video * width),
            num_own, den_own, num_received,
        )
        other_attended.append(lax.ppermute(attended[-1], "head", swap_head))

    out_cost = cost(2 * video * width * out_features, 2 * width * out_features)
    (part,) = plain_call(
        part_kernel, [((video, out_features), F32)], "part_out", out_cost, *attended, w_own
    )
    (mixed,) = plain_call(
        final_kernel, [((video, out_features), BF16)], "final_out", out_cost,
        part, *other_attended, w_other, hidden, branch_gate,
    )
    return (mixed, new_cache)


def solution(mesh):
    in_specs = (
        P("section", "head"),
        P(None, "head"),
        P(),
        P(None, "section", "head"),
        P("head", None),
        P(None, "head"),
        P(),
        P(),
        P("head"),
        P("head"),
        P("head"),
    )
    out_specs = (P("section", "head"), P(None, "section", "head"))
    return jax.shard_map(
        functools.partial(per_device, mesh.shape["section"]),
        mesh=mesh, in_specs=in_specs, out_specs=out_specs, check_vma=False,
    )
```

```python
import functools
import math

import jax
import jax.numpy as jnp
from jax import lax
from jax.experimental import pallas as pl
from jax.experimental.pallas import tpu as pltpu
from jax.sharding import PartitionSpec as P

HEAD_DIM = 128
TRIPLE = 3 * HEAD_DIM
EXTRA = 16
STAT_ROW = 8
PIECE = 2 * HEAD_DIM
IN_FLIGHT = 6
EPS = 1e-06
F32 = jnp.float32
BF16 = jnp.bfloat16


def split_bf16(value, parts):
    pieces = []
    rest = value
    for _ in range(parts):
        piece = rest.astype(BF16)
        pieces.append(piece)
        rest = rest - piece.astype(F32)
    return pieces


def chunk_copies(w_ref, first, targets, sems, base):
    copies = []
    for index, target in enumerate(targets):
        start = pl.multiple_of(first + index * PIECE, HEAD_DIM)
        copies.append(
            pltpu.make_async_copy(w_ref.at[:, pl.ds(start, PIECE)], target, sems.at[base + index])
        )
    return copies


def send_kernel(
    place_ref, x_ref, t_ref, scale_ref, shift_ref, w_ref,
    a_ref, msg_ref, stat_ref, ahead_ref,
    x_buffer, t_buffer, scale_buffer, shift_buffer, w_buffer, in_sems, w_sems,
):
    video, features = x_buffer.shape
    text = t_buffer.shape[0]
    top = video + EXTRA
    chunks = w_buffer.shape[0]
    width = chunks * PIECE
    copies = [
        pltpu.make_async_copy(scale_ref, scale_buffer, in_sems.at[0]),
        pltpu.make_async_copy(shift_ref, shift_buffer, in_sems.at[1]),
        pltpu.make_async_copy(x_ref, x_buffer, in_sems.at[2]),
        pltpu.make_async_copy(
            t_ref.at[pl.ds(pl.multiple_of(place_ref[1] * text, text), text)], t_buffer, in_sems.at[3]
        ),
    ]
    w_copies = chunk_copies(
        w_ref, (1 - place_ref[0]) * width, [w_buffer.at[i] for i in range(chunks)], w_sems, 0
    ) + chunk_copies(
        w_ref, place_ref[0] * width, [ahead_ref.at[i] for i in range(ahead_ref.shape[0])],
        w_sems, chunks,
    )
    for copy in copies + w_copies[:IN_FLIGHT]:
        copy.start()

    copies[0].wait()
    copies[1].wait()
    gain = 1.0 + scale_buffer[...].reshape(1, features)
    pieces = split_bf16(gain, 2) + split_bf16(shift_buffer[...].reshape(1, features), 2)
    row = lax.broadcasted_iota(jnp.int32, (EXTRA, features), 0)
    extra = jnp.zeros((EXTRA, features), F32)
    for index, piece in enumerate(pieces):
        extra = jnp.where(row == index, piece.astype(F32), extra)
    a_ref[video:top, :] = extra.astype(BF16)

    def prepare(rows_ref, start):
        rows = rows_ref[...].astype(F32)
        count = rows.shape[0]
        mean = jnp.sum(rows, axis=1, keepdims=True) * (1.0 / features)
        centered = rows - mean
        second = jnp.sum(centered * centered, axis=1, keepdims=True)
        a_ref[start : start + count, :] = (centered * gain).astype(BF16)
        lane = lax.broadcasted_iota(jnp.int32, (count, HEAD_DIM), 1)
        packed = jnp.zeros((count, HEAD_DIM), F32)
        for index, piece in enumerate(split_bf16(mean, 3) + split_bf16(second, 3)):
            packed = jnp.where(lane == STAT_ROW + index, piece.astype(F32), packed)
        stat_ref[start : start + count, :] = jnp.where(
            lane == 0, mean, jnp.where(lane == 1, second, 0.0)
        )
        return jnp.transpose(packed)[:EXTRA]

    copies[2].wait()
    video_stats = prepare(x_buffer, 0)
    copies[3].wait()
    text_stats = prepare(t_buffer, top)
    stat_ref[video:top, :] = jnp.zeros((EXTRA, HEAD_DIM), F32)

    for index, copy in enumerate(w_copies):
        copy.wait()
        if index + IN_FLIGHT < len(w_copies):
            w_copies[index + IN_FLIGHT].start()
        if index >= chunks:
            continue
        start = index * PIECE
        product = jnp.dot(a_ref[...], w_buffer[index], preferred_element_type=F32)
        msg_ref[:top, start : start + PIECE] = product[:top].astype(BF16)
        if index == 0:
            stats = jnp.concatenate([video_stats, text_stats], axis=1)
            msg_ref[video:top, : video + text] = (product[video:top] + stats).astype(BF16)
        for source, target in text_columns(start):
            part = product[top:, source].astype(BF16)
            for quarter in range(4):
                rows, cells = text_slot(text, width, target, quarter)
                msg_ref[top + rows.start : top + rows.stop, cells] = part[
                    quarter * text // 4 : (quarter + 1) * text // 4
                ]


def text_slot(text, width, column, quarter):
    slots = width // PIECE
    band, slot = divmod(column // PIECE * 4 + quarter, slots)
    depth = text // 4
    start = slot * PIECE + column % PIECE
    return slice(band * depth, (band + 1) * depth), slice(start, start + HEAD_DIM)


def text_columns(first):
    for start in range(0, PIECE, HEAD_DIM):
        head, kind = divmod((first + start) // HEAD_DIM, 3)
        if kind:
            yield slice(start, start + HEAD_DIM), (2 * head + kind - 1) * HEAD_DIM


def own_kernel(place_ref, a_ref, ahead_ref, w_ref, out_weight_ref, *refs):
    small = (len(refs) - 7) // 2
    out_ref, text_ref, w_own_ref, w_other_ref = refs[small : small + 4]
    w_buffer, w_sems, sems = refs[-3:]
    top = out_ref.shape[0]
    depth = w_own_ref.shape[0]
    group = place_ref[0]
    ahead, later = ahead_ref.shape[0], w_buffer.shape[0]
    w_copies = chunk_copies(
        w_ref, (group * (ahead + later) + ahead) * PIECE, [w_buffer.at[i] for i in range(later)],
        w_sems, 0,
    )
    pairs = list(zip(refs[:small], refs[small + 4 : -3]))
    for half, target in ((group, w_own_ref), (1 - group, w_other_ref)):
        rows = pl.ds(pl.multiple_of(half * depth, depth), depth)
        pairs.append((out_weight_ref.at[rows], target))
    copies = [
        pltpu.make_async_copy(source, target, sems.at[index])
        for index, (source, target) in enumerate(pairs)
    ]
    for copy in w_copies + copies:
        copy.start()

    for index in range(ahead + later):
        if index < ahead:
            columns = ahead_ref[index]
        else:
            w_copies[index - ahead].wait()
            columns = w_buffer[index - ahead]
        product = jnp.dot(a_ref[...], columns, preferred_element_type=F32)
        out_ref[:, index * PIECE : (index + 1) * PIECE] = product[:top]
        for source, target in text_columns(index * PIECE):
            text_ref[:, target : target + HEAD_DIM] = product[top:, source]
    for copy in copies:
        copy.wait()


def row_stats(total_features, own, received):
    count = own.shape[0]
    received = received.astype(F32)
    padding = jnp.zeros((HEAD_DIM - received.shape[0], count), F32)
    received = jnp.transpose(jnp.concatenate([received, padding], axis=0))
    parts = [received[:, STAT_ROW + index : STAT_ROW + index + 1] for index in range(6)]
    gap = 0.5 * (own[:, 0:1] - (parts[0] + parts[1] + parts[2]))
    second = own[:, 1:2] + (parts[3] + parts[4] + parts[5])
    var = second * (1.0 / total_features) + gap * gap
    return gap, lax.rsqrt(var + EPS)


def column_terms(own, other):
    other = other.astype(F32)
    scale = (own[0:1] + own[1:2]) - (other[0:1] + other[1:2])
    shift = (own[2:3] + own[3:4]) + (other[2:3] + other[3:4])
    return scale, shift


def head_norm(part, gain):
    square = jnp.sum(part * part, axis=1, keepdims=True) * (1.0 / HEAD_DIM)
    return part * lax.rsqrt(square + EPS) * gain


def norm_kernel(
    total_features, own_ref, msg_ref, stat_ref, qg_ref, kg_ref, q_ref, cache_ref, kv_ref,
):
    video = q_ref.shape[0]
    top = video + EXTRA
    query_gain = qg_ref[...].reshape(1, HEAD_DIM)
    key_gain = kg_ref[...].reshape(1, HEAD_DIM)
    heads = q_ref.shape[1] // HEAD_DIM
    gap, inverse = row_stats(total_features, stat_ref[:video, :], msg_ref[video:top, :video])
    for head in range(heads):
        part = slice(head * TRIPLE, (head + 1) * TRIPLE)
        columns = slice(head * HEAD_DIM, (head + 1) * HEAD_DIM)
        scale, shift = column_terms(own_ref[video:, part], msg_ref[video:top, part])
        total = own_ref[:video, part] + msg_ref[:video, part].astype(F32)
        total = (total + gap * scale) * inverse + shift
        q_ref[:, columns] = head_norm(total[:, :HEAD_DIM], query_gain).astype(BF16)
        keys = head_norm(total[:, HEAD_DIM : 2 * HEAD_DIM], key_gain).astype(BF16)
        values = total[:, 2 * HEAD_DIM :].astype(BF16)
        cache_ref[0, :, columns] = keys
        cache_ref[1, :, columns] = values
        kv_ref[0, :, columns] = keys
        kv_ref[1, :, columns] = values


def text_kernel(total_features, own_ref, msg_ref, stat_ref, top_ref, kg_ref, kv_ref):
    text = kv_ref.shape[1]
    heads = kv_ref.shape[2] // HEAD_DIM
    top, width = top_ref.shape
    video = top - EXTRA
    key_gain = kg_ref[...].reshape(1, HEAD_DIM)
    gap, inverse = row_stats(
        total_features, stat_ref[top:, :], msg_ref[video:top, video : video + text]
    )
    for head in range(heads):
        part = slice(head * TRIPLE + HEAD_DIM, (head + 1) * TRIPLE)
        pair = slice(head * PIECE, (head + 1) * PIECE)
        columns = slice(head * HEAD_DIM, (head + 1) * HEAD_DIM)
        scale, shift = column_terms(top_ref[video:, part], msg_ref[video:top, part])
        other = []
        for quarter in range(4):
            rows, cells = text_slot(text, width, head * PIECE, quarter)
            cells = slice(cells.start, cells.start + PIECE)
            other.append(msg_ref[top + rows.start : top + rows.stop, cells])
        total = own_ref[:, pair] + jnp.concatenate(other, axis=0).astype(F32)
        total = (total + gap * scale) * inverse + shift
        kv_ref[0, :, columns] = head_norm(total[:, :HEAD_DIM], key_gain).astype(BF16)
        kv_ref[1, :, columns] = total[:, HEAD_DIM:].astype(BF16)


FACTOR = math.log2(math.e) / math.sqrt(HEAD_DIM)


def weigh(rows, keys):
    scores = lax.dot_general(rows, keys, (((1,), (1,)), ((), ())), preferred_element_type=F32)
    return jnp.exp2(scores * FACTOR)


def lanes(weights):
    total = weights[:, :HEAD_DIM]
    for start in range(HEAD_DIM, weights.shape[1], HEAD_DIM):
        total = total + weights[:, start : start + HEAD_DIM]
    return total


def times(weights, values):
    return jnp.dot(weights.astype(BF16), values, preferred_element_type=F32)


def absorb(queries, blocks, num, den):
    for first in range(0, len(blocks), 2):
        pair = blocks[first : first + 2]
        keys = jnp.concatenate([ref[0, :, columns] for ref, columns in pair], axis=0)
        values = jnp.concatenate([ref[1, :, columns] for ref, columns in pair], axis=0)
        weights = weigh(queries, keys)
        num = num + times(weights, values)
        den = den + lanes(weights)
    return num, den


def first_kernel(place_ref, qo_ref, qp_ref, fresh_ref, stale_ref, text_ref, mask_ref, *refs):
    num_ref, den_ref = refs[-2:]
    video, width = qo_ref.shape
    text = text_ref.shape[1]
    lane = lax.broadcasted_iota(jnp.int32, (2 * video, HEAD_DIM), 1)
    mask = mask_ref[...].reshape(1, 2 * text).astype(F32)
    mask = jnp.where(place_ref[1] == 0, mask[:, :text], mask[:, text:])
    packed = jnp.zeros((2 * video, HEAD_DIM), F32)
    for head in range(width // HEAD_DIM):
        columns = slice(head * HEAD_DIM, (head + 1) * HEAD_DIM)
        own, other = qo_ref[:, columns], qp_ref[:, columns]
        queries = jnp.concatenate([own, other], axis=0)
        fresh = weigh(own, fresh_ref[0, :, columns])
        stale = weigh(other, stale_ref[0, :, columns])
        num = jnp.concatenate(
            [times(fresh, fresh_ref[1, :, columns]), times(stale, stale_ref[1, :, columns])], axis=0
        )
        den = jnp.concatenate([fresh, stale], axis=0)
        weights = weigh(queries, text_ref[0, :, columns]) * mask
        num = num + times(weights, text_ref[1, :, columns])
        den = den + lanes(weights)
        num, den = absorb(queries, [(ref, columns) for ref in refs[:-2]], num, den)
        num_ref[:, columns] = num
        packed = jnp.where(lane == head, jnp.sum(den, axis=1, keepdims=True), packed)
    den_ref[...] = packed


def last_kernel(first, qo_ref, qp_ref, num_ref, den_ref, far_ref, own_ref, own_den_ref, msg_ref):
    video = qo_ref.shape[0]
    width = own_ref.shape[1]
    lane = lax.broadcasted_iota(jnp.int32, (2 * video, HEAD_DIM), 1)
    packed = den_ref[...]
    for head in range(width // HEAD_DIM):
        cells = slice(head * HEAD_DIM, (head + 1) * HEAD_DIM)
        columns = slice((first + head) * HEAD_DIM, (first + head + 1) * HEAD_DIM)
        queries = jnp.concatenate([qo_ref[:, columns], qp_ref[:, columns]], axis=0)
        weights = weigh(queries, far_ref[0, :, columns])
        num = num_ref[:, columns] + times(weights, far_ref[1, :, columns])
        own_ref[:, cells] = num[:video]
        msg_ref[:, cells] = num[video:]
        total = jnp.sum(lanes(weights), axis=1, keepdims=True)
        packed = packed + jnp.where(lane == first + head, total, 0.0)
    own_den_ref[...] = packed[:video]
    msg_ref[:, width:] = packed[video:]


def merge_kernel(first, own_ref, den_ref, msg_ref, att_ref):
    width = att_ref.shape[1]
    for head in range(width // HEAD_DIM):
        columns = slice(head * HEAD_DIM, (head + 1) * HEAD_DIM)
        lane = first + head
        num = own_ref[:, columns] + msg_ref[:, columns]
        den = den_ref[:, lane : lane + 1] + msg_ref[:, width + lane : width + lane + 1]
        att_ref[:, columns] = (num / den).astype(BF16)


def project_out(first_ref, second_ref, w_ref):
    half = first_ref.shape[1]
    return jnp.dot(first_ref[...], w_ref[:half, :], preferred_element_type=F32) + jnp.dot(
        second_ref[...], w_ref[half:, :], preferred_element_type=F32
    )


def part_kernel(first_ref, second_ref, w_ref, out_ref):
    out_ref[...] = project_out(first_ref, second_ref, w_ref)


def final_kernel(part_ref, first_ref, second_ref, w_ref, hidden_ref, gate_ref, out_ref):
    total = part_ref[...] + project_out(first_ref, second_ref, w_ref)
    gate = gate_ref[...].reshape(1, total.shape[1])
    out_ref[...] = (hidden_ref[...].astype(F32) + gate * total).astype(BF16)


def params(megabytes):
    return pltpu.CompilerParams(vmem_limit_bytes=megabytes * 1024 * 1024)


def in_hbm(array):
    return pltpu.with_memory_space_constraint(array, pltpu.HBM)


def cost(flops, nbytes, transcendentals=0):
    return pl.CostEstimate(
        flops=int(flops), bytes_accessed=int(nbytes), transcendentals=int(transcendentals)
    )


def plain_call(kernel, outs, name, estimate, *operands):
    return pl.pallas_call(
        kernel,
        in_specs=[pl.BlockSpec(memory_space=pltpu.VMEM)] * len(operands),
        out_specs=[pl.BlockSpec(memory_space=pltpu.VMEM)] * len(outs),
        out_shape=[jax.ShapeDtypeStruct(shape, dtype) for shape, dtype in outs],
        compiler_params=params(24),
        cost_estimate=estimate,
        name=name,
    )(*operands)


def ring_moves(sections):
    chips = sections // 2
    order = list(range(0, chips, 2)) + list(range(chips - 1, 0, -2))
    moves = [], []
    for here, there in zip(order, order[1:] + order[:1]):
        for core in range(2):
            moves[core].append((2 * here + core, 2 * there + core))
            moves[1 - core].append((2 * there + core, 2 * here + core))
    return sorted(moves[0]), sorted(moves[1])


def per_device(
    sections, hidden, text_hidden, text_mask, stale_cache, qkv_weight, out_weight, query_gain,
    key_gain, norm_shift, norm_scale, branch_gate,
):
    video, features = hidden.shape
    text = text_hidden.shape[0] // 2
    width = stale_cache.shape[2]
    heads = width // HEAD_DIM
    group_columns = heads * TRIPLE
    chips = sections // 2
    out_features = out_weight.shape[1]
    top = video + EXTRA
    rows = top + text

    group = lax.axis_index("head")
    core = lax.axis_index("section") % 2
    place = jnp.stack([group, core]).astype(jnp.int32)
    swap_core = [(s, s ^ 1) for s in range(sections)]
    swap_head = [(0, 1), (1, 0)]
    ways = ring_moves(sections)
    half_way = chips // 2

    def ring_step(blocks):
        return [lax.ppermute(block, "section", way) for block, way in zip(blocks, ways)]

    vmem = pl.BlockSpec(memory_space=pltpu.VMEM)
    hbm = pl.BlockSpec(memory_space=pltpu.HBM)
    smem = pl.BlockSpec(memory_space=pltpu.SMEM)
    ring = [ring_step((stale_cache, stale_cache))]

    chunks = group_columns // PIECE
    ahead = chunks * 2 // 3
    bands = -(-heads * 4 // chunks)
    message_rows = top + bands * text // 4
    project_cost = cost(8 * rows * features * group_columns, 2 * features * group_columns)
    a_rows, message, stats, w_ahead = pl.pallas_call(
        send_kernel,
        in_specs=[smem] + [hbm] * 5,
        out_specs=[vmem] * 4,
        out_shape=[
            jax.ShapeDtypeStruct((rows, features), BF16),
            jax.ShapeDtypeStruct((message_rows, group_columns), BF16),
            jax.ShapeDtypeStruct((rows, HEAD_DIM), F32),
            jax.ShapeDtypeStruct((ahead, features, PIECE), BF16),
        ],
        scratch_shapes=[
            pltpu.VMEM((video, features), BF16),
            pltpu.VMEM((text, features), BF16),
            pltpu.VMEM((features,), F32),
            pltpu.VMEM((features,), F32),
            pltpu.VMEM((chunks, features, PIECE), BF16),
            pltpu.SemaphoreType.DMA((4,)),
            pltpu.SemaphoreType.DMA((chunks + ahead,)),
        ],
        compiler_params=params(40),
        cost_estimate=project_cost,
        name="project_send",
    )(place, *map(in_hbm, (hidden, text_hidden, norm_scale, norm_shift, qkv_weight)))

    received = lax.ppermute(message, "head", swap_head)
    ring.append(ring_step(lax.optimization_barrier((*ring[-1], message))[:2]))

    small = (query_gain, key_gain, text_mask, branch_gate, hidden, stale_cache)
    outs = pl.pallas_call(
        own_kernel,
        in_specs=[smem, vmem, vmem, hbm, hbm] + [hbm] * len(small),
        out_specs=[vmem] * (4 + len(small)),
        out_shape=[
            jax.ShapeDtypeStruct((top, group_columns), F32),
            jax.ShapeDtypeStruct((text, 2 * width), F32),
            jax.ShapeDtypeStruct((width, out_features), BF16),
            jax.ShapeDtypeStruct((width, out_features), BF16),
        ]
        + [jax.ShapeDtypeStruct(array.shape, array.dtype) for array in small],
        scratch_shapes=[
            pltpu.VMEM((chunks - ahead, features, PIECE), BF16),
            pltpu.SemaphoreType.DMA((chunks - ahead,)),
            pltpu.SemaphoreType.DMA((len(small) + 2,)),
        ],
        compiler_params=params(36),
        cost_estimate=project_cost,
        name="project_own",
    )(place, a_rows, w_ahead, *map(in_hbm, (qkv_weight, out_weight) + small))
    own, own_text, w_own, w_other = outs[:4]
    query_gain, key_gain, text_mask, branch_gate, hidden, stale = outs[4:]

    for _ in range(half_way - 3):
        ring.append(ring_step(lax.optimization_barrier((*ring[-1], own))[:2]))
    far = lax.ppermute(ring[-1][0], "section", ways[0])

    queries, new_cache, fresh = plain_call(
        functools.partial(norm_kernel, features * 2),
        [((video, width), BF16), ((2, video, width), BF16), ((2, video, width), BF16)],
        "norm_video",
        cost(1000 * top * group_columns, 8 * top * group_columns),
        own, received, stats, query_gain, key_gain,
    )
    other_queries = lax.ppermute(queries, "section", swap_core)
    (text_kv,) = plain_call(
        functools.partial(text_kernel, features * 2),
        [((2, text, width), BF16)],
        "norm_text",
        cost(1000 * text * group_columns, 8 * text * group_columns),
        own_text, received, stats, own, key_gain,
    )

    blocks = [block for step in ring for block in step]
    context = (len(blocks) + 1) * video + text
    num, den = pl.pallas_call(
        first_kernel,
        in_specs=[smem] + [vmem] * (6 + len(blocks)),
        out_specs=[vmem] * 2,
        out_shape=[
            jax.ShapeDtypeStruct((2 * video, width), F32),
            jax.ShapeDtypeStruct((2 * video, HEAD_DIM), F32),
        ],
        compiler_params=params(24),
        cost_estimate=cost(
            32 * video * context * width, 4 * context * width, 2 * video * context * heads
        ),
        name="attend_first",
    )(place, queries, other_queries, fresh, stale, text_kv, text_mask, *blocks)

    attended, other_attended = [], []
    for first in (0, heads // 2):
        num_own, den_own, num_message = plain_call(
            functools.partial(last_kernel, first),
            [
                ((video, width // 2), F32),
                ((video, HEAD_DIM), F32),
                ((video, width // 2 + HEAD_DIM), F32),
            ],
            "attend_last",
            cost(16 * video * video * width, 6 * video * width, video * video * heads),
            queries, other_queries, num, den, far,
        )
        num_received = lax.ppermute(num_message, "section", swap_core)
        attended += plain_call(
            functools.partial(merge_kernel, first),
            [((video, width // 2), BF16)],
            "merge",
            cost(2 * video * width, 5 * video * width),
            num_own, den_own, num_received,
        )
        other_attended.append(lax.ppermute(attended[-1], "head", swap_head))

    out_cost = cost(4 * video * width * out_features, 2 * width * out_features)
    (part,) = plain_call(
        part_kernel, [((video, out_features), F32)], "part_out", out_cost, *attended, w_own
    )
    (mixed,) = plain_call(
        final_kernel, [((video, out_features), BF16)], "final_out", out_cost,
        part, *other_attended, w_other, hidden, branch_gate,
    )
    return (mixed, new_cache)


def solution(mesh):
    in_specs = (
        P("section", "head"),
        P(None, "head"),
        P(),
        P(None, "section", "head"),
        P("head", None),
        P(None, "head"),
        P(),
        P(),
        P("head"),
        P("head"),
        P("head"),
    )
    out_specs = (P("section", "head"), P(None, "section", "head"))
    return jax.shard_map(
        functools.partial(per_device, mesh.shape["section"]),
        mesh=mesh, in_specs=in_specs, out_specs=out_specs, check_vma=False,
    )
```

```python
import functools
import math

import jax
import jax.numpy as jnp
from jax import lax
from jax.experimental import pallas as pl
from jax.experimental.pallas import tpu as pltpu
from jax.sharding import PartitionSpec as P

HEAD_DIM = 128
TRIPLE = 3 * HEAD_DIM
EXTRA = 16
STAT_ROW = 8
PIECE = 2 * HEAD_DIM
EPS = 1e-06
F32 = jnp.float32
BF16 = jnp.bfloat16


def split_bf16(value, parts):
    pieces = []
    rest = value
    for _ in range(parts):
        piece = rest.astype(BF16)
        pieces.append(piece)
        rest = rest - piece.astype(F32)
    return pieces


def block_copies(w_ref, first, targets, sems, base):
    copies = []
    for index, target in enumerate(targets):
        columns = target.shape[1]
        start = pl.multiple_of(first + index * columns, HEAD_DIM)
        copies.append(
            pltpu.make_async_copy(w_ref.at[:, pl.ds(start, columns)], target, sems.at[base + index])
        )
    return copies


def send_kernel(
    place_ref, x_ref, t_ref, scale_ref, shift_ref, w_ref,
    a_ref, msg_ref, stat_ref, ahead_ref,
    x_buffer, t_buffer, scale_buffer, shift_buffer, w_buffer, in_sems, w_sems,
):
    video, features = x_buffer.shape
    text = t_buffer.shape[0]
    top = video + EXTRA
    blocks, _, columns = w_buffer.shape
    width = blocks * columns
    copies = [
        pltpu.make_async_copy(scale_ref, scale_buffer, in_sems.at[0]),
        pltpu.make_async_copy(shift_ref, shift_buffer, in_sems.at[1]),
        pltpu.make_async_copy(x_ref, x_buffer, in_sems.at[2]),
        pltpu.make_async_copy(
            t_ref.at[pl.ds(pl.multiple_of(place_ref[1] * text, text), text)], t_buffer, in_sems.at[3]
        ),
    ]
    w_copies = block_copies(
        w_ref, (1 - place_ref[0]) * width, [w_buffer.at[i] for i in range(blocks)], w_sems, 0
    ) + block_copies(
        w_ref, place_ref[0] * width, [ahead_ref.at[i] for i in range(ahead_ref.shape[0])],
        w_sems, blocks,
    )
    for copy in copies + w_copies[:1]:
        copy.start()

    copies[0].wait()
    copies[1].wait()
    gain = 1.0 + scale_buffer[...].reshape(1, features)
    pieces = split_bf16(gain, 2) + split_bf16(shift_buffer[...].reshape(1, features), 2)
    row = lax.broadcasted_iota(jnp.int32, (EXTRA, features), 0)
    extra = jnp.zeros((EXTRA, features), F32)
    for index, piece in enumerate(pieces):
        extra = jnp.where(row == index, piece.astype(F32), extra)
    a_ref[video:top, :] = extra.astype(BF16)

    def prepare(rows_ref, start):
        rows = rows_ref[...].astype(F32)
        count = rows.shape[0]
        mean = jnp.sum(rows, axis=1, keepdims=True) * (1.0 / features)
        centered = rows - mean
        second = jnp.sum(centered * centered, axis=1, keepdims=True)
        a_ref[start : start + count, :] = (centered * gain).astype(BF16)
        lane = lax.broadcasted_iota(jnp.int32, (count, HEAD_DIM), 1)
        packed = jnp.zeros((count, HEAD_DIM), F32)
        for index, piece in enumerate(split_bf16(mean, 3) + split_bf16(second, 3)):
            packed = jnp.where(lane == STAT_ROW + index, piece.astype(F32), packed)
        stat_ref[start : start + count, :] = jnp.where(
            lane == 0, mean, jnp.where(lane == 1, second, 0.0)
        )
        return jnp.transpose(packed)[:EXTRA]

    copies[2].wait()
    w_copies[1].start()
    video_stats = prepare(x_buffer, 0)
    copies[3].wait()
    w_copies[2].start()
    text_stats = prepare(t_buffer, top)
    stat_ref[video:top, :] = jnp.zeros((EXTRA, HEAD_DIM), F32)

    for block in range(blocks):
        w_copies[block].wait()
        if block + 3 < len(w_copies):
            w_copies[block + 3].start()
        for piece in range(columns // PIECE):
            start = block * columns + piece * PIECE
            product = jnp.dot(
                a_ref[...], w_buffer[block, :, piece * PIECE : (piece + 1) * PIECE],
                preferred_element_type=F32,
            )
            msg_ref[:top, start : start + PIECE] = product[:top].astype(BF16)
            if start == 0:
                stats = jnp.concatenate([video_stats, text_stats], axis=1)
                msg_ref[video:top, : video + text] = (product[video:top] + stats).astype(BF16)
            for source, target in text_columns(start):
                part = product[top:, source].astype(BF16)
                for quarter in range(4):
                    rows, cells = text_slot(text, width, target, quarter)
                    msg_ref[top + rows.start : top + rows.stop, cells] = part[
                        quarter * text // 4 : (quarter + 1) * text // 4
                    ]
    for copy in w_copies[blocks:]:
        copy.wait()


def text_slot(text, width, column, quarter):
    slots = width // PIECE
    band, slot = divmod(column // PIECE * 4 + quarter, slots)
    depth = text // 4
    start = slot * PIECE + column % PIECE
    return slice(band * depth, (band + 1) * depth), slice(start, start + HEAD_DIM)


def text_columns(first):
    for start in range(0, PIECE, HEAD_DIM):
        head, kind = divmod((first + start) // HEAD_DIM, 3)
        if kind:
            yield slice(start, start + HEAD_DIM), (2 * head + kind - 1) * HEAD_DIM


def own_kernel(place_ref, a_ref, ahead_ref, w_ref, out_weight_ref, *refs):
    small = (len(refs) - 7) // 2
    out_ref, text_ref, w_own_ref, w_other_ref = refs[small : small + 4]
    w_buffer, w_sems, sems = refs[-3:]
    top = out_ref.shape[0]
    depth = w_own_ref.shape[0]
    group = place_ref[0]
    ahead, _, columns = ahead_ref.shape
    later = w_buffer.shape[0]
    w_copies = block_copies(
        w_ref, (group * (ahead + later) + ahead) * columns, [w_buffer.at[i] for i in range(later)],
        w_sems, 0,
    )
    pairs = list(zip(refs[:small], refs[small + 4 : -3]))
    for half, target in ((group, w_own_ref), (1 - group, w_other_ref)):
        rows = pl.ds(pl.multiple_of(half * depth, depth), depth)
        pairs.append((out_weight_ref.at[rows], target))
    copies = [
        pltpu.make_async_copy(source, target, sems.at[index])
        for index, (source, target) in enumerate(pairs)
    ]
    for copy in w_copies:
        copy.start()

    def write(start, product):
        out_ref[:, start : start + PIECE] = product[:top]
        for source, target in text_columns(start):
            text_ref[:, target : target + HEAD_DIM] = product[top:, source]

    for block in range(ahead + later):
        if block == ahead:
            for copy in w_copies:
                copy.wait()
        if block == min(1, ahead):
            for copy in copies:
                copy.start()
        for piece in range(columns // PIECE):
            cells = slice(piece * PIECE, (piece + 1) * PIECE)
            part = ahead_ref[block, :, cells] if block < ahead else w_buffer[block - ahead, :, cells]
            write(
                block * columns + piece * PIECE,
                jnp.dot(a_ref[...], part, preferred_element_type=F32),
            )
    for copy in copies:
        copy.wait()


def row_stats(total_features, own, received):
    count = own.shape[0]
    received = received.astype(F32)
    padding = jnp.zeros((HEAD_DIM - received.shape[0], count), F32)
    received = jnp.transpose(jnp.concatenate([received, padding], axis=0))
    parts = [received[:, STAT_ROW + index : STAT_ROW + index + 1] for index in range(6)]
    gap = 0.5 * (own[:, 0:1] - (parts[0] + parts[1] + parts[2]))
    second = own[:, 1:2] + (parts[3] + parts[4] + parts[5])
    var = second * (1.0 / total_features) + gap * gap
    return gap, lax.rsqrt(var + EPS)


def column_terms(own, other):
    other = other.astype(F32)
    scale = (own[0:1] + own[1:2]) - (other[0:1] + other[1:2])
    shift = (own[2:3] + own[3:4]) + (other[2:3] + other[3:4])
    return scale, shift


def head_norm(part, gain):
    square = jnp.sum(part * part, axis=1, keepdims=True) * (1.0 / HEAD_DIM)
    return part * lax.rsqrt(square + EPS) * gain


def norm_kernel(
    total_features, own_ref, msg_ref, stat_ref, qg_ref, kg_ref, q_ref, cache_ref, kv_ref,
):
    video = q_ref.shape[0]
    top = video + EXTRA
    query_gain = qg_ref[...].reshape(1, HEAD_DIM)
    key_gain = kg_ref[...].reshape(1, HEAD_DIM)
    heads = q_ref.shape[1] // HEAD_DIM
    gap, inverse = row_stats(total_features, stat_ref[:video, :], msg_ref[video:top, :video])
    for head in range(heads):
        part = slice(head * TRIPLE, (head + 1) * TRIPLE)
        columns = slice(head * HEAD_DIM, (head + 1) * HEAD_DIM)
        scale, shift = column_terms(own_ref[video:, part], msg_ref[video:top, part])
        total = own_ref[:video, part] + msg_ref[:video, part].astype(F32)
        total = (total + gap * scale) * inverse + shift
        q_ref[:, columns] = head_norm(total[:, :HEAD_DIM], query_gain).astype(BF16)
        keys = head_norm(total[:, HEAD_DIM : 2 * HEAD_DIM], key_gain).astype(BF16)
        values = total[:, 2 * HEAD_DIM :].astype(BF16)
        cache_ref[0, :, columns] = keys
        cache_ref[1, :, columns] = values
        kv_ref[0, :, columns] = keys
        kv_ref[1, :, columns] = values


def text_kernel(total_features, own_ref, msg_ref, stat_ref, top_ref, kg_ref, kv_ref):
    text = kv_ref.shape[1]
    heads = kv_ref.shape[2] // HEAD_DIM
    top, width = top_ref.shape
    video = top - EXTRA
    key_gain = kg_ref[...].reshape(1, HEAD_DIM)
    gap, inverse = row_stats(
        total_features, stat_ref[top:, :], msg_ref[video:top, video : video + text]
    )
    for head in range(heads):
        part = slice(head * TRIPLE + HEAD_DIM, (head + 1) * TRIPLE)
        pair = slice(head * PIECE, (head + 1) * PIECE)
        columns = slice(head * HEAD_DIM, (head + 1) * HEAD_DIM)
        scale, shift = column_terms(top_ref[video:, part], msg_ref[video:top, part])
        other = []
        for quarter in range(4):
            rows, cells = text_slot(text, width, head * PIECE, quarter)
            cells = slice(cells.start, cells.start + PIECE)
            other.append(msg_ref[top + rows.start : top + rows.stop, cells])
        total = own_ref[:, pair] + jnp.concatenate(other, axis=0).astype(F32)
        total = (total + gap * scale) * inverse + shift
        kv_ref[0, :, columns] = head_norm(total[:, :HEAD_DIM], key_gain).astype(BF16)
        kv_ref[1, :, columns] = total[:, HEAD_DIM:].astype(BF16)


FACTOR = math.log2(math.e) / math.sqrt(HEAD_DIM)


def weigh(rows, keys):
    scores = lax.dot_general(rows, keys, (((1,), (1,)), ((), ())), preferred_element_type=F32)
    return jnp.exp2(scores * FACTOR)


def lanes(weights):
    total = weights[:, :HEAD_DIM]
    for start in range(HEAD_DIM, weights.shape[1], HEAD_DIM):
        total = total + weights[:, start : start + HEAD_DIM]
    return total


def times(weights, values):
    return jnp.dot(weights.astype(BF16), values, preferred_element_type=F32)


def absorb(queries, blocks, num, den):
    for first in range(0, len(blocks), 2):
        pair = blocks[first : first + 2]
        keys = jnp.concatenate([ref[0, :, columns] for ref, columns in pair], axis=0)
        values = jnp.concatenate([ref[1, :, columns] for ref, columns in pair], axis=0)
        weights = weigh(queries, keys)
        num = num + times(weights, values)
        den = den + lanes(weights)
    return num, den


def first_kernel(place_ref, qo_ref, qp_ref, fresh_ref, stale_ref, text_ref, mask_ref, *refs):
    num_ref, den_ref = refs[-2:]
    video, width = qo_ref.shape
    text = text_ref.shape[1]
    lane = lax.broadcasted_iota(jnp.int32, (2 * video, HEAD_DIM), 1)
    mask = mask_ref[...].reshape(1, 2 * text).astype(F32)
    mask = jnp.where(place_ref[1] == 0, mask[:, :text], mask[:, text:])
    packed = jnp.zeros((2 * video, HEAD_DIM), F32)
    for head in range(width // HEAD_DIM):
        columns = slice(head * HEAD_DIM, (head + 1) * HEAD_DIM)
        own, other = qo_ref[:, columns], qp_ref[:, columns]
        queries = jnp.concatenate([own, other], axis=0)
        fresh = weigh(own, fresh_ref[0, :, columns])
        stale = weigh(other, stale_ref[0, :, columns])
        num = jnp.concatenate(
            [times(fresh, fresh_ref[1, :, columns]), times(stale, stale_ref[1, :, columns])], axis=0
        )
        den = jnp.concatenate([fresh, stale], axis=0)
        weights = weigh(queries, text_ref[0, :, columns]) * mask
        num = num + times(weights, text_ref[1, :, columns])
        den = den + lanes(weights)
        num, den = absorb(queries, [(ref, columns) for ref in refs[:-2]], num, den)
        num_ref[:, columns] = num
        packed = jnp.where(lane == head, jnp.sum(den, axis=1, keepdims=True), packed)
    den_ref[...] = packed


def last_kernel(first, qo_ref, qp_ref, num_ref, den_ref, far_ref, own_ref, own_den_ref, msg_ref):
    video = qo_ref.shape[0]
    width = own_ref.shape[1]
    lane = lax.broadcasted_iota(jnp.int32, (2 * video, HEAD_DIM), 1)
    packed = den_ref[...]
    for head in range(width // HEAD_DIM):
        cells = slice(head * HEAD_DIM, (head + 1) * HEAD_DIM)
        columns = slice((first + head) * HEAD_DIM, (first + head + 1) * HEAD_DIM)
        queries = jnp.concatenate([qo_ref[:, columns], qp_ref[:, columns]], axis=0)
        weights = weigh(queries, far_ref[0, :, columns])
        num = num_ref[:, columns] + times(weights, far_ref[1, :, columns])
        own_ref[:, cells] = num[:video]
        msg_ref[:, cells] = num[video:]
        total = jnp.sum(lanes(weights), axis=1, keepdims=True)
        packed = packed + jnp.where(lane == first + head, total, 0.0)
    own_den_ref[...] = packed[:video]
    msg_ref[:, width:] = packed[video:]


def merge_kernel(first, own_ref, den_ref, msg_ref, att_ref):
    width = att_ref.shape[1]
    for head in range(width // HEAD_DIM):
        columns = slice(head * HEAD_DIM, (head + 1) * HEAD_DIM)
        lane = first + head
        num = own_ref[:, columns] + msg_ref[:, columns]
        den = den_ref[:, lane : lane + 1] + msg_ref[:, width + lane : width + lane + 1]
        att_ref[:, columns] = (num / den).astype(BF16)


def part_kernel(first_ref, second_ref, w_ref, out_ref):
    half = first_ref.shape[1]
    out_ref[...] = jnp.dot(
        first_ref[...], w_ref[:half, :], preferred_element_type=F32
    ) + jnp.dot(second_ref[...], w_ref[half:, :], preferred_element_type=F32)


def more_kernel(part_ref, att_ref, w_ref, out_ref):
    half = att_ref.shape[1]
    out_ref[...] = part_ref[...] + jnp.dot(
        att_ref[...], w_ref[:half, :], preferred_element_type=F32
    )


def final_kernel(part_ref, att_ref, w_ref, hidden_ref, gate_ref, out_ref):
    half = att_ref.shape[1]
    total = part_ref[...] + jnp.dot(att_ref[...], w_ref[half:, :], preferred_element_type=F32)
    gate = gate_ref[...].reshape(1, total.shape[1])
    out_ref[...] = (hidden_ref[...].astype(F32) + gate * total).astype(BF16)


def params(megabytes):
    return pltpu.CompilerParams(vmem_limit_bytes=megabytes * 1024 * 1024)


def in_hbm(array):
    return pltpu.with_memory_space_constraint(array, pltpu.HBM)


def cost(flops, nbytes, transcendentals=0):
    return pl.CostEstimate(
        flops=int(flops), bytes_accessed=int(nbytes), transcendentals=int(transcendentals)
    )


def plain_call(kernel, outs, name, estimate, *operands):
    return pl.pallas_call(
        kernel,
        in_specs=[pl.BlockSpec(memory_space=pltpu.VMEM)] * len(operands),
        out_specs=[pl.BlockSpec(memory_space=pltpu.VMEM)] * len(outs),
        out_shape=[jax.ShapeDtypeStruct(shape, dtype) for shape, dtype in outs],
        compiler_params=params(24),
        cost_estimate=estimate,
        name=name,
    )(*operands)


def ring_moves(sections):
    chips = sections // 2
    order = list(range(0, chips, 2)) + list(range(chips - 1, 0, -2))
    moves = [], []
    for here, there in zip(order, order[1:] + order[:1]):
        for core in range(2):
            moves[core].append((2 * here + core, 2 * there + core))
            moves[1 - core].append((2 * there + core, 2 * here + core))
    return sorted(moves[0]), sorted(moves[1])


def per_device(
    sections, hidden, text_hidden, text_mask, stale_cache, qkv_weight, out_weight, query_gain,
    key_gain, norm_shift, norm_scale, branch_gate,
):
    video, features = hidden.shape
    text = text_hidden.shape[0] // 2
    width = stale_cache.shape[2]
    heads = width // HEAD_DIM
    group_columns = heads * TRIPLE
    chips = sections // 2
    out_features = out_weight.shape[1]
    top = video + EXTRA
    rows = top + text

    group = lax.axis_index("head")
    core = lax.axis_index("section") % 2
    place = jnp.stack([group, core]).astype(jnp.int32)
    swap_core = [(s, s ^ 1) for s in range(sections)]
    swap_head = [(0, 1), (1, 0)]
    ways = ring_moves(sections)
    half_way = chips // 2

    def ring_step(blocks):
        return [lax.ppermute(block, "section", way) for block, way in zip(blocks, ways)]

    vmem = pl.BlockSpec(memory_space=pltpu.VMEM)
    hbm = pl.BlockSpec(memory_space=pltpu.HBM)
    smem = pl.BlockSpec(memory_space=pltpu.SMEM)
    ring = [ring_step((stale_cache, stale_cache))]

    columns = 2 * TRIPLE
    blocks = group_columns // columns
    ahead = blocks - 1
    bands = -(-heads * 4 // (group_columns // PIECE))
    message_rows = top + bands * text // 4
    project_cost = cost(8 * rows * features * group_columns, 2 * features * group_columns)
    a_rows, message, stats, w_ahead = pl.pallas_call(
        send_kernel,
        in_specs=[smem] + [hbm] * 5,
        out_specs=[vmem] * 4,
        out_shape=[
            jax.ShapeDtypeStruct((rows, features), BF16),
            jax.ShapeDtypeStruct((message_rows, group_columns), BF16),
            jax.ShapeDtypeStruct((rows, HEAD_DIM), F32),
            jax.ShapeDtypeStruct((ahead, features, columns), BF16),
        ],
        scratch_shapes=[
            pltpu.VMEM((video, features), BF16),
            pltpu.VMEM((text, features), BF16),
            pltpu.VMEM((features,), F32),
            pltpu.VMEM((features,), F32),
            pltpu.VMEM((blocks, features, columns), BF16),
            pltpu.SemaphoreType.DMA((4,)),
            pltpu.SemaphoreType.DMA((blocks + ahead,)),
        ],
        compiler_params=params(40),
        cost_estimate=project_cost,
        name="project_send",
    )(place, *map(in_hbm, (hidden, text_hidden, norm_scale, norm_shift, qkv_weight)))

    received = lax.ppermute(message, "head", swap_head)
    ring.append(ring_step(lax.optimization_barrier((*ring[-1], message))[:2]))

    small = (query_gain, key_gain, text_mask, branch_gate, hidden, stale_cache)
    outs = pl.pallas_call(
        own_kernel,
        in_specs=[smem, vmem, vmem, hbm, hbm] + [hbm] * len(small),
        out_specs=[vmem] * (4 + len(small)),
        out_shape=[
            jax.ShapeDtypeStruct((top, group_columns), F32),
            jax.ShapeDtypeStruct((text, 2 * width), F32),
            jax.ShapeDtypeStruct((width, out_features), BF16),
            jax.ShapeDtypeStruct((width, out_features), BF16),
        ]
        + [jax.ShapeDtypeStruct(array.shape, array.dtype) for array in small],
        scratch_shapes=[
            pltpu.VMEM((blocks - ahead, features, columns), BF16),
            pltpu.SemaphoreType.DMA((blocks - ahead,)),
            pltpu.SemaphoreType.DMA((len(small) + 2,)),
        ],
        compiler_params=params(36),
        cost_estimate=project_cost,
        name="project_own",
    )(place, a_rows, w_ahead, *map(in_hbm, (qkv_weight, out_weight) + small))
    own, own_text, w_own, w_other = outs[:4]
    query_gain, key_gain, text_mask, branch_gate, hidden, stale = outs[4:]

    for _ in range(half_way - 3):
        ring.append(ring_step(lax.optimization_barrier((*ring[-1], own))[:2]))
    far = lax.ppermute(ring[-1][0], "section", ways[0])

    queries, new_cache, fresh = plain_call(
        functools.partial(norm_kernel, features * 2),
        [((video, width), BF16), ((2, video, width), BF16), ((2, video, width), BF16)],
        "norm_video",
        cost(1000 * top * group_columns, 8 * top * group_columns),
        own, received, stats, query_gain, key_gain,
    )
    other_queries = lax.ppermute(queries, "section", swap_core)
    (text_kv,) = plain_call(
        functools.partial(text_kernel, features * 2),
        [((2, text, width), BF16)],
        "norm_text",
        cost(1000 * text * group_columns, 8 * text * group_columns),
        own_text, received, stats, own, key_gain,
    )

    arrived = [block for step in ring for block in step]
    context = (len(arrived) + 1) * video + text
    num, den = pl.pallas_call(
        first_kernel,
        in_specs=[smem] + [vmem] * (6 + len(arrived)),
        out_specs=[vmem] * 2,
        out_shape=[
            jax.ShapeDtypeStruct((2 * video, width), F32),
            jax.ShapeDtypeStruct((2 * video, HEAD_DIM), F32),
        ],
        compiler_params=params(24),
        cost_estimate=cost(
            32 * video * context * width, 4 * context * width, 2 * video * context * heads
        ),
        name="attend_first",
    )(place, queries, other_queries, fresh, stale, text_kv, text_mask, *arrived)

    attended, other_attended = [], []
    for first in (0, heads // 2):
        if attended:
            num = lax.optimization_barrier((num, num_own))[0]
        num_own, den_own, num_message = plain_call(
            functools.partial(last_kernel, first),
            [
                ((video, width // 2), F32),
                ((video, HEAD_DIM), F32),
                ((video, width // 2 + HEAD_DIM), F32),
            ],
            "attend_last",
            cost(16 * video * video * width, 6 * video * width, video * video * heads),
            queries, other_queries, num, den, far,
        )
        num_received = lax.ppermute(num_message, "section", swap_core)
        attended += plain_call(
            functools.partial(merge_kernel, first),
            [((video, width // 2), BF16)],
            "merge",
            cost(2 * video * width, 5 * video * width),
            num_own, den_own, num_received,
        )
        other_attended.append(lax.ppermute(attended[-1], "head", swap_head))

    out_cost = cost(4 * video * width * out_features, 2 * width * out_features)
    (part,) = plain_call(
        part_kernel, [((video, out_features), F32)], "part_out", out_cost, *attended, w_own
    )
    (part,) = plain_call(
        more_kernel, [((video, out_features), F32)], "more_out", out_cost,
        part, other_attended[0], w_other,
    )
    (mixed,) = plain_call(
        final_kernel, [((video, out_features), BF16)], "final_out", out_cost,
        part, other_attended[1], w_other, hidden, branch_gate,
    )
    return (mixed, new_cache)


def solution(mesh):
    in_specs = (
        P("section", "head"),
        P(None, "head"),
        P(),
        P(None, "section", "head"),
        P("head", None),
        P(None, "head"),
        P(),
        P(),
        P("head"),
        P("head"),
        P("head"),
    )
    out_specs = (P("section", "head"), P(None, "section", "head"))
    return jax.shard_map(
        functools.partial(per_device, mesh.shape["section"]),
        mesh=mesh, in_specs=in_specs, out_specs=out_specs, check_vma=False,
    )
```

```python
import functools
import math

import jax
import jax.numpy as jnp
from jax import lax
from jax.experimental import pallas as pl
from jax.experimental.pallas import tpu as pltpu
from jax.sharding import PartitionSpec as P

HEAD_DIM = 128
TRIPLE = 3 * HEAD_DIM
EXTRA = 16
STAT_ROW = 8
PIECE = 2 * HEAD_DIM
EPS = 1e-06
F32 = jnp.float32
BF16 = jnp.bfloat16


def split_bf16(value, parts):
    pieces = []
    rest = value
    for _ in range(parts):
        piece = rest.astype(BF16)
        pieces.append(piece)
        rest = rest - piece.astype(F32)
    return pieces


def block_copies(w_ref, first, targets, sems, base):
    copies = []
    for index, target in enumerate(targets):
        columns = target.shape[1]
        start = pl.multiple_of(first + index * columns, HEAD_DIM)
        copies.append(
            pltpu.make_async_copy(w_ref.at[:, pl.ds(start, columns)], target, sems.at[base + index])
        )
    return copies


def send_kernel(
    place_ref, x_ref, t_ref, scale_ref, shift_ref, w_ref,
    a_ref, msg_ref, tmsg_ref, stat_ref, ahead_ref,
    x_buffer, t_buffer, scale_buffer, shift_buffer, w_buffer, in_sems, w_sems,
):
    video, features = x_buffer.shape
    text = t_buffer.shape[0]
    top = video + EXTRA
    blocks, _, columns = w_buffer.shape
    width = blocks * columns
    copies = [
        pltpu.make_async_copy(scale_ref, scale_buffer, in_sems.at[0]),
        pltpu.make_async_copy(shift_ref, shift_buffer, in_sems.at[1]),
        pltpu.make_async_copy(x_ref, x_buffer, in_sems.at[2]),
        pltpu.make_async_copy(
            t_ref.at[pl.ds(pl.multiple_of(place_ref[1] * text, text), text)], t_buffer, in_sems.at[3]
        ),
    ]
    w_copies = block_copies(
        w_ref, (1 - place_ref[0]) * width, [w_buffer.at[i] for i in range(blocks)], w_sems, 0
    ) + block_copies(
        w_ref, place_ref[0] * width, [ahead_ref.at[i] for i in range(ahead_ref.shape[0])],
        w_sems, blocks,
    )
    for copy in copies + w_copies[:1]:
        copy.start()

    copies[0].wait()
    copies[1].wait()
    gain = 1.0 + scale_buffer[...].reshape(1, features)
    pieces = split_bf16(gain, 2) + split_bf16(shift_buffer[...].reshape(1, features), 2)
    row = lax.broadcasted_iota(jnp.int32, (EXTRA, features), 0)
    extra = jnp.zeros((EXTRA, features), F32)
    for index, piece in enumerate(pieces):
        extra = jnp.where(row == index, piece.astype(F32), extra)
    a_ref[video:top, :] = extra.astype(BF16)

    def prepare(rows_ref, start):
        rows = rows_ref[...].astype(F32)
        count = rows.shape[0]
        mean = jnp.sum(rows, axis=1, keepdims=True) * (1.0 / features)
        centered = rows - mean
        second = jnp.sum(centered * centered, axis=1, keepdims=True)
        a_ref[start : start + count, :] = (centered * gain).astype(BF16)
        lane = lax.broadcasted_iota(jnp.int32, (count, HEAD_DIM), 1)
        packed = jnp.zeros((count, HEAD_DIM), F32)
        for index, piece in enumerate(split_bf16(mean, 3) + split_bf16(second, 3)):
            packed = jnp.where(lane == STAT_ROW + index, piece.astype(F32), packed)
        stat_ref[start : start + count, :] = jnp.where(
            lane == 0, mean, jnp.where(lane == 1, second, 0.0)
        )
        return jnp.transpose(packed)[:EXTRA]

    copies[2].wait()
    w_copies[1].start()
    video_stats = prepare(x_buffer, 0)
    copies[3].wait()
    w_copies[2].start()
    text_stats = prepare(t_buffer, top)
    stat_ref[video:top, :] = jnp.zeros((EXTRA, HEAD_DIM), F32)

    for block in range(blocks):
        w_copies[block].wait()
        if block + 3 < len(w_copies):
            w_copies[block + 3].start()
        for piece in range(columns // PIECE):
            start = block * columns + piece * PIECE
            product = jnp.dot(
                a_ref[...], w_buffer[block, :, piece * PIECE : (piece + 1) * PIECE],
                preferred_element_type=F32,
            )
            msg_ref[:, start : start + PIECE] = product[:top].astype(BF16)
            if start == 0:
                stats = jnp.concatenate([video_stats, text_stats], axis=1)
                msg_ref[video:, : video + text] = (product[video:top] + stats).astype(BF16)
            for source, target in text_columns(start):
                tmsg_ref[:, target : target + HEAD_DIM] = product[top:, source].astype(BF16)
    for copy in w_copies[blocks:]:
        copy.wait()


def text_columns(first):
    for start in range(0, PIECE, HEAD_DIM):
        head, kind = divmod((first + start) // HEAD_DIM, 3)
        if kind:
            yield slice(start, start + HEAD_DIM), (2 * head + kind - 1) * HEAD_DIM


def own_kernel(place_ref, a_ref, ahead_ref, w_ref, out_weight_ref, *refs):
    small = (len(refs) - 7) // 2
    out_ref, text_ref, w_own_ref, w_other_ref = refs[small : small + 4]
    w_buffer, w_sems, sems = refs[-3:]
    top = out_ref.shape[0]
    depth = w_own_ref.shape[0]
    group = place_ref[0]
    ahead, _, columns = ahead_ref.shape
    later = w_buffer.shape[0]
    w_copies = block_copies(
        w_ref, (group * (ahead + later) + ahead) * columns, [w_buffer.at[i] for i in range(later)],
        w_sems, 0,
    )
    pairs = list(zip(refs[:small], refs[small + 4 : -3]))
    for half, target in ((group, w_own_ref), (1 - group, w_other_ref)):
        rows = pl.ds(pl.multiple_of(half * depth, depth), depth)
        pairs.append((out_weight_ref.at[rows], target))
    copies = [
        pltpu.make_async_copy(source, target, sems.at[index])
        for index, (source, target) in enumerate(pairs)
    ]
    for copy in w_copies:
        copy.start()

    def write(start, product):
        out_ref[:, start : start + PIECE] = product[:top]
        for source, target in text_columns(start):
            text_ref[:, target : target + HEAD_DIM] = product[top:, source]

    for block in range(ahead + later):
        if block == ahead:
            for copy in w_copies:
                copy.wait()
        if block == min(1, ahead):
            for copy in copies:
                copy.start()
        for piece in range(columns // PIECE):
            cells = slice(piece * PIECE, (piece + 1) * PIECE)
            part = ahead_ref[block, :, cells] if block < ahead else w_buffer[block - ahead, :, cells]
            write(
                block * columns + piece * PIECE,
                jnp.dot(a_ref[...], part, preferred_element_type=F32),
            )
    for copy in copies:
        copy.wait()


def row_stats(total_features, own, received):
    count = own.shape[0]
    received = received.astype(F32)
    padding = jnp.zeros((HEAD_DIM - received.shape[0], count), F32)
    received = jnp.transpose(jnp.concatenate([received, padding], axis=0))
    parts = [received[:, STAT_ROW + index : STAT_ROW + index + 1] for index in range(6)]
    gap = 0.5 * (own[:, 0:1] - (parts[0] + parts[1] + parts[2]))
    second = own[:, 1:2] + (parts[3] + parts[4] + parts[5])
    var = second * (1.0 / total_features) + gap * gap
    return gap, lax.rsqrt(var + EPS)


def column_terms(own, other):
    other = other.astype(F32)
    scale = (own[0:1] + own[1:2]) - (other[0:1] + other[1:2])
    shift = (own[2:3] + own[3:4]) + (other[2:3] + other[3:4])
    return scale, shift


def head_norm(part, gain):
    square = jnp.sum(part * part, axis=1, keepdims=True) * (1.0 / HEAD_DIM)
    return part * lax.rsqrt(square + EPS) * gain


def norm_kernel(
    total_features, own_ref, msg_ref, stat_ref, qg_ref, kg_ref, q_ref, cache_ref, kv_ref,
):
    video = q_ref.shape[0]
    top = video + EXTRA
    query_gain = qg_ref[...].reshape(1, HEAD_DIM)
    key_gain = kg_ref[...].reshape(1, HEAD_DIM)
    heads = q_ref.shape[1] // HEAD_DIM
    gap, inverse = row_stats(total_features, stat_ref[:video, :], msg_ref[video:top, :video])
    for head in range(heads):
        part = slice(head * TRIPLE, (head + 1) * TRIPLE)
        columns = slice(head * HEAD_DIM, (head + 1) * HEAD_DIM)
        scale, shift = column_terms(own_ref[video:, part], msg_ref[video:top, part])
        total = own_ref[:video, part] + msg_ref[:video, part].astype(F32)
        total = (total + gap * scale) * inverse + shift
        q_ref[:, columns] = head_norm(total[:, :HEAD_DIM], query_gain).astype(BF16)
        keys = head_norm(total[:, HEAD_DIM : 2 * HEAD_DIM], key_gain).astype(BF16)
        values = total[:, 2 * HEAD_DIM :].astype(BF16)
        cache_ref[0, :, columns] = keys
        cache_ref[1, :, columns] = values
        kv_ref[0, :, columns] = keys
        kv_ref[1, :, columns] = values


def text_kernel(total_features, own_ref, tmsg_ref, stat_ref, top_ref, msg_ref, kg_ref, kv_ref):
    text = kv_ref.shape[1]
    heads = kv_ref.shape[2] // HEAD_DIM
    top = top_ref.shape[0]
    video = top - EXTRA
    key_gain = kg_ref[...].reshape(1, HEAD_DIM)
    gap, inverse = row_stats(
        total_features, stat_ref[top:, :], msg_ref[video:top, video : video + text]
    )
    for head in range(heads):
        part = slice(head * TRIPLE + HEAD_DIM, (head + 1) * TRIPLE)
        pair = slice(head * PIECE, (head + 1) * PIECE)
        columns = slice(head * HEAD_DIM, (head + 1) * HEAD_DIM)
        scale, shift = column_terms(top_ref[video:, part], msg_ref[video:top, part])
        total = own_ref[:, pair] + tmsg_ref[:, pair].astype(F32)
        total = (total + gap * scale) * inverse + shift
        kv_ref[0, :, columns] = head_norm(total[:, :HEAD_DIM], key_gain).astype(BF16)
        kv_ref[1, :, columns] = total[:, HEAD_DIM:].astype(BF16)


FACTOR = math.log2(math.e) / math.sqrt(HEAD_DIM)


def weigh(rows, keys):
    scores = lax.dot_general(rows, keys, (((1,), (1,)), ((), ())), preferred_element_type=F32)
    return jnp.exp2(scores * FACTOR)


def lanes(weights):
    total = weights[:, :HEAD_DIM]
    for start in range(HEAD_DIM, weights.shape[1], HEAD_DIM):
        total = total + weights[:, start : start + HEAD_DIM]
    return total


def times(weights, values):
    return jnp.dot(weights.astype(BF16), values, preferred_element_type=F32)


def absorb(queries, blocks, num, den):
    for first in range(0, len(blocks), 2):
        pair = blocks[first : first + 2]
        keys = jnp.concatenate([ref[0, :, columns] for ref, columns in pair], axis=0)
        values = jnp.concatenate([ref[1, :, columns] for ref, columns in pair], axis=0)
        weights = weigh(queries, keys)
        num = num + times(weights, values)
        den = den + lanes(weights)
    return num, den


def split_kernel(*refs):
    count = len(refs) // 3
    for index in range(count):
        half = refs[index].shape[2] // 2
        refs[count + 2 * index][...] = refs[index][:, :, :half]
        refs[count + 2 * index + 1][...] = refs[index][:, :, half:]


def first_kernel(count, qo_ref, qp_ref, fresh_ref, stale_ref, *refs):
    num_ref, den_ref = refs[-2:]
    whole, halves = refs[:count], refs[count:-2]
    video, width = qo_ref.shape
    lane = lax.broadcasted_iota(jnp.int32, (2 * video, HEAD_DIM), 1)
    packed = jnp.zeros((2 * video, HEAD_DIM), F32)
    for head in range(width // HEAD_DIM):
        columns = slice(head * HEAD_DIM, (head + 1) * HEAD_DIM)
        second, start = divmod(head * HEAD_DIM, width // 2)
        cells = slice(start, start + HEAD_DIM)
        own, other = qo_ref[:, columns], qp_ref[:, columns]
        queries = jnp.concatenate([own, other], axis=0)
        fresh = weigh(own, fresh_ref[0, :, columns])
        stale = weigh(other, stale_ref[0, :, columns])
        num = jnp.concatenate(
            [times(fresh, fresh_ref[1, :, columns]), times(stale, stale_ref[1, :, columns])], axis=0
        )
        den = jnp.concatenate([fresh, stale], axis=0)
        blocks = [(ref, columns) for ref in whole] + [(ref, cells) for ref in halves[second::2]]
        num, den = absorb(queries, blocks, num, den)
        num_ref[:, columns] = num
        packed = jnp.where(lane == head, jnp.sum(den, axis=1, keepdims=True), packed)
    den_ref[...] = packed


def last_kernel(
    first, place_ref, qo_ref, qp_ref, num_ref, den_ref, text_ref, mask_ref, far_ref,
    own_ref, own_den_ref, msg_ref,
):
    video = qo_ref.shape[0]
    text, width = text_ref.shape[1], far_ref.shape[2]
    lane = lax.broadcasted_iota(jnp.int32, (2 * video, HEAD_DIM), 1)
    mask = mask_ref[...].reshape(1, 2 * text).astype(F32)
    mask = jnp.where(place_ref[1] == 0, mask[:, :text], mask[:, text:])
    keep = jnp.concatenate([mask, jnp.ones((1, video), F32)], axis=1)
    packed = den_ref[...]
    for head in range(width // HEAD_DIM):
        cells = slice(head * HEAD_DIM, (head + 1) * HEAD_DIM)
        columns = slice((first + head) * HEAD_DIM, (first + head + 1) * HEAD_DIM)
        queries = jnp.concatenate([qo_ref[:, columns], qp_ref[:, columns]], axis=0)
        keys = jnp.concatenate([text_ref[0, :, columns], far_ref[0, :, cells]], axis=0)
        values = jnp.concatenate([text_ref[1, :, columns], far_ref[1, :, cells]], axis=0)
        weights = weigh(queries, keys) * keep
        num = num_ref[:, columns] + times(weights, values)
        own_ref[:, cells] = num[:video]
        msg_ref[:, cells] = num[video:]
        total = jnp.sum(lanes(weights), axis=1, keepdims=True)
        packed = packed + jnp.where(lane == first + head, total, 0.0)
    own_den_ref[...] = packed[:video]
    msg_ref[:, width:] = packed[video:]


def merge_kernel(first, own_ref, den_ref, msg_ref, att_ref):
    width = att_ref.shape[1]
    for head in range(width // HEAD_DIM):
        columns = slice(head * HEAD_DIM, (head + 1) * HEAD_DIM)
        lane = first + head
        num = own_ref[:, columns] + msg_ref[:, columns]
        den = den_ref[:, lane : lane + 1] + msg_ref[:, width + lane : width + lane + 1]
        att_ref[:, columns] = (num / den).astype(BF16)


def part_kernel(first_ref, second_ref, w_ref, out_ref):
    half = first_ref.shape[1]
    out_ref[...] = jnp.dot(
        first_ref[...], w_ref[:half, :], preferred_element_type=F32
    ) + jnp.dot(second_ref[...], w_ref[half:, :], preferred_element_type=F32)


def more_kernel(part_ref, att_ref, w_ref, out_ref):
    half = att_ref.shape[1]
    out_ref[...] = part_ref[...] + jnp.dot(
        att_ref[...], w_ref[:half, :], preferred_element_type=F32
    )


def final_kernel(part_ref, att_ref, w_ref, hidden_ref, gate_ref, out_ref):
    half = att_ref.shape[1]
    total = part_ref[...] + jnp.dot(att_ref[...], w_ref[half:, :], preferred_element_type=F32)
    gate = gate_ref[...].reshape(1, total.shape[1])
    out_ref[...] = (hidden_ref[...].astype(F32) + gate * total).astype(BF16)


def params(megabytes):
    return pltpu.CompilerParams(vmem_limit_bytes=megabytes * 1024 * 1024)


def in_hbm(array):
    return pltpu.with_memory_space_constraint(array, pltpu.HBM)


def cost(flops, nbytes, transcendentals=0):
    return pl.CostEstimate(
        flops=int(flops), bytes_accessed=int(nbytes), transcendentals=int(transcendentals)
    )


def plain_call(kernel, outs, name, estimate, *operands):
    return pl.pallas_call(
        kernel,
        in_specs=[pl.BlockSpec(memory_space=pltpu.VMEM)] * len(operands),
        out_specs=[pl.BlockSpec(memory_space=pltpu.VMEM)] * len(outs),
        out_shape=[jax.ShapeDtypeStruct(shape, dtype) for shape, dtype in outs],
        compiler_params=params(24),
        cost_estimate=estimate,
        name=name,
    )(*operands)


def ring_moves(sections):
    chips = sections // 2
    order = list(range(0, chips, 2)) + list(range(chips - 1, 0, -2))
    moves = [], []
    for here, there in zip(order, order[1:] + order[:1]):
        for core in range(2):
            moves[core].append((2 * here + core, 2 * there + core))
            moves[1 - core].append((2 * there + core, 2 * here + core))
    return sorted(moves[0]), sorted(moves[1])


def per_device(
    sections, hidden, text_hidden, text_mask, stale_cache, qkv_weight, out_weight, query_gain,
    key_gain, norm_shift, norm_scale, branch_gate,
):
    video, features = hidden.shape
    text = text_hidden.shape[0] // 2
    width = stale_cache.shape[2]
    heads = width // HEAD_DIM
    group_columns = heads * TRIPLE
    chips = sections // 2
    out_features = out_weight.shape[1]
    top = video + EXTRA
    rows = top + text

    group = lax.axis_index("head")
    core = lax.axis_index("section") % 2
    place = jnp.stack([group, core]).astype(jnp.int32)
    swap_core = [(s, s ^ 1) for s in range(sections)]
    swap_head = [(0, 1), (1, 0)]
    ways = ring_moves(sections)
    half_way = chips // 2

    def ring_step(blocks):
        return [lax.ppermute(block, "section", way) for block, way in zip(blocks, ways)]

    vmem = pl.BlockSpec(memory_space=pltpu.VMEM)
    hbm = pl.BlockSpec(memory_space=pltpu.HBM)
    smem = pl.BlockSpec(memory_space=pltpu.SMEM)
    whole = ring_step((stale_cache, stale_cache))

    columns = 2 * TRIPLE
    blocks = group_columns // columns
    ahead = blocks - 1
    project_cost = cost(8 * rows * features * group_columns, 2 * features * group_columns)
    a_rows, message, text_message, stats, w_ahead = pl.pallas_call(
        send_kernel,
        in_specs=[smem] + [hbm] * 5,
        out_specs=[vmem] * 5,
        out_shape=[
            jax.ShapeDtypeStruct((rows, features), BF16),
            jax.ShapeDtypeStruct((top, group_columns), BF16),
            jax.ShapeDtypeStruct((text, 2 * width), BF16),
            jax.ShapeDtypeStruct((rows, HEAD_DIM), F32),
            jax.ShapeDtypeStruct((ahead, features, columns), BF16),
        ],
        scratch_shapes=[
            pltpu.VMEM((video, features), BF16),
            pltpu.VMEM((text, features), BF16),
            pltpu.VMEM((features,), F32),
            pltpu.VMEM((features,), F32),
            pltpu.VMEM((blocks, features, columns), BF16),
            pltpu.SemaphoreType.DMA((4,)),
            pltpu.SemaphoreType.DMA((blocks + ahead,)),
        ],
        compiler_params=params(40),
        cost_estimate=project_cost,
        name="project_send",
    )(place, *map(in_hbm, (hidden, text_hidden, norm_scale, norm_shift, qkv_weight)))

    received = lax.ppermute(message, "head", swap_head)
    split = plain_call(
        split_kernel, [((2, video, width // 2), BF16)] * 4, "split_heads", cost(0, 8 * video * width),
        *lax.optimization_barrier((*whole, message))[:2],
    )
    chains = [[ring_step((split[0], split[2]))], [ring_step((split[1], split[3]))]]

    small = (query_gain, key_gain, text_mask, branch_gate, hidden, stale_cache)
    outs = pl.pallas_call(
        own_kernel,
        in_specs=[smem, vmem, vmem, hbm, hbm] + [hbm] * len(small),
        out_specs=[vmem] * (4 + len(small)),
        out_shape=[
            jax.ShapeDtypeStruct((top, group_columns), F32),
            jax.ShapeDtypeStruct((text, 2 * width), F32),
            jax.ShapeDtypeStruct((width, out_features), BF16),
            jax.ShapeDtypeStruct((width, out_features), BF16),
        ]
        + [jax.ShapeDtypeStruct(array.shape, array.dtype) for array in small],
        scratch_shapes=[
            pltpu.VMEM((blocks - ahead, features, columns), BF16),
            pltpu.SemaphoreType.DMA((blocks - ahead,)),
            pltpu.SemaphoreType.DMA((len(small) + 2,)),
        ],
        compiler_params=params(36),
        cost_estimate=project_cost,
        name="project_own",
    )(place, a_rows, w_ahead, *map(in_hbm, (qkv_weight, out_weight) + small))
    own, own_text, w_own, w_other = outs[:4]
    query_gain, key_gain, text_mask, branch_gate, hidden, stale = outs[4:]

    for _ in range(half_way - 3):
        for chain in chains:
            chain.append(ring_step(lax.optimization_barrier((*chain[-1], own))[:2]))
    far = [lax.ppermute(chain[-1][0], "section", ways[0]) for chain in chains]

    received = lax.optimization_barrier((received, *chains[0][0], *chains[1][0]))[0]
    queries, new_cache, fresh = plain_call(
        functools.partial(norm_kernel, features * 2),
        [((video, width), BF16), ((2, video, width), BF16), ((2, video, width), BF16)],
        "norm_video",
        cost(1000 * top * group_columns, 8 * top * group_columns),
        own, received, stats, query_gain, key_gain,
    )
    other_queries = lax.ppermute(queries, "section", swap_core)
    text_received = lax.ppermute(
        lax.optimization_barrier((text_message, queries))[0], "head", swap_head
    )

    halves = [
        block
        for steps in zip(*chains)
        for way in range(2)
        for block in (steps[0][way], steps[1][way])
    ]
    context = (len(halves) // 2 + 3) * video
    num, den = plain_call(
        functools.partial(first_kernel, 2),
        [((2 * video, width), F32), ((2 * video, HEAD_DIM), F32)],
        "attend_first",
        cost(32 * video * context * width, 4 * context * width, 2 * video * context * heads),
        queries, other_queries, fresh, stale, *whole, *halves,
    )
    (text_kv,) = plain_call(
        functools.partial(text_kernel, features * 2),
        [((2, text, width), BF16)],
        "norm_text",
        cost(1000 * text * group_columns, 8 * text * group_columns),
        own_text, text_received, stats, own, received, key_gain,
    )

    last_context = video + text
    attended, other_attended = [], []
    for index, block in enumerate(far):
        first = index * heads // 2
        if attended:
            num = lax.optimization_barrier((num, num_own))[0]
        num_own, den_own, num_message = pl.pallas_call(
            functools.partial(last_kernel, first),
            in_specs=[smem] + [vmem] * 7,
            out_specs=[vmem] * 3,
            out_shape=[
                jax.ShapeDtypeStruct((video, width // 2), F32),
                jax.ShapeDtypeStruct((video, HEAD_DIM), F32),
                jax.ShapeDtypeStruct((video, width // 2 + HEAD_DIM), F32),
            ],
            compiler_params=params(24),
            cost_estimate=cost(
                16 * video * last_context * width, 6 * video * width, video * last_context * heads
            ),
            name="attend_last",
        )(place, queries, other_queries, num, den, text_kv, text_mask, block)
        num_received = lax.ppermute(num_message, "section", swap_core)
        attended += plain_call(
            functools.partial(merge_kernel, first),
            [((video, width // 2), BF16)],
            "merge",
            cost(2 * video * width, 5 * video * width),
            num_own, den_own, num_received,
        )
        other_attended.append(lax.ppermute(attended[-1], "head", swap_head))

    out_cost = cost(4 * video * width * out_features, 2 * width * out_features)
    (part,) = plain_call(
        part_kernel, [((video, out_features), F32)], "part_out", out_cost, *attended, w_own
    )
    (part,) = plain_call(
        more_kernel, [((video, out_features), F32)], "more_out", out_cost,
        part, other_attended[0], w_other,
    )
    (mixed,) = plain_call(
        final_kernel, [((video, out_features), BF16)], "final_out", out_cost,
        part, other_attended[1], w_other, hidden, branch_gate,
    )
    return (mixed, new_cache)


def solution(mesh):
    in_specs = (
        P("section", "head"),
        P(None, "head"),
        P(),
        P(None, "section", "head"),
        P("head", None),
        P(None, "head"),
        P(),
        P(),
        P("head"),
        P("head"),
        P("head"),
    )
    out_specs = (P("section", "head"), P(None, "section", "head"))
    return jax.shard_map(
        functools.partial(per_device, mesh.shape["section"]),
        mesh=mesh, in_specs=in_specs, out_specs=out_specs, check_vma=False,
    )
```

```python
import functools
import math

import jax
import jax.numpy as jnp
from jax import lax
from jax.experimental import pallas as pl
from jax.experimental.pallas import tpu as pltpu
from jax.sharding import PartitionSpec as P

HEAD_DIM = 128
TRIPLE = 3 * HEAD_DIM
EXTRA = 16
STAT_ROW = 8
PIECE = 2 * HEAD_DIM
EPS = 1e-06
F32 = jnp.float32
BF16 = jnp.bfloat16


def split_bf16(value, parts):
    pieces = []
    rest = value
    for _ in range(parts):
        piece = rest.astype(BF16)
        pieces.append(piece)
        rest = rest - piece.astype(F32)
    return pieces


def block_copies(w_ref, first, targets, sems, base):
    copies = []
    for index, target in enumerate(targets):
        columns = target.shape[1]
        start = pl.multiple_of(first + index * columns, HEAD_DIM)
        copies.append(
            pltpu.make_async_copy(w_ref.at[:, pl.ds(start, columns)], target, sems.at[base + index])
        )
    return copies


def send_kernel(
    place_ref, x_ref, t_ref, scale_ref, shift_ref, w_ref,
    a_ref, msg_ref, stat_ref, ahead_ref,
    x_buffer, t_buffer, scale_buffer, shift_buffer, w_buffer, in_sems, w_sems,
):
    video, features = x_buffer.shape
    text = t_buffer.shape[0]
    top = video + EXTRA
    blocks, _, columns = w_buffer.shape
    width = blocks * columns
    copies = [
        pltpu.make_async_copy(scale_ref, scale_buffer, in_sems.at[0]),
        pltpu.make_async_copy(shift_ref, shift_buffer, in_sems.at[1]),
        pltpu.make_async_copy(x_ref, x_buffer, in_sems.at[2]),
        pltpu.make_async_copy(
            t_ref.at[pl.ds(pl.multiple_of(place_ref[1] * text, text), text)], t_buffer, in_sems.at[3]
        ),
    ]
    w_copies = block_copies(
        w_ref, (1 - place_ref[0]) * width, [w_buffer.at[i] for i in range(blocks)], w_sems, 0
    ) + block_copies(
        w_ref, place_ref[0] * width, [ahead_ref.at[i] for i in range(ahead_ref.shape[0])],
        w_sems, blocks,
    )
    for copy in copies + w_copies[:1]:
        copy.start()

    copies[0].wait()
    copies[1].wait()
    gain = 1.0 + scale_buffer[...].reshape(1, features)
    pieces = split_bf16(gain, 2) + split_bf16(shift_buffer[...].reshape(1, features), 2)
    row = lax.broadcasted_iota(jnp.int32, (EXTRA, features), 0)
    extra = jnp.zeros((EXTRA, features), F32)
    for index, piece in enumerate(pieces):
        extra = jnp.where(row % 4 == index, piece.astype(F32), extra)
    a_ref[video:top, :] = extra.astype(BF16)

    def prepare(rows_ref, start):
        rows = rows_ref[...].astype(F32)
        count = rows.shape[0]
        mean = jnp.sum(rows, axis=1, keepdims=True) * (1.0 / features)
        centered = rows - mean
        second = jnp.sum(centered * centered, axis=1, keepdims=True)
        a_ref[start : start + count, :] = (centered * gain).astype(BF16)
        lane = lax.broadcasted_iota(jnp.int32, (count, HEAD_DIM), 1)
        packed = jnp.zeros((count, HEAD_DIM), F32)
        for index, piece in enumerate(split_bf16(mean, 3) + split_bf16(second, 3)):
            packed = jnp.where(lane == STAT_ROW + index, piece.astype(F32), packed)
        stat_ref[start : start + count, :] = jnp.where(
            lane == 0, mean, jnp.where(lane == 1, second, 0.0)
        )
        return jnp.transpose(packed)[:EXTRA]

    copies[2].wait()
    w_copies[1].start()
    video_stats = prepare(x_buffer, 0)
    copies[3].wait()
    w_copies[2].start()
    text_stats = prepare(t_buffer, top)
    stat_ref[video:top, :] = jnp.zeros((EXTRA, HEAD_DIM), F32)

    band = lax.broadcasted_iota(jnp.int32, (EXTRA, PIECE), 0) // 4
    spare = heads_of(width) * 4
    for block in range(blocks):
        w_copies[block].wait()
        if block + 3 < len(w_copies):
            w_copies[block + 3].start()
        for piece in range(block * columns // PIECE, (block + 1) * columns // PIECE):
            start = piece * PIECE
            local = start - block * columns
            product = jnp.dot(
                a_ref[...], w_buffer[block, :, local : local + PIECE], preferred_element_type=F32
            )
            msg_ref[:video, start : start + PIECE] = product[:video].astype(BF16)
            group, member = divmod(piece, 4)
            if member == 0:
                terms = product[video:top]
            else:
                terms = jnp.where(band == member, product[video:top], terms)
            if member == 3 or start + PIECE == width:
                rows, cells = slot(text, width, spare, group)
                msg_ref[video + rows.start : video + rows.stop, cells] = terms.astype(BF16)
            for source, target in text_columns(start):
                part = product[top:, source].astype(BF16)
                for quarter in range(4):
                    rows, cells = slot(text, width, target // PIECE * 4 + quarter)
                    first = cells.start + target % PIECE
                    msg_ref[
                        video + rows.start : video + rows.stop, first : first + HEAD_DIM
                    ] = part[quarter * text // 4 : (quarter + 1) * text // 4]
    rows, cells = slot(text, width, spare, -(-width // PIECE // 4))
    msg_ref[video + rows.start : video + rows.stop, cells] = jnp.concatenate(
        [video_stats, text_stats], axis=1
    ).astype(BF16)
    for copy in w_copies[blocks:]:
        copy.wait()


def heads_of(width):
    return width // TRIPLE


def slot(text, width, index, part=None):
    depth = text // 4
    if part is not None:
        index += part // (depth // EXTRA)
    band, place = divmod(index, width // PIECE)
    rows = slice(band * depth, (band + 1) * depth)
    if part is not None:
        first = rows.start + part % (depth // EXTRA) * EXTRA
        rows = slice(first, first + EXTRA)
    return rows, slice(place * PIECE, (place + 1) * PIECE)


def text_columns(first):
    for start in range(0, PIECE, HEAD_DIM):
        head, kind = divmod((first + start) // HEAD_DIM, 3)
        if kind:
            yield slice(start, start + HEAD_DIM), (2 * head + kind - 1) * HEAD_DIM


def own_kernel(place_ref, a_ref, ahead_ref, w_ref, out_weight_ref, *refs):
    small = (len(refs) - 7) // 2
    out_ref, text_ref, w_own_ref, w_other_ref = refs[small : small + 4]
    w_buffer, w_sems, sems = refs[-3:]
    top = out_ref.shape[0]
    depth = w_own_ref.shape[0]
    group = place_ref[0]
    ahead, _, columns = ahead_ref.shape
    later = w_buffer.shape[0]
    w_copies = block_copies(
        w_ref, (group * (ahead + later) + ahead) * columns, [w_buffer.at[i] for i in range(later)],
        w_sems, 0,
    )
    pairs = list(zip(refs[:small], refs[small + 4 : -3]))
    for half, target in ((group, w_own_ref), (1 - group, w_other_ref)):
        rows = pl.ds(pl.multiple_of(half * depth, depth), depth)
        pairs.append((out_weight_ref.at[rows], target))
    copies = [
        pltpu.make_async_copy(source, target, sems.at[index])
        for index, (source, target) in enumerate(pairs)
    ]
    for copy in w_copies:
        copy.start()

    def write(start, product):
        out_ref[:, start : start + PIECE] = product[:top]
        for source, target in text_columns(start):
            text_ref[:, target : target + HEAD_DIM] = product[top:, source]

    for block in range(ahead + later):
        if block == ahead:
            for copy in w_copies:
                copy.wait()
        if block == min(1, ahead):
            for copy in copies:
                copy.start()
        for piece in range(columns // PIECE):
            cells = slice(piece * PIECE, (piece + 1) * PIECE)
            part = ahead_ref[block, :, cells] if block < ahead else w_buffer[block - ahead, :, cells]
            write(
                block * columns + piece * PIECE,
                jnp.dot(a_ref[...], part, preferred_element_type=F32),
            )
    for copy in copies:
        copy.wait()


def row_stats(total_features, own, received):
    count = own.shape[0]
    received = received.astype(F32)
    padding = jnp.zeros((HEAD_DIM - received.shape[0], count), F32)
    received = jnp.transpose(jnp.concatenate([received, padding], axis=0))
    parts = [received[:, STAT_ROW + index : STAT_ROW + index + 1] for index in range(6)]
    gap = 0.5 * (own[:, 0:1] - (parts[0] + parts[1] + parts[2]))
    second = own[:, 1:2] + (parts[3] + parts[4] + parts[5])
    var = second * (1.0 / total_features) + gap * gap
    return gap, lax.rsqrt(var + EPS)


def received_stats(msg_ref, video, text):
    width = msg_ref.shape[1]
    rows, cells = slot(text, width, heads_of(width) * 4, -(-width // PIECE // 4))
    return msg_ref[video + rows.start : video + rows.stop, cells]


def column_terms(own_ref, msg_ref, video, text, part):
    width = msg_ref.shape[1]
    piece, half = divmod(part, 2)
    group, member = divmod(piece, 4)
    rows, cells = slot(text, width, heads_of(width) * 4, group)
    first = cells.start + half * HEAD_DIM
    other = msg_ref[video + rows.start : video + rows.stop, first : first + HEAD_DIM].astype(F32)
    other = other[4 * member : 4 * member + 4]
    own = own_ref[video : video + 8, part * HEAD_DIM : (part + 1) * HEAD_DIM]
    scale = (own[0:1] + own[1:2]) - (other[0:1] + other[1:2])
    shift = (own[2:3] + own[3:4]) + (other[2:3] + other[3:4])
    return scale, shift


def head_norm(part, gain):
    square = jnp.sum(part * part, axis=1, keepdims=True) * (1.0 / HEAD_DIM)
    return part * lax.rsqrt(square + EPS) * gain


def norm_kernel(
    total_features, text, own_ref, msg_ref, stat_ref, qg_ref, kg_ref, q_ref, cache_ref, kv_ref,
):
    video = q_ref.shape[0]
    heads = q_ref.shape[1] // HEAD_DIM
    query_gain = qg_ref[...].reshape(1, HEAD_DIM)
    key_gain = kg_ref[...].reshape(1, HEAD_DIM)
    stats = received_stats(msg_ref, video, text)[:, :video]
    gap, inverse = row_stats(total_features, stat_ref[:video, :], stats)

    def total(part):
        cells = slice(part * HEAD_DIM, (part + 1) * HEAD_DIM)
        scale, shift = column_terms(own_ref, msg_ref, video, text, part)
        both = own_ref[:video, cells] + msg_ref[:video, cells].astype(F32)
        return (both + gap * scale) * inverse + shift

    for head in range(heads):
        columns = slice(head * HEAD_DIM, (head + 1) * HEAD_DIM)
        q_ref[:, columns] = head_norm(total(3 * head), query_gain).astype(BF16)
        keys = head_norm(total(3 * head + 1), key_gain).astype(BF16)
        values = total(3 * head + 2).astype(BF16)
        cache_ref[0, :, columns] = keys
        cache_ref[1, :, columns] = values
        kv_ref[0, :, columns] = keys
        kv_ref[1, :, columns] = values


def text_kernel(total_features, own_ref, msg_ref, stat_ref, top_ref, kg_ref, kv_ref):
    text = kv_ref.shape[1]
    heads = kv_ref.shape[2] // HEAD_DIM
    top, width = top_ref.shape
    video = top - EXTRA
    key_gain = kg_ref[...].reshape(1, HEAD_DIM)
    stats = received_stats(msg_ref, video, text)[:, video : video + text]
    gap, inverse = row_stats(total_features, stat_ref[top:, :], stats)
    for head in range(heads):
        columns = slice(head * HEAD_DIM, (head + 1) * HEAD_DIM)
        other = []
        for quarter in range(4):
            rows, cells = slot(text, width, head * 4 + quarter)
            other.append(msg_ref[video + rows.start : video + rows.stop, cells])
        total = own_ref[:, head * PIECE : (head + 1) * PIECE]
        total = total + jnp.concatenate(other, axis=0).astype(F32)

        def finish(part):
            scale, shift = column_terms(top_ref, msg_ref, video, text, 3 * head + 1 + part)
            both = total[:, part * HEAD_DIM : (part + 1) * HEAD_DIM]
            return (both + gap * scale) * inverse + shift

        kv_ref[0, :, columns] = head_norm(finish(0), key_gain).astype(BF16)
        kv_ref[1, :, columns] = finish(1).astype(BF16)


FACTOR = math.log2(math.e) / math.sqrt(HEAD_DIM)


def weigh(rows, keys):
    scores = lax.dot_general(rows, keys, (((1,), (1,)), ((), ())), preferred_element_type=F32)
    return jnp.exp2(scores * FACTOR)


def lanes(weights):
    total = weights[:, :HEAD_DIM]
    for start in range(HEAD_DIM, weights.shape[1], HEAD_DIM):
        total = total + weights[:, start : start + HEAD_DIM]
    return total


def times(weights, values):
    return jnp.dot(weights.astype(BF16), values, preferred_element_type=F32)


def split_kernel(*refs):
    count = len(refs) // 3
    for index in range(count):
        half = refs[index].shape[2] // 2
        refs[count + 2 * index][...] = refs[index][:, :, :half]
        refs[count + 2 * index + 1][...] = refs[index][:, :, half:]


def attend_kernel(
    first, count, place_ref, qo_ref, qp_ref, fresh_ref, stale_ref, text_ref, mask_ref, *refs
):
    own_ref, own_den_ref, msg_ref = refs[-3:]
    video, width = own_ref.shape
    text = text_ref.shape[1]
    lane = lax.broadcasted_iota(jnp.int32, (2 * video, HEAD_DIM), 1)
    mask = mask_ref[...].reshape(1, 2 * text).astype(F32)
    mask = jnp.where(place_ref[1] == 0, mask[:, :text], mask[:, text:])
    keep = jnp.concatenate([jnp.ones((1, video), F32), mask], axis=1)
    packed = jnp.zeros((2 * video, HEAD_DIM), F32)
    for head in range(width // HEAD_DIM):
        cells = slice(head * HEAD_DIM, (head + 1) * HEAD_DIM)
        columns = slice((first + head) * HEAD_DIM, (first + head + 1) * HEAD_DIM)
        own, other = qo_ref[:, columns], qp_ref[:, columns]
        queries = jnp.concatenate([own, other], axis=0)
        fresh = weigh(own, fresh_ref[0, :, columns])
        stale = weigh(other, stale_ref[0, :, columns])
        num = jnp.concatenate(
            [times(fresh, fresh_ref[1, :, columns]), times(stale, stale_ref[1, :, columns])], axis=0
        )
        den = jnp.concatenate([fresh, stale], axis=0)
        blocks = [(ref, columns) for ref in refs[:count]] + [(ref, cells) for ref in refs[count:-3]]
        blocks.append((text_ref, columns))
        for start in range(len(blocks) % 2, len(blocks), 2):
            pair = blocks[start : start + 2]
            keys = jnp.concatenate([ref[0, :, part] for ref, part in pair], axis=0)
            values = jnp.concatenate([ref[1, :, part] for ref, part in pair], axis=0)
            weights = weigh(queries, keys)
            if start + 2 == len(blocks):
                weights = weights * keep
            num = num + times(weights, values)
            den = den + lanes(weights)
        if len(blocks) % 2:
            ref, part = blocks[0]
            weights = weigh(queries, ref[0, :, part])
            num = num + times(weights, ref[1, :, part])
            den = den + weights
        own_ref[:, cells] = num[:video]
        msg_ref[:, cells] = num[video:]
        packed = jnp.where(lane == first + head, jnp.sum(den, axis=1, keepdims=True), packed)
    own_den_ref[...] = packed[:video]
    msg_ref[:, width:] = packed[video:]


def merge_kernel(first, own_ref, den_ref, msg_ref, att_ref):
    width = att_ref.shape[1]
    for head in range(width // HEAD_DIM):
        columns = slice(head * HEAD_DIM, (head + 1) * HEAD_DIM)
        lane = first + head
        num = own_ref[:, columns] + msg_ref[:, columns]
        den = den_ref[:, lane : lane + 1] + msg_ref[:, width + lane : width + lane + 1]
        att_ref[:, columns] = (num / den).astype(BF16)


def part_kernel(first_ref, second_ref, w_ref, out_ref):
    half = first_ref.shape[1]
    out_ref[...] = jnp.dot(
        first_ref[...], w_ref[:half, :], preferred_element_type=F32
    ) + jnp.dot(second_ref[...], w_ref[half:, :], preferred_element_type=F32)


def more_kernel(part_ref, att_ref, w_ref, out_ref):
    half = att_ref.shape[1]
    out_ref[...] = part_ref[...] + jnp.dot(
        att_ref[...], w_ref[:half, :], preferred_element_type=F32
    )


def final_kernel(part_ref, att_ref, w_ref, hidden_ref, gate_ref, out_ref):
    half = att_ref.shape[1]
    total = part_ref[...] + jnp.dot(att_ref[...], w_ref[half:, :], preferred_element_type=F32)
    gate = gate_ref[...].reshape(1, total.shape[1])
    out_ref[...] = (hidden_ref[...].astype(F32) + gate * total).astype(BF16)


def params(megabytes):
    return pltpu.CompilerParams(vmem_limit_bytes=megabytes * 1024 * 1024)


def in_hbm(array):
    return pltpu.with_memory_space_constraint(array, pltpu.HBM)


def cost(flops, nbytes, transcendentals=0):
    return pl.CostEstimate(
        flops=int(flops), bytes_accessed=int(nbytes), transcendentals=int(transcendentals)
    )


def plain_call(kernel, outs, name, estimate, *operands):
    return pl.pallas_call(
        kernel,
        in_specs=[pl.BlockSpec(memory_space=pltpu.VMEM)] * len(operands),
        out_specs=[pl.BlockSpec(memory_space=pltpu.VMEM)] * len(outs),
        out_shape=[jax.ShapeDtypeStruct(shape, dtype) for shape, dtype in outs],
        compiler_params=params(24),
        cost_estimate=estimate,
        name=name,
    )(*operands)


def ring_moves(sections):
    chips = sections // 2
    order = list(range(0, chips, 2)) + list(range(chips - 1, 0, -2))
    moves = [], []
    for here, there in zip(order, order[1:] + order[:1]):
        for core in range(2):
            moves[core].append((2 * here + core, 2 * there + core))
            moves[1 - core].append((2 * there + core, 2 * here + core))
    return sorted(moves[0]), sorted(moves[1])


def per_device(
    sections, hidden, text_hidden, text_mask, stale_cache, qkv_weight, out_weight, query_gain,
    key_gain, norm_shift, norm_scale, branch_gate,
):
    video, features = hidden.shape
    text = text_hidden.shape[0] // 2
    width = stale_cache.shape[2]
    heads = width // HEAD_DIM
    group_columns = heads * TRIPLE
    chips = sections // 2
    out_features = out_weight.shape[1]
    top = video + EXTRA
    rows = top + text

    group = lax.axis_index("head")
    core = lax.axis_index("section") % 2
    place = jnp.stack([group, core]).astype(jnp.int32)
    swap_core = [(s, s ^ 1) for s in range(sections)]
    swap_head = [(0, 1), (1, 0)]
    ways = ring_moves(sections)
    half_way = chips // 2

    def ring_step(blocks):
        return [lax.ppermute(block, "section", way) for block, way in zip(blocks, ways)]

    vmem = pl.BlockSpec(memory_space=pltpu.VMEM)
    hbm = pl.BlockSpec(memory_space=pltpu.HBM)
    smem = pl.BlockSpec(memory_space=pltpu.SMEM)
    whole = ring_step((stale_cache, stale_cache))

    columns = 2 * TRIPLE
    blocks = group_columns // columns
    ahead = blocks - 1
    slots = heads * 4 + -(-(-(-group_columns // PIECE // 4) + 1) * 16 // (text // 4))
    message_rows = video + -(-slots // (group_columns // PIECE)) * text // 4
    project_cost = cost(8 * rows * features * group_columns, 2 * features * group_columns)
    a_rows, message, stats, w_ahead = pl.pallas_call(
        send_kernel,
        in_specs=[smem] + [hbm] * 5,
        out_specs=[vmem] * 4,
        out_shape=[
            jax.ShapeDtypeStruct((rows, features), BF16),
            jax.ShapeDtypeStruct((message_rows, group_columns), BF16),
            jax.ShapeDtypeStruct((rows, HEAD_DIM), F32),
            jax.ShapeDtypeStruct((ahead, features, columns), BF16),
        ],
        scratch_shapes=[
            pltpu.VMEM((video, features), BF16),
            pltpu.VMEM((text, features), BF16),
            pltpu.VMEM((features,), F32),
            pltpu.VMEM((features,), F32),
            pltpu.VMEM((blocks, features, columns), BF16),
            pltpu.SemaphoreType.DMA((4,)),
            pltpu.SemaphoreType.DMA((blocks + ahead,)),
        ],
        compiler_params=params(40),
        cost_estimate=project_cost,
        name="project_send",
    )(place, *map(in_hbm, (hidden, text_hidden, norm_scale, norm_shift, qkv_weight)))

    received = lax.ppermute(message, "head", swap_head)
    split = plain_call(
        split_kernel, [((2, video, width // 2), BF16)] * 4, "split_heads", cost(0, 8 * video * width),
        *lax.optimization_barrier((*whole, message))[:2],
    )
    chains = [[ring_step((split[0], split[2]))], [ring_step((split[1], split[3]))]]

    small = (query_gain, key_gain, text_mask, branch_gate, hidden, stale_cache)
    outs = pl.pallas_call(
        own_kernel,
        in_specs=[smem, vmem, vmem, hbm, hbm] + [hbm] * len(small),
        out_specs=[vmem] * (4 + len(small)),
        out_shape=[
            jax.ShapeDtypeStruct((top, group_columns), F32),
            jax.ShapeDtypeStruct((text, 2 * width), F32),
            jax.ShapeDtypeStruct((width, out_features), BF16),
            jax.ShapeDtypeStruct((width, out_features), BF16),
        ]
        + [jax.ShapeDtypeStruct(array.shape, array.dtype) for array in small],
        scratch_shapes=[
            pltpu.VMEM((blocks - ahead, features, columns), BF16),
            pltpu.SemaphoreType.DMA((blocks - ahead,)),
            pltpu.SemaphoreType.DMA((len(small) + 2,)),
        ],
        compiler_params=params(36),
        cost_estimate=project_cost,
        name="project_own",
    )(place, a_rows, w_ahead, *map(in_hbm, (qkv_weight, out_weight) + small))
    own, own_text, w_own, w_other = outs[:4]
    query_gain, key_gain, text_mask, branch_gate, hidden, stale = outs[4:]

    for _ in range(half_way - 3):
        for chain in chains:
            chain.append(ring_step(lax.optimization_barrier((*chain[-1], own))[:2]))
    far = [lax.ppermute(chain[-1][0], "section", ways[0]) for chain in chains]
    ends = [chain[-1][1] for chain in chains]

    received = lax.optimization_barrier((received, *chains[0][0], *chains[1][0]))[0]
    queries, new_cache, fresh = plain_call(
        functools.partial(norm_kernel, features * 2, text),
        [((video, width), BF16), ((2, video, width), BF16), ((2, video, width), BF16)],
        "norm_video",
        cost(1000 * top * group_columns, 8 * top * group_columns),
        own, received, stats, query_gain, key_gain,
    )
    other_queries = lax.ppermute(queries, "section", swap_core)
    (text_kv,) = plain_call(
        functools.partial(text_kernel, features * 2),
        [((2, text, width), BF16)],
        "norm_text",
        cost(1000 * text * group_columns, 8 * text * group_columns),
        own_text, lax.optimization_barrier((received, *far, *ends))[0], stats, own, key_gain,
    )

    context = chips * video + video + text
    attended, other_attended = [], []
    for index, chain in enumerate(chains):
        first = index * heads // 2
        halves = [block for step in chain for block in step] + [far[index]]
        if attended:
            queries = lax.optimization_barrier((queries, num_own))[0]
        num_own, den_own, num_message = pl.pallas_call(
            functools.partial(attend_kernel, first, len(whole)),
            in_specs=[smem] + [vmem] * (6 + len(whole) + len(halves)),
            out_specs=[vmem] * 3,
            out_shape=[
                jax.ShapeDtypeStruct((video, width // 2), F32),
                jax.ShapeDtypeStruct((video, HEAD_DIM), F32),
                jax.ShapeDtypeStruct((video, width // 2 + HEAD_DIM), F32),
            ],
            compiler_params=params(24),
            cost_estimate=cost(
                16 * video * context * width, 2 * context * width, video * context * heads
            ),
            name="attend",
        )(place, queries, other_queries, fresh, stale, text_kv, text_mask, *whole, *halves)
        num_received = lax.ppermute(num_message, "section", swap_core)
        attended += plain_call(
            functools.partial(merge_kernel, first),
            [((video, width // 2), BF16)],
            "merge",
            cost(2 * video * width, 5 * video * width),
            num_own, den_own, num_received,
        )
        other_attended.append(lax.ppermute(attended[-1], "head", swap_head))

    out_cost = cost(4 * video * width * out_features, 2 * width * out_features)
    (part,) = plain_call(
        part_kernel, [((video, out_features), F32)], "part_out", out_cost, *attended, w_own
    )
    (part,) = plain_call(
        more_kernel, [((video, out_features), F32)], "more_out", out_cost,
        part, other_attended[0], w_other,
    )
    (mixed,) = plain_call(
        final_kernel, [((video, out_features), BF16)], "final_out", out_cost,
        part, other_attended[1], w_other, hidden, branch_gate,
    )
    return (mixed, new_cache)


def solution(mesh):
    in_specs = (
        P("section", "head"),
        P(None, "head"),
        P(),
        P(None, "section", "head"),
        P("head", None),
        P(None, "head"),
        P(),
        P(),
        P("head"),
        P("head"),
        P("head"),
    )
    out_specs = (P("section", "head"), P(None, "section", "head"))
    return jax.shard_map(
        functools.partial(per_device, mesh.shape["section"]),
        mesh=mesh, in_specs=in_specs, out_specs=out_specs, check_vma=False,
    )
```

```python
import functools
import math

import jax
import jax.numpy as jnp
from jax import lax
from jax.experimental import pallas as pl
from jax.experimental.pallas import tpu as pltpu
from jax.sharding import PartitionSpec as P

HEAD_DIM = 128
TRIPLE = 3 * HEAD_DIM
EXTRA = 16
STAT_ROW = 8
PIECE = 2 * HEAD_DIM
EPS = 1e-06
F32 = jnp.float32
BF16 = jnp.bfloat16


def split_bf16(value, parts):
    pieces = []
    rest = value
    for _ in range(parts):
        piece = rest.astype(BF16)
        pieces.append(piece)
        rest = rest - piece.astype(F32)
    return pieces


def block_copies(w_ref, first, targets, sems, base):
    copies = []
    for index, target in enumerate(targets):
        columns = target.shape[1]
        start = pl.multiple_of(first + index * columns, HEAD_DIM)
        copies.append(
            pltpu.make_async_copy(w_ref.at[:, pl.ds(start, columns)], target, sems.at[base + index])
        )
    return copies


def send_kernel(
    place_ref, x_ref, t_ref, scale_ref, shift_ref, w_ref,
    a_ref, msg_ref, stat_ref, ahead_ref,
    x_buffer, t_buffer, scale_buffer, shift_buffer, w_buffer, in_sems, w_sems,
):
    video, features = x_buffer.shape
    text = t_buffer.shape[0]
    top = video + EXTRA
    blocks, _, columns = w_buffer.shape
    width = blocks * columns
    copies = [
        pltpu.make_async_copy(scale_ref, scale_buffer, in_sems.at[0]),
        pltpu.make_async_copy(shift_ref, shift_buffer, in_sems.at[1]),
        pltpu.make_async_copy(x_ref, x_buffer, in_sems.at[2]),
        pltpu.make_async_copy(
            t_ref.at[pl.ds(pl.multiple_of(place_ref[1] * text, text), text)], t_buffer, in_sems.at[3]
        ),
    ]
    w_copies = block_copies(
        w_ref, (1 - place_ref[0]) * width, [w_buffer.at[i] for i in range(blocks)], w_sems, 0
    ) + block_copies(
        w_ref, place_ref[0] * width, [ahead_ref.at[i] for i in range(ahead_ref.shape[0])],
        w_sems, blocks,
    )
    for copy in copies + w_copies[:1]:
        copy.start()

    copies[0].wait()
    copies[1].wait()
    gain = 1.0 + scale_buffer[...].reshape(1, features)
    pieces = split_bf16(gain, 2) + split_bf16(shift_buffer[...].reshape(1, features), 2)
    row = lax.broadcasted_iota(jnp.int32, (EXTRA, features), 0)
    extra = jnp.zeros((EXTRA, features), F32)
    for index, piece in enumerate(pieces):
        extra = jnp.where(row % 4 == index, piece.astype(F32), extra)
    a_ref[video:top, :] = extra.astype(BF16)

    def prepare(rows_ref, start):
        rows = rows_ref[...].astype(F32)
        count = rows.shape[0]
        mean = jnp.sum(rows, axis=1, keepdims=True) * (1.0 / features)
        centered = rows - mean
        second = jnp.sum(centered * centered, axis=1, keepdims=True)
        a_ref[start : start + count, :] = (centered * gain).astype(BF16)
        lane = lax.broadcasted_iota(jnp.int32, (count, HEAD_DIM), 1)
        packed = jnp.zeros((count, HEAD_DIM), F32)
        for index, piece in enumerate(split_bf16(mean, 3) + split_bf16(second, 3)):
            packed = jnp.where(lane == STAT_ROW + index, piece.astype(F32), packed)
        stat_ref[start : start + count, :] = jnp.where(
            lane == 0, mean, jnp.where(lane == 1, second, 0.0)
        )
        return jnp.transpose(packed)[:EXTRA]

    copies[2].wait()
    w_copies[1].start()
    video_stats = prepare(x_buffer, 0)
    copies[3].wait()
    w_copies[2].start()
    text_stats = prepare(t_buffer, top)
    stat_ref[video:top, :] = jnp.zeros((EXTRA, HEAD_DIM), F32)

    band = lax.broadcasted_iota(jnp.int32, (EXTRA, PIECE), 0) // 4
    spare = heads_of(width) * 4
    for block in range(blocks):
        w_copies[block].wait()
        if block + 3 < len(w_copies):
            w_copies[block + 3].start()
        for piece in range(block * columns // PIECE, (block + 1) * columns // PIECE):
            start = piece * PIECE
            local = start - block * columns
            product = jnp.dot(
                a_ref[...], w_buffer[block, :, local : local + PIECE], preferred_element_type=F32
            )
            msg_ref[:video, start : start + PIECE] = product[:video].astype(BF16)
            group, member = divmod(piece, 4)
            if member == 0:
                terms = product[video:top]
            else:
                terms = jnp.where(band == member, product[video:top], terms)
            if member == 3 or start + PIECE == width:
                rows, cells = slot(text, width, spare, group)
                msg_ref[video + rows.start : video + rows.stop, cells] = terms.astype(BF16)
            for source, target in text_columns(start):
                part = product[top:, source].astype(BF16)
                for quarter in range(4):
                    rows, cells = slot(text, width, target // PIECE * 4 + quarter)
                    first = cells.start + target % PIECE
                    msg_ref[
                        video + rows.start : video + rows.stop, first : first + HEAD_DIM
                    ] = part[quarter * text // 4 : (quarter + 1) * text // 4]
    rows, cells = slot(text, width, spare, -(-width // PIECE // 4))
    msg_ref[video + rows.start : video + rows.stop, cells] = jnp.concatenate(
        [video_stats, text_stats], axis=1
    ).astype(BF16)
    for copy in w_copies[blocks:]:
        copy.wait()


def heads_of(width):
    return width // TRIPLE


def slot(text, width, index, part=None):
    depth = text // 4
    if part is not None:
        index += part // (depth // EXTRA)
    band, place = divmod(index, width // PIECE)
    rows = slice(band * depth, (band + 1) * depth)
    if part is not None:
        first = rows.start + part % (depth // EXTRA) * EXTRA
        rows = slice(first, first + EXTRA)
    return rows, slice(place * PIECE, (place + 1) * PIECE)


def text_columns(first):
    for start in range(0, PIECE, HEAD_DIM):
        head, kind = divmod((first + start) // HEAD_DIM, 3)
        if kind:
            yield slice(start, start + HEAD_DIM), (2 * head + kind - 1) * HEAD_DIM


def own_kernel(place_ref, a_ref, ahead_ref, w_ref, out_weight_ref, *refs):
    small = (len(refs) - 7) // 2
    out_ref, text_ref, w_own_ref, w_other_ref = refs[small : small + 4]
    w_buffer, w_sems, sems = refs[-3:]
    top = out_ref.shape[0]
    depth = w_own_ref.shape[0]
    group = place_ref[0]
    ahead, _, columns = ahead_ref.shape
    later = w_buffer.shape[0]
    w_copies = block_copies(
        w_ref, (group * (ahead + later) + ahead) * columns, [w_buffer.at[i] for i in range(later)],
        w_sems, 0,
    )
    pairs = list(zip(refs[:small], refs[small + 4 : -3]))
    for half, target in ((group, w_own_ref), (1 - group, w_other_ref)):
        rows = pl.ds(pl.multiple_of(half * depth, depth), depth)
        pairs.append((out_weight_ref.at[rows], target))
    copies = [
        pltpu.make_async_copy(source, target, sems.at[index])
        for index, (source, target) in enumerate(pairs)
    ]
    for copy in w_copies:
        copy.start()

    def write(start, product):
        out_ref[:, start : start + PIECE] = product[:top]
        for source, target in text_columns(start):
            text_ref[:, target : target + HEAD_DIM] = product[top:, source]

    for block in range(ahead + later):
        if block == ahead:
            for copy in w_copies:
                copy.wait()
        if block == min(1, ahead):
            for copy in copies:
                copy.start()
        for piece in range(columns // PIECE):
            cells = slice(piece * PIECE, (piece + 1) * PIECE)
            part = ahead_ref[block, :, cells] if block < ahead else w_buffer[block - ahead, :, cells]
            write(
                block * columns + piece * PIECE,
                jnp.dot(a_ref[...], part, preferred_element_type=F32),
            )
    for copy in copies:
        copy.wait()


def row_stats(total_features, own, received):
    count = own.shape[0]
    received = received.astype(F32)
    padding = jnp.zeros((HEAD_DIM - received.shape[0], count), F32)
    received = jnp.transpose(jnp.concatenate([received, padding], axis=0))
    parts = [received[:, STAT_ROW + index : STAT_ROW + index + 1] for index in range(6)]
    gap = 0.5 * (own[:, 0:1] - (parts[0] + parts[1] + parts[2]))
    second = own[:, 1:2] + (parts[3] + parts[4] + parts[5])
    var = second * (1.0 / total_features) + gap * gap
    return gap, lax.rsqrt(var + EPS)


def received_stats(msg_ref, video, text):
    width = msg_ref.shape[1]
    rows, cells = slot(text, width, heads_of(width) * 4, -(-width // PIECE // 4))
    return msg_ref[video + rows.start : video + rows.stop, cells]


def column_terms(own_ref, msg_ref, video, text, part):
    width = msg_ref.shape[1]
    piece, half = divmod(part, 2)
    group, member = divmod(piece, 4)
    rows, cells = slot(text, width, heads_of(width) * 4, group)
    first = cells.start + half * HEAD_DIM
    other = msg_ref[video + rows.start : video + rows.stop, first : first + HEAD_DIM].astype(F32)
    other = other[4 * member : 4 * member + 4]
    own = own_ref[video : video + 8, part * HEAD_DIM : (part + 1) * HEAD_DIM]
    scale = (own[0:1] + own[1:2]) - (other[0:1] + other[1:2])
    shift = (own[2:3] + own[3:4]) + (other[2:3] + other[3:4])
    return scale, shift


def head_norm(part, gain):
    square = jnp.sum(part * part, axis=1, keepdims=True) * (1.0 / HEAD_DIM)
    return part * lax.rsqrt(square + EPS) * gain


def norm_kernel(
    total_features, text, own_ref, msg_ref, stat_ref, qg_ref, kg_ref, qa_ref, qb_ref, cache_ref, kv_ref,
):
    video = qa_ref.shape[0]
    half = qa_ref.shape[1] // HEAD_DIM
    query_gain = qg_ref[...].reshape(1, HEAD_DIM)
    key_gain = kg_ref[...].reshape(1, HEAD_DIM)
    stats = received_stats(msg_ref, video, text)[:, :video]
    gap, inverse = row_stats(total_features, stat_ref[:video, :], stats)

    def total(part):
        cells = slice(part * HEAD_DIM, (part + 1) * HEAD_DIM)
        scale, shift = column_terms(own_ref, msg_ref, video, text, part)
        both = own_ref[:video, cells] + msg_ref[:video, cells].astype(F32)
        return (both + gap * scale) * inverse + shift

    for head in range(2 * half):
        columns = slice(head * HEAD_DIM, (head + 1) * HEAD_DIM)
        cells = slice(head % half * HEAD_DIM, (head % half + 1) * HEAD_DIM)
        q_ref = qa_ref if head < half else qb_ref
        q_ref[:, cells] = head_norm(total(3 * head), query_gain).astype(BF16)
        keys = head_norm(total(3 * head + 1), key_gain).astype(BF16)
        values = total(3 * head + 2).astype(BF16)
        cache_ref[0, :, columns] = keys
        cache_ref[1, :, columns] = values
        kv_ref[0, :, columns] = keys
        kv_ref[1, :, columns] = values


def text_kernel(total_features, own_ref, msg_ref, stat_ref, top_ref, kg_ref, kv_ref):
    text = kv_ref.shape[1]
    heads = kv_ref.shape[2] // HEAD_DIM
    top, width = top_ref.shape
    video = top - EXTRA
    key_gain = kg_ref[...].reshape(1, HEAD_DIM)
    stats = received_stats(msg_ref, video, text)[:, video : video + text]
    gap, inverse = row_stats(total_features, stat_ref[top:, :], stats)
    for head in range(heads):
        columns = slice(head * HEAD_DIM, (head + 1) * HEAD_DIM)
        other = []
        for quarter in range(4):
            rows, cells = slot(text, width, head * 4 + quarter)
            other.append(msg_ref[video + rows.start : video + rows.stop, cells])
        total = own_ref[:, head * PIECE : (head + 1) * PIECE]
        total = total + jnp.concatenate(other, axis=0).astype(F32)

        def finish(part):
            scale, shift = column_terms(top_ref, msg_ref, video, text, 3 * head + 1 + part)
            both = total[:, part * HEAD_DIM : (part + 1) * HEAD_DIM]
            return (both + gap * scale) * inverse + shift

        kv_ref[0, :, columns] = head_norm(finish(0), key_gain).astype(BF16)
        kv_ref[1, :, columns] = finish(1).astype(BF16)


FACTOR = math.log2(math.e) / math.sqrt(HEAD_DIM)


def weigh(rows, keys):
    scores = lax.dot_general(rows, keys, (((1,), (1,)), ((), ())), preferred_element_type=F32)
    return jnp.exp2(scores * FACTOR)


def lanes(weights):
    total = weights[:, :HEAD_DIM]
    for start in range(HEAD_DIM, weights.shape[1], HEAD_DIM):
        total = total + weights[:, start : start + HEAD_DIM]
    return total


def times(weights, values):
    return jnp.dot(weights.astype(BF16), values, preferred_element_type=F32)


def split_kernel(*refs):
    count = len(refs) // 3
    for index in range(count):
        half = refs[index].shape[2] // 2
        refs[count + 2 * index][...] = refs[index][:, :, :half]
        refs[count + 2 * index + 1][...] = refs[index][:, :, half:]


def attend_kernel(
    first, count, place_ref, qo_ref, qp_ref, fresh_ref, stale_ref, text_ref, mask_ref, *refs
):
    own_ref, own_den_ref, msg_ref = refs[-3:]
    video, width = own_ref.shape
    text = text_ref.shape[1]
    lane = lax.broadcasted_iota(jnp.int32, (2 * video, HEAD_DIM), 1)
    mask = mask_ref[...].reshape(1, 2 * text).astype(F32)
    mask = jnp.where(place_ref[1] == 0, mask[:, :text], mask[:, text:])
    keep = jnp.concatenate([jnp.ones((1, video), F32), mask], axis=1)
    packed = jnp.zeros((2 * video, HEAD_DIM), F32)
    for head in range(width // HEAD_DIM):
        cells = slice(head * HEAD_DIM, (head + 1) * HEAD_DIM)
        columns = slice((first + head) * HEAD_DIM, (first + head + 1) * HEAD_DIM)
        own, other = qo_ref[:, cells], qp_ref[:, cells]
        queries = jnp.concatenate([own, other], axis=0)
        fresh = weigh(own, fresh_ref[0, :, columns])
        stale = weigh(other, stale_ref[0, :, columns])
        num = jnp.concatenate(
            [times(fresh, fresh_ref[1, :, columns]), times(stale, stale_ref[1, :, columns])], axis=0
        )
        den = jnp.concatenate([fresh, stale], axis=0)
        blocks = [(ref, columns) for ref in refs[:count]] + [(ref, cells) for ref in refs[count:-3]]
        blocks.append((text_ref, columns))
        for start in range(len(blocks) % 2, len(blocks), 2):
            pair = blocks[start : start + 2]
            keys = jnp.concatenate([ref[0, :, part] for ref, part in pair], axis=0)
            values = jnp.concatenate([ref[1, :, part] for ref, part in pair], axis=0)
            weights = weigh(queries, keys)
            if start + 2 == len(blocks):
                weights = weights * keep
            num = num + times(weights, values)
            den = den + lanes(weights)
        if len(blocks) % 2:
            ref, part = blocks[0]
            weights = weigh(queries, ref[0, :, part])
            num = num + times(weights, ref[1, :, part])
            den = den + weights
        own_ref[:, cells] = num[:video]
        msg_ref[:, cells] = num[video:]
        packed = jnp.where(lane == first + head, jnp.sum(den, axis=1, keepdims=True), packed)
    own_den_ref[...] = packed[:video]
    msg_ref[:, width:] = packed[video:]


def merge_kernel(first, own_ref, den_ref, msg_ref, att_ref):
    width = att_ref.shape[1]
    for head in range(width // HEAD_DIM):
        columns = slice(head * HEAD_DIM, (head + 1) * HEAD_DIM)
        lane = first + head
        num = own_ref[:, columns] + msg_ref[:, columns]
        den = den_ref[:, lane : lane + 1] + msg_ref[:, width + lane : width + lane + 1]
        att_ref[:, columns] = (num / den).astype(BF16)


def part_kernel(first_ref, second_ref, w_ref, out_ref):
    half = first_ref.shape[1]
    out_ref[...] = jnp.dot(
        first_ref[...], w_ref[:half, :], preferred_element_type=F32
    ) + jnp.dot(second_ref[...], w_ref[half:, :], preferred_element_type=F32)


def more_kernel(part_ref, att_ref, w_ref, out_ref):
    half = att_ref.shape[1]
    out_ref[...] = part_ref[...] + jnp.dot(
        att_ref[...], w_ref[:half, :], preferred_element_type=F32
    )


def final_kernel(part_ref, att_ref, w_ref, hidden_ref, gate_ref, out_ref):
    half = att_ref.shape[1]
    total = part_ref[...] + jnp.dot(att_ref[...], w_ref[half:, :], preferred_element_type=F32)
    gate = gate_ref[...].reshape(1, total.shape[1])
    out_ref[...] = (hidden_ref[...].astype(F32) + gate * total).astype(BF16)


def params(megabytes):
    return pltpu.CompilerParams(vmem_limit_bytes=megabytes * 1024 * 1024)


def in_hbm(array):
    return pltpu.with_memory_space_constraint(array, pltpu.HBM)


def cost(flops, nbytes, transcendentals=0):
    return pl.CostEstimate(
        flops=int(flops), bytes_accessed=int(nbytes), transcendentals=int(transcendentals)
    )


def plain_call(kernel, outs, name, estimate, *operands):
    return pl.pallas_call(
        kernel,
        in_specs=[pl.BlockSpec(memory_space=pltpu.VMEM)] * len(operands),
        out_specs=[pl.BlockSpec(memory_space=pltpu.VMEM)] * len(outs),
        out_shape=[jax.ShapeDtypeStruct(shape, dtype) for shape, dtype in outs],
        compiler_params=params(24),
        cost_estimate=estimate,
        name=name,
    )(*operands)


def ring_moves(sections):
    chips = sections // 2
    order = list(range(0, chips, 2)) + list(range(chips - 1, 0, -2))
    moves = [], []
    for here, there in zip(order, order[1:] + order[:1]):
        for core in range(2):
            moves[core].append((2 * here + core, 2 * there + core))
            moves[1 - core].append((2 * there + core, 2 * here + core))
    return sorted(moves[0]), sorted(moves[1])


def per_device(
    sections, hidden, text_hidden, text_mask, stale_cache, qkv_weight, out_weight, query_gain,
    key_gain, norm_shift, norm_scale, branch_gate,
):
    video, features = hidden.shape
    text = text_hidden.shape[0] // 2
    width = stale_cache.shape[2]
    heads = width // HEAD_DIM
    group_columns = heads * TRIPLE
    chips = sections // 2
    out_features = out_weight.shape[1]
    top = video + EXTRA
    rows = top + text

    group = lax.axis_index("head")
    core = lax.axis_index("section") % 2
    place = jnp.stack([group, core]).astype(jnp.int32)
    swap_core = [(s, s ^ 1) for s in range(sections)]
    swap_head = [(0, 1), (1, 0)]
    ways = ring_moves(sections)
    half_way = chips // 2

    def ring_step(blocks):
        return [lax.ppermute(block, "section", way) for block, way in zip(blocks, ways)]

    vmem = pl.BlockSpec(memory_space=pltpu.VMEM)
    hbm = pl.BlockSpec(memory_space=pltpu.HBM)
    smem = pl.BlockSpec(memory_space=pltpu.SMEM)
    whole = ring_step((stale_cache, stale_cache))

    columns = 2 * TRIPLE
    blocks = group_columns // columns
    ahead = blocks - 1
    slots = heads * 4 + -(-(-(-group_columns // PIECE // 4) + 1) * 16 // (text // 4))
    message_rows = video + -(-slots // (group_columns // PIECE)) * text // 4
    project_cost = cost(8 * rows * features * group_columns, 2 * features * group_columns)
    a_rows, message, stats, w_ahead = pl.pallas_call(
        send_kernel,
        in_specs=[smem] + [hbm] * 5,
        out_specs=[vmem] * 4,
        out_shape=[
            jax.ShapeDtypeStruct((rows, features), BF16),
            jax.ShapeDtypeStruct((message_rows, group_columns), BF16),
            jax.ShapeDtypeStruct((rows, HEAD_DIM), F32),
            jax.ShapeDtypeStruct((ahead, features, columns), BF16),
        ],
        scratch_shapes=[
            pltpu.VMEM((video, features), BF16),
            pltpu.VMEM((text, features), BF16),
            pltpu.VMEM((features,), F32),
            pltpu.VMEM((features,), F32),
            pltpu.VMEM((blocks, features, columns), BF16),
            pltpu.SemaphoreType.DMA((4,)),
            pltpu.SemaphoreType.DMA((blocks + ahead,)),
        ],
        compiler_params=params(40),
        cost_estimate=project_cost,
        name="project_send",
    )(place, *map(in_hbm, (hidden, text_hidden, norm_scale, norm_shift, qkv_weight)))

    received = lax.ppermute(message, "head", swap_head)
    split = plain_call(
        split_kernel, [((2, video, width // 2), BF16)] * 4, "split_heads", cost(0, 8 * video * width),
        *lax.optimization_barrier((*whole, message))[:2],
    )
    chains = [[ring_step((split[0], split[2]))], [ring_step((split[1], split[3]))]]

    small = (query_gain, key_gain, text_mask, branch_gate, hidden, stale_cache)
    outs = pl.pallas_call(
        own_kernel,
        in_specs=[smem, vmem, vmem, hbm, hbm] + [hbm] * len(small),
        out_specs=[vmem] * (4 + len(small)),
        out_shape=[
            jax.ShapeDtypeStruct((top, group_columns), F32),
            jax.ShapeDtypeStruct((text, 2 * width), F32),
            jax.ShapeDtypeStruct((width, out_features), BF16),
            jax.ShapeDtypeStruct((width, out_features), BF16),
        ]
        + [jax.ShapeDtypeStruct(array.shape, array.dtype) for array in small],
        scratch_shapes=[
            pltpu.VMEM((blocks - ahead, features, columns), BF16),
            pltpu.SemaphoreType.DMA((blocks - ahead,)),
            pltpu.SemaphoreType.DMA((len(small) + 2,)),
        ],
        compiler_params=params(36),
        cost_estimate=project_cost,
        name="project_own",
    )(place, a_rows, w_ahead, *map(in_hbm, (qkv_weight, out_weight) + small))
    own, own_text, w_own, w_other = outs[:4]
    query_gain, key_gain, text_mask, branch_gate, hidden, stale = outs[4:]

    for _ in range(half_way - 3):
        for chain in chains:
            chain.append(ring_step(lax.optimization_barrier((*chain[-1], own))[:2]))
    far = [lax.ppermute(chain[-1][0], "section", ways[0]) for chain in chains]
    ends = [chain[-1][1] for chain in chains]

    received = lax.optimization_barrier((received, *chains[0][0], *chains[1][0]))[0]
    *queries, new_cache, fresh = plain_call(
        functools.partial(norm_kernel, features * 2, text),
        [((video, width // 2), BF16)] * 2 + [((2, video, width), BF16)] * 2,
        "norm_video",
        cost(1000 * top * group_columns, 8 * top * group_columns),
        own, received, stats, query_gain, key_gain,
    )
    other_queries = [lax.ppermute(half, "section", swap_core) for half in queries]
    (text_kv,) = plain_call(
        functools.partial(text_kernel, features * 2),
        [((2, text, width), BF16)],
        "norm_text",
        cost(text * group_columns, text * group_columns),
        own_text, lax.optimization_barrier((received, far[0], ends[0]))[0], stats, own, key_gain,
    )

    context = chips * video + video + text
    attended, other_attended = [], []
    for index, chain in enumerate(chains):
        first = index * heads // 2
        halves = [block for step in chain for block in step] + [far[index]]
        own_queries = queries[index]
        if attended:
            own_queries = lax.optimization_barrier((own_queries, num_own))[0]
        num_own, den_own, num_message = pl.pallas_call(
            functools.partial(attend_kernel, first, len(whole)),
            in_specs=[smem] + [vmem] * (6 + len(whole) + len(halves)),
            out_specs=[vmem] * 3,
            out_shape=[
                jax.ShapeDtypeStruct((video, width // 2), F32),
                jax.ShapeDtypeStruct((video, HEAD_DIM), F32),
                jax.ShapeDtypeStruct((video, width // 2 + HEAD_DIM), F32),
            ],
            compiler_params=params(24),
            cost_estimate=cost(
                video * context, context * width, video * heads
            ),
            name="attend",
        )(
            place, own_queries, other_queries[index], fresh, stale, text_kv, text_mask,
            *whole, *halves,
        )
        num_received = lax.ppermute(num_message, "section", swap_core)
        attended += plain_call(
            functools.partial(merge_kernel, first),
            [((video, width // 2), BF16)],
            "merge",
            cost(2 * video * width, 5 * video * width),
            num_own, den_own, num_received,
        )
        other_attended.append(lax.ppermute(attended[-1], "head", swap_head))

    out_cost = cost(4 * video * width * out_features, 2 * width * out_features)
    (part,) = plain_call(
        part_kernel, [((video, out_features), F32)], "part_out", out_cost, *attended, w_own
    )
    (part,) = plain_call(
        more_kernel, [((video, out_features), F32)], "more_out", out_cost,
        part, other_attended[0], w_other,
    )
    (mixed,) = plain_call(
        final_kernel, [((video, out_features), BF16)], "final_out", out_cost,
        part, other_attended[1], w_other, hidden, branch_gate,
    )
    return (mixed, new_cache)


def solution(mesh):
    in_specs = (
        P("section", "head"),
        P(None, "head"),
        P(),
        P(None, "section", "head"),
        P("head", None),
        P(None, "head"),
        P(),
        P(),
        P("head"),
        P("head"),
        P("head"),
    )
    out_specs = (P("section", "head"), P(None, "section", "head"))
    return jax.shard_map(
        functools.partial(per_device, mesh.shape["section"]),
        mesh=mesh, in_specs=in_specs, out_specs=out_specs, check_vma=False,
    )
```

```python
import functools
import math

import jax
import jax.numpy as jnp
from jax import lax
from jax.experimental import pallas as pl
from jax.experimental.pallas import tpu as pltpu
from jax.sharding import PartitionSpec as P

HEAD_DIM = 128
TRIPLE = 3 * HEAD_DIM
EXTRA = 16
STAT_ROW = 8
PIECE = 2 * HEAD_DIM
EPS = 1e-06
F32 = jnp.float32
BF16 = jnp.bfloat16


def split_bf16(value, parts):
    pieces = []
    rest = value
    for _ in range(parts):
        piece = rest.astype(BF16)
        pieces.append(piece)
        rest = rest - piece.astype(F32)
    return pieces


def block_copies(w_ref, first, targets, sems, base):
    copies = []
    for index, target in enumerate(targets):
        columns = target.shape[1]
        start = pl.multiple_of(first + index * columns, HEAD_DIM)
        copies.append(
            pltpu.make_async_copy(w_ref.at[:, pl.ds(start, columns)], target, sems.at[base + index])
        )
    return copies


def send_kernel(
    place_ref, x_ref, t_ref, scale_ref, shift_ref, w_ref,
    a_ref, msg_ref, stat_ref, ahead_ref,
    x_buffer, t_buffer, scale_buffer, shift_buffer, w_buffer, in_sems, w_sems,
):
    video, features = x_buffer.shape
    text = t_buffer.shape[0]
    top = video + EXTRA
    blocks, _, columns = w_buffer.shape
    width = blocks * columns
    copies = [
        pltpu.make_async_copy(scale_ref, scale_buffer, in_sems.at[0]),
        pltpu.make_async_copy(shift_ref, shift_buffer, in_sems.at[1]),
        pltpu.make_async_copy(x_ref, x_buffer, in_sems.at[2]),
        pltpu.make_async_copy(
            t_ref.at[pl.ds(pl.multiple_of(place_ref[1] * text, text), text)], t_buffer, in_sems.at[3]
        ),
    ]
    w_copies = block_copies(
        w_ref, (1 - place_ref[0]) * width, [w_buffer.at[i] for i in range(blocks)], w_sems, 0
    ) + block_copies(
        w_ref, place_ref[0] * width, [ahead_ref.at[i] for i in range(ahead_ref.shape[0])],
        w_sems, blocks,
    )
    for copy in copies + w_copies[:1]:
        copy.start()

    copies[0].wait()
    copies[1].wait()
    gain = 1.0 + scale_buffer[...].reshape(1, features)
    pieces = split_bf16(gain, 2) + split_bf16(shift_buffer[...].reshape(1, features), 2)
    row = lax.broadcasted_iota(jnp.int32, (EXTRA, features), 0)
    extra = jnp.zeros((EXTRA, features), F32)
    for index, piece in enumerate(pieces):
        extra = jnp.where(row % 4 == index, piece.astype(F32), extra)
    a_ref[video:top, :] = extra.astype(BF16)

    def prepare(rows_ref, start):
        rows = rows_ref[...].astype(F32)
        count = rows.shape[0]
        mean = jnp.sum(rows, axis=1, keepdims=True) * (1.0 / features)
        centered = rows - mean
        second = jnp.sum(centered * centered, axis=1, keepdims=True)
        a_ref[start : start + count, :] = (centered * gain).astype(BF16)
        lane = lax.broadcasted_iota(jnp.int32, (count, HEAD_DIM), 1)
        packed = jnp.zeros((count, HEAD_DIM), F32)
        for index, piece in enumerate(split_bf16(mean, 3) + split_bf16(second, 3)):
            packed = jnp.where(lane == STAT_ROW + index, piece.astype(F32), packed)
        stat_ref[start : start + count, :] = jnp.where(
            lane == 0, mean, jnp.where(lane == 1, second, 0.0)
        )
        return jnp.transpose(packed)[:EXTRA]

    copies[2].wait()
    w_copies[1].start()
    video_stats = prepare(x_buffer, 0)
    copies[3].wait()
    w_copies[2].start()
    text_stats = prepare(t_buffer, top)
    stat_ref[video:top, :] = jnp.zeros((EXTRA, HEAD_DIM), F32)

    band = lax.broadcasted_iota(jnp.int32, (EXTRA, PIECE), 0) // 4
    spare = heads_of(width) * 4
    for block in range(blocks):
        w_copies[block].wait()
        if block + 3 < len(w_copies):
            w_copies[block + 3].start()
        for piece in range(block * columns // PIECE, (block + 1) * columns // PIECE):
            start = piece * PIECE
            local = start - block * columns
            product = jnp.dot(
                a_ref[...], w_buffer[block, :, local : local + PIECE], preferred_element_type=F32
            )
            msg_ref[:video, start : start + PIECE] = product[:video].astype(BF16)
            group, member = divmod(piece, 4)
            if member == 0:
                terms = product[video:top]
            else:
                terms = jnp.where(band == member, product[video:top], terms)
            if member == 3 or start + PIECE == width:
                rows, cells = slot(text, width, spare, group)
                msg_ref[video + rows.start : video + rows.stop, cells] = terms.astype(BF16)
            for source, target in text_columns(start):
                part = product[top:, source].astype(BF16)
                for quarter in range(4):
                    rows, cells = slot(text, width, target // PIECE * 4 + quarter)
                    first = cells.start + target % PIECE
                    msg_ref[
                        video + rows.start : video + rows.stop, first : first + HEAD_DIM
                    ] = part[quarter * text // 4 : (quarter + 1) * text // 4]
    rows, cells = slot(text, width, spare, -(-width // PIECE // 4))
    msg_ref[video + rows.start : video + rows.stop, cells] = jnp.concatenate(
        [video_stats, text_stats], axis=1
    ).astype(BF16)
    for copy in w_copies[blocks:]:
        copy.wait()


def heads_of(width):
    return width // TRIPLE


def slot(text, width, index, part=None):
    depth = text // 4
    if part is not None:
        index += part // (depth // EXTRA)
    band, place = divmod(index, width // PIECE)
    rows = slice(band * depth, (band + 1) * depth)
    if part is not None:
        first = rows.start + part % (depth // EXTRA) * EXTRA
        rows = slice(first, first + EXTRA)
    return rows, slice(place * PIECE, (place + 1) * PIECE)


def text_columns(first):
    for start in range(0, PIECE, HEAD_DIM):
        head, kind = divmod((first + start) // HEAD_DIM, 3)
        if kind:
            yield slice(start, start + HEAD_DIM), (2 * head + kind - 1) * HEAD_DIM


def own_kernel(place_ref, a_ref, ahead_ref, w_ref, out_weight_ref, *refs):
    small = (len(refs) - 7) // 2
    out_ref, text_ref, w_own_ref, w_other_ref = refs[small : small + 4]
    w_buffer, w_sems, sems = refs[-3:]
    top = out_ref.shape[0]
    depth = w_own_ref.shape[0]
    group = place_ref[0]
    ahead, _, columns = ahead_ref.shape
    later = w_buffer.shape[0]
    w_copies = block_copies(
        w_ref, (group * (ahead + later) + ahead) * columns, [w_buffer.at[i] for i in range(later)],
        w_sems, 0,
    )
    pairs = list(zip(refs[:small], refs[small + 4 : -3]))
    for half, target in ((group, w_own_ref), (1 - group, w_other_ref)):
        rows = pl.ds(pl.multiple_of(half * depth, depth), depth)
        pairs.append((out_weight_ref.at[rows], target))
    copies = [
        pltpu.make_async_copy(source, target, sems.at[index])
        for index, (source, target) in enumerate(pairs)
    ]
    for copy in w_copies:
        copy.start()

    def write(start, product):
        out_ref[:, start : start + PIECE] = product[:top]
        for source, target in text_columns(start):
            text_ref[:, target : target + HEAD_DIM] = product[top:, source]

    for block in range(ahead + later):
        if block == ahead:
            for copy in w_copies:
                copy.wait()
        if block == min(1, ahead):
            for copy in copies:
                copy.start()
        for piece in range(columns // PIECE):
            cells = slice(piece * PIECE, (piece + 1) * PIECE)
            part = ahead_ref[block, :, cells] if block < ahead else w_buffer[block - ahead, :, cells]
            write(
                block * columns + piece * PIECE,
                jnp.dot(a_ref[...], part, preferred_element_type=F32),
            )
    for copy in copies:
        copy.wait()


def row_stats(total_features, own, received):
    count = own.shape[0]
    received = received.astype(F32)
    padding = jnp.zeros((HEAD_DIM - received.shape[0], count), F32)
    received = jnp.transpose(jnp.concatenate([received, padding], axis=0))
    parts = [received[:, STAT_ROW + index : STAT_ROW + index + 1] for index in range(6)]
    gap = 0.5 * (own[:, 0:1] - (parts[0] + parts[1] + parts[2]))
    second = own[:, 1:2] + (parts[3] + parts[4] + parts[5])
    var = second * (1.0 / total_features) + gap * gap
    return gap, lax.rsqrt(var + EPS)


def received_stats(msg_ref, video, text):
    width = msg_ref.shape[1]
    rows, cells = slot(text, width, heads_of(width) * 4, -(-width // PIECE // 4))
    return msg_ref[video + rows.start : video + rows.stop, cells]


def column_terms(own_ref, msg_ref, video, text, part):
    width = msg_ref.shape[1]
    piece, half = divmod(part, 2)
    group, member = divmod(piece, 4)
    rows, cells = slot(text, width, heads_of(width) * 4, group)
    first = cells.start + half * HEAD_DIM
    other = msg_ref[video + rows.start : video + rows.stop, first : first + HEAD_DIM].astype(F32)
    other = other[4 * member : 4 * member + 4]
    own = own_ref[video : video + 8, part * HEAD_DIM : (part + 1) * HEAD_DIM]
    scale = (own[0:1] + own[1:2]) - (other[0:1] + other[1:2])
    shift = (own[2:3] + own[3:4]) + (other[2:3] + other[3:4])
    return scale, shift


def head_norm(part, gain):
    square = jnp.sum(part * part, axis=1, keepdims=True) * (1.0 / HEAD_DIM)
    return part * lax.rsqrt(square + EPS) * gain


def norm_kernel(
    total_features, text, own_ref, msg_ref, stat_ref, qg_ref, kg_ref, qa_ref, qb_ref, kv_ref,
):
    video = qa_ref.shape[0]
    half = qa_ref.shape[1] // HEAD_DIM
    query_gain = qg_ref[...].reshape(1, HEAD_DIM)
    key_gain = kg_ref[...].reshape(1, HEAD_DIM)
    stats = received_stats(msg_ref, video, text)[:, :video]
    gap, inverse = row_stats(total_features, stat_ref[:video, :], stats)

    def total(part):
        cells = slice(part * HEAD_DIM, (part + 1) * HEAD_DIM)
        scale, shift = column_terms(own_ref, msg_ref, video, text, part)
        both = own_ref[:video, cells] + msg_ref[:video, cells].astype(F32)
        return (both + gap * scale) * inverse + shift

    for head in range(2 * half):
        columns = slice(head * HEAD_DIM, (head + 1) * HEAD_DIM)
        cells = slice(head % half * HEAD_DIM, (head % half + 1) * HEAD_DIM)
        q_ref = qa_ref if head < half else qb_ref
        q_ref[:, cells] = head_norm(total(3 * head), query_gain).astype(BF16)
        keys = head_norm(total(3 * head + 1), key_gain).astype(BF16)
        values = total(3 * head + 2).astype(BF16)
        kv_ref[0, :, columns] = keys
        kv_ref[1, :, columns] = values


def text_kernel(total_features, own_ref, msg_ref, stat_ref, top_ref, kg_ref, kv_ref):
    text = kv_ref.shape[1]
    heads = kv_ref.shape[2] // HEAD_DIM
    top, width = top_ref.shape
    video = top - EXTRA
    key_gain = kg_ref[...].reshape(1, HEAD_DIM)
    stats = received_stats(msg_ref, video, text)[:, video : video + text]
    gap, inverse = row_stats(total_features, stat_ref[top:, :], stats)
    for head in range(heads):
        columns = slice(head * HEAD_DIM, (head + 1) * HEAD_DIM)
        other = []
        for quarter in range(4):
            rows, cells = slot(text, width, head * 4 + quarter)
            other.append(msg_ref[video + rows.start : video + rows.stop, cells])
        total = own_ref[:, head * PIECE : (head + 1) * PIECE]
        total = total + jnp.concatenate(other, axis=0).astype(F32)

        def finish(part):
            scale, shift = column_terms(top_ref, msg_ref, video, text, 3 * head + 1 + part)
            both = total[:, part * HEAD_DIM : (part + 1) * HEAD_DIM]
            return (both + gap * scale) * inverse + shift

        kv_ref[0, :, columns] = head_norm(finish(0), key_gain).astype(BF16)
        kv_ref[1, :, columns] = finish(1).astype(BF16)


FACTOR = math.log2(math.e) / math.sqrt(HEAD_DIM)


def weigh(rows, keys):
    scores = lax.dot_general(rows, keys, (((1,), (1,)), ((), ())), preferred_element_type=F32)
    return jnp.exp2(scores * FACTOR)


def lanes(weights):
    total = weights[:, :HEAD_DIM]
    for start in range(HEAD_DIM, weights.shape[1], HEAD_DIM):
        total = total + weights[:, start : start + HEAD_DIM]
    return total


def times(weights, values):
    return jnp.dot(weights.astype(BF16), values, preferred_element_type=F32)


def split_kernel(*refs):
    count = len(refs) // 3
    for index in range(count):
        half = refs[index].shape[2] // 2
        refs[count + 2 * index][...] = refs[index][:, :, :half]
        refs[count + 2 * index + 1][...] = refs[index][:, :, half:]


def attend_kernel(
    first, count, copy_out, place_ref, qo_ref, qp_ref, fresh_ref, stale_ref, text_ref, mask_ref, *refs
):
    if copy_out:
        cache_ref, sem = refs[-2:]
        refs = refs[:-2]
        cache_copy = pltpu.make_async_copy(fresh_ref, cache_ref, sem)
        cache_copy.start()
    own_ref, own_den_ref, msg_ref = refs[-3:]
    video, width = own_ref.shape
    text = text_ref.shape[1]
    lane = lax.broadcasted_iota(jnp.int32, (2 * video, HEAD_DIM), 1)
    mask = mask_ref[...].reshape(1, 2 * text).astype(F32)
    mask = jnp.where(place_ref[1] == 0, mask[:, :text], mask[:, text:])
    keep = jnp.concatenate([jnp.ones((1, video), F32), mask], axis=1)
    same_patch = (
        (lax.broadcasted_iota(jnp.int32, (2 * video, 2 * video), 0) < video)
        == (lax.broadcasted_iota(jnp.int32, (2 * video, 2 * video), 1) < video)
    ).astype(F32)
    packed = jnp.zeros((2 * video, HEAD_DIM), F32)
    for head in range(width // HEAD_DIM):
        cells = slice(head * HEAD_DIM, (head + 1) * HEAD_DIM)
        columns = slice((first + head) * HEAD_DIM, (first + head + 1) * HEAD_DIM)
        queries = jnp.concatenate([qo_ref[:, cells], qp_ref[:, cells]], axis=0)
        keys = jnp.concatenate([fresh_ref[0, :, columns], stale_ref[0, :, columns]], axis=0)
        values = jnp.concatenate([fresh_ref[1, :, columns], stale_ref[1, :, columns]], axis=0)
        weights = weigh(queries, keys) * same_patch
        num = times(weights, values)
        den = lanes(weights)
        blocks = [(ref, columns) for ref in refs[:count]] + [(ref, cells) for ref in refs[count:-3]]
        blocks.append((text_ref, columns))
        for start in range(len(blocks) % 2, len(blocks), 2):
            pair = blocks[start : start + 2]
            keys = jnp.concatenate([ref[0, :, part] for ref, part in pair], axis=0)
            values = jnp.concatenate([ref[1, :, part] for ref, part in pair], axis=0)
            weights = weigh(queries, keys)
            if start + 2 == len(blocks):
                weights = weights * keep
            num = num + times(weights, values)
            den = den + lanes(weights)
        if len(blocks) % 2:
            ref, part = blocks[0]
            weights = weigh(queries, ref[0, :, part])
            num = num + times(weights, ref[1, :, part])
            den = den + weights
        own_ref[:, cells] = num[:video]
        msg_ref[:, cells] = num[video:]
        packed = jnp.where(lane == first + head, jnp.sum(den, axis=1, keepdims=True), packed)
    own_den_ref[...] = packed[:video]
    msg_ref[:, width:] = packed[video:]
    if copy_out:
        cache_copy.wait()


def merge_kernel(first, own_ref, den_ref, msg_ref, att_ref):
    width = att_ref.shape[1]
    for head in range(width // HEAD_DIM):
        columns = slice(head * HEAD_DIM, (head + 1) * HEAD_DIM)
        lane = first + head
        num = own_ref[:, columns] + msg_ref[:, columns]
        den = den_ref[:, lane : lane + 1] + msg_ref[:, width + lane : width + lane + 1]
        att_ref[:, columns] = (num / den).astype(BF16)


def part_kernel(first_ref, second_ref, w_ref, out_ref):
    half = first_ref.shape[1]
    out_ref[...] = jnp.dot(
        first_ref[...], w_ref[:half, :], preferred_element_type=F32
    ) + jnp.dot(second_ref[...], w_ref[half:, :], preferred_element_type=F32)


def more_kernel(part_ref, att_ref, w_ref, out_ref):
    half = att_ref.shape[1]
    out_ref[...] = part_ref[...] + jnp.dot(
        att_ref[...], w_ref[:half, :], preferred_element_type=F32
    )


def final_kernel(part_ref, att_ref, w_ref, hidden_ref, gate_ref, out_ref):
    half = att_ref.shape[1]
    total = part_ref[...] + jnp.dot(att_ref[...], w_ref[half:, :], preferred_element_type=F32)
    gate = gate_ref[...].reshape(1, total.shape[1])
    out_ref[...] = (hidden_ref[...].astype(F32) + gate * total).astype(BF16)


def params(megabytes):
    return pltpu.CompilerParams(vmem_limit_bytes=megabytes * 1024 * 1024)


def in_hbm(array):
    return pltpu.with_memory_space_constraint(array, pltpu.HBM)


def cost(flops, nbytes, transcendentals=0):
    return pl.CostEstimate(
        flops=int(flops), bytes_accessed=int(nbytes), transcendentals=int(transcendentals)
    )


def plain_call(kernel, outs, name, estimate, *operands):
    return pl.pallas_call(
        kernel,
        in_specs=[pl.BlockSpec(memory_space=pltpu.VMEM)] * len(operands),
        out_specs=[pl.BlockSpec(memory_space=pltpu.VMEM)] * len(outs),
        out_shape=[jax.ShapeDtypeStruct(shape, dtype) for shape, dtype in outs],
        compiler_params=params(24),
        cost_estimate=estimate,
        name=name,
    )(*operands)


def ring_moves(sections):
    chips = sections // 2
    order = list(range(0, chips, 2)) + list(range(chips - 1, 0, -2))
    moves = [], []
    for here, there in zip(order, order[1:] + order[:1]):
        for core in range(2):
            moves[core].append((2 * here + core, 2 * there + core))
            moves[1 - core].append((2 * there + core, 2 * here + core))
    return sorted(moves[0]), sorted(moves[1])


def per_device(
    sections, hidden, text_hidden, text_mask, stale_cache, qkv_weight, out_weight, query_gain,
    key_gain, norm_shift, norm_scale, branch_gate,
):
    video, features = hidden.shape
    text = text_hidden.shape[0] // 2
    width = stale_cache.shape[2]
    heads = width // HEAD_DIM
    group_columns = heads * TRIPLE
    chips = sections // 2
    out_features = out_weight.shape[1]
    top = video + EXTRA
    rows = top + text

    group = lax.axis_index("head")
    core = lax.axis_index("section") % 2
    place = jnp.stack([group, core]).astype(jnp.int32)
    swap_core = [(s, s ^ 1) for s in range(sections)]
    swap_head = [(0, 1), (1, 0)]
    ways = ring_moves(sections)
    half_way = chips // 2

    def ring_step(blocks):
        return [lax.ppermute(block, "section", way) for block, way in zip(blocks, ways)]

    vmem = pl.BlockSpec(memory_space=pltpu.VMEM)
    hbm = pl.BlockSpec(memory_space=pltpu.HBM)
    smem = pl.BlockSpec(memory_space=pltpu.SMEM)
    whole = ring_step((stale_cache, stale_cache))

    columns = 2 * TRIPLE
    blocks = group_columns // columns
    ahead = blocks - 1
    slots = heads * 4 + -(-(-(-group_columns // PIECE // 4) + 1) * 16 // (text // 4))
    message_rows = video + -(-slots // (group_columns // PIECE)) * text // 4
    project_cost = cost(8 * rows * features * group_columns, 2 * features * group_columns)
    a_rows, message, stats, w_ahead = pl.pallas_call(
        send_kernel,
        in_specs=[smem] + [hbm] * 5,
        out_specs=[vmem] * 4,
        out_shape=[
            jax.ShapeDtypeStruct((rows, features), BF16),
            jax.ShapeDtypeStruct((message_rows, group_columns), BF16),
            jax.ShapeDtypeStruct((rows, HEAD_DIM), F32),
            jax.ShapeDtypeStruct((ahead, features, columns), BF16),
        ],
        scratch_shapes=[
            pltpu.VMEM((video, features), BF16),
            pltpu.VMEM((text, features), BF16),
            pltpu.VMEM((features,), F32),
            pltpu.VMEM((features,), F32),
            pltpu.VMEM((blocks, features, columns), BF16),
            pltpu.SemaphoreType.DMA((4,)),
            pltpu.SemaphoreType.DMA((blocks + ahead,)),
        ],
        compiler_params=params(40),
        cost_estimate=project_cost,
        name="project_send",
    )(place, *map(in_hbm, (hidden, text_hidden, norm_scale, norm_shift, qkv_weight)))

    received = lax.ppermute(message, "head", swap_head)
    split = plain_call(
        split_kernel, [((2, video, width // 2), BF16)] * 4, "split_heads", cost(0, 8 * video * width),
        *lax.optimization_barrier((*whole, message))[:2],
    )
    chains = [[ring_step((split[0], split[2]))], [ring_step((split[1], split[3]))]]

    small = (query_gain, key_gain, text_mask, branch_gate, hidden, stale_cache)
    outs = pl.pallas_call(
        own_kernel,
        in_specs=[smem, vmem, vmem, hbm, hbm] + [hbm] * len(small),
        out_specs=[vmem] * (4 + len(small)),
        out_shape=[
            jax.ShapeDtypeStruct((top, group_columns), F32),
            jax.ShapeDtypeStruct((text, 2 * width), F32),
            jax.ShapeDtypeStruct((width, out_features), BF16),
            jax.ShapeDtypeStruct((width, out_features), BF16),
        ]
        + [jax.ShapeDtypeStruct(array.shape, array.dtype) for array in small],
        scratch_shapes=[
            pltpu.VMEM((blocks - ahead, features, columns), BF16),
            pltpu.SemaphoreType.DMA((blocks - ahead,)),
            pltpu.SemaphoreType.DMA((len(small) + 2,)),
        ],
        compiler_params=params(36),
        cost_estimate=project_cost,
        name="project_own",
    )(place, a_rows, w_ahead, *map(in_hbm, (qkv_weight, out_weight) + small))
    own, own_text, w_own, w_other = outs[:4]
    query_gain, key_gain, text_mask, branch_gate, hidden, stale = outs[4:]

    for _ in range(half_way - 3):
        for chain in chains:
            chain.append(ring_step(lax.optimization_barrier((*chain[-1], own))[:2]))
    far = [lax.ppermute(chain[-1][0], "section", ways[0]) for chain in chains]
    ends = [chain[-1][1] for chain in chains]

    received = lax.optimization_barrier((received, *chains[0][0], *chains[1][0]))[0]
    *queries, fresh = plain_call(
        functools.partial(norm_kernel, features * 2, text),
        [((video, width // 2), BF16)] * 2 + [((2, video, width), BF16)],
        "norm_video",
        cost(1000 * top * group_columns, 8 * top * group_columns),
        own, received, stats, query_gain, key_gain,
    )
    other_queries = [lax.ppermute(half, "section", swap_core) for half in queries]
    (text_kv,) = plain_call(
        functools.partial(text_kernel, features * 2),
        [((2, text, width), BF16)],
        "norm_text",
        cost(text * group_columns, text * group_columns),
        own_text, received, stats, own, key_gain,
    )

    context = chips * video + video + text
    attended, other_attended = [], []
    for index, chain in enumerate(chains):
        first = index * heads // 2
        halves = [block for step in chain for block in step] + [far[index]]
        own_queries = queries[index]
        if attended:
            own_queries = lax.optimization_barrier((own_queries, num_own))[0]
        copy_out = index == 1
        num_own, den_own, num_message, *copied = pl.pallas_call(
            functools.partial(attend_kernel, first, len(whole), copy_out),
            in_specs=[smem] + [vmem] * (6 + len(whole) + len(halves)),
            out_specs=[vmem] * 3 + [hbm] * copy_out,
            out_shape=[
                jax.ShapeDtypeStruct((video, width // 2), F32),
                jax.ShapeDtypeStruct((video, HEAD_DIM), F32),
                jax.ShapeDtypeStruct((video, width // 2 + HEAD_DIM), F32),
            ]
            + [jax.ShapeDtypeStruct(fresh.shape, BF16)] * copy_out,
            scratch_shapes=[pltpu.SemaphoreType.DMA] * copy_out,
            compiler_params=params(24),
            cost_estimate=cost(
                video * context, context * width, video * heads
            ),
            name="attend",
        )(
            place, own_queries, other_queries[index], fresh, stale, text_kv, text_mask,
            *whole, *halves,
        )
        num_received = lax.ppermute(num_message, "section", swap_core)
        attended += plain_call(
            functools.partial(merge_kernel, first),
            [((video, width // 2), BF16)],
            "merge",
            cost(2 * video * width, 5 * video * width),
            num_own, den_own, num_received,
        )
        other_attended.append(lax.ppermute(attended[-1], "head", swap_head))

    out_cost = cost(4 * video * width * out_features, 2 * width * out_features)
    (part,) = plain_call(
        part_kernel, [((video, out_features), F32)], "part_out", out_cost, *attended, w_own
    )
    (part,) = plain_call(
        more_kernel, [((video, out_features), F32)], "more_out", out_cost,
        part, other_attended[0], w_other,
    )
    (mixed,) = plain_call(
        final_kernel, [((video, out_features), BF16)], "final_out", out_cost,
        part, other_attended[1], w_other, hidden, branch_gate,
    )
    return (mixed, copied[0])


def solution(mesh):
    in_specs = (
        P("section", "head"),
        P(None, "head"),
        P(),
        P(None, "section", "head"),
        P("head", None),
        P(None, "head"),
        P(),
        P(),
        P("head"),
        P("head"),
        P("head"),
    )
    out_specs = (P("section", "head"), P(None, "section", "head"))
    return jax.shard_map(
        functools.partial(per_device, mesh.shape["section"]),
        mesh=mesh, in_specs=in_specs, out_specs=out_specs, check_vma=False,
    )
```

```python
import functools
import math

import jax
import jax.numpy as jnp
from jax import lax
from jax.experimental import pallas as pl
from jax.experimental.pallas import tpu as pltpu
from jax.sharding import PartitionSpec as P

HEAD_DIM = 128
TRIPLE = 3 * HEAD_DIM
EXTRA = 16
PIECE = 2 * HEAD_DIM
EPS = 1e-06
F32 = jnp.float32
BF16 = jnp.bfloat16


def split_bf16(value, parts):
    pieces = []
    rest = value
    for _ in range(parts):
        piece = rest.astype(BF16)
        pieces.append(piece)
        rest = rest - piece.astype(F32)
    return pieces


def head_rows(video, text):
    return 3 * video + 2 * text + EXTRA


def column_copy(w_ref, first, target, sem):
    columns = target.shape[1]
    start = pl.multiple_of(first, HEAD_DIM)
    return pltpu.make_async_copy(w_ref.at[:, pl.ds(start, columns)], target, sem)


def partial_sums(a_ref, w_ref, video, text, msg_ref, first):
    band = lax.broadcasted_iota(jnp.int32, (EXTRA, HEAD_DIM), 0) // 4
    top = video + EXTRA
    terms = None
    for start in range(0, w_ref.shape[1], PIECE):
        stop = min(start + PIECE, w_ref.shape[1])
        product = jnp.dot(a_ref[...], w_ref[:, start:stop], preferred_element_type=F32)
        for local in range(0, stop - start, HEAD_DIM):
            part = product[:, local : local + HEAD_DIM]
            head, kind = divmod((start + local) // HEAD_DIM, 3)
            base = (first + head) * head_rows(video, text)
            msg_ref[base + kind * video : base + (kind + 1) * video, :] = part[:video].astype(BF16)
            terms = part[video:top] if kind == 0 else jnp.where(band == kind, part[video:top], terms)
            base += 3 * video
            if kind:
                rows = slice(base + (kind - 1) * text, base + kind * text)
                msg_ref[rows, :] = part[top:].astype(BF16)
            if kind == 2:
                base += 2 * text
                msg_ref[base : base + EXTRA, :] = terms.astype(BF16)


def send_kernel(
    place_ref, x_ref, t_ref, scale_ref, shift_ref, w_ref,
    a_ref, msg_ref, stat_ref, ahead_ref,
    x_buffer, t_buffer, scale_buffer, shift_buffer, w_buffer, sems,
):
    video, features = x_buffer.shape
    text = t_buffer.shape[0]
    top = video + EXTRA
    columns = w_buffer.shape[1]
    base = (1 - place_ref[0]) * (w_ref.shape[1] // 2)
    copies = [
        pltpu.make_async_copy(scale_ref, scale_buffer, sems.at[0]),
        pltpu.make_async_copy(shift_ref, shift_buffer, sems.at[1]),
        pltpu.make_async_copy(x_ref, x_buffer, sems.at[2]),
        pltpu.make_async_copy(
            t_ref.at[pl.ds(pl.multiple_of(place_ref[1] * text, text), text)], t_buffer, sems.at[3]
        ),
        column_copy(w_ref, base, w_buffer, sems.at[4]),
        column_copy(w_ref, base + columns, ahead_ref, sems.at[5]),
    ]
    for copy in copies[:5]:
        copy.start()

    copies[0].wait()
    copies[1].wait()
    gain = 1.0 + scale_buffer[...].reshape(1, features)
    pieces = split_bf16(gain, 2) + split_bf16(shift_buffer[...].reshape(1, features), 2)
    row = lax.broadcasted_iota(jnp.int32, (EXTRA, features), 0)
    extra = jnp.zeros((EXTRA, features), F32)
    for index, piece in enumerate(pieces):
        extra = jnp.where(row % 4 == index, piece.astype(F32), extra)
    a_ref[video:top, :] = extra.astype(BF16)

    def prepare(rows_ref, start):
        rows = rows_ref[...].astype(F32)
        count = rows.shape[0]
        mean = jnp.sum(rows, axis=1, keepdims=True) * (1.0 / features)
        centered = rows - mean
        second = jnp.sum(centered * centered, axis=1, keepdims=True)
        a_ref[start : start + count, :] = (centered * gain).astype(BF16)
        lane = lax.broadcasted_iota(jnp.int32, (count, HEAD_DIM), 1)
        packed = jnp.zeros((count, HEAD_DIM), F32)
        for index, piece in enumerate(split_bf16(mean, 3) + split_bf16(second, 3)):
            packed = jnp.where(lane == index, piece.astype(F32), packed)
        stat_ref[start : start + count, :] = jnp.where(
            lane == 0, mean, jnp.where(lane == 1, second, 0.0)
        )
        return jnp.transpose(packed)[:EXTRA]

    copies[2].wait()
    copies[5].start()
    stats = [prepare(x_buffer, 0)]
    copies[3].wait()
    stats.append(prepare(t_buffer, top))
    stat_ref[video:top, :] = jnp.zeros((EXTRA, HEAD_DIM), F32)
    start = head_rows(video, text) * columns // TRIPLE
    msg_ref[start : start + 2 * EXTRA, :] = jnp.concatenate(stats, axis=0).astype(BF16)
    copies[4].wait()
    partial_sums(a_ref, w_buffer, video, text, msg_ref, 0)
    copies[5].wait()


def send_more_kernel(
    video, place_ref, a_ref, ahead_ref, w_ref, msg_ref, own_ahead_ref, w_buffer, last_buffer, sems,
):
    text = a_ref.shape[0] - video - EXTRA
    width = w_ref.shape[1] // 2
    other, own = (1 - place_ref[0]) * width, place_ref[0] * width
    first = width - last_buffer.shape[1]
    copies = [
        column_copy(w_ref, other + first - w_buffer.shape[1], w_buffer, sems.at[0]),
        column_copy(w_ref, other + first, last_buffer, sems.at[1]),
        column_copy(w_ref, own, own_ahead_ref, sems.at[2]),
    ]
    copies[0].start()
    copies[1].start()
    partial_sums(a_ref, ahead_ref, video, text, msg_ref, 0)
    copies[0].wait()
    copies[2].start()
    head = ahead_ref.shape[1] // TRIPLE
    partial_sums(a_ref, w_buffer, video, text, msg_ref, head)
    copies[1].wait()
    head += w_buffer.shape[1] // TRIPLE
    partial_sums(a_ref, last_buffer, video, text, msg_ref, head)
    copies[2].wait()


def own_kernel(place_ref, a_ref, ahead_ref, w_ref, *refs):
    small = (len(refs) - 4) // 2
    out_ref, text_ref = refs[small : small + 2]
    w_buffer, sems = refs[-2:]
    top = out_ref.shape[0]
    later, _, columns = w_buffer.shape
    base = place_ref[0] * (w_ref.shape[1] // 2) + columns
    copies = [
        column_copy(w_ref, base + index * columns, w_buffer.at[index], sems.at[index])
        for index in range(later)
    ]
    for source, target in zip(refs[:small], refs[small + 2 : -2]):
        copies.append(pltpu.make_async_copy(source, target, sems.at[len(copies)]))
    for copy in copies:
        copy.start()

    for block in range(later + 1):
        if block:
            copies[block - 1].wait()
        for start in range(0, columns, PIECE):
            cells = slice(start, start + PIECE)
            part = w_buffer[block - 1, :, cells] if block else ahead_ref[:, cells]
            product = jnp.dot(a_ref[...], part, preferred_element_type=F32)
            first = block * columns + start
            out_ref[:, first : first + PIECE] = product[:top]
            for local in range(0, PIECE, HEAD_DIM):
                head, kind = divmod((first + local) // HEAD_DIM, 3)
                if kind:
                    target = (2 * head + kind - 1) * HEAD_DIM
                    text_ref[:, target : target + HEAD_DIM] = product[
                        top:, local : local + HEAD_DIM
                    ]
    for copy in copies[later:]:
        copy.wait()


def row_stats(total_features, own, received):
    count = own.shape[0]
    received = received.astype(F32)
    padding = jnp.zeros((HEAD_DIM - received.shape[0], count), F32)
    received = jnp.transpose(jnp.concatenate([received, padding], axis=0))
    parts = [received[:, index : index + 1] for index in range(6)]
    gap = 0.5 * (own[:, 0:1] - (parts[0] + parts[1] + parts[2]))
    second = own[:, 1:2] + (parts[3] + parts[4] + parts[5])
    var = second * (1.0 / total_features) + gap * gap
    return gap, lax.rsqrt(var + EPS)


def column_terms(own_ref, msg_ref, video, base, part):
    other = msg_ref[base : base + EXTRA, :].astype(F32)
    other = other[4 * (part % 3) : 4 * (part % 3) + 4]
    own = own_ref[video : video + 8, part * HEAD_DIM : (part + 1) * HEAD_DIM]
    scale = (own[0:1] + own[1:2]) - (other[0:1] + other[1:2])
    shift = (own[2:3] + own[3:4]) + (other[2:3] + other[3:4])
    return scale, shift


def head_place(head, rows, first_ref, more_ref):
    early = first_ref.shape[0] // rows
    return (first_ref, head * rows) if head < early else (more_ref, (head - early) * rows)


def head_norm(part, gain):
    square = jnp.sum(part * part, axis=1, keepdims=True) * (1.0 / HEAD_DIM)
    return part * lax.rsqrt(square + EPS) * gain


def norm_kernel(
    total_features, text, own_ref, first_ref, more_ref, stat_ref, qg_ref, kg_ref,
    qa_ref, qb_ref, kv_ref,
):
    video = qa_ref.shape[0]
    half = qa_ref.shape[1] // HEAD_DIM
    rows = head_rows(video, text)
    query_gain = qg_ref[...].reshape(1, HEAD_DIM)
    key_gain = kg_ref[...].reshape(1, HEAD_DIM)
    start = first_ref.shape[0] - 2 * EXTRA
    gap, inverse = row_stats(
        total_features, stat_ref[:video, :], first_ref[start : start + EXTRA, :video]
    )
    for head in range(2 * half):
        msg_ref, base = head_place(head, rows, first_ref, more_ref)

        def total(kind):
            part = 3 * head + kind
            scale, shift = column_terms(own_ref, msg_ref, video, base + rows - EXTRA, part)
            other = msg_ref[base + kind * video : base + (kind + 1) * video, :].astype(F32)
            both = own_ref[:video, part * HEAD_DIM : (part + 1) * HEAD_DIM] + other
            return (both + gap * scale) * inverse + shift

        columns = slice(head * HEAD_DIM, (head + 1) * HEAD_DIM)
        cells = slice(head % half * HEAD_DIM, (head % half + 1) * HEAD_DIM)
        q_ref = qa_ref if head < half else qb_ref
        q_ref[:, cells] = head_norm(total(0), query_gain).astype(BF16)
        kv_ref[0, :, columns] = head_norm(total(1), key_gain).astype(BF16)
        kv_ref[1, :, columns] = total(2).astype(BF16)


def text_kernel(
    total_features, own_ref, first_ref, more_ref, stat_ref, top_ref, kg_ref, kv_ref
):
    text = kv_ref.shape[1]
    heads = kv_ref.shape[2] // HEAD_DIM
    video = top_ref.shape[0] - EXTRA
    rows = head_rows(video, text)
    key_gain = kg_ref[...].reshape(1, HEAD_DIM)
    start = first_ref.shape[0] - EXTRA
    gap, inverse = row_stats(
        total_features, stat_ref[video + EXTRA :, :], first_ref[start : start + EXTRA, :text]
    )
    for head in range(heads):
        msg_ref, base = head_place(head, rows, first_ref, more_ref)

        def total(kind):
            scale, shift = column_terms(
                top_ref, msg_ref, video, base + rows - EXTRA, 3 * head + 1 + kind
            )
            start = base + 3 * video + kind * text
            other = msg_ref[start : start + text, :].astype(F32)
            first = (2 * head + kind) * HEAD_DIM
            return (own_ref[:, first : first + HEAD_DIM] + other + gap * scale) * inverse + shift

        columns = slice(head * HEAD_DIM, (head + 1) * HEAD_DIM)
        kv_ref[0, :, columns] = head_norm(total(0), key_gain).astype(BF16)
        kv_ref[1, :, columns] = total(1).astype(BF16)


FACTOR = math.log2(math.e) / math.sqrt(HEAD_DIM)


def split_kernel(*refs):
    count = len(refs) // 3
    for index in range(count):
        half = refs[index].shape[2] // 2
        refs[count + 2 * index][...] = refs[index][:, :, :half]
        refs[count + 2 * index + 1][...] = refs[index][:, :, half:]


AT_ONCE = 10


def attend_kernel(
    first, count, second, place_ref, weight_ref, qo_ref, qp_ref, fresh_ref, stale_ref, text_ref,
    mask_ref, *refs,
):
    if second:
        *refs, own_ref, own_den_ref, msg_ref, w_ref, cache_ref, sems = refs
    else:
        *refs, own_ref, own_den_ref, msg_ref, w_ref, sems = refs
    depth = w_ref.shape[0]
    half = 1 - place_ref[0] if second else place_ref[0]
    rows = pl.ds(pl.multiple_of(half * depth, depth), depth)
    copies = [pltpu.make_async_copy(weight_ref.at[rows], w_ref, sems.at[0])]
    if second:
        copies.append(pltpu.make_async_copy(fresh_ref, cache_ref, sems.at[1]))
    for copy in copies:
        copy.start()

    video, width = own_ref.shape
    text = text_ref.shape[1]
    lane = lax.broadcasted_iota(jnp.int32, (2 * video, HEAD_DIM), 1)
    mask = mask_ref[...].reshape(1, 2 * text).astype(F32)
    mask = jnp.where(place_ref[1] == 0, mask[:, :text], mask[:, text:])
    own_row = lax.broadcasted_iota(jnp.int32, (2 * video, 1), 0) < video
    packed = jnp.zeros((2 * video, HEAD_DIM), F32)
    for head in range(width // HEAD_DIM):
        cells = slice(head * HEAD_DIM, (head + 1) * HEAD_DIM)
        columns = slice((first + head) * HEAD_DIM, (first + head + 1) * HEAD_DIM)
        queries = jnp.concatenate([qo_ref[:, cells], qp_ref[:, cells]], axis=0)
        keeps = [jnp.where(own_row, 1.0, 0.0), jnp.where(own_row, 0.0, 1.0), mask]
        blocks = [(fresh_ref, columns), (stale_ref, columns), (text_ref, columns)]
        blocks += [(ref, columns) for ref in refs[:count]] + [(ref, cells) for ref in refs[count:]]
        total = None
        for start in range(0, len(blocks), AT_ONCE):
            group = blocks[start : start + AT_ONCE]
            keys = jnp.concatenate([ref[0, :, part] for ref, part in group], axis=0)
            values = jnp.concatenate([ref[1, :, part] for ref, part in group], axis=0)
            scores = lax.dot_general(
                queries, keys, (((1,), (1,)), ((), ())), preferred_element_type=F32
            )
            weights, place = [], 0
            for index, (ref, _) in enumerate(group):
                size = ref.shape[1]
                part = jnp.exp2(scores[:, place : place + size] * FACTOR)
                if start + index < len(keeps):
                    part = part * keeps[start + index]
                weights.append(part.astype(BF16))
                place += size
            values = jnp.concatenate([values, jnp.ones((place, HEAD_DIM), BF16)], axis=1)
            sums = jnp.dot(
                jnp.concatenate(weights, axis=1), values, preferred_element_type=F32
            )
            total = sums if total is None else total + sums
        own_ref[:, cells] = total[:video, :HEAD_DIM]
        msg_ref[:, cells] = total[video:, :HEAD_DIM]
        packed = jnp.where(lane == first + head, total[:, HEAD_DIM:], packed)
    own_den_ref[...] = packed[:video]
    msg_ref[:, width:] = packed[video:]
    for copy in copies:
        copy.wait()


def merge_kernel(first, own_ref, den_ref, msg_ref, att_ref):
    width = att_ref.shape[1]
    for head in range(width // HEAD_DIM):
        columns = slice(head * HEAD_DIM, (head + 1) * HEAD_DIM)
        lane = first + head
        num = own_ref[:, columns] + msg_ref[:, columns]
        den = den_ref[:, lane : lane + 1] + msg_ref[:, width + lane : width + lane + 1]
        att_ref[:, columns] = (num / den).astype(BF16)


def part_kernel(first_ref, second_ref, w_ref, out_ref):
    half = first_ref.shape[1]
    out_ref[...] = jnp.dot(
        first_ref[...], w_ref[:half, :], preferred_element_type=F32
    ) + jnp.dot(second_ref[...], w_ref[half:, :], preferred_element_type=F32)


def more_kernel(part_ref, att_ref, w_ref, out_ref):
    half = att_ref.shape[1]
    out_ref[...] = part_ref[...] + jnp.dot(
        att_ref[...], w_ref[:half, :], preferred_element_type=F32
    )


def final_kernel(part_ref, att_ref, w_ref, hidden_ref, gate_ref, out_ref):
    half = att_ref.shape[1]
    total = part_ref[...] + jnp.dot(att_ref[...], w_ref[half:, :], preferred_element_type=F32)
    gate = gate_ref[...].reshape(1, total.shape[1])
    out_ref[...] = (hidden_ref[...].astype(F32) + gate * total).astype(BF16)


def params(megabytes):
    return pltpu.CompilerParams(vmem_limit_bytes=megabytes * 1024 * 1024)


def in_hbm(array):
    return pltpu.with_memory_space_constraint(array, pltpu.HBM)


def cost(flops, nbytes, transcendentals=0):
    return pl.CostEstimate(
        flops=int(flops), bytes_accessed=int(nbytes), transcendentals=int(transcendentals)
    )


def plain_call(kernel, outs, name, estimate, *operands):
    return pl.pallas_call(
        kernel,
        in_specs=[pl.BlockSpec(memory_space=pltpu.VMEM)] * len(operands),
        out_specs=[pl.BlockSpec(memory_space=pltpu.VMEM)] * len(outs),
        out_shape=[jax.ShapeDtypeStruct(shape, dtype) for shape, dtype in outs],
        compiler_params=params(24),
        cost_estimate=estimate,
        name=name,
    )(*operands)


def ring_moves(sections):
    chips = sections // 2
    order = list(range(0, chips, 2)) + list(range(chips - 1, 0, -2))
    moves = [], []
    for here, there in zip(order, order[1:] + order[:1]):
        for core in range(2):
            moves[core].append((2 * here + core, 2 * there + core))
            moves[1 - core].append((2 * there + core, 2 * here + core))
    return sorted(moves[0]), sorted(moves[1])


def per_device(
    sections, hidden, text_hidden, text_mask, stale_cache, qkv_weight, out_weight, query_gain,
    key_gain, norm_shift, norm_scale, branch_gate,
):
    video, features = hidden.shape
    text = text_hidden.shape[0] // 2
    width = stale_cache.shape[2]
    heads = width // HEAD_DIM
    group_columns = heads * TRIPLE
    chips = sections // 2
    out_features = out_weight.shape[1]
    top = video + EXTRA
    rows = top + text

    group = lax.axis_index("head")
    core = lax.axis_index("section") % 2
    place = jnp.stack([group, core]).astype(jnp.int32)
    swap_core = [(s, s ^ 1) for s in range(sections)]
    swap_head = [(0, 1), (1, 0)]
    ways = ring_moves(sections)
    half_way = chips // 2

    def ring_step(blocks):
        return [lax.ppermute(block, "section", way) for block, way in zip(blocks, ways)]

    vmem = pl.BlockSpec(memory_space=pltpu.VMEM)
    hbm = pl.BlockSpec(memory_space=pltpu.HBM)
    smem = pl.BlockSpec(memory_space=pltpu.SMEM)
    whole = ring_step((stale_cache, stale_cache))

    columns = 2 * TRIPLE
    blocks = group_columns // columns
    per_head = head_rows(video, text)

    def project_cost(share):
        share = 8 * rows * features * group_columns * share
        return cost(share, share // (4 * rows))

    a_rows, message, stats, ahead = pl.pallas_call(
        send_kernel,
        in_specs=[smem] + [hbm] * 5,
        out_specs=[vmem] * 4,
        out_shape=[
            jax.ShapeDtypeStruct((rows, features), BF16),
            jax.ShapeDtypeStruct((per_head + 2 * EXTRA, HEAD_DIM), BF16),
            jax.ShapeDtypeStruct((rows, HEAD_DIM), F32),
            jax.ShapeDtypeStruct((features, columns), BF16),
        ],
        scratch_shapes=[
            pltpu.VMEM((video, features), BF16),
            pltpu.VMEM((text, features), BF16),
            pltpu.VMEM((features,), F32),
            pltpu.VMEM((features,), F32),
            pltpu.VMEM((features, TRIPLE), BF16),
            pltpu.SemaphoreType.DMA((6,)),
        ],
        compiler_params=params(40),
        cost_estimate=project_cost(0.4),
        name="project_send",
    )(place, *map(in_hbm, (hidden, text_hidden, norm_scale, norm_shift, qkv_weight)))
    received = lax.ppermute(message, "head", swap_head)

    message_more, own_ahead = pl.pallas_call(
        functools.partial(send_more_kernel, video),
        in_specs=[smem, vmem, vmem, hbm],
        out_specs=[vmem] * 2,
        out_shape=[
            jax.ShapeDtypeStruct(((heads - 1) * per_head, HEAD_DIM), BF16),
            jax.ShapeDtypeStruct((features, columns), BF16),
        ],
        scratch_shapes=[
            pltpu.VMEM((features, group_columns - columns - 2 * TRIPLE), BF16),
            pltpu.VMEM((features, TRIPLE), BF16),
            pltpu.SemaphoreType.DMA((3,)),
        ],
        compiler_params=params(40),
        cost_estimate=project_cost(0.6),
        name="project_send_more",
    )(place, a_rows, ahead, in_hbm(qkv_weight))
    received_more = lax.ppermute(message_more, "head", swap_head)

    split = plain_call(
        split_kernel, [((2, video, width // 2), BF16)] * 4, "split_heads", cost(0, 8 * video * width),
        *lax.optimization_barrier((*whole, message_more, received))[:2],
    )
    chains = [[ring_step((split[0], split[2]))], [ring_step((split[1], split[3]))]]

    small = (query_gain, key_gain, text_mask, branch_gate, hidden, stale_cache)
    outs = pl.pallas_call(
        own_kernel,
        in_specs=[smem, vmem, vmem, hbm] + [hbm] * len(small),
        out_specs=[vmem] * (2 + len(small)),
        out_shape=[
            jax.ShapeDtypeStruct((top, group_columns), F32),
            jax.ShapeDtypeStruct((text, 2 * width), F32),
        ]
        + [jax.ShapeDtypeStruct(array.shape, array.dtype) for array in small],
        scratch_shapes=[
            pltpu.VMEM((blocks - 1, features, columns), BF16),
            pltpu.SemaphoreType.DMA((blocks - 1 + len(small),)),
        ],
        compiler_params=params(40),
        cost_estimate=project_cost(1),
        name="project_own",
    )(place, a_rows, own_ahead, *map(in_hbm, (qkv_weight,) + small))
    own, own_text = outs[:2]
    query_gain, key_gain, text_mask, branch_gate, hidden, stale = outs[2:]

    for _ in range(half_way - 3):
        for chain in chains:
            chain.append(ring_step(lax.optimization_barrier((*chain[-1], own))[:2]))
    far = [lax.ppermute(chain[-1][0], "section", ways[0]) for chain in chains]
    ends = [chain[-1][1] for chain in chains]

    received_more = lax.optimization_barrier((received_more, *chains[0][0], *chains[1][0]))[0]
    *queries, fresh = plain_call(
        functools.partial(norm_kernel, features * 2, text),
        [((video, width // 2), BF16)] * 2 + [((2, video, width), BF16)],
        "norm_video",
        cost(1000 * top * group_columns, 8 * top * group_columns),
        own, received, received_more, stats, query_gain, key_gain,
    )
    other_queries = [lax.ppermute(half, "section", swap_core) for half in queries]
    (text_kv,) = plain_call(
        functools.partial(text_kernel, features * 2),
        [((2, text, width), BF16)],
        "norm_text",
        cost(text * group_columns, text * group_columns),
        own_text, received, received_more, stats, own, key_gain,
    )

    context = chips * video + video + text
    attended, other_attended, w_halves = [], [], []
    for index, chain in enumerate(chains):
        first = index * heads // 2
        halves = [block for step in chain for block in step] + [far[index]]
        own_queries = queries[index]
        if attended:
            own_queries = lax.optimization_barrier((own_queries, num_own))[0]
        second = index == 1
        num_own, den_own, num_message, w_half, *copied = pl.pallas_call(
            functools.partial(attend_kernel, first, len(whole), second),
            in_specs=[smem, hbm] + [vmem] * (6 + len(whole) + len(halves)),
            out_specs=[vmem] * 4 + [hbm] * second,
            out_shape=[
                jax.ShapeDtypeStruct((video, width // 2), F32),
                jax.ShapeDtypeStruct((video, HEAD_DIM), F32),
                jax.ShapeDtypeStruct((video, width // 2 + HEAD_DIM), F32),
                jax.ShapeDtypeStruct((width, out_features), BF16),
            ]
            + [jax.ShapeDtypeStruct(fresh.shape, BF16)] * second,
            scratch_shapes=[pltpu.SemaphoreType.DMA((2,))],
            compiler_params=params(24),
            cost_estimate=cost(
                video * context, context * width, video * heads
            ),
            name="attend",
        )(
            place, in_hbm(out_weight), own_queries, other_queries[index], fresh, stale, text_kv,
            text_mask, *whole, *halves,
        )
        w_halves.append(w_half)
        num_received = lax.ppermute(num_message, "section", swap_core)
        attended += plain_call(
            functools.partial(merge_kernel, first),
            [((video, width // 2), BF16)],
            "merge",
            cost(2 * video * width, 5 * video * width),
            num_own, den_own, num_received,
        )
        other_attended.append(lax.ppermute(attended[-1], "head", swap_head))

    out_cost = cost(4 * video * width * out_features, 2 * width * out_features)
    (part,) = plain_call(
        part_kernel, [((video, out_features), F32)], "part_out", out_cost, *attended, w_halves[0]
    )
    (part,) = plain_call(
        more_kernel, [((video, out_features), F32)], "more_out", out_cost,
        part, other_attended[0], w_halves[1],
    )
    (mixed,) = plain_call(
        final_kernel, [((video, out_features), BF16)], "final_out", out_cost,
        part, other_attended[1], w_halves[1], hidden, branch_gate,
    )
    return (mixed, copied[0])


def solution(mesh):
    in_specs = (
        P("section", "head"),
        P(None, "head"),
        P(),
        P(None, "section", "head"),
        P("head", None),
        P(None, "head"),
        P(),
        P(),
        P("head"),
        P("head"),
        P("head"),
    )
    out_specs = (P("section", "head"), P(None, "section", "head"))
    return jax.shard_map(
        functools.partial(per_device, mesh.shape["section"]),
        mesh=mesh, in_specs=in_specs, out_specs=out_specs, check_vma=False,
    )
```

```python
import functools
import math

import jax
import jax.numpy as jnp
from jax import lax
from jax.experimental import pallas as pl
from jax.experimental.pallas import tpu as pltpu
from jax.sharding import PartitionSpec as P

HEAD_DIM = 128
TRIPLE = 3 * HEAD_DIM
EXTRA = 16
PIECE = 2 * HEAD_DIM
EPS = 1e-06
F32 = jnp.float32
BF16 = jnp.bfloat16


def split_bf16(value, parts):
    pieces = []
    rest = value
    for _ in range(parts):
        piece = rest.astype(BF16)
        pieces.append(piece)
        rest = rest - piece.astype(F32)
    return pieces


def head_rows(video, text):
    return 3 * video + 2 * text + EXTRA


def column_copy(w_ref, first, target, sem):
    columns = target.shape[1]
    start = pl.multiple_of(first, HEAD_DIM)
    return pltpu.make_async_copy(w_ref.at[:, pl.ds(start, columns)], target, sem)


def partial_sums(a_ref, w_ref, video, text, msg_ref, first):
    band = lax.broadcasted_iota(jnp.int32, (EXTRA, HEAD_DIM), 0) // 4
    top = video + EXTRA
    terms = None
    for start in range(0, w_ref.shape[1], PIECE):
        stop = min(start + PIECE, w_ref.shape[1])
        product = jnp.dot(a_ref[...], w_ref[:, start:stop], preferred_element_type=F32)
        for local in range(0, stop - start, HEAD_DIM):
            part = product[:, local : local + HEAD_DIM]
            head, kind = divmod((start + local) // HEAD_DIM, 3)
            base = (first + head) * head_rows(video, text)
            msg_ref[base + kind * video : base + (kind + 1) * video, :] = part[:video].astype(BF16)
            terms = part[video:top] if kind == 0 else jnp.where(band == kind, part[video:top], terms)
            base += 3 * video
            if kind:
                rows = slice(base + (kind - 1) * text, base + kind * text)
                msg_ref[rows, :] = part[top:].astype(BF16)
            if kind == 2:
                base += 2 * text
                msg_ref[base : base + EXTRA, :] = terms.astype(BF16)


def send_kernel(
    place_ref, x_ref, t_ref, scale_ref, shift_ref, w_ref,
    a_ref, msg_ref, stat_ref, ahead_ref,
    x_buffer, t_buffer, scale_buffer, shift_buffer, w_buffer, sems,
):
    video, features = x_buffer.shape
    text = t_buffer.shape[0]
    top = video + EXTRA
    columns = w_buffer.shape[1]
    base = (1 - place_ref[0]) * (w_ref.shape[1] // 2)
    copies = [
        pltpu.make_async_copy(scale_ref, scale_buffer, sems.at[0]),
        pltpu.make_async_copy(shift_ref, shift_buffer, sems.at[1]),
        pltpu.make_async_copy(x_ref, x_buffer, sems.at[2]),
        pltpu.make_async_copy(
            t_ref.at[pl.ds(pl.multiple_of(place_ref[1] * text, text), text)], t_buffer, sems.at[3]
        ),
        column_copy(w_ref, base, w_buffer, sems.at[4]),
        column_copy(w_ref, base + columns, ahead_ref, sems.at[5]),
    ]
    for copy in copies[:5]:
        copy.start()

    copies[0].wait()
    copies[1].wait()
    gain = 1.0 + scale_buffer[...].reshape(1, features)
    pieces = split_bf16(gain, 2) + split_bf16(shift_buffer[...].reshape(1, features), 2)
    row = lax.broadcasted_iota(jnp.int32, (EXTRA, features), 0)
    extra = jnp.zeros((EXTRA, features), F32)
    for index, piece in enumerate(pieces):
        extra = jnp.where(row % 4 == index, piece.astype(F32), extra)
    a_ref[video:top, :] = extra.astype(BF16)

    def prepare(rows_ref, start):
        rows = rows_ref[...].astype(F32)
        count = rows.shape[0]
        mean = jnp.sum(rows, axis=1, keepdims=True) * (1.0 / features)
        centered = rows - mean
        second = jnp.sum(centered * centered, axis=1, keepdims=True)
        a_ref[start : start + count, :] = (centered * gain).astype(BF16)
        lane = lax.broadcasted_iota(jnp.int32, (count, HEAD_DIM), 1)
        packed = jnp.zeros((count, HEAD_DIM), F32)
        for index, piece in enumerate(split_bf16(mean, 3) + split_bf16(second, 3)):
            packed = jnp.where(lane == index, piece.astype(F32), packed)
        stat_ref[start : start + count, :] = jnp.where(
            lane == 0, mean, jnp.where(lane == 1, second, 0.0)
        )
        return jnp.transpose(packed)[:EXTRA]

    copies[2].wait()
    copies[5].start()
    stats = [prepare(x_buffer, 0)]
    copies[3].wait()
    stats.append(prepare(t_buffer, top))
    stat_ref[video:top, :] = jnp.zeros((EXTRA, HEAD_DIM), F32)
    start = head_rows(video, text) * columns // TRIPLE
    msg_ref[start : start + 2 * EXTRA, :] = jnp.concatenate(stats, axis=0).astype(BF16)
    copies[4].wait()
    partial_sums(a_ref, w_buffer, video, text, msg_ref, 0)
    copies[5].wait()


def send_more_kernel(
    video, place_ref, a_ref, ahead_ref, w_ref, msg_ref, own_ahead_ref, w_buffer, last_buffer, sems,
):
    text = a_ref.shape[0] - video - EXTRA
    width = w_ref.shape[1] // 2
    other, own = (1 - place_ref[0]) * width, place_ref[0] * width
    first = width - last_buffer.shape[1]
    copies = [
        column_copy(w_ref, other + first - w_buffer.shape[1], w_buffer, sems.at[0]),
        column_copy(w_ref, other + first, last_buffer, sems.at[1]),
        column_copy(w_ref, own, own_ahead_ref, sems.at[2]),
    ]
    copies[0].start()
    copies[1].start()
    partial_sums(a_ref, ahead_ref, video, text, msg_ref, 0)
    copies[0].wait()
    copies[2].start()
    head = ahead_ref.shape[1] // TRIPLE
    partial_sums(a_ref, w_buffer, video, text, msg_ref, head)
    copies[1].wait()
    head += w_buffer.shape[1] // TRIPLE
    partial_sums(a_ref, last_buffer, video, text, msg_ref, head)
    copies[2].wait()


def own_kernel(place_ref, a_ref, ahead_ref, w_ref, *refs):
    small = (len(refs) - 4) // 2
    out_ref, text_ref = refs[small : small + 2]
    w_buffer, sems = refs[-2:]
    top = out_ref.shape[0]
    later, _, columns = w_buffer.shape
    base = place_ref[0] * (w_ref.shape[1] // 2) + columns
    copies = [
        column_copy(w_ref, base + index * columns, w_buffer.at[index], sems.at[index])
        for index in range(later)
    ]
    for source, target in zip(refs[:small], refs[small + 2 : -2]):
        copies.append(pltpu.make_async_copy(source, target, sems.at[len(copies)]))
    for copy in copies:
        copy.start()

    for block in range(later + 1):
        if block:
            copies[block - 1].wait()
        for start in range(0, columns, PIECE):
            cells = slice(start, start + PIECE)
            part = w_buffer[block - 1, :, cells] if block else ahead_ref[:, cells]
            product = jnp.dot(a_ref[...], part, preferred_element_type=F32)
            first = block * columns + start
            out_ref[:, first : first + PIECE] = product[:top]
            for local in range(0, PIECE, HEAD_DIM):
                head, kind = divmod((first + local) // HEAD_DIM, 3)
                if kind:
                    target = (2 * head + kind - 1) * HEAD_DIM
                    text_ref[:, target : target + HEAD_DIM] = product[
                        top:, local : local + HEAD_DIM
                    ]
    for copy in copies[later:]:
        copy.wait()


def row_stats(total_features, own, received):
    count = own.shape[0]
    received = received.astype(F32)
    padding = jnp.zeros((HEAD_DIM - received.shape[0], count), F32)
    received = jnp.transpose(jnp.concatenate([received, padding], axis=0))
    parts = [received[:, index : index + 1] for index in range(6)]
    gap = 0.5 * (own[:, 0:1] - (parts[0] + parts[1] + parts[2]))
    second = own[:, 1:2] + (parts[3] + parts[4] + parts[5])
    var = second * (1.0 / total_features) + gap * gap
    return gap, lax.rsqrt(var + EPS)


def column_terms(own_ref, msg_ref, video, base, part):
    other = msg_ref[base : base + EXTRA, :].astype(F32)
    other = other[4 * (part % 3) : 4 * (part % 3) + 4]
    own = own_ref[video : video + 8, part * HEAD_DIM : (part + 1) * HEAD_DIM]
    scale = (own[0:1] + own[1:2]) - (other[0:1] + other[1:2])
    shift = (own[2:3] + own[3:4]) + (other[2:3] + other[3:4])
    return scale, shift


def head_place(head, rows, first_ref, more_ref):
    early = first_ref.shape[0] // rows
    return (first_ref, head * rows) if head < early else (more_ref, (head - early) * rows)


def head_norm(part, gain):
    square = jnp.sum(part * part, axis=1, keepdims=True) * (1.0 / HEAD_DIM)
    return part * lax.rsqrt(square + EPS) * gain


def norm_kernel(
    total_features, text, own_ref, first_ref, more_ref, stat_ref, qg_ref, kg_ref,
    qa_ref, qb_ref, kv_ref,
):
    video = qa_ref.shape[0]
    half = qa_ref.shape[1] // HEAD_DIM
    rows = head_rows(video, text)
    query_gain = qg_ref[...].reshape(1, HEAD_DIM)
    key_gain = kg_ref[...].reshape(1, HEAD_DIM)
    start = first_ref.shape[0] - 2 * EXTRA
    gap, inverse = row_stats(
        total_features, stat_ref[:video, :], first_ref[start : start + EXTRA, :video]
    )
    for head in range(2 * half):
        msg_ref, base = head_place(head, rows, first_ref, more_ref)

        def total(kind):
            part = 3 * head + kind
            scale, shift = column_terms(own_ref, msg_ref, video, base + rows - EXTRA, part)
            other = msg_ref[base + kind * video : base + (kind + 1) * video, :].astype(F32)
            both = own_ref[:video, part * HEAD_DIM : (part + 1) * HEAD_DIM] + other
            return (both + gap * scale) * inverse + shift

        columns = slice(head * HEAD_DIM, (head + 1) * HEAD_DIM)
        cells = slice(head % half * HEAD_DIM, (head % half + 1) * HEAD_DIM)
        q_ref = qa_ref if head < half else qb_ref
        q_ref[:, cells] = head_norm(total(0), query_gain).astype(BF16)
        kv_ref[0, :, columns] = head_norm(total(1), key_gain).astype(BF16)
        kv_ref[1, :, columns] = total(2).astype(BF16)


def text_kernel(
    total_features, own_ref, first_ref, more_ref, stat_ref, top_ref, kg_ref, kv_ref
):
    text = kv_ref.shape[1]
    heads = kv_ref.shape[2] // HEAD_DIM
    video = top_ref.shape[0] - EXTRA
    rows = head_rows(video, text)
    key_gain = kg_ref[...].reshape(1, HEAD_DIM)
    start = first_ref.shape[0] - EXTRA
    gap, inverse = row_stats(
        total_features, stat_ref[video + EXTRA :, :], first_ref[start : start + EXTRA, :text]
    )
    for head in range(heads):
        msg_ref, base = head_place(head, rows, first_ref, more_ref)

        def total(kind):
            scale, shift = column_terms(
                top_ref, msg_ref, video, base + rows - EXTRA, 3 * head + 1 + kind
            )
            start = base + 3 * video + kind * text
            other = msg_ref[start : start + text, :].astype(F32)
            first = (2 * head + kind) * HEAD_DIM
            return (own_ref[:, first : first + HEAD_DIM] + other + gap * scale) * inverse + shift

        columns = slice(head * HEAD_DIM, (head + 1) * HEAD_DIM)
        kv_ref[0, :, columns] = head_norm(total(0), key_gain).astype(BF16)
        kv_ref[1, :, columns] = total(1).astype(BF16)


FACTOR = math.log2(math.e) / math.sqrt(HEAD_DIM)


def split_kernel(*refs):
    count = len(refs) // 3
    for index in range(count):
        half = refs[index].shape[2] // 2
        refs[count + 2 * index][...] = refs[index][:, :, :half]
        refs[count + 2 * index + 1][...] = refs[index][:, :, half:]


def weigh(rows, keys):
    scores = lax.dot_general(rows, keys, (((1,), (1,)), ((), ())), preferred_element_type=F32)
    return jnp.exp2(scores * FACTOR)


def lanes(weights):
    total = weights[:, :HEAD_DIM]
    for start in range(HEAD_DIM, weights.shape[1], HEAD_DIM):
        total = total + weights[:, start : start + HEAD_DIM]
    return total


def times(weights, values):
    return jnp.dot(weights.astype(BF16), values, preferred_element_type=F32)


def both(group, index):
    return jnp.concatenate([ref[index, :, part] for ref, part in group], axis=0)


def attend_kernel(
    first, count, place_ref, qo_ref, qp_ref, fresh_ref, stale_ref, text_ref, mask_ref, *refs,
):
    finish = len(refs[-1].shape) == 0
    if finish:
        *refs, own_ref, own_den_ref, msg_ref, cache_ref, sem = refs
        cache_copy = pltpu.make_async_copy(fresh_ref, cache_ref, sem)
        cache_copy.start()
    else:
        *refs, num_ref, den_ref = refs
    video, width = qo_ref.shape
    text = text_ref.shape[1]
    lane = lax.broadcasted_iota(jnp.int32, (2 * video, HEAD_DIM), 1)
    mask = mask_ref[...].reshape(1, 2 * text).astype(F32)
    mask = jnp.where(place_ref[1] == 0, mask[:, :text], mask[:, text:])
    keep = jnp.concatenate([jnp.ones((1, video), F32), mask], axis=1)
    same_patch = (
        (lax.broadcasted_iota(jnp.int32, (2 * video, 2 * video), 0) < video)
        == (lax.broadcasted_iota(jnp.int32, (2 * video, 2 * video), 1) < video)
    ).astype(F32)
    packed = jnp.zeros((2 * video, HEAD_DIM), F32)
    for head in range(width // HEAD_DIM):
        cells = slice(head * HEAD_DIM, (head + 1) * HEAD_DIM)
        columns = slice((first + head) * HEAD_DIM, (first + head + 1) * HEAD_DIM)
        queries = jnp.concatenate([qo_ref[:, cells], qp_ref[:, cells]], axis=0)
        pair = [(fresh_ref, columns), (stale_ref, columns)]
        weights = weigh(queries, both(pair, 0)) * same_patch
        num = times(weights, both(pair, 1))
        den = lanes(weights)
        blocks = [(ref, columns) for ref in refs[:count]] + [(ref, cells) for ref in refs[count:]]
        blocks.append((text_ref, columns))
        odd = len(blocks) % 2
        for start in range(odd, len(blocks), 2):
            pair = blocks[start : start + 2]
            weights = weigh(queries, both(pair, 0))
            if start + 2 == len(blocks):
                weights = weights * keep
            num = num + times(weights, both(pair, 1))
            den = den + lanes(weights)
        if odd:
            weights = weigh(queries, both(blocks[:1], 0))
            num = num + times(weights, both(blocks[:1], 1))
            den = den + weights
        if finish:
            own_ref[:, cells] = num[:video]
            msg_ref[:, cells] = num[video:]
        else:
            num_ref[:, cells] = num
        packed = jnp.where(lane == first + head, jnp.sum(den, axis=1, keepdims=True), packed)
    if finish:
        own_den_ref[...] = packed[:video]
        msg_ref[:, width:] = packed[video:]
        cache_copy.wait()
    else:
        den_ref[...] = packed


def last_kernel(first, qo_ref, qp_ref, num_ref, den_ref, far_ref, own_ref, own_den_ref, msg_ref):
    video, width = qo_ref.shape
    lane = lax.broadcasted_iota(jnp.int32, (2 * video, HEAD_DIM), 1)
    packed = den_ref[...]
    for head in range(width // HEAD_DIM):
        cells = slice(head * HEAD_DIM, (head + 1) * HEAD_DIM)
        queries = jnp.concatenate([qo_ref[:, cells], qp_ref[:, cells]], axis=0)
        weights = weigh(queries, far_ref[0, :, cells])
        num = num_ref[:, cells] + times(weights, far_ref[1, :, cells])
        own_ref[:, cells] = num[:video]
        msg_ref[:, cells] = num[video:]
        total = jnp.sum(lanes(weights), axis=1, keepdims=True)
        packed = packed + jnp.where(lane == first + head, total, 0.0)
    own_den_ref[...] = packed[:video]
    msg_ref[:, width:] = packed[video:]


def merge_kernel(first, own_ref, den_ref, msg_ref, att_ref):
    width = att_ref.shape[1]
    for head in range(width // HEAD_DIM):
        columns = slice(head * HEAD_DIM, (head + 1) * HEAD_DIM)
        lane = first + head
        num = own_ref[:, columns] + msg_ref[:, columns]
        den = den_ref[:, lane : lane + 1] + msg_ref[:, width + lane : width + lane + 1]
        att_ref[:, columns] = (num / den).astype(BF16)


def part_kernel(place_ref, weight_ref, first_ref, second_ref, out_ref, w_other_ref, w_ref, sems):
    depth = w_ref.shape[0]
    half = first_ref.shape[1]
    copies = []
    for index, (group, target) in enumerate(
        ((place_ref[0], w_ref), (1 - place_ref[0], w_other_ref))
    ):
        rows = pl.ds(pl.multiple_of(group * depth, depth), depth)
        copies.append(pltpu.make_async_copy(weight_ref.at[rows], target, sems.at[index]))
        copies[-1].start()
    copies[0].wait()
    out_ref[...] = jnp.dot(
        first_ref[...], w_ref[:half, :], preferred_element_type=F32
    ) + jnp.dot(second_ref[...], w_ref[half:, :], preferred_element_type=F32)
    copies[1].wait()


def more_kernel(part_ref, att_ref, w_ref, out_ref):
    half = att_ref.shape[1]
    out_ref[...] = part_ref[...] + jnp.dot(
        att_ref[...], w_ref[:half, :], preferred_element_type=F32
    )


def final_kernel(part_ref, att_ref, w_ref, hidden_ref, gate_ref, out_ref):
    half = att_ref.shape[1]
    total = part_ref[...] + jnp.dot(att_ref[...], w_ref[half:, :], preferred_element_type=F32)
    gate = gate_ref[...].reshape(1, total.shape[1])
    out_ref[...] = (hidden_ref[...].astype(F32) + gate * total).astype(BF16)


def params(megabytes):
    return pltpu.CompilerParams(vmem_limit_bytes=megabytes * 1024 * 1024)


def in_hbm(array):
    return pltpu.with_memory_space_constraint(array, pltpu.HBM)


def cost(flops, nbytes, transcendentals=0):
    return pl.CostEstimate(
        flops=int(flops), bytes_accessed=int(nbytes), transcendentals=int(transcendentals)
    )


def plain_call(kernel, outs, name, estimate, *operands):
    return pl.pallas_call(
        kernel,
        in_specs=[pl.BlockSpec(memory_space=pltpu.VMEM)] * len(operands),
        out_specs=[pl.BlockSpec(memory_space=pltpu.VMEM)] * len(outs),
        out_shape=[jax.ShapeDtypeStruct(shape, dtype) for shape, dtype in outs],
        compiler_params=params(24),
        cost_estimate=estimate,
        name=name,
    )(*operands)


def ring_moves(sections):
    chips = sections // 2
    order = list(range(0, chips, 2)) + list(range(chips - 1, 0, -2))
    moves = [], []
    for here, there in zip(order, order[1:] + order[:1]):
        for core in range(2):
            moves[core].append((2 * here + core, 2 * there + core))
            moves[1 - core].append((2 * there + core, 2 * here + core))
    return sorted(moves[0]), sorted(moves[1])


def per_device(
    sections, hidden, text_hidden, text_mask, stale_cache, qkv_weight, out_weight, query_gain,
    key_gain, norm_shift, norm_scale, branch_gate,
):
    video, features = hidden.shape
    text = text_hidden.shape[0] // 2
    width = stale_cache.shape[2]
    heads = width // HEAD_DIM
    group_columns = heads * TRIPLE
    chips = sections // 2
    out_features = out_weight.shape[1]
    top = video + EXTRA
    rows = top + text

    group = lax.axis_index("head")
    core = lax.axis_index("section") % 2
    place = jnp.stack([group, core]).astype(jnp.int32)
    swap_core = [(s, s ^ 1) for s in range(sections)]
    swap_head = [(0, 1), (1, 0)]
    ways = ring_moves(sections)
    half_way = chips // 2

    def ring_step(blocks):
        return [lax.ppermute(block, "section", way) for block, way in zip(blocks, ways)]

    vmem = pl.BlockSpec(memory_space=pltpu.VMEM)
    hbm = pl.BlockSpec(memory_space=pltpu.HBM)
    smem = pl.BlockSpec(memory_space=pltpu.SMEM)
    whole = ring_step((stale_cache, stale_cache))

    columns = 2 * TRIPLE
    blocks = group_columns // columns
    per_head = head_rows(video, text)

    def project_cost(share):
        share = 8 * rows * features * group_columns * share
        return cost(share, share // (4 * rows))

    a_rows, message, stats, ahead = pl.pallas_call(
        send_kernel,
        in_specs=[smem] + [hbm] * 5,
        out_specs=[vmem] * 4,
        out_shape=[
            jax.ShapeDtypeStruct((rows, features), BF16),
            jax.ShapeDtypeStruct((per_head + 2 * EXTRA, HEAD_DIM), BF16),
            jax.ShapeDtypeStruct((rows, HEAD_DIM), F32),
            jax.ShapeDtypeStruct((features, columns), BF16),
        ],
        scratch_shapes=[
            pltpu.VMEM((video, features), BF16),
            pltpu.VMEM((text, features), BF16),
            pltpu.VMEM((features,), F32),
            pltpu.VMEM((features,), F32),
            pltpu.VMEM((features, TRIPLE), BF16),
            pltpu.SemaphoreType.DMA((6,)),
        ],
        compiler_params=params(40),
        cost_estimate=project_cost(0.4),
        name="project_send",
    )(place, *map(in_hbm, (hidden, text_hidden, norm_scale, norm_shift, qkv_weight)))
    received = lax.ppermute(message, "head", swap_head)

    message_more, own_ahead = pl.pallas_call(
        functools.partial(send_more_kernel, video),
        in_specs=[smem, vmem, vmem, hbm],
        out_specs=[vmem] * 2,
        out_shape=[
            jax.ShapeDtypeStruct(((heads - 1) * per_head, HEAD_DIM), BF16),
            jax.ShapeDtypeStruct((features, columns), BF16),
        ],
        scratch_shapes=[
            pltpu.VMEM((features, group_columns - columns - 2 * TRIPLE), BF16),
            pltpu.VMEM((features, TRIPLE), BF16),
            pltpu.SemaphoreType.DMA((3,)),
        ],
        compiler_params=params(40),
        cost_estimate=project_cost(0.6),
        name="project_send_more",
    )(place, a_rows, ahead, in_hbm(qkv_weight))
    received_more = lax.ppermute(message_more, "head", swap_head)

    split = plain_call(
        split_kernel, [((2, video, width // 2), BF16)] * 4, "split_heads", cost(0, 8 * video * width),
        *lax.optimization_barrier((*whole, message_more, received))[:2],
    )
    chains = [[ring_step((split[0], split[2]))], [ring_step((split[1], split[3]))]]

    small = (query_gain, key_gain, text_mask, branch_gate, hidden, stale_cache)
    outs = pl.pallas_call(
        own_kernel,
        in_specs=[smem, vmem, vmem, hbm] + [hbm] * len(small),
        out_specs=[vmem] * (2 + len(small)),
        out_shape=[
            jax.ShapeDtypeStruct((top, group_columns), F32),
            jax.ShapeDtypeStruct((text, 2 * width), F32),
        ]
        + [jax.ShapeDtypeStruct(array.shape, array.dtype) for array in small],
        scratch_shapes=[
            pltpu.VMEM((blocks - 1, features, columns), BF16),
            pltpu.SemaphoreType.DMA((blocks - 1 + len(small),)),
        ],
        compiler_params=params(40),
        cost_estimate=project_cost(1),
        name="project_own",
    )(place, a_rows, own_ahead, *map(in_hbm, (qkv_weight,) + small))
    own, own_text = outs[:2]
    query_gain, key_gain, text_mask, branch_gate, hidden, stale = outs[2:]

    for _ in range(half_way - 3):
        for chain in chains:
            chain.append(ring_step(lax.optimization_barrier((*chain[-1], own))[:2]))
    far = [lax.ppermute(chains[0][-1][0], "section", ways[0])]

    received_more = lax.optimization_barrier((received_more, *chains[0][0], *chains[1][0]))[0]
    *queries, fresh = plain_call(
        functools.partial(norm_kernel, features * 2, text),
        [((video, width // 2), BF16)] * 2 + [((2, video, width), BF16)],
        "norm_video",
        cost(1000 * top * group_columns, 8 * top * group_columns),
        own, received, received_more, stats, query_gain, key_gain,
    )
    other_queries = [lax.ppermute(half, "section", swap_core) for half in queries]
    (text_kv,) = plain_call(
        functools.partial(text_kernel, features * 2),
        [((2, text, width), BF16)],
        "norm_text",
        cost(text * group_columns, text * group_columns),
        own_text, received, received_more, stats, own, key_gain,
    )

    last = lax.optimization_barrier((chains[1][-1][0], text_kv, queries[0]))[0]
    far.append(lax.ppermute(last, "section", ways[0]))
    context = chips * video + video + text
    finished = [
        jax.ShapeDtypeStruct((video, width // 2), F32),
        jax.ShapeDtypeStruct((video, HEAD_DIM), F32),
        jax.ShapeDtypeStruct((video, width // 2 + HEAD_DIM), F32),
    ]
    attended, other_attended = [], []
    for index, chain in enumerate(chains):
        first = index * heads // 2
        halves = [block for step in chain for block in step]
        finish = index == 1
        own_queries = queries[index]
        if finish:
            halves.append(far[index])
            own_queries = lax.optimization_barrier((own_queries, num_own))[0]
            outs = finished + [jax.ShapeDtypeStruct(fresh.shape, BF16)]
        else:
            outs = [
                jax.ShapeDtypeStruct((2 * video, width // 2), F32),
                jax.ShapeDtypeStruct((2 * video, HEAD_DIM), F32),
            ]
        outs = pl.pallas_call(
            functools.partial(attend_kernel, first, len(whole)),
            in_specs=[smem] + [vmem] * (6 + len(whole) + len(halves)),
            out_specs=[vmem] * (len(outs) - finish) + [hbm] * finish,
            out_shape=outs,
            scratch_shapes=[pltpu.SemaphoreType.DMA] * finish,
            compiler_params=params(24),
            cost_estimate=cost(video * context, context * width, video * heads),
            name="attend",
        )(
            place, own_queries, other_queries[index], fresh, stale, text_kv, text_mask,
            *whole, *halves,
        )
        if finish:
            *outs, new_cache = outs
        else:
            outs = plain_call(
                functools.partial(last_kernel, first),
                [(out.shape, out.dtype) for out in finished],
                "attend_last",
                cost(video * video, video * width),
                own_queries, other_queries[index], *outs, far[index],
            )
        num_own, den_own, num_message = outs
        num_received = lax.ppermute(num_message, "section", swap_core)
        attended += plain_call(
            functools.partial(merge_kernel, first),
            [((video, width // 2), BF16)],
            "merge",
            cost(2 * video * width, 5 * video * width),
            num_own, den_own, num_received,
        )
        other_attended.append(lax.ppermute(attended[-1], "head", swap_head))

    out_cost = cost(4 * video * width * out_features, 2 * width * out_features)
    part, w_other = pl.pallas_call(
        part_kernel,
        in_specs=[smem, hbm, vmem, vmem],
        out_specs=[vmem] * 2,
        out_shape=[
            jax.ShapeDtypeStruct((video, out_features), F32),
            jax.ShapeDtypeStruct((width, out_features), BF16),
        ],
        scratch_shapes=[
            pltpu.VMEM((width, out_features), BF16),
            pltpu.SemaphoreType.DMA((2,)),
        ],
        compiler_params=params(24),
        cost_estimate=out_cost,
        name="part_out",
    )(place, in_hbm(out_weight), *attended)
    (part,) = plain_call(
        more_kernel, [((video, out_features), F32)], "more_out", out_cost,
        part, other_attended[0], w_other,
    )
    (mixed,) = plain_call(
        final_kernel, [((video, out_features), BF16)], "final_out", out_cost,
        part, other_attended[1], w_other, hidden, branch_gate,
    )
    return (mixed, new_cache)


def solution(mesh):
    in_specs = (
        P("section", "head"),
        P(None, "head"),
        P(),
        P(None, "section", "head"),
        P("head", None),
        P(None, "head"),
        P(),
        P(),
        P("head"),
        P("head"),
        P("head"),
    )
    out_specs = (P("section", "head"), P(None, "section", "head"))
    return jax.shard_map(
        functools.partial(per_device, mesh.shape["section"]),
        mesh=mesh, in_specs=in_specs, out_specs=out_specs, check_vma=False,
    )
```

```python
import functools
import math

import jax
import jax.numpy as jnp
from jax import lax
from jax.experimental import pallas as pl
from jax.experimental.pallas import tpu as pltpu
from jax.sharding import PartitionSpec as P

HEAD_DIM = 128
TRIPLE = 3 * HEAD_DIM
EXTRA = 16
PIECE = 2 * HEAD_DIM
EPS = 1e-06
F32 = jnp.float32
BF16 = jnp.bfloat16


def split_bf16(value, parts):
    pieces = []
    rest = value
    for _ in range(parts):
        piece = rest.astype(BF16)
        pieces.append(piece)
        rest = rest - piece.astype(F32)
    return pieces


def head_rows(video, text):
    return 3 * video + 2 * text + EXTRA


def column_copy(w_ref, first, target, sem):
    columns = target.shape[1]
    start = pl.multiple_of(first, HEAD_DIM)
    return pltpu.make_async_copy(w_ref.at[:, pl.ds(start, columns)], target, sem)


def partial_sums(a_ref, w_ref, video, text, msg_ref, first):
    band = lax.broadcasted_iota(jnp.int32, (EXTRA, HEAD_DIM), 0) // 4
    top = video + EXTRA
    terms = None
    for start in range(0, w_ref.shape[1], PIECE):
        stop = min(start + PIECE, w_ref.shape[1])
        product = jnp.dot(a_ref[...], w_ref[:, start:stop], preferred_element_type=F32)
        for local in range(0, stop - start, HEAD_DIM):
            part = product[:, local : local + HEAD_DIM]
            head, kind = divmod((start + local) // HEAD_DIM, 3)
            base = (first + head) * head_rows(video, text)
            msg_ref[base + kind * video : base + (kind + 1) * video, :] = part[:video].astype(BF16)
            terms = part[video:top] if kind == 0 else jnp.where(band == kind, part[video:top], terms)
            base += 3 * video
            if kind:
                rows = slice(base + (kind - 1) * text, base + kind * text)
                msg_ref[rows, :] = part[top:].astype(BF16)
            if kind == 2:
                base += 2 * text
                msg_ref[base : base + EXTRA, :] = terms.astype(BF16)


def send_kernel(
    place_ref, x_ref, t_ref, scale_ref, shift_ref, w_ref,
    a_ref, msg_ref, stat_ref, ahead_ref,
    x_buffer, t_buffer, scale_buffer, shift_buffer, w_buffer, sems,
):
    video, features = x_buffer.shape
    text = t_buffer.shape[0]
    top = video + EXTRA
    columns = w_buffer.shape[1]
    base = (1 - place_ref[0]) * (w_ref.shape[1] // 2)
    copies = [
        pltpu.make_async_copy(scale_ref, scale_buffer, sems.at[0]),
        pltpu.make_async_copy(shift_ref, shift_buffer, sems.at[1]),
        pltpu.make_async_copy(x_ref, x_buffer, sems.at[2]),
        pltpu.make_async_copy(
            t_ref.at[pl.ds(pl.multiple_of(place_ref[1] * text, text), text)], t_buffer, sems.at[3]
        ),
        column_copy(w_ref, base, w_buffer, sems.at[4]),
        column_copy(w_ref, base + columns, ahead_ref, sems.at[5]),
    ]
    for copy in copies[:5]:
        copy.start()

    copies[0].wait()
    copies[1].wait()
    gain = 1.0 + scale_buffer[...].reshape(1, features)
    pieces = split_bf16(gain, 2) + split_bf16(shift_buffer[...].reshape(1, features), 2)
    row = lax.broadcasted_iota(jnp.int32, (EXTRA, features), 0)
    extra = jnp.zeros((EXTRA, features), F32)
    for index, piece in enumerate(pieces):
        extra = jnp.where(row % 4 == index, piece.astype(F32), extra)
    a_ref[video:top, :] = extra.astype(BF16)

    def prepare(rows_ref, start):
        rows = rows_ref[...].astype(F32)
        count = rows.shape[0]
        mean = jnp.sum(rows, axis=1, keepdims=True) * (1.0 / features)
        centered = rows - mean
        second = jnp.sum(centered * centered, axis=1, keepdims=True)
        a_ref[start : start + count, :] = (centered * gain).astype(BF16)
        lane = lax.broadcasted_iota(jnp.int32, (count, HEAD_DIM), 1)
        packed = jnp.zeros((count, HEAD_DIM), F32)
        for index, piece in enumerate(split_bf16(mean, 3) + split_bf16(second, 3)):
            packed = jnp.where(lane == index, piece.astype(F32), packed)
        stat_ref[start : start + count, :] = jnp.where(
            lane == 0, mean, jnp.where(lane == 1, second, 0.0)
        )
        return jnp.transpose(packed)[:EXTRA]

    copies[2].wait()
    copies[5].start()
    stats = [prepare(x_buffer, 0)]
    copies[3].wait()
    stats.append(prepare(t_buffer, top))
    stat_ref[video:top, :] = jnp.zeros((EXTRA, HEAD_DIM), F32)
    start = head_rows(video, text) * columns // TRIPLE
    msg_ref[start : start + 2 * EXTRA, :] = jnp.concatenate(stats, axis=0).astype(BF16)
    copies[4].wait()
    partial_sums(a_ref, w_buffer, video, text, msg_ref, 0)
    copies[5].wait()


def send_more_kernel(
    video, place_ref, a_ref, ahead_ref, w_ref, msg_ref, w_buffer, last_buffer, sems,
):
    text = a_ref.shape[0] - video - EXTRA
    width = w_ref.shape[1] // 2
    other = (1 - place_ref[0]) * width
    first = width - last_buffer.shape[1]
    copies = [
        column_copy(w_ref, other + first - w_buffer.shape[1], w_buffer, sems.at[0]),
        column_copy(w_ref, other + first, last_buffer, sems.at[1]),
    ]
    copies[0].start()
    copies[1].start()
    partial_sums(a_ref, ahead_ref, video, text, msg_ref, 0)
    copies[0].wait()
    head = ahead_ref.shape[1] // TRIPLE
    partial_sums(a_ref, w_buffer, video, text, msg_ref, head)
    copies[1].wait()
    head += w_buffer.shape[1] // TRIPLE
    partial_sums(a_ref, last_buffer, video, text, msg_ref, head)


def own_kernel(place_ref, a_ref, w_ref, *refs):
    small = (len(refs) - 4) // 2
    out_ref, text_ref = refs[small : small + 2]
    w_buffer, sems = refs[-2:]
    top = out_ref.shape[0]
    blocks, _, columns = w_buffer.shape
    base = place_ref[0] * (w_ref.shape[1] // 2)
    copies = [
        column_copy(w_ref, base + index * columns, w_buffer.at[index], sems.at[index])
        for index in range(blocks)
    ]
    for source, target in zip(refs[:small], refs[small + 2 : -2]):
        copies.append(pltpu.make_async_copy(source, target, sems.at[len(copies)]))
    for copy in copies[:2]:
        copy.start()

    for block in range(blocks):
        copies[block].wait()
        for copy in copies[2:3] if block == 0 else copies[3:] if block == 1 else ():
            copy.start()
        for start in range(0, columns, PIECE):
            part = w_buffer[block, :, start : start + PIECE]
            product = jnp.dot(a_ref[...], part, preferred_element_type=F32)
            first = block * columns + start
            out_ref[:, first : first + PIECE] = product[:top]
            for local in range(0, PIECE, HEAD_DIM):
                head, kind = divmod((first + local) // HEAD_DIM, 3)
                if kind:
                    target = (2 * head + kind - 1) * HEAD_DIM
                    text_ref[:, target : target + HEAD_DIM] = product[
                        top:, local : local + HEAD_DIM
                    ]
    for copy in copies[blocks:]:
        copy.wait()


def row_stats(total_features, own, received):
    count = own.shape[0]
    received = received.astype(F32)
    padding = jnp.zeros((HEAD_DIM - received.shape[0], count), F32)
    received = jnp.transpose(jnp.concatenate([received, padding], axis=0))
    parts = [received[:, index : index + 1] for index in range(6)]
    gap = 0.5 * (own[:, 0:1] - (parts[0] + parts[1] + parts[2]))
    second = own[:, 1:2] + (parts[3] + parts[4] + parts[5])
    var = second * (1.0 / total_features) + gap * gap
    return gap, lax.rsqrt(var + EPS)


def column_terms(own_ref, msg_ref, video, base, part):
    other = msg_ref[base : base + EXTRA, :].astype(F32)
    other = other[4 * (part % 3) : 4 * (part % 3) + 4]
    own = own_ref[video : video + 8, part * HEAD_DIM : (part + 1) * HEAD_DIM]
    scale = (own[0:1] + own[1:2]) - (other[0:1] + other[1:2])
    shift = (own[2:3] + own[3:4]) + (other[2:3] + other[3:4])
    return scale, shift


def head_place(head, rows, first_ref, more_ref):
    early = first_ref.shape[0] // rows
    return (first_ref, head * rows) if head < early else (more_ref, (head - early) * rows)


def head_norm(part, gain):
    square = jnp.sum(part * part, axis=1, keepdims=True) * (1.0 / HEAD_DIM)
    return part * lax.rsqrt(square + EPS) * gain


def norm_kernel(
    total_features, text, own_ref, first_ref, more_ref, stat_ref, qg_ref, kg_ref,
    qa_ref, qb_ref, kv_ref,
):
    video = qa_ref.shape[0]
    half = qa_ref.shape[1] // HEAD_DIM
    rows = head_rows(video, text)
    query_gain = qg_ref[...].reshape(1, HEAD_DIM)
    key_gain = kg_ref[...].reshape(1, HEAD_DIM)
    start = first_ref.shape[0] - 2 * EXTRA
    gap, inverse = row_stats(
        total_features, stat_ref[:video, :], first_ref[start : start + EXTRA, :video]
    )
    for head in range(2 * half):
        msg_ref, base = head_place(head, rows, first_ref, more_ref)

        def total(kind):
            part = 3 * head + kind
            scale, shift = column_terms(own_ref, msg_ref, video, base + rows - EXTRA, part)
            other = msg_ref[base + kind * video : base + (kind + 1) * video, :].astype(F32)
            both = own_ref[:video, part * HEAD_DIM : (part + 1) * HEAD_DIM] + other
            return (both + gap * scale) * inverse + shift

        columns = slice(head * HEAD_DIM, (head + 1) * HEAD_DIM)
        cells = slice(head % half * HEAD_DIM, (head % half + 1) * HEAD_DIM)
        q_ref = qa_ref if head < half else qb_ref
        q_ref[:, cells] = head_norm(total(0), query_gain).astype(BF16)
        kv_ref[0, :, columns] = head_norm(total(1), key_gain).astype(BF16)
        kv_ref[1, :, columns] = total(2).astype(BF16)


def text_kernel(
    total_features, own_ref, first_ref, more_ref, stat_ref, top_ref, kg_ref, kv_ref
):
    text = kv_ref.shape[1]
    heads = kv_ref.shape[2] // HEAD_DIM
    video = top_ref.shape[0] - EXTRA
    rows = head_rows(video, text)
    key_gain = kg_ref[...].reshape(1, HEAD_DIM)
    start = first_ref.shape[0] - EXTRA
    gap, inverse = row_stats(
        total_features, stat_ref[video + EXTRA :, :], first_ref[start : start + EXTRA, :text]
    )
    for head in range(heads):
        msg_ref, base = head_place(head, rows, first_ref, more_ref)

        def total(kind):
            scale, shift = column_terms(
                top_ref, msg_ref, video, base + rows - EXTRA, 3 * head + 1 + kind
            )
            start = base + 3 * video + kind * text
            other = msg_ref[start : start + text, :].astype(F32)
            first = (2 * head + kind) * HEAD_DIM
            return (own_ref[:, first : first + HEAD_DIM] + other + gap * scale) * inverse + shift

        columns = slice(head * HEAD_DIM, (head + 1) * HEAD_DIM)
        kv_ref[0, :, columns] = head_norm(total(0), key_gain).astype(BF16)
        kv_ref[1, :, columns] = total(1).astype(BF16)


FACTOR = math.log2(math.e) / math.sqrt(HEAD_DIM)


def split_kernel(*refs):
    count = len(refs) // 3
    for index in range(count):
        half = refs[index].shape[2] // 2
        refs[count + 2 * index][...] = refs[index][:, :, :half]
        refs[count + 2 * index + 1][...] = refs[index][:, :, half:]


def weigh(rows, keys):
    scores = lax.dot_general(rows, keys, (((1,), (1,)), ((), ())), preferred_element_type=F32)
    return jnp.exp2(scores * FACTOR)


def lanes(weights):
    total = weights[:, :HEAD_DIM]
    for start in range(HEAD_DIM, weights.shape[1], HEAD_DIM):
        total = total + weights[:, start : start + HEAD_DIM]
    return total


def times(weights, values):
    return jnp.dot(weights.astype(BF16), values, preferred_element_type=F32)


def both(group, index):
    return jnp.concatenate([ref[index, :, part] for ref, part in group], axis=0)


def attend_kernel(
    first, count, place_ref, qo_ref, qp_ref, fresh_ref, stale_ref, text_ref, mask_ref, *refs,
):
    finish = len(refs[-1].shape) == 0
    if finish:
        *refs, own_ref, own_den_ref, msg_ref, cache_ref, sem = refs
        cache_copy = pltpu.make_async_copy(fresh_ref, cache_ref, sem)
        cache_copy.start()
    else:
        *refs, num_ref, den_ref = refs
    video, width = qo_ref.shape
    text = text_ref.shape[1]
    lane = lax.broadcasted_iota(jnp.int32, (2 * video, HEAD_DIM), 1)
    mask = mask_ref[...].reshape(1, 2 * text).astype(F32)
    mask = jnp.where(place_ref[1] == 0, mask[:, :text], mask[:, text:])
    keep = jnp.concatenate([jnp.ones((1, video), F32), mask], axis=1)
    same_patch = (
        (lax.broadcasted_iota(jnp.int32, (2 * video, 2 * video), 0) < video)
        == (lax.broadcasted_iota(jnp.int32, (2 * video, 2 * video), 1) < video)
    ).astype(F32)
    packed = jnp.zeros((2 * video, HEAD_DIM), F32)
    for head in range(width // HEAD_DIM):
        cells = slice(head * HEAD_DIM, (head + 1) * HEAD_DIM)
        columns = slice((first + head) * HEAD_DIM, (first + head + 1) * HEAD_DIM)
        queries = jnp.concatenate([qo_ref[:, cells], qp_ref[:, cells]], axis=0)
        pair = [(fresh_ref, columns), (stale_ref, columns)]
        weights = weigh(queries, both(pair, 0)) * same_patch
        num = times(weights, both(pair, 1))
        den = lanes(weights)
        blocks = [(ref, columns) for ref in refs[:count]] + [(ref, cells) for ref in refs[count:]]
        blocks.append((text_ref, columns))
        odd = len(blocks) % 2
        for start in range(odd, len(blocks), 2):
            pair = blocks[start : start + 2]
            weights = weigh(queries, both(pair, 0))
            if start + 2 == len(blocks):
                weights = weights * keep
            num = num + times(weights, both(pair, 1))
            den = den + lanes(weights)
        if odd:
            weights = weigh(queries, both(blocks[:1], 0))
            num = num + times(weights, both(blocks[:1], 1))
            den = den + weights
        if finish:
            own_ref[:, cells] = num[:video]
            msg_ref[:, cells] = num[video:]
        else:
            num_ref[:, cells] = num
        packed = jnp.where(lane == first + head, jnp.sum(den, axis=1, keepdims=True), packed)
    if finish:
        own_den_ref[...] = packed[:video]
        msg_ref[:, width:] = packed[video:]
        cache_copy.wait()
    else:
        den_ref[...] = packed


def last_kernel(first, qo_ref, qp_ref, num_ref, den_ref, far_ref, own_ref, own_den_ref, msg_ref):
    video, width = qo_ref.shape
    lane = lax.broadcasted_iota(jnp.int32, (2 * video, HEAD_DIM), 1)
    packed = den_ref[...]
    for head in range(width // HEAD_DIM):
        cells = slice(head * HEAD_DIM, (head + 1) * HEAD_DIM)
        queries = jnp.concatenate([qo_ref[:, cells], qp_ref[:, cells]], axis=0)
        weights = weigh(queries, far_ref[0, :, cells])
        num = num_ref[:, cells] + times(weights, far_ref[1, :, cells])
        own_ref[:, cells] = num[:video]
        msg_ref[:, cells] = num[video:]
        total = jnp.sum(lanes(weights), axis=1, keepdims=True)
        packed = packed + jnp.where(lane == first + head, total, 0.0)
    own_den_ref[...] = packed[:video]
    msg_ref[:, width:] = packed[video:]


def merge_kernel(first, own_ref, den_ref, msg_ref, att_ref):
    width = att_ref.shape[1]
    for head in range(width // HEAD_DIM):
        columns = slice(head * HEAD_DIM, (head + 1) * HEAD_DIM)
        lane = first + head
        num = own_ref[:, columns] + msg_ref[:, columns]
        den = den_ref[:, lane : lane + 1] + msg_ref[:, width + lane : width + lane + 1]
        att_ref[:, columns] = (num / den).astype(BF16)


def part_kernel(place_ref, weight_ref, first_ref, second_ref, out_ref, w_other_ref, w_ref, sems):
    depth = w_ref.shape[0]
    half = first_ref.shape[1]
    copies = []
    for index, (group, target) in enumerate(
        ((place_ref[0], w_ref), (1 - place_ref[0], w_other_ref))
    ):
        rows = pl.ds(pl.multiple_of(group * depth, depth), depth)
        copies.append(pltpu.make_async_copy(weight_ref.at[rows], target, sems.at[index]))
        copies[-1].start()
    copies[0].wait()
    out_ref[...] = jnp.dot(
        first_ref[...], w_ref[:half, :], preferred_element_type=F32
    ) + jnp.dot(second_ref[...], w_ref[half:, :], preferred_element_type=F32)
    copies[1].wait()


def more_kernel(part_ref, att_ref, w_ref, out_ref):
    half = att_ref.shape[1]
    out_ref[...] = part_ref[...] + jnp.dot(
        att_ref[...], w_ref[:half, :], preferred_element_type=F32
    )


def final_kernel(part_ref, att_ref, w_ref, hidden_ref, gate_ref, out_ref):
    half = att_ref.shape[1]
    total = part_ref[...] + jnp.dot(att_ref[...], w_ref[half:, :], preferred_element_type=F32)
    gate = gate_ref[...].reshape(1, total.shape[1])
    out_ref[...] = (hidden_ref[...].astype(F32) + gate * total).astype(BF16)


def params(megabytes):
    return pltpu.CompilerParams(vmem_limit_bytes=megabytes * 1024 * 1024)


def in_hbm(array):
    return pltpu.with_memory_space_constraint(array, pltpu.HBM)


def cost(flops, nbytes, transcendentals=0):
    return pl.CostEstimate(
        flops=int(flops), bytes_accessed=int(nbytes), transcendentals=int(transcendentals)
    )


def plain_call(kernel, outs, name, estimate, *operands):
    return pl.pallas_call(
        kernel,
        in_specs=[pl.BlockSpec(memory_space=pltpu.VMEM)] * len(operands),
        out_specs=[pl.BlockSpec(memory_space=pltpu.VMEM)] * len(outs),
        out_shape=[jax.ShapeDtypeStruct(shape, dtype) for shape, dtype in outs],
        compiler_params=params(24),
        cost_estimate=estimate,
        name=name,
    )(*operands)


def ring_moves(sections):
    chips = sections // 2
    order = list(range(0, chips, 2)) + list(range(chips - 1, 0, -2))
    moves = [], []
    for here, there in zip(order, order[1:] + order[:1]):
        for core in range(2):
            moves[core].append((2 * here + core, 2 * there + core))
            moves[1 - core].append((2 * there + core, 2 * here + core))
    return sorted(moves[0]), sorted(moves[1])


def per_device(
    sections, hidden, text_hidden, text_mask, stale_cache, qkv_weight, out_weight, query_gain,
    key_gain, norm_shift, norm_scale, branch_gate,
):
    video, features = hidden.shape
    text = text_hidden.shape[0] // 2
    width = stale_cache.shape[2]
    heads = width // HEAD_DIM
    group_columns = heads * TRIPLE
    chips = sections // 2
    out_features = out_weight.shape[1]
    top = video + EXTRA
    rows = top + text

    group = lax.axis_index("head")
    core = lax.axis_index("section") % 2
    place = jnp.stack([group, core]).astype(jnp.int32)
    swap_core = [(s, s ^ 1) for s in range(sections)]
    swap_head = [(0, 1), (1, 0)]
    ways = ring_moves(sections)
    half_way = chips // 2

    def ring_step(blocks):
        return [lax.ppermute(block, "section", way) for block, way in zip(blocks, ways)]

    vmem = pl.BlockSpec(memory_space=pltpu.VMEM)
    hbm = pl.BlockSpec(memory_space=pltpu.HBM)
    smem = pl.BlockSpec(memory_space=pltpu.SMEM)
    whole = ring_step((stale_cache, stale_cache))

    columns = 2 * TRIPLE
    blocks = group_columns // columns
    per_head = head_rows(video, text)

    def project_cost(share):
        share = 8 * rows * features * group_columns * share
        return cost(share, share // (4 * rows))

    a_rows, message, stats, ahead = pl.pallas_call(
        send_kernel,
        in_specs=[smem] + [hbm] * 5,
        out_specs=[vmem] * 4,
        out_shape=[
            jax.ShapeDtypeStruct((rows, features), BF16),
            jax.ShapeDtypeStruct((per_head + 2 * EXTRA, HEAD_DIM), BF16),
            jax.ShapeDtypeStruct((rows, HEAD_DIM), F32),
            jax.ShapeDtypeStruct((features, columns), BF16),
        ],
        scratch_shapes=[
            pltpu.VMEM((video, features), BF16),
            pltpu.VMEM((text, features), BF16),
            pltpu.VMEM((features,), F32),
            pltpu.VMEM((features,), F32),
            pltpu.VMEM((features, TRIPLE), BF16),
            pltpu.SemaphoreType.DMA((6,)),
        ],
        compiler_params=params(40),
        cost_estimate=project_cost(0.4),
        name="project_send",
    )(place, *map(in_hbm, (hidden, text_hidden, norm_scale, norm_shift, qkv_weight)))
    received = lax.ppermute(message, "head", swap_head)

    message_more = pl.pallas_call(
        functools.partial(send_more_kernel, video),
        in_specs=[smem, vmem, vmem, hbm],
        out_specs=vmem,
        out_shape=jax.ShapeDtypeStruct(((heads - 1) * per_head, HEAD_DIM), BF16),
        scratch_shapes=[
            pltpu.VMEM((features, group_columns - columns - 2 * TRIPLE), BF16),
            pltpu.VMEM((features, TRIPLE), BF16),
            pltpu.SemaphoreType.DMA((2,)),
        ],
        compiler_params=params(40),
        cost_estimate=project_cost(0.6),
        name="project_send_more",
    )(place, a_rows, ahead, in_hbm(qkv_weight))
    received_more = lax.ppermute(message_more, "head", swap_head)

    split = plain_call(
        split_kernel, [((2, video, width // 2), BF16)] * 4, "split_heads", cost(0, 8 * video * width),
        *lax.optimization_barrier((*whole, message_more, received))[:2],
    )
    chains = [[ring_step((split[0], split[2]))], [ring_step((split[1], split[3]))]]

    small = (query_gain, key_gain, text_mask, branch_gate, hidden, stale_cache)
    outs = pl.pallas_call(
        own_kernel,
        in_specs=[smem, vmem, hbm] + [hbm] * len(small),
        out_specs=[vmem] * (2 + len(small)),
        out_shape=[
            jax.ShapeDtypeStruct((top, group_columns), F32),
            jax.ShapeDtypeStruct((text, 2 * width), F32),
        ]
        + [jax.ShapeDtypeStruct(array.shape, array.dtype) for array in small],
        scratch_shapes=[
            pltpu.VMEM((blocks, features, columns), BF16),
            pltpu.SemaphoreType.DMA((blocks + len(small),)),
        ],
        compiler_params=params(40),
        cost_estimate=project_cost(1),
        name="project_own",
    )(place, a_rows, *map(in_hbm, (qkv_weight,) + small))
    own, own_text = outs[:2]
    query_gain, key_gain, text_mask, branch_gate, hidden, stale = outs[2:]

    for _ in range(half_way - 3):
        for chain in chains:
            chain.append(ring_step(lax.optimization_barrier((*chain[-1], own))[:2]))
    far = [lax.ppermute(chains[0][-1][0], "section", ways[0])]

    received_more = lax.optimization_barrier((received_more, *chains[0][0], *chains[1][0]))[0]
    *queries, fresh = plain_call(
        functools.partial(norm_kernel, features * 2, text),
        [((video, width // 2), BF16)] * 2 + [((2, video, width), BF16)],
        "norm_video",
        cost(1000 * top * group_columns, 8 * top * group_columns),
        own, received, received_more, stats, query_gain, key_gain,
    )
    other_queries = [lax.ppermute(half, "section", swap_core) for half in queries]
    (text_kv,) = plain_call(
        functools.partial(text_kernel, features * 2),
        [((2, text, width), BF16)],
        "norm_text",
        cost(text * group_columns, text * group_columns),
        lax.optimization_barrier((own_text, queries[0]))[0], received, received_more, stats, own,
        key_gain,
    )

    last = lax.optimization_barrier((chains[1][-1][0], text_kv, queries[0]))[0]
    far.append(lax.ppermute(last, "section", ways[0]))
    context = chips * video + video + text
    finished = [
        jax.ShapeDtypeStruct((video, width // 2), F32),
        jax.ShapeDtypeStruct((video, HEAD_DIM), F32),
        jax.ShapeDtypeStruct((video, width // 2 + HEAD_DIM), F32),
    ]
    attended, other_attended = [], []
    for index, chain in enumerate(chains):
        first = index * heads // 2
        halves = [block for step in chain for block in step]
        finish = index == 1
        own_queries = queries[index]
        if finish:
            halves.append(far[index])
            own_queries = lax.optimization_barrier((own_queries, num_own))[0]
            outs = finished + [jax.ShapeDtypeStruct(fresh.shape, BF16)]
        else:
            outs = [
                jax.ShapeDtypeStruct((2 * video, width // 2), F32),
                jax.ShapeDtypeStruct((2 * video, HEAD_DIM), F32),
            ]
        outs = pl.pallas_call(
            functools.partial(attend_kernel, first, len(whole)),
            in_specs=[smem] + [vmem] * (6 + len(whole) + len(halves)),
            out_specs=[vmem] * (len(outs) - finish) + [hbm] * finish,
            out_shape=outs,
            scratch_shapes=[pltpu.SemaphoreType.DMA] * finish,
            compiler_params=params(24),
            cost_estimate=cost(video * context, context * width, video * heads),
            name="attend",
        )(
            place, own_queries, other_queries[index], fresh, stale, text_kv, text_mask,
            *whole, *halves,
        )
        if finish:
            *outs, new_cache = outs
        else:
            outs = plain_call(
                functools.partial(last_kernel, first),
                [(out.shape, out.dtype) for out in finished],
                "attend_last",
                cost(video * video, video * width),
                own_queries, other_queries[index], *outs, far[index],
            )
        num_own, den_own, num_message = outs
        num_received = lax.ppermute(num_message, "section", swap_core)
        attended += plain_call(
            functools.partial(merge_kernel, first),
            [((video, width // 2), BF16)],
            "merge",
            cost(2 * video * width, 5 * video * width),
            num_own, den_own, num_received,
        )
        other_attended.append(lax.ppermute(attended[-1], "head", swap_head))

    out_cost = cost(4 * video * width * out_features, 2 * width * out_features)
    part, w_other = pl.pallas_call(
        part_kernel,
        in_specs=[smem, hbm, vmem, vmem],
        out_specs=[vmem] * 2,
        out_shape=[
            jax.ShapeDtypeStruct((video, out_features), F32),
            jax.ShapeDtypeStruct((width, out_features), BF16),
        ],
        scratch_shapes=[
            pltpu.VMEM((width, out_features), BF16),
            pltpu.SemaphoreType.DMA((2,)),
        ],
        compiler_params=params(24),
        cost_estimate=out_cost,
        name="part_out",
    )(place, in_hbm(out_weight), *attended)
    (part,) = plain_call(
        more_kernel, [((video, out_features), F32)], "more_out", out_cost,
        part, other_attended[0], w_other,
    )
    (mixed,) = plain_call(
        final_kernel, [((video, out_features), BF16)], "final_out", out_cost,
        part, other_attended[1], w_other, hidden, branch_gate,
    )
    return (mixed, new_cache)


def solution(mesh):
    in_specs = (
        P("section", "head"),
        P(None, "head"),
        P(),
        P(None, "section", "head"),
        P("head", None),
        P(None, "head"),
        P(),
        P(),
        P("head"),
        P("head"),
        P("head"),
    )
    out_specs = (P("section", "head"), P(None, "section", "head"))
    return jax.shard_map(
        functools.partial(per_device, mesh.shape["section"]),
        mesh=mesh, in_specs=in_specs, out_specs=out_specs, check_vma=False,
    )
```

```python
import functools
import math

import jax
import jax.numpy as jnp
from jax import lax
from jax.experimental import pallas as pl
from jax.experimental.pallas import tpu as pltpu
from jax.sharding import PartitionSpec as P

HEAD_DIM = 128
TRIPLE = 3 * HEAD_DIM
EXTRA = 16
PIECE = 2 * HEAD_DIM
EPS = 1e-06
F32 = jnp.float32
BF16 = jnp.bfloat16


def split_bf16(value, parts):
    pieces = []
    rest = value
    for _ in range(parts):
        piece = rest.astype(BF16)
        pieces.append(piece)
        rest = rest - piece.astype(F32)
    return pieces


def head_rows(video, text):
    return 3 * video + 2 * text + EXTRA


def column_copy(w_ref, first, target, sem):
    columns = target.shape[1]
    start = pl.multiple_of(first, HEAD_DIM)
    return pltpu.make_async_copy(w_ref.at[:, pl.ds(start, columns)], target, sem)


def partial_sums(a_ref, w_ref, video, text, msg_ref, first):
    band = lax.broadcasted_iota(jnp.int32, (EXTRA, HEAD_DIM), 0) // 4
    top = video + EXTRA
    terms = None
    for start in range(0, w_ref.shape[1], PIECE):
        stop = min(start + PIECE, w_ref.shape[1])
        product = jnp.dot(a_ref[...], w_ref[:, start:stop], preferred_element_type=F32)
        for local in range(0, stop - start, HEAD_DIM):
            part = product[:, local : local + HEAD_DIM]
            head, kind = divmod((start + local) // HEAD_DIM, 3)
            base = (first + head) * head_rows(video, text)
            msg_ref[base + kind * video : base + (kind + 1) * video, :] = part[:video].astype(BF16)
            terms = part[video:top] if kind == 0 else jnp.where(band == kind, part[video:top], terms)
            base += 3 * video
            if kind:
                rows = slice(base + (kind - 1) * text, base + kind * text)
                msg_ref[rows, :] = part[top:].astype(BF16)
            if kind == 2:
                base += 2 * text
                msg_ref[base : base + EXTRA, :] = terms.astype(BF16)


def send_kernel(
    place_ref, x_ref, t_ref, scale_ref, shift_ref, w_ref,
    a_ref, msg_ref, stat_ref, ahead_ref,
    x_buffer, t_buffer, scale_buffer, shift_buffer, w_buffer, sems,
):
    video, features = x_buffer.shape
    text = t_buffer.shape[0]
    top = video + EXTRA
    columns = w_buffer.shape[1]
    base = (1 - place_ref[0]) * (w_ref.shape[1] // 2)
    copies = [
        pltpu.make_async_copy(scale_ref, scale_buffer, sems.at[0]),
        pltpu.make_async_copy(shift_ref, shift_buffer, sems.at[1]),
        pltpu.make_async_copy(x_ref, x_buffer, sems.at[2]),
        pltpu.make_async_copy(
            t_ref.at[pl.ds(pl.multiple_of(place_ref[1] * text, text), text)], t_buffer, sems.at[3]
        ),
        column_copy(w_ref, base, w_buffer, sems.at[4]),
        column_copy(w_ref, base + columns, ahead_ref, sems.at[5]),
    ]
    for copy in copies[:5]:
        copy.start()

    copies[0].wait()
    copies[1].wait()
    gain = 1.0 + scale_buffer[...].reshape(1, features)
    pieces = split_bf16(gain, 2) + split_bf16(shift_buffer[...].reshape(1, features), 2)
    row = lax.broadcasted_iota(jnp.int32, (EXTRA, features), 0)
    extra = jnp.zeros((EXTRA, features), F32)
    for index, piece in enumerate(pieces):
        extra = jnp.where(row % 4 == index, piece.astype(F32), extra)
    a_ref[video:top, :] = extra.astype(BF16)

    def prepare(rows_ref, start):
        rows = rows_ref[...].astype(F32)
        count = rows.shape[0]
        mean = jnp.sum(rows, axis=1, keepdims=True) * (1.0 / features)
        centered = rows - mean
        second = jnp.sum(centered * centered, axis=1, keepdims=True)
        a_ref[start : start + count, :] = (centered * gain).astype(BF16)
        lane = lax.broadcasted_iota(jnp.int32, (count, HEAD_DIM), 1)
        packed = jnp.zeros((count, HEAD_DIM), F32)
        for index, piece in enumerate(split_bf16(mean, 3) + split_bf16(second, 3)):
            packed = jnp.where(lane == index, piece.astype(F32), packed)
        stat_ref[start : start + count, :] = jnp.where(
            lane == 0, mean, jnp.where(lane == 1, second, 0.0)
        )
        return jnp.transpose(packed)[:EXTRA]

    copies[2].wait()
    copies[5].start()
    stats = [prepare(x_buffer, 0)]
    copies[3].wait()
    stats.append(prepare(t_buffer, top))
    stat_ref[video:top, :] = jnp.zeros((EXTRA, HEAD_DIM), F32)
    start = head_rows(video, text) * columns // TRIPLE
    msg_ref[start : start + 2 * EXTRA, :] = jnp.concatenate(stats, axis=0).astype(BF16)
    copies[4].wait()
    partial_sums(a_ref, w_buffer, video, text, msg_ref, 0)
    copies[5].wait()


def send_more_kernel(
    video, place_ref, a_ref, ahead_ref, w_ref, msg_ref, own_ahead_ref, w_buffer, last_buffer, sems,
):
    text = a_ref.shape[0] - video - EXTRA
    width = w_ref.shape[1] // 2
    other, own = (1 - place_ref[0]) * width, place_ref[0] * width
    first = width - last_buffer.shape[1]
    copies = [
        column_copy(w_ref, other + first - w_buffer.shape[1], w_buffer, sems.at[0]),
        column_copy(w_ref, other + first, last_buffer, sems.at[1]),
        column_copy(w_ref, own, own_ahead_ref, sems.at[2]),
    ]
    copies[0].start()
    copies[1].start()
    partial_sums(a_ref, ahead_ref, video, text, msg_ref, 0)
    copies[0].wait()
    copies[2].start()
    head = ahead_ref.shape[1] // TRIPLE
    partial_sums(a_ref, w_buffer, video, text, msg_ref, head)
    copies[1].wait()
    head += w_buffer.shape[1] // TRIPLE
    partial_sums(a_ref, last_buffer, video, text, msg_ref, head)
    copies[2].wait()


def own_kernel(place_ref, a_ref, ahead_ref, w_ref, *refs):
    small = (len(refs) - 4) // 2
    out_ref, text_ref = refs[small : small + 2]
    w_buffer, sems = refs[-2:]
    top = out_ref.shape[0]
    later, _, columns = w_buffer.shape
    base = place_ref[0] * (w_ref.shape[1] // 2) + columns
    copies = [
        column_copy(w_ref, base + index * columns, w_buffer.at[index], sems.at[index])
        for index in range(later)
    ]
    for source, target in zip(refs[:small], refs[small + 2 : -2]):
        copies.append(pltpu.make_async_copy(source, target, sems.at[len(copies)]))
    for copy in copies:
        copy.start()

    for block in range(later + 1):
        if block:
            copies[block - 1].wait()
        for start in range(0, columns, PIECE):
            cells = slice(start, start + PIECE)
            part = w_buffer[block - 1, :, cells] if block else ahead_ref[:, cells]
            product = jnp.dot(a_ref[...], part, preferred_element_type=F32)
            first = block * columns + start
            out_ref[:, first : first + PIECE] = product[:top]
            for local in range(0, PIECE, HEAD_DIM):
                head, kind = divmod((first + local) // HEAD_DIM, 3)
                if kind:
                    target = (2 * head + kind - 1) * HEAD_DIM
                    text_ref[:, target : target + HEAD_DIM] = product[
                        top:, local : local + HEAD_DIM
                    ]
    for copy in copies[later:]:
        copy.wait()


def row_stats(total_features, own, received):
    count = own.shape[0]
    received = received.astype(F32)
    padding = jnp.zeros((HEAD_DIM - received.shape[0], count), F32)
    received = jnp.transpose(jnp.concatenate([received, padding], axis=0))
    parts = [received[:, index : index + 1] for index in range(6)]
    gap = 0.5 * (own[:, 0:1] - (parts[0] + parts[1] + parts[2]))
    second = own[:, 1:2] + (parts[3] + parts[4] + parts[5])
    var = second * (1.0 / total_features) + gap * gap
    return gap, lax.rsqrt(var + EPS)


def column_terms(own_ref, msg_ref, video, base, part):
    other = msg_ref[base : base + EXTRA, :].astype(F32)
    other = other[4 * (part % 3) : 4 * (part % 3) + 4]
    own = own_ref[video : video + 8, part * HEAD_DIM : (part + 1) * HEAD_DIM]
    scale = (own[0:1] + own[1:2]) - (other[0:1] + other[1:2])
    shift = (own[2:3] + own[3:4]) + (other[2:3] + other[3:4])
    return scale, shift


def head_place(head, rows, first_ref, more_ref):
    early = first_ref.shape[0] // rows
    return (first_ref, head * rows) if head < early else (more_ref, (head - early) * rows)


def head_norm(part, gain):
    square = jnp.sum(part * part, axis=1, keepdims=True) * (1.0 / HEAD_DIM)
    return part * lax.rsqrt(square + EPS) * gain


def norm_kernel(
    total_features, text, own_ref, first_ref, more_ref, stat_ref, qg_ref, kg_ref,
    qa_ref, qb_ref, kv_ref,
):
    video = qa_ref.shape[0]
    half = qa_ref.shape[1] // HEAD_DIM
    rows = head_rows(video, text)
    query_gain = qg_ref[...].reshape(1, HEAD_DIM)
    key_gain = kg_ref[...].reshape(1, HEAD_DIM)
    start = first_ref.shape[0] - 2 * EXTRA
    gap, inverse = row_stats(
        total_features, stat_ref[:video, :], first_ref[start : start + EXTRA, :video]
    )
    for head in range(2 * half):
        msg_ref, base = head_place(head, rows, first_ref, more_ref)

        def total(kind):
            part = 3 * head + kind
            scale, shift = column_terms(own_ref, msg_ref, video, base + rows - EXTRA, part)
            other = msg_ref[base + kind * video : base + (kind + 1) * video, :].astype(F32)
            both = own_ref[:video, part * HEAD_DIM : (part + 1) * HEAD_DIM] + other
            return (both + gap * scale) * inverse + shift

        columns = slice(head * HEAD_DIM, (head + 1) * HEAD_DIM)
        cells = slice(head % half * HEAD_DIM, (head % half + 1) * HEAD_DIM)
        q_ref = qa_ref if head < half else qb_ref
        q_ref[:, cells] = head_norm(total(0), query_gain).astype(BF16)
        kv_ref[0, :, columns] = head_norm(total(1), key_gain).astype(BF16)
        kv_ref[1, :, columns] = total(2).astype(BF16)


def text_kernel(
    total_features, own_ref, first_ref, more_ref, stat_ref, top_ref, kg_ref, kv_ref
):
    text = kv_ref.shape[1]
    heads = kv_ref.shape[2] // HEAD_DIM
    video = top_ref.shape[0] - EXTRA
    rows = head_rows(video, text)
    key_gain = kg_ref[...].reshape(1, HEAD_DIM)
    start = first_ref.shape[0] - EXTRA
    gap, inverse = row_stats(
        total_features, stat_ref[video + EXTRA :, :], first_ref[start : start + EXTRA, :text]
    )
    for head in range(heads):
        msg_ref, base = head_place(head, rows, first_ref, more_ref)

        def total(kind):
            scale, shift = column_terms(
                top_ref, msg_ref, video, base + rows - EXTRA, 3 * head + 1 + kind
            )
            start = base + 3 * video + kind * text
            other = msg_ref[start : start + text, :].astype(F32)
            first = (2 * head + kind) * HEAD_DIM
            return (own_ref[:, first : first + HEAD_DIM] + other + gap * scale) * inverse + shift

        columns = slice(head * HEAD_DIM, (head + 1) * HEAD_DIM)
        kv_ref[0, :, columns] = head_norm(total(0), key_gain).astype(BF16)
        kv_ref[1, :, columns] = total(1).astype(BF16)


FACTOR = math.log2(math.e) / math.sqrt(HEAD_DIM)


def split_kernel(*refs):
    count = len(refs) // 3
    for index in range(count):
        half = refs[index].shape[2] // 2
        refs[count + 2 * index][...] = refs[index][:, :, :half]
        refs[count + 2 * index + 1][...] = refs[index][:, :, half:]


def weigh(rows, keys):
    scores = lax.dot_general(rows, keys, (((1,), (1,)), ((), ())), preferred_element_type=F32)
    return jnp.exp2(scores * FACTOR)


def lanes(weights):
    total = weights[:, :HEAD_DIM]
    for start in range(HEAD_DIM, weights.shape[1], HEAD_DIM):
        total = total + weights[:, start : start + HEAD_DIM]
    return total


def times(weights, values):
    return jnp.dot(weights.astype(BF16), values, preferred_element_type=F32)


def both(group, index):
    return jnp.concatenate([ref[index, :, part] for ref, part in group], axis=0)


def attend_kernel(
    first, count, place_ref, qo_ref, qp_ref, fresh_ref, stale_ref, text_ref, mask_ref, *refs,
):
    finish = len(refs[-1].shape) == 0
    if finish:
        *refs, own_ref, own_den_ref, msg_ref, cache_ref, sem = refs
        cache_copy = pltpu.make_async_copy(fresh_ref, cache_ref, sem)
        cache_copy.start()
    else:
        *refs, num_ref, den_ref = refs
    video, width = qo_ref.shape
    text = text_ref.shape[1]
    lane = lax.broadcasted_iota(jnp.int32, (2 * video, HEAD_DIM), 1)
    mask = mask_ref[...].reshape(1, 2 * text).astype(F32)
    mask = jnp.where(place_ref[1] == 0, mask[:, :text], mask[:, text:])
    keep = jnp.concatenate([jnp.ones((1, video), F32), mask], axis=1)
    same_patch = (
        (lax.broadcasted_iota(jnp.int32, (2 * video, 2 * video), 0) < video)
        == (lax.broadcasted_iota(jnp.int32, (2 * video, 2 * video), 1) < video)
    ).astype(F32)
    packed = jnp.zeros((2 * video, HEAD_DIM), F32)
    for head in range(width // HEAD_DIM):
        cells = slice(head * HEAD_DIM, (head + 1) * HEAD_DIM)
        columns = slice((first + head) * HEAD_DIM, (first + head + 1) * HEAD_DIM)
        queries = jnp.concatenate([qo_ref[:, cells], qp_ref[:, cells]], axis=0)
        pair = [(fresh_ref, columns), (stale_ref, columns)]
        weights = weigh(queries, both(pair, 0)) * same_patch
        num = times(weights, both(pair, 1))
        den = lanes(weights)
        blocks = [(ref, columns) for ref in refs[:count]] + [(ref, cells) for ref in refs[count:]]
        blocks.append((text_ref, columns))
        odd = len(blocks) % 2
        for start in range(odd, len(blocks), 2):
            pair = blocks[start : start + 2]
            weights = weigh(queries, both(pair, 0))
            if start + 2 == len(blocks):
                weights = weights * keep
            num = num + times(weights, both(pair, 1))
            den = den + lanes(weights)
        if odd:
            weights = weigh(queries, both(blocks[:1], 0))
            num = num + times(weights, both(blocks[:1], 1))
            den = den + weights
        if finish:
            own_ref[:, cells] = num[:video]
            msg_ref[:, cells] = num[video:]
        else:
            num_ref[:, cells] = num
        packed = jnp.where(lane == first + head, jnp.sum(den, axis=1, keepdims=True), packed)
    if finish:
        own_den_ref[...] = packed[:video]
        msg_ref[:, width:] = packed[video:]
        cache_copy.wait()
    else:
        den_ref[...] = packed


def last_kernel(first, qo_ref, qp_ref, num_ref, den_ref, far_ref, own_ref, own_den_ref, msg_ref):
    video, width = qo_ref.shape
    lane = lax.broadcasted_iota(jnp.int32, (2 * video, HEAD_DIM), 1)
    packed = den_ref[...]
    for head in range(width // HEAD_DIM):
        cells = slice(head * HEAD_DIM, (head + 1) * HEAD_DIM)
        queries = jnp.concatenate([qo_ref[:, cells], qp_ref[:, cells]], axis=0)
        weights = weigh(queries, far_ref[0, :, cells])
        num = num_ref[:, cells] + times(weights, far_ref[1, :, cells])
        own_ref[:, cells] = num[:video]
        msg_ref[:, cells] = num[video:]
        total = jnp.sum(lanes(weights), axis=1, keepdims=True)
        packed = packed + jnp.where(lane == first + head, total, 0.0)
    own_den_ref[...] = packed[:video]
    msg_ref[:, width:] = packed[video:]


def merge_kernel(first, own_ref, den_ref, msg_ref, att_ref):
    width = att_ref.shape[1]
    for head in range(width // HEAD_DIM):
        columns = slice(head * HEAD_DIM, (head + 1) * HEAD_DIM)
        lane = first + head
        num = own_ref[:, columns] + msg_ref[:, columns]
        den = den_ref[:, lane : lane + 1] + msg_ref[:, width + lane : width + lane + 1]
        att_ref[:, columns] = (num / den).astype(BF16)


def part_kernel(place_ref, weight_ref, first_ref, second_ref, out_ref, w_other_ref, w_ref, sems):
    depth = w_ref.shape[0]
    half = first_ref.shape[1]
    copies = []
    for index, (group, target) in enumerate(
        ((place_ref[0], w_ref), (1 - place_ref[0], w_other_ref))
    ):
        rows = pl.ds(pl.multiple_of(group * depth, depth), depth)
        copies.append(pltpu.make_async_copy(weight_ref.at[rows], target, sems.at[index]))
        copies[-1].start()
    copies[0].wait()
    out_ref[...] = jnp.dot(
        first_ref[...], w_ref[:half, :], preferred_element_type=F32
    ) + jnp.dot(second_ref[...], w_ref[half:, :], preferred_element_type=F32)
    copies[1].wait()


def more_kernel(part_ref, att_ref, w_ref, out_ref):
    half = att_ref.shape[1]
    out_ref[...] = part_ref[...] + jnp.dot(
        att_ref[...], w_ref[:half, :], preferred_element_type=F32
    )


def final_kernel(part_ref, att_ref, w_ref, hidden_ref, gate_ref, out_ref, buffer_ref, sems):
    half = att_ref.shape[1]
    gate = gate_ref[...].reshape(1, part_ref.shape[1])
    count = sems.shape[0]
    step = part_ref.shape[1] // count
    copies = []
    for index in range(count):
        cells = slice(index * step, (index + 1) * step)
        total = part_ref[:, cells] + jnp.dot(
            att_ref[...], w_ref[half:, cells], preferred_element_type=F32
        )
        mixed = hidden_ref[:, cells].astype(F32) + gate[:, cells] * total
        buffer_ref[:, cells] = mixed.astype(BF16)
        copies.append(
            pltpu.make_async_copy(buffer_ref.at[:, cells], out_ref.at[:, cells], sems.at[index])
        )
        copies[-1].start()
    for copy in copies:
        copy.wait()


def params(megabytes):
    return pltpu.CompilerParams(vmem_limit_bytes=megabytes * 1024 * 1024)


def in_hbm(array):
    return pltpu.with_memory_space_constraint(array, pltpu.HBM)


def cost(flops, nbytes, transcendentals=0):
    return pl.CostEstimate(
        flops=int(flops), bytes_accessed=int(nbytes), transcendentals=int(transcendentals)
    )


def plain_call(kernel, outs, name, estimate, *operands):
    return pl.pallas_call(
        kernel,
        in_specs=[pl.BlockSpec(memory_space=pltpu.VMEM)] * len(operands),
        out_specs=[pl.BlockSpec(memory_space=pltpu.VMEM)] * len(outs),
        out_shape=[jax.ShapeDtypeStruct(shape, dtype) for shape, dtype in outs],
        compiler_params=params(24),
        cost_estimate=estimate,
        name=name,
    )(*operands)


def ring_moves(sections):
    chips = sections // 2
    order = list(range(0, chips, 2)) + list(range(chips - 1, 0, -2))
    moves = [], []
    for here, there in zip(order, order[1:] + order[:1]):
        for core in range(2):
            moves[core].append((2 * here + core, 2 * there + core))
            moves[1 - core].append((2 * there + core, 2 * here + core))
    return sorted(moves[0]), sorted(moves[1])


def per_device(
    sections, hidden, text_hidden, text_mask, stale_cache, qkv_weight, out_weight, query_gain,
    key_gain, norm_shift, norm_scale, branch_gate,
):
    video, features = hidden.shape
    text = text_hidden.shape[0] // 2
    width = stale_cache.shape[2]
    heads = width // HEAD_DIM
    group_columns = heads * TRIPLE
    chips = sections // 2
    out_features = out_weight.shape[1]
    top = video + EXTRA
    rows = top + text

    group = lax.axis_index("head")
    core = lax.axis_index("section") % 2
    place = jnp.stack([group, core]).astype(jnp.int32)
    swap_core = [(s, s ^ 1) for s in range(sections)]
    swap_head = [(0, 1), (1, 0)]
    ways = ring_moves(sections)
    half_way = chips // 2

    def ring_step(blocks):
        return [lax.ppermute(block, "section", way) for block, way in zip(blocks, ways)]

    vmem = pl.BlockSpec(memory_space=pltpu.VMEM)
    hbm = pl.BlockSpec(memory_space=pltpu.HBM)
    smem = pl.BlockSpec(memory_space=pltpu.SMEM)
    whole = ring_step((stale_cache, stale_cache))

    columns = 2 * TRIPLE
    blocks = group_columns // columns
    per_head = head_rows(video, text)

    def project_cost(share):
        share = 8 * rows * features * group_columns * share
        return cost(share, share // (4 * rows))

    a_rows, message, stats, ahead = pl.pallas_call(
        send_kernel,
        in_specs=[smem] + [hbm] * 5,
        out_specs=[vmem] * 4,
        out_shape=[
            jax.ShapeDtypeStruct((rows, features), BF16),
            jax.ShapeDtypeStruct((per_head + 2 * EXTRA, HEAD_DIM), BF16),
            jax.ShapeDtypeStruct((rows, HEAD_DIM), F32),
            jax.ShapeDtypeStruct((features, columns), BF16),
        ],
        scratch_shapes=[
            pltpu.VMEM((video, features), BF16),
            pltpu.VMEM((text, features), BF16),
            pltpu.VMEM((features,), F32),
            pltpu.VMEM((features,), F32),
            pltpu.VMEM((features, TRIPLE), BF16),
            pltpu.SemaphoreType.DMA((6,)),
        ],
        compiler_params=params(40),
        cost_estimate=project_cost(0.4),
        name="project_send",
    )(place, *map(in_hbm, (hidden, text_hidden, norm_scale, norm_shift, qkv_weight)))
    received = lax.ppermute(message, "head", swap_head)

    message_more, own_ahead = pl.pallas_call(
        functools.partial(send_more_kernel, video),
        in_specs=[smem, vmem, vmem, hbm],
        out_specs=[vmem] * 2,
        out_shape=[
            jax.ShapeDtypeStruct(((heads - 1) * per_head, HEAD_DIM), BF16),
            jax.ShapeDtypeStruct((features, columns), BF16),
        ],
        scratch_shapes=[
            pltpu.VMEM((features, group_columns - columns - 2 * TRIPLE), BF16),
            pltpu.VMEM((features, TRIPLE), BF16),
            pltpu.SemaphoreType.DMA((3,)),
        ],
        compiler_params=params(40),
        cost_estimate=project_cost(0.6),
        name="project_send_more",
    )(place, a_rows, ahead, in_hbm(qkv_weight))
    received_more = lax.ppermute(message_more, "head", swap_head)

    split = plain_call(
        split_kernel, [((2, video, width // 2), BF16)] * 4, "split_heads", cost(0, 8 * video * width),
        *lax.optimization_barrier((*whole, message_more, received))[:2],
    )
    chains = [[ring_step((split[0], split[2]))], [ring_step((split[1], split[3]))]]

    small = (query_gain, key_gain, text_mask, branch_gate, hidden, stale_cache)
    outs = pl.pallas_call(
        own_kernel,
        in_specs=[smem, vmem, vmem, hbm] + [hbm] * len(small),
        out_specs=[vmem] * (2 + len(small)),
        out_shape=[
            jax.ShapeDtypeStruct((top, group_columns), F32),
            jax.ShapeDtypeStruct((text, 2 * width), F32),
        ]
        + [jax.ShapeDtypeStruct(array.shape, array.dtype) for array in small],
        scratch_shapes=[
            pltpu.VMEM((blocks - 1, features, columns), BF16),
            pltpu.SemaphoreType.DMA((blocks - 1 + len(small),)),
        ],
        compiler_params=params(40),
        cost_estimate=project_cost(1),
        name="project_own",
    )(place, a_rows, own_ahead, *map(in_hbm, (qkv_weight,) + small))
    own, own_text = outs[:2]
    query_gain, key_gain, text_mask, branch_gate, hidden, stale = outs[2:]

    for _ in range(half_way - 3):
        for chain in chains:
            chain.append(ring_step(lax.optimization_barrier((*chain[-1], own))[:2]))
    far = [lax.ppermute(chains[0][-1][0], "section", ways[0])]

    received_more = lax.optimization_barrier((received_more, *chains[0][0], *chains[1][0]))[0]
    *queries, fresh = plain_call(
        functools.partial(norm_kernel, features * 2, text),
        [((video, width // 2), BF16)] * 2 + [((2, video, width), BF16)],
        "norm_video",
        cost(1000 * top * group_columns, 8 * top * group_columns),
        own, received, received_more, stats, query_gain, key_gain,
    )
    other_queries = [lax.ppermute(queries[0], "section", swap_core)]
    (text_kv,) = plain_call(
        functools.partial(text_kernel, features * 2),
        [((2, text, width), BF16)],
        "norm_text",
        cost(text * group_columns, text * group_columns),
        own_text, received, received_more, stats, own, key_gain,
    )

    last = lax.optimization_barrier((chains[1][-1][0], text_kv, queries[0]))[0]
    far.append(lax.ppermute(last, "section", ways[0]))
    context = chips * video + video + text
    finished = [
        jax.ShapeDtypeStruct((video, width // 2), F32),
        jax.ShapeDtypeStruct((video, HEAD_DIM), F32),
        jax.ShapeDtypeStruct((video, width // 2 + HEAD_DIM), F32),
    ]
    attended, other_attended = [], []
    for index, chain in enumerate(chains):
        first = index * heads // 2
        halves = [block for step in chain for block in step]
        finish = index == 1
        own_queries = queries[index]
        if finish:
            halves.append(far[index])
            own_queries = lax.optimization_barrier((own_queries, num_own))[0]
            outs = finished + [jax.ShapeDtypeStruct(fresh.shape, BF16)]
        else:
            outs = [
                jax.ShapeDtypeStruct((2 * video, width // 2), F32),
                jax.ShapeDtypeStruct((2 * video, HEAD_DIM), F32),
            ]
        outs = pl.pallas_call(
            functools.partial(attend_kernel, first, len(whole)),
            in_specs=[smem] + [vmem] * (6 + len(whole) + len(halves)),
            out_specs=[vmem] * (len(outs) - finish) + [hbm] * finish,
            out_shape=outs,
            scratch_shapes=[pltpu.SemaphoreType.DMA] * finish,
            compiler_params=params(24),
            cost_estimate=cost(video * context, context * width, video * heads),
            name="attend",
        )(
            place, own_queries, other_queries[index], fresh, stale, text_kv, text_mask,
            *whole, *halves,
        )
        if finish:
            *outs, new_cache = outs
        else:
            later = lax.optimization_barrier((queries[1], outs[0]))[0]
            other_queries.append(lax.ppermute(later, "section", swap_core))
            outs = plain_call(
                functools.partial(last_kernel, first),
                [(out.shape, out.dtype) for out in finished],
                "attend_last",
                cost(video * video, video * width),
                own_queries, other_queries[index], *outs, far[index],
            )
        num_own, den_own, num_message = outs
        num_received = lax.ppermute(num_message, "section", swap_core)
        attended += plain_call(
            functools.partial(merge_kernel, first),
            [((video, width // 2), BF16)],
            "merge",
            cost(2 * video * width, 5 * video * width),
            num_own, den_own, num_received,
        )
        other_attended.append(lax.ppermute(attended[-1], "head", swap_head))

    out_cost = cost(4 * video * width * out_features, 2 * width * out_features)
    part, w_other = pl.pallas_call(
        part_kernel,
        in_specs=[smem, hbm, vmem, vmem],
        out_specs=[vmem] * 2,
        out_shape=[
            jax.ShapeDtypeStruct((video, out_features), F32),
            jax.ShapeDtypeStruct((width, out_features), BF16),
        ],
        scratch_shapes=[
            pltpu.VMEM((width, out_features), BF16),
            pltpu.SemaphoreType.DMA((2,)),
        ],
        compiler_params=params(24),
        cost_estimate=out_cost,
        name="part_out",
    )(place, in_hbm(out_weight), *attended)
    (part,) = plain_call(
        more_kernel, [((video, out_features), F32)], "more_out", out_cost,
        part, other_attended[0], w_other,
    )
    mixed = pl.pallas_call(
        final_kernel,
        in_specs=[vmem] * 5,
        out_specs=hbm,
        out_shape=jax.ShapeDtypeStruct((video, out_features), BF16),
        scratch_shapes=[
            pltpu.VMEM((video, out_features), BF16),
            pltpu.SemaphoreType.DMA((out_features // 512,)),
        ],
        compiler_params=params(24),
        cost_estimate=out_cost,
        name="final_out",
    )(part, other_attended[1], w_other, hidden, branch_gate)
    return (mixed, new_cache)


def solution(mesh):
    in_specs = (
        P("section", "head"),
        P(None, "head"),
        P(),
        P(None, "section", "head"),
        P("head", None),
        P(None, "head"),
        P(),
        P(),
        P("head"),
        P("head"),
        P("head"),
    )
    out_specs = (P("section", "head"), P(None, "section", "head"))
    return jax.shard_map(
        functools.partial(per_device, mesh.shape["section"]),
        mesh=mesh, in_specs=in_specs, out_specs=out_specs, check_vma=False,
    )
```

```python
import functools
import math

import jax
import jax.numpy as jnp
from jax import lax
from jax.experimental import pallas as pl
from jax.experimental.pallas import tpu as pltpu
from jax.sharding import PartitionSpec as P

HEAD_DIM = 128
TRIPLE = 3 * HEAD_DIM
EXTRA = 16
PIECE = 2 * HEAD_DIM
EPS = 1e-06
F32 = jnp.float32
BF16 = jnp.bfloat16


def split_bf16(value, parts):
    pieces = []
    rest = value
    for _ in range(parts):
        piece = rest.astype(BF16)
        pieces.append(piece)
        rest = rest - piece.astype(F32)
    return pieces


def head_rows(video, text):
    return 3 * video + 2 * text + EXTRA


def column_copy(w_ref, first, target, sem):
    columns = target.shape[1]
    start = pl.multiple_of(first, HEAD_DIM)
    return pltpu.make_async_copy(w_ref.at[:, pl.ds(start, columns)], target, sem)


def partial_sums(a_ref, w_ref, video, text, msg_ref, first):
    band = lax.broadcasted_iota(jnp.int32, (EXTRA, HEAD_DIM), 0) // 4
    top = video + EXTRA
    terms = None
    for start in range(0, w_ref.shape[1], PIECE):
        stop = min(start + PIECE, w_ref.shape[1])
        product = jnp.dot(a_ref[...], w_ref[:, start:stop], preferred_element_type=F32)
        for local in range(0, stop - start, HEAD_DIM):
            part = product[:, local : local + HEAD_DIM]
            head, kind = divmod((start + local) // HEAD_DIM, 3)
            base = (first + head) * head_rows(video, text)
            msg_ref[base + kind * video : base + (kind + 1) * video, :] = part[:video].astype(BF16)
            terms = part[video:top] if kind == 0 else jnp.where(band == kind, part[video:top], terms)
            base += 3 * video
            if kind:
                rows = slice(base + (kind - 1) * text, base + kind * text)
                msg_ref[rows, :] = part[top:].astype(BF16)
            if kind == 2:
                base += 2 * text
                msg_ref[base : base + EXTRA, :] = terms.astype(BF16)


def send_kernel(
    place_ref, x_ref, t_ref, scale_ref, shift_ref, w_ref,
    a_ref, msg_ref, stat_ref, ahead_ref,
    x_buffer, t_buffer, scale_buffer, shift_buffer, w_buffer, sems,
):
    video, features = x_buffer.shape
    text = t_buffer.shape[0]
    top = video + EXTRA
    columns = w_buffer.shape[1]
    base = (1 - place_ref[0]) * (w_ref.shape[1] // 2)
    copies = [
        pltpu.make_async_copy(scale_ref, scale_buffer, sems.at[0]),
        pltpu.make_async_copy(shift_ref, shift_buffer, sems.at[1]),
        pltpu.make_async_copy(x_ref, x_buffer, sems.at[2]),
        pltpu.make_async_copy(
            t_ref.at[pl.ds(pl.multiple_of(place_ref[1] * text, text), text)], t_buffer, sems.at[3]
        ),
        column_copy(w_ref, base, w_buffer, sems.at[4]),
        column_copy(w_ref, base + columns, ahead_ref, sems.at[5]),
    ]
    for copy in copies[:5]:
        copy.start()

    copies[0].wait()
    copies[1].wait()
    gain = 1.0 + scale_buffer[...].reshape(1, features)
    pieces = split_bf16(gain, 2) + split_bf16(shift_buffer[...].reshape(1, features), 2)
    row = lax.broadcasted_iota(jnp.int32, (EXTRA, features), 0)
    extra = jnp.zeros((EXTRA, features), F32)
    for index, piece in enumerate(pieces):
        extra = jnp.where(row % 4 == index, piece.astype(F32), extra)
    a_ref[video:top, :] = extra.astype(BF16)

    def prepare(rows_ref, start):
        rows = rows_ref[...].astype(F32)
        count = rows.shape[0]
        mean = jnp.sum(rows, axis=1, keepdims=True) * (1.0 / features)
        centered = rows - mean
        second = jnp.sum(centered * centered, axis=1, keepdims=True)
        a_ref[start : start + count, :] = (centered * gain).astype(BF16)
        lane = lax.broadcasted_iota(jnp.int32, (count, HEAD_DIM), 1)
        packed = jnp.zeros((count, HEAD_DIM), F32)
        for index, piece in enumerate(split_bf16(mean, 3) + split_bf16(second, 3)):
            packed = jnp.where(lane == index, piece.astype(F32), packed)
        stat_ref[start : start + count, :] = jnp.where(
            lane == 0, mean, jnp.where(lane == 1, second, 0.0)
        )
        return jnp.transpose(packed)[:EXTRA]

    copies[2].wait()
    copies[5].start()
    stats = [prepare(x_buffer, 0)]
    copies[3].wait()
    stats.append(prepare(t_buffer, top))
    stat_ref[video:top, :] = jnp.zeros((EXTRA, HEAD_DIM), F32)
    start = head_rows(video, text) * columns // TRIPLE
    msg_ref[start : start + 2 * EXTRA, :] = jnp.concatenate(stats, axis=0).astype(BF16)
    copies[4].wait()
    partial_sums(a_ref, w_buffer, video, text, msg_ref, 0)
    copies[5].wait()


def send_more_kernel(
    video, place_ref, a_ref, ahead_ref, w_ref, msg_ref, own_ahead_ref, w_buffer, last_buffer, sems,
):
    text = a_ref.shape[0] - video - EXTRA
    width = w_ref.shape[1] // 2
    other, own = (1 - place_ref[0]) * width, place_ref[0] * width
    first = width - last_buffer.shape[1]
    copies = [
        column_copy(w_ref, other + first - w_buffer.shape[1], w_buffer, sems.at[0]),
        column_copy(w_ref, other + first, last_buffer, sems.at[1]),
        column_copy(w_ref, own, own_ahead_ref, sems.at[2]),
    ]
    copies[0].start()
    copies[1].start()
    partial_sums(a_ref, ahead_ref, video, text, msg_ref, 0)
    copies[0].wait()
    copies[2].start()
    head = ahead_ref.shape[1] // TRIPLE
    partial_sums(a_ref, w_buffer, video, text, msg_ref, head)
    copies[1].wait()
    head += w_buffer.shape[1] // TRIPLE
    partial_sums(a_ref, last_buffer, video, text, msg_ref, head)
    copies[2].wait()


def own_kernel(place_ref, a_ref, ahead_ref, w_ref, *refs):
    small = (len(refs) - 4) // 2
    out_ref, text_ref = refs[small : small + 2]
    w_buffer, sems = refs[-2:]
    top = out_ref.shape[0]
    later, _, columns = w_buffer.shape
    base = place_ref[0] * (w_ref.shape[1] // 2) + columns
    copies = [
        column_copy(w_ref, base + index * columns, w_buffer.at[index], sems.at[index])
        for index in range(later)
    ]
    for source, target in zip(refs[:small], refs[small + 2 : -2]):
        copies.append(pltpu.make_async_copy(source, target, sems.at[len(copies)]))
    for copy in copies:
        copy.start()

    for block in range(later + 1):
        if block:
            copies[block - 1].wait()
        for start in range(0, columns, PIECE):
            cells = slice(start, start + PIECE)
            part = w_buffer[block - 1, :, cells] if block else ahead_ref[:, cells]
            product = jnp.dot(a_ref[...], part, preferred_element_type=F32)
            first = block * columns + start
            out_ref[:, first : first + PIECE] = product[:top]
            for local in range(0, PIECE, HEAD_DIM):
                head, kind = divmod((first + local) // HEAD_DIM, 3)
                if kind:
                    target = (2 * head + kind - 1) * HEAD_DIM
                    text_ref[:, target : target + HEAD_DIM] = product[
                        top:, local : local + HEAD_DIM
                    ]
    for copy in copies[later:]:
        copy.wait()


def row_stats(total_features, own, received):
    count = own.shape[0]
    received = received.astype(F32)
    padding = jnp.zeros((HEAD_DIM - received.shape[0], count), F32)
    received = jnp.transpose(jnp.concatenate([received, padding], axis=0))
    parts = [received[:, index : index + 1] for index in range(6)]
    gap = 0.5 * (own[:, 0:1] - (parts[0] + parts[1] + parts[2]))
    second = own[:, 1:2] + (parts[3] + parts[4] + parts[5])
    var = second * (1.0 / total_features) + gap * gap
    return gap, lax.rsqrt(var + EPS)


def column_terms(own_ref, msg_ref, video, base, part):
    other = msg_ref[base : base + EXTRA, :].astype(F32)
    other = other[4 * (part % 3) : 4 * (part % 3) + 4]
    own = own_ref[video : video + 8, part * HEAD_DIM : (part + 1) * HEAD_DIM]
    scale = (own[0:1] + own[1:2]) - (other[0:1] + other[1:2])
    shift = (own[2:3] + own[3:4]) + (other[2:3] + other[3:4])
    return scale, shift


def head_place(head, rows, first_ref, more_ref):
    early = first_ref.shape[0] // rows
    return (first_ref, head * rows) if head < early else (more_ref, (head - early) * rows)


def head_norm(part, gain):
    square = jnp.sum(part * part, axis=1, keepdims=True) * (1.0 / HEAD_DIM)
    return part * lax.rsqrt(square + EPS) * gain


def norm_kernel(
    total_features, text, own_ref, first_ref, more_ref, stat_ref, qg_ref, kg_ref,
    qa_ref, qb_ref, kv_ref,
):
    video = qa_ref.shape[0]
    half = qa_ref.shape[1] // HEAD_DIM
    rows = head_rows(video, text)
    query_gain = qg_ref[...].reshape(1, HEAD_DIM)
    key_gain = kg_ref[...].reshape(1, HEAD_DIM)
    start = first_ref.shape[0] - 2 * EXTRA
    gap, inverse = row_stats(
        total_features, stat_ref[:video, :], first_ref[start : start + EXTRA, :video]
    )
    for head in range(2 * half):
        msg_ref, base = head_place(head, rows, first_ref, more_ref)

        def total(kind):
            part = 3 * head + kind
            scale, shift = column_terms(own_ref, msg_ref, video, base + rows - EXTRA, part)
            other = msg_ref[base + kind * video : base + (kind + 1) * video, :].astype(F32)
            both = own_ref[:video, part * HEAD_DIM : (part + 1) * HEAD_DIM] + other
            return (both + gap * scale) * inverse + shift

        columns = slice(head * HEAD_DIM, (head + 1) * HEAD_DIM)
        cells = slice(head % half * HEAD_DIM, (head % half + 1) * HEAD_DIM)
        q_ref = qa_ref if head < half else qb_ref
        q_ref[:, cells] = head_norm(total(0), query_gain).astype(BF16)
        kv_ref[0, :, columns] = head_norm(total(1), key_gain).astype(BF16)
        kv_ref[1, :, columns] = total(2).astype(BF16)


def text_kernel(
    total_features, own_ref, first_ref, more_ref, stat_ref, top_ref, kg_ref, kv_ref
):
    text = kv_ref.shape[1]
    heads = kv_ref.shape[2] // HEAD_DIM
    video = top_ref.shape[0] - EXTRA
    rows = head_rows(video, text)
    key_gain = kg_ref[...].reshape(1, HEAD_DIM)
    start = first_ref.shape[0] - EXTRA
    gap, inverse = row_stats(
        total_features, stat_ref[video + EXTRA :, :], first_ref[start : start + EXTRA, :text]
    )
    for head in range(heads):
        msg_ref, base = head_place(head, rows, first_ref, more_ref)

        def total(kind):
            scale, shift = column_terms(
                top_ref, msg_ref, video, base + rows - EXTRA, 3 * head + 1 + kind
            )
            start = base + 3 * video + kind * text
            other = msg_ref[start : start + text, :].astype(F32)
            first = (2 * head + kind) * HEAD_DIM
            return (own_ref[:, first : first + HEAD_DIM] + other + gap * scale) * inverse + shift

        columns = slice(head * HEAD_DIM, (head + 1) * HEAD_DIM)
        kv_ref[0, :, columns] = head_norm(total(0), key_gain).astype(BF16)
        kv_ref[1, :, columns] = total(1).astype(BF16)


FACTOR = math.log2(math.e) / math.sqrt(HEAD_DIM)


def split_kernel(*refs):
    count = len(refs) // 3
    for index in range(count):
        half = refs[index].shape[2] // 2
        refs[count + 2 * index][...] = refs[index][:, :, :half]
        refs[count + 2 * index + 1][...] = refs[index][:, :, half:]


def weigh(rows, keys):
    scores = lax.dot_general(rows, keys, (((1,), (1,)), ((), ())), preferred_element_type=F32)
    return jnp.exp2(scores * FACTOR)


def lanes(weights):
    total = weights[:, :HEAD_DIM]
    for start in range(HEAD_DIM, weights.shape[1], HEAD_DIM):
        total = total + weights[:, start : start + HEAD_DIM]
    return total


def times(weights, values):
    return jnp.dot(weights.astype(BF16), values, preferred_element_type=F32)


def both(group, index):
    return jnp.concatenate([ref[index, :, part] for ref, part in group], axis=0)


def attend_kernel(
    first, count, place_ref, qo_ref, qp_ref, fresh_ref, stale_ref, text_ref, mask_ref, *refs,
):
    finish = len(refs[-1].shape) == 0
    if finish:
        *refs, own_ref, own_den_ref, msg_ref, cache_ref, sem = refs
        cache_copy = pltpu.make_async_copy(fresh_ref, cache_ref, sem)
        cache_copy.start()
    else:
        *refs, num_ref, den_ref = refs
    video, width = qo_ref.shape
    text = text_ref.shape[1]
    lane = lax.broadcasted_iota(jnp.int32, (2 * video, HEAD_DIM), 1)
    mask = mask_ref[...].reshape(1, 2 * text).astype(F32)
    mask = jnp.where(place_ref[1] == 0, mask[:, :text], mask[:, text:])
    keep = jnp.concatenate([jnp.ones((1, video), F32), mask], axis=1)
    same_patch = (
        (lax.broadcasted_iota(jnp.int32, (2 * video, 2 * video), 0) < video)
        == (lax.broadcasted_iota(jnp.int32, (2 * video, 2 * video), 1) < video)
    ).astype(F32)
    packed = jnp.zeros((2 * video, HEAD_DIM), F32)

    def scores_of(head, group):
        cells = slice(head * HEAD_DIM, (head + 1) * HEAD_DIM)
        queries = jnp.concatenate([qo_ref[:, cells], qp_ref[:, cells]], axis=0)
        return lax.dot_general(
            queries, both(group, 0), (((1,), (1,)), ((), ())), preferred_element_type=F32
        )

    work = []
    for head in range(width // HEAD_DIM):
        cells = slice(head * HEAD_DIM, (head + 1) * HEAD_DIM)
        columns = slice((first + head) * HEAD_DIM, (first + head + 1) * HEAD_DIM)
        blocks = [(ref, columns) for ref in refs[:count]] + [(ref, cells) for ref in refs[count:]]
        blocks.append((text_ref, columns))
        work.append((head, [(fresh_ref, columns), (stale_ref, columns)], same_patch))
        odd = len(blocks) % 2
        if odd:
            work.append((head, blocks[:1], None))
        for start in range(odd, len(blocks), 2):
            last = start + 2 == len(blocks)
            work.append((head, blocks[start : start + 2], keep if last else None))

    upcoming = scores_of(*work[0][:2])
    num = den = None
    for index, (head, group, kept) in enumerate(work):
        scores = upcoming
        if index + 1 < len(work):
            upcoming = scores_of(*work[index + 1][:2])
        weights = jnp.exp2(scores * FACTOR)
        if kept is not None:
            weights = weights * kept
        part, total = times(weights, both(group, 1)), lanes(weights)
        num = part if num is None else num + part
        den = total if den is None else den + total
        if index + 1 == len(work) or work[index + 1][0] != head:
            cells = slice(head * HEAD_DIM, (head + 1) * HEAD_DIM)
            if finish:
                own_ref[:, cells] = num[:video]
                msg_ref[:, cells] = num[video:]
            else:
                num_ref[:, cells] = num
            packed = jnp.where(lane == first + head, jnp.sum(den, axis=1, keepdims=True), packed)
            num = den = None
    if finish:
        own_den_ref[...] = packed[:video]
        msg_ref[:, width:] = packed[video:]
        cache_copy.wait()
    else:
        den_ref[...] = packed


def last_kernel(first, qo_ref, qp_ref, num_ref, den_ref, far_ref, own_ref, own_den_ref, msg_ref):
    video, width = qo_ref.shape
    lane = lax.broadcasted_iota(jnp.int32, (2 * video, HEAD_DIM), 1)
    packed = den_ref[...]
    for head in range(width // HEAD_DIM):
        cells = slice(head * HEAD_DIM, (head + 1) * HEAD_DIM)
        queries = jnp.concatenate([qo_ref[:, cells], qp_ref[:, cells]], axis=0)
        weights = weigh(queries, far_ref[0, :, cells])
        num = num_ref[:, cells] + times(weights, far_ref[1, :, cells])
        own_ref[:, cells] = num[:video]
        msg_ref[:, cells] = num[video:]
        total = jnp.sum(lanes(weights), axis=1, keepdims=True)
        packed = packed + jnp.where(lane == first + head, total, 0.0)
    own_den_ref[...] = packed[:video]
    msg_ref[:, width:] = packed[video:]


def merge_kernel(first, own_ref, den_ref, msg_ref, att_ref):
    width = att_ref.shape[1]
    for head in range(width // HEAD_DIM):
        columns = slice(head * HEAD_DIM, (head + 1) * HEAD_DIM)
        lane = first + head
        num = own_ref[:, columns] + msg_ref[:, columns]
        den = den_ref[:, lane : lane + 1] + msg_ref[:, width + lane : width + lane + 1]
        att_ref[:, columns] = (num / den).astype(BF16)


def part_kernel(place_ref, weight_ref, first_ref, second_ref, out_ref, w_other_ref, w_ref, sems):
    depth = w_ref.shape[0]
    half = first_ref.shape[1]
    copies = []
    for index, (group, target) in enumerate(
        ((place_ref[0], w_ref), (1 - place_ref[0], w_other_ref))
    ):
        rows = pl.ds(pl.multiple_of(group * depth, depth), depth)
        copies.append(pltpu.make_async_copy(weight_ref.at[rows], target, sems.at[index]))
        copies[-1].start()
    copies[0].wait()
    out_ref[...] = jnp.dot(
        first_ref[...], w_ref[:half, :], preferred_element_type=F32
    ) + jnp.dot(second_ref[...], w_ref[half:, :], preferred_element_type=F32)
    copies[1].wait()


def more_kernel(part_ref, att_ref, w_ref, out_ref):
    half = att_ref.shape[1]
    out_ref[...] = part_ref[...] + jnp.dot(
        att_ref[...], w_ref[:half, :], preferred_element_type=F32
    )


def final_kernel(part_ref, att_ref, w_ref, hidden_ref, gate_ref, out_ref, buffer_ref, sems):
    half = att_ref.shape[1]
    gate = gate_ref[...].reshape(1, part_ref.shape[1])
    count = sems.shape[0]
    step = part_ref.shape[1] // count
    copies = []
    for index in range(count):
        cells = slice(index * step, (index + 1) * step)
        total = part_ref[:, cells] + jnp.dot(
            att_ref[...], w_ref[half:, cells], preferred_element_type=F32
        )
        mixed = hidden_ref[:, cells].astype(F32) + gate[:, cells] * total
        buffer_ref[:, cells] = mixed.astype(BF16)
        copies.append(
            pltpu.make_async_copy(buffer_ref.at[:, cells], out_ref.at[:, cells], sems.at[index])
        )
        copies[-1].start()
    for copy in copies:
        copy.wait()


def params(megabytes):
    return pltpu.CompilerParams(vmem_limit_bytes=megabytes * 1024 * 1024)


def in_hbm(array):
    return pltpu.with_memory_space_constraint(array, pltpu.HBM)


def cost(flops, nbytes, transcendentals=0):
    return pl.CostEstimate(
        flops=int(flops), bytes_accessed=int(nbytes), transcendentals=int(transcendentals)
    )


def plain_call(kernel, outs, name, estimate, *operands):
    return pl.pallas_call(
        kernel,
        in_specs=[pl.BlockSpec(memory_space=pltpu.VMEM)] * len(operands),
        out_specs=[pl.BlockSpec(memory_space=pltpu.VMEM)] * len(outs),
        out_shape=[jax.ShapeDtypeStruct(shape, dtype) for shape, dtype in outs],
        compiler_params=params(24),
        cost_estimate=estimate,
        name=name,
    )(*operands)


def ring_moves(sections):
    chips = sections // 2
    order = list(range(0, chips, 2)) + list(range(chips - 1, 0, -2))
    moves = [], []
    for here, there in zip(order, order[1:] + order[:1]):
        for core in range(2):
            moves[core].append((2 * here + core, 2 * there + core))
            moves[1 - core].append((2 * there + core, 2 * here + core))
    return sorted(moves[0]), sorted(moves[1])


def per_device(
    sections, hidden, text_hidden, text_mask, stale_cache, qkv_weight, out_weight, query_gain,
    key_gain, norm_shift, norm_scale, branch_gate,
):
    video, features = hidden.shape
    text = text_hidden.shape[0] // 2
    width = stale_cache.shape[2]
    heads = width // HEAD_DIM
    group_columns = heads * TRIPLE
    chips = sections // 2
    out_features = out_weight.shape[1]
    top = video + EXTRA
    rows = top + text

    group = lax.axis_index("head")
    core = lax.axis_index("section") % 2
    place = jnp.stack([group, core]).astype(jnp.int32)
    swap_core = [(s, s ^ 1) for s in range(sections)]
    swap_head = [(0, 1), (1, 0)]
    ways = ring_moves(sections)
    half_way = chips // 2

    def ring_step(blocks):
        return [lax.ppermute(block, "section", way) for block, way in zip(blocks, ways)]

    vmem = pl.BlockSpec(memory_space=pltpu.VMEM)
    hbm = pl.BlockSpec(memory_space=pltpu.HBM)
    smem = pl.BlockSpec(memory_space=pltpu.SMEM)
    whole = ring_step((stale_cache, stale_cache))

    columns = 2 * TRIPLE
    blocks = group_columns // columns
    per_head = head_rows(video, text)

    def project_cost(share):
        share = 8 * rows * features * group_columns * share
        return cost(share, share // (4 * rows))

    a_rows, message, stats, ahead = pl.pallas_call(
        send_kernel,
        in_specs=[smem] + [hbm] * 5,
        out_specs=[vmem] * 4,
        out_shape=[
            jax.ShapeDtypeStruct((rows, features), BF16),
            jax.ShapeDtypeStruct((per_head + 2 * EXTRA, HEAD_DIM), BF16),
            jax.ShapeDtypeStruct((rows, HEAD_DIM), F32),
            jax.ShapeDtypeStruct((features, columns), BF16),
        ],
        scratch_shapes=[
            pltpu.VMEM((video, features), BF16),
            pltpu.VMEM((text, features), BF16),
            pltpu.VMEM((features,), F32),
            pltpu.VMEM((features,), F32),
            pltpu.VMEM((features, TRIPLE), BF16),
            pltpu.SemaphoreType.DMA((6,)),
        ],
        compiler_params=params(40),
        cost_estimate=project_cost(0.4),
        name="project_send",
    )(place, *map(in_hbm, (hidden, text_hidden, norm_scale, norm_shift, qkv_weight)))
    received = lax.ppermute(message, "head", swap_head)

    message_more, own_ahead = pl.pallas_call(
        functools.partial(send_more_kernel, video),
        in_specs=[smem, vmem, vmem, hbm],
        out_specs=[vmem] * 2,
        out_shape=[
            jax.ShapeDtypeStruct(((heads - 1) * per_head, HEAD_DIM), BF16),
            jax.ShapeDtypeStruct((features, columns), BF16),
        ],
        scratch_shapes=[
            pltpu.VMEM((features, group_columns - columns - 2 * TRIPLE), BF16),
            pltpu.VMEM((features, TRIPLE), BF16),
            pltpu.SemaphoreType.DMA((3,)),
        ],
        compiler_params=params(40),
        cost_estimate=project_cost(0.6),
        name="project_send_more",
    )(place, a_rows, ahead, in_hbm(qkv_weight))
    received_more = lax.ppermute(message_more, "head", swap_head)

    split = plain_call(
        split_kernel, [((2, video, width // 2), BF16)] * 4, "split_heads", cost(0, 8 * video * width),
        *lax.optimization_barrier((*whole, message_more, received))[:2],
    )
    chains = [[ring_step((split[0], split[2]))], [ring_step((split[1], split[3]))]]

    small = (query_gain, key_gain, text_mask, branch_gate, hidden, stale_cache)
    outs = pl.pallas_call(
        own_kernel,
        in_specs=[smem, vmem, vmem, hbm] + [hbm] * len(small),
        out_specs=[vmem] * (2 + len(small)),
        out_shape=[
            jax.ShapeDtypeStruct((top, group_columns), F32),
            jax.ShapeDtypeStruct((text, 2 * width), F32),
        ]
        + [jax.ShapeDtypeStruct(array.shape, array.dtype) for array in small],
        scratch_shapes=[
            pltpu.VMEM((blocks - 1, features, columns), BF16),
            pltpu.SemaphoreType.DMA((blocks - 1 + len(small),)),
        ],
        compiler_params=params(40),
        cost_estimate=project_cost(1),
        name="project_own",
    )(place, a_rows, own_ahead, *map(in_hbm, (qkv_weight,) + small))
    own, own_text = outs[:2]
    query_gain, key_gain, text_mask, branch_gate, hidden, stale = outs[2:]

    for _ in range(half_way - 3):
        for chain in chains:
            chain.append(ring_step(lax.optimization_barrier((*chain[-1], own))[:2]))
    far = [lax.ppermute(chains[0][-1][0], "section", ways[0])]

    received_more = lax.optimization_barrier((received_more, *chains[0][0], *chains[1][0]))[0]
    *queries, fresh = plain_call(
        functools.partial(norm_kernel, features * 2, text),
        [((video, width // 2), BF16)] * 2 + [((2, video, width), BF16)],
        "norm_video",
        cost(1000 * top * group_columns, 8 * top * group_columns),
        own, received, received_more, stats, query_gain, key_gain,
    )
    other_queries = [lax.ppermute(half, "section", swap_core) for half in queries]
    (text_kv,) = plain_call(
        functools.partial(text_kernel, features * 2),
        [((2, text, width), BF16)],
        "norm_text",
        cost(text * group_columns, text * group_columns),
        own_text, received, received_more, stats, own, key_gain,
    )

    last = lax.optimization_barrier((chains[1][-1][0], text_kv, queries[0]))[0]
    far.append(lax.ppermute(last, "section", ways[0]))
    context = chips * video + video + text
    finished = [
        jax.ShapeDtypeStruct((video, width // 2), F32),
        jax.ShapeDtypeStruct((video, HEAD_DIM), F32),
        jax.ShapeDtypeStruct((video, width // 2 + HEAD_DIM), F32),
    ]
    attended, other_attended = [], []
    for index, chain in enumerate(chains):
        first = index * heads // 2
        halves = [block for step in chain for block in step]
        finish = index == 1
        own_queries = queries[index]
        if finish:
            halves.append(far[index])
            own_queries = lax.optimization_barrier((own_queries, num_own))[0]
            outs = finished + [jax.ShapeDtypeStruct(fresh.shape, BF16)]
        else:
            outs = [
                jax.ShapeDtypeStruct((2 * video, width // 2), F32),
                jax.ShapeDtypeStruct((2 * video, HEAD_DIM), F32),
            ]
        outs = pl.pallas_call(
            functools.partial(attend_kernel, first, len(whole)),
            in_specs=[smem] + [vmem] * (6 + len(whole) + len(halves)),
            out_specs=[vmem] * (len(outs) - finish) + [hbm] * finish,
            out_shape=outs,
            scratch_shapes=[pltpu.SemaphoreType.DMA] * finish,
            compiler_params=params(24),
            cost_estimate=cost(video * context, context * width, video * heads),
            name="attend",
        )(
            place, own_queries, other_queries[index], fresh, stale, text_kv, text_mask,
            *whole, *halves,
        )
        if finish:
            *outs, new_cache = outs
        else:
            outs = plain_call(
                functools.partial(last_kernel, first),
                [(out.shape, out.dtype) for out in finished],
                "attend_last",
                cost(video * video, video * width),
                own_queries, other_queries[index], *outs, far[index],
            )
        num_own, den_own, num_message = outs
        num_received = lax.ppermute(num_message, "section", swap_core)
        attended += plain_call(
            functools.partial(merge_kernel, first),
            [((video, width // 2), BF16)],
            "merge",
            cost(2 * video * width, 5 * video * width),
            num_own, den_own, num_received,
        )
        other_attended.append(lax.ppermute(attended[-1], "head", swap_head))

    out_cost = cost(4 * video * width * out_features, 2 * width * out_features)
    part, w_other = pl.pallas_call(
        part_kernel,
        in_specs=[smem, hbm, vmem, vmem],
        out_specs=[vmem] * 2,
        out_shape=[
            jax.ShapeDtypeStruct((video, out_features), F32),
            jax.ShapeDtypeStruct((width, out_features), BF16),
        ],
        scratch_shapes=[
            pltpu.VMEM((width, out_features), BF16),
            pltpu.SemaphoreType.DMA((2,)),
        ],
        compiler_params=params(24),
        cost_estimate=out_cost,
        name="part_out",
    )(place, in_hbm(out_weight), *attended)
    (part,) = plain_call(
        more_kernel, [((video, out_features), F32)], "more_out", out_cost,
        part, other_attended[0], w_other,
    )
    mixed = pl.pallas_call(
        final_kernel,
        in_specs=[vmem] * 5,
        out_specs=hbm,
        out_shape=jax.ShapeDtypeStruct((video, out_features), BF16),
        scratch_shapes=[
            pltpu.VMEM((video, out_features), BF16),
            pltpu.SemaphoreType.DMA((out_features // 512,)),
        ],
        compiler_params=params(24),
        cost_estimate=out_cost,
        name="final_out",
    )(part, other_attended[1], w_other, hidden, branch_gate)
    return (mixed, new_cache)


def solution(mesh):
    in_specs = (
        P("section", "head"),
        P(None, "head"),
        P(),
        P(None, "section", "head"),
        P("head", None),
        P(None, "head"),
        P(),
        P(),
        P("head"),
        P("head"),
        P("head"),
    )
    out_specs = (P("section", "head"), P(None, "section", "head"))
    return jax.shard_map(
        functools.partial(per_device, mesh.shape["section"]),
        mesh=mesh, in_specs=in_specs, out_specs=out_specs, check_vma=False,
    )
```

```python
import functools
import math

import jax
import jax.numpy as jnp
from jax import lax
from jax.experimental import pallas as pl
from jax.experimental.pallas import tpu as pltpu
from jax.sharding import PartitionSpec as P

HEAD_DIM = 128
TRIPLE = 3 * HEAD_DIM
EXTRA = 16
PIECE = 2 * HEAD_DIM
EPS = 1e-06
F32 = jnp.float32
BF16 = jnp.bfloat16


def split_bf16(value, parts):
    pieces = []
    rest = value
    for _ in range(parts):
        piece = rest.astype(BF16)
        pieces.append(piece)
        rest = rest - piece.astype(F32)
    return pieces


def head_rows(video, text):
    return 3 * video + 2 * text + EXTRA


def column_copy(w_ref, first, target, sem):
    columns = target.shape[1]
    start = pl.multiple_of(first, HEAD_DIM)
    return pltpu.make_async_copy(w_ref.at[:, pl.ds(start, columns)], target, sem)


def partial_sums(a_ref, w_ref, video, text, msg_ref, first):
    band = lax.broadcasted_iota(jnp.int32, (EXTRA, HEAD_DIM), 0) // 4
    top = video + EXTRA
    terms = None
    for start in range(0, w_ref.shape[1], PIECE):
        stop = min(start + PIECE, w_ref.shape[1])
        product = jnp.dot(a_ref[...], w_ref[:, start:stop], preferred_element_type=F32)
        for local in range(0, stop - start, HEAD_DIM):
            part = product[:, local : local + HEAD_DIM]
            head, kind = divmod((start + local) // HEAD_DIM, 3)
            base = (first + head) * head_rows(video, text)
            msg_ref[base + kind * video : base + (kind + 1) * video, :] = part[:video].astype(BF16)
            terms = part[video:top] if kind == 0 else jnp.where(band == kind, part[video:top], terms)
            base += 3 * video
            if kind:
                rows = slice(base + (kind - 1) * text, base + kind * text)
                msg_ref[rows, :] = part[top:].astype(BF16)
            if kind == 2:
                base += 2 * text
                msg_ref[base : base + EXTRA, :] = terms.astype(BF16)


def send_kernel(
    place_ref, x_ref, t_ref, scale_ref, shift_ref, w_ref,
    a_ref, msg_ref, stat_ref, ahead_ref,
    x_buffer, t_buffer, scale_buffer, shift_buffer, w_buffer, sems,
):
    video, features = x_buffer.shape
    text = t_buffer.shape[0]
    top = video + EXTRA
    columns = w_buffer.shape[1]
    base = (1 - place_ref[0]) * (w_ref.shape[1] // 2)
    copies = [
        pltpu.make_async_copy(scale_ref, scale_buffer, sems.at[0]),
        pltpu.make_async_copy(shift_ref, shift_buffer, sems.at[1]),
        pltpu.make_async_copy(x_ref, x_buffer, sems.at[2]),
        pltpu.make_async_copy(
            t_ref.at[pl.ds(pl.multiple_of(place_ref[1] * text, text), text)], t_buffer, sems.at[3]
        ),
        column_copy(w_ref, base, w_buffer, sems.at[4]),
        column_copy(w_ref, base + columns, ahead_ref, sems.at[5]),
    ]
    for copy in copies[:5]:
        copy.start()

    copies[0].wait()
    copies[1].wait()
    gain = 1.0 + scale_buffer[...].reshape(1, features)
    pieces = split_bf16(gain, 2) + split_bf16(shift_buffer[...].reshape(1, features), 2)
    row = lax.broadcasted_iota(jnp.int32, (EXTRA, features), 0)
    extra = jnp.zeros((EXTRA, features), F32)
    for index, piece in enumerate(pieces):
        extra = jnp.where(row % 4 == index, piece.astype(F32), extra)
    a_ref[video:top, :] = extra.astype(BF16)

    def prepare(rows_ref, start):
        rows = rows_ref[...].astype(F32)
        count = rows.shape[0]
        mean = jnp.sum(rows, axis=1, keepdims=True) * (1.0 / features)
        centered = rows - mean
        second = jnp.sum(centered * centered, axis=1, keepdims=True)
        a_ref[start : start + count, :] = (centered * gain).astype(BF16)
        lane = lax.broadcasted_iota(jnp.int32, (count, HEAD_DIM), 1)
        packed = jnp.zeros((count, HEAD_DIM), F32)
        for index, piece in enumerate(split_bf16(mean, 3) + split_bf16(second, 3)):
            packed = jnp.where(lane == index, piece.astype(F32), packed)
        stat_ref[start : start + count, :] = jnp.where(
            lane == 0, mean, jnp.where(lane == 1, second, 0.0)
        )
        return jnp.transpose(packed)[:EXTRA]

    copies[2].wait()
    copies[5].start()
    stats = [prepare(x_buffer, 0)]
    copies[3].wait()
    stats.append(prepare(t_buffer, top))
    stat_ref[video:top, :] = jnp.zeros((EXTRA, HEAD_DIM), F32)
    start = head_rows(video, text) * columns // TRIPLE
    msg_ref[start : start + 2 * EXTRA, :] = jnp.concatenate(stats, axis=0).astype(BF16)
    copies[4].wait()
    partial_sums(a_ref, w_buffer, video, text, msg_ref, 0)
    copies[5].wait()


def send_more_kernel(
    video, place_ref, a_ref, ahead_ref, w_ref, msg_ref, own_ahead_ref, w_buffer, last_buffer, sems,
):
    text = a_ref.shape[0] - video - EXTRA
    width = w_ref.shape[1] // 2
    other, own = (1 - place_ref[0]) * width, place_ref[0] * width
    first = width - last_buffer.shape[1]
    copies = [
        column_copy(w_ref, other + first - w_buffer.shape[1], w_buffer, sems.at[0]),
        column_copy(w_ref, other + first, last_buffer, sems.at[1]),
        column_copy(w_ref, own, own_ahead_ref, sems.at[2]),
    ]
    copies[0].start()
    copies[1].start()
    partial_sums(a_ref, ahead_ref, video, text, msg_ref, 0)
    copies[0].wait()
    copies[2].start()
    head = ahead_ref.shape[1] // TRIPLE
    partial_sums(a_ref, w_buffer, video, text, msg_ref, head)
    copies[1].wait()
    head += w_buffer.shape[1] // TRIPLE
    partial_sums(a_ref, last_buffer, video, text, msg_ref, head)
    copies[2].wait()


def own_kernel(place_ref, a_ref, ahead_ref, w_ref, *refs):
    small = (len(refs) - 4) // 2
    out_ref, text_ref = refs[small : small + 2]
    w_buffer, sems = refs[-2:]
    top = out_ref.shape[0]
    later, _, columns = w_buffer.shape
    base = place_ref[0] * (w_ref.shape[1] // 2) + columns
    copies = [
        column_copy(w_ref, base + index * columns, w_buffer.at[index], sems.at[index])
        for index in range(later)
    ]
    for source, target in zip(refs[:small], refs[small + 2 : -2]):
        copies.append(pltpu.make_async_copy(source, target, sems.at[len(copies)]))
    for copy in copies:
        copy.start()

    for block in range(later + 1):
        if block:
            copies[block - 1].wait()
        for start in range(0, columns, PIECE):
            cells = slice(start, start + PIECE)
            part = w_buffer[block - 1, :, cells] if block else ahead_ref[:, cells]
            product = jnp.dot(a_ref[...], part, preferred_element_type=F32)
            first = block * columns + start
            out_ref[:, first : first + PIECE] = product[:top]
            for local in range(0, PIECE, HEAD_DIM):
                head, kind = divmod((first + local) // HEAD_DIM, 3)
                if kind:
                    target = (2 * head + kind - 1) * HEAD_DIM
                    text_ref[:, target : target + HEAD_DIM] = product[
                        top:, local : local + HEAD_DIM
                    ]
    for copy in copies[later:]:
        copy.wait()


def row_stats(total_features, own, received):
    count = own.shape[0]
    received = received.astype(F32)
    padding = jnp.zeros((HEAD_DIM - received.shape[0], count), F32)
    received = jnp.transpose(jnp.concatenate([received, padding], axis=0))
    parts = [received[:, index : index + 1] for index in range(6)]
    gap = 0.5 * (own[:, 0:1] - (parts[0] + parts[1] + parts[2]))
    second = own[:, 1:2] + (parts[3] + parts[4] + parts[5])
    var = second * (1.0 / total_features) + gap * gap
    return gap, lax.rsqrt(var + EPS)


def column_terms(own_ref, msg_ref, video, base, part):
    other = msg_ref[base : base + EXTRA, :].astype(F32)
    other = other[4 * (part % 3) : 4 * (part % 3) + 4]
    own = own_ref[video : video + 8, part * HEAD_DIM : (part + 1) * HEAD_DIM]
    scale = (own[0:1] + own[1:2]) - (other[0:1] + other[1:2])
    shift = (own[2:3] + own[3:4]) + (other[2:3] + other[3:4])
    return scale, shift


def head_place(head, rows, first_ref, more_ref):
    early = first_ref.shape[0] // rows
    return (first_ref, head * rows) if head < early else (more_ref, (head - early) * rows)


def head_norm(part, gain):
    square = jnp.sum(part * part, axis=1, keepdims=True) * (1.0 / HEAD_DIM)
    return part * lax.rsqrt(square + EPS) * gain


def norm_kernel(
    total_features, text, own_ref, first_ref, more_ref, stat_ref, qg_ref, kg_ref,
    qa_ref, qb_ref, kv_ref,
):
    video = qa_ref.shape[0]
    half = qa_ref.shape[1] // HEAD_DIM
    rows = head_rows(video, text)
    query_gain = qg_ref[...].reshape(1, HEAD_DIM)
    key_gain = kg_ref[...].reshape(1, HEAD_DIM)
    start = first_ref.shape[0] - 2 * EXTRA
    gap, inverse = row_stats(
        total_features, stat_ref[:video, :], first_ref[start : start + EXTRA, :video]
    )
    for head in range(2 * half):
        msg_ref, base = head_place(head, rows, first_ref, more_ref)

        def total(kind):
            part = 3 * head + kind
            scale, shift = column_terms(own_ref, msg_ref, video, base + rows - EXTRA, part)
            other = msg_ref[base + kind * video : base + (kind + 1) * video, :].astype(F32)
            both = own_ref[:video, part * HEAD_DIM : (part + 1) * HEAD_DIM] + other
            return (both + gap * scale) * inverse + shift

        columns = slice(head * HEAD_DIM, (head + 1) * HEAD_DIM)
        cells = slice(head % half * HEAD_DIM, (head % half + 1) * HEAD_DIM)
        q_ref = qa_ref if head < half else qb_ref
        q_ref[:, cells] = head_norm(total(0), query_gain).astype(BF16)
        kv_ref[0, :, columns] = head_norm(total(1), key_gain).astype(BF16)
        kv_ref[1, :, columns] = total(2).astype(BF16)


def text_kernel(
    total_features, own_ref, first_ref, more_ref, stat_ref, top_ref, kg_ref, kv_ref
):
    text = kv_ref.shape[1]
    heads = kv_ref.shape[2] // HEAD_DIM
    video = top_ref.shape[0] - EXTRA
    rows = head_rows(video, text)
    key_gain = kg_ref[...].reshape(1, HEAD_DIM)
    start = first_ref.shape[0] - EXTRA
    gap, inverse = row_stats(
        total_features, stat_ref[video + EXTRA :, :], first_ref[start : start + EXTRA, :text]
    )
    for head in range(heads):
        msg_ref, base = head_place(head, rows, first_ref, more_ref)

        def total(kind):
            scale, shift = column_terms(
                top_ref, msg_ref, video, base + rows - EXTRA, 3 * head + 1 + kind
            )
            start = base + 3 * video + kind * text
            other = msg_ref[start : start + text, :].astype(F32)
            first = (2 * head + kind) * HEAD_DIM
            return (own_ref[:, first : first + HEAD_DIM] + other + gap * scale) * inverse + shift

        columns = slice(head * HEAD_DIM, (head + 1) * HEAD_DIM)
        kv_ref[0, :, columns] = head_norm(total(0), key_gain).astype(BF16)
        kv_ref[1, :, columns] = total(1).astype(BF16)


FACTOR = math.log2(math.e) / math.sqrt(HEAD_DIM)


def split_kernel(*refs):
    count = len(refs) // 3
    for index in range(count):
        half = refs[index].shape[2] // 2
        refs[count + 2 * index][...] = refs[index][:, :, :half]
        refs[count + 2 * index + 1][...] = refs[index][:, :, half:]


def weigh(rows, keys):
    scores = lax.dot_general(rows, keys, (((1,), (1,)), ((), ())), preferred_element_type=F32)
    return jnp.exp2(scores * FACTOR)


def lanes(weights):
    total = weights[:, :HEAD_DIM]
    for start in range(HEAD_DIM, weights.shape[1], HEAD_DIM):
        total = total + weights[:, start : start + HEAD_DIM]
    return total


def times(weights, values):
    return jnp.dot(weights.astype(BF16), values, preferred_element_type=F32)


def both(group, index):
    return jnp.concatenate([ref[index, :, part] for ref, part in group], axis=0)


def attend_kernel(
    first, count, place_ref, qo_ref, qp_ref, fresh_ref, stale_ref, text_ref, mask_ref, *refs,
):
    copy_out = len(refs[-1].shape) == 0
    if copy_out:
        *refs, cache_ref, sem = refs
        cache_copy = pltpu.make_async_copy(fresh_ref, cache_ref, sem)
        cache_copy.start()
    *refs, own_ref, own_den_ref, msg_ref = refs
    video, width = qo_ref.shape
    text = text_ref.shape[1]
    lane = lax.broadcasted_iota(jnp.int32, (2 * video, HEAD_DIM), 1)
    mask = mask_ref[...].reshape(1, 2 * text).astype(F32)
    mask = jnp.where(place_ref[1] == 0, mask[:, :text], mask[:, text:])
    keep = jnp.concatenate([jnp.ones((1, video), F32), mask], axis=1)
    same_patch = (
        (lax.broadcasted_iota(jnp.int32, (2 * video, 2 * video), 0) < video)
        == (lax.broadcasted_iota(jnp.int32, (2 * video, 2 * video), 1) < video)
    ).astype(F32)
    packed = jnp.zeros((2 * video, HEAD_DIM), F32)

    def scores_of(head, group):
        cells = slice(head * HEAD_DIM, (head + 1) * HEAD_DIM)
        queries = jnp.concatenate([qo_ref[:, cells], qp_ref[:, cells]], axis=0)
        return lax.dot_general(
            queries, both(group, 0), (((1,), (1,)), ((), ())), preferred_element_type=F32
        )

    work = []
    for head in range(width // HEAD_DIM):
        cells = slice(head * HEAD_DIM, (head + 1) * HEAD_DIM)
        columns = slice((first + head) * HEAD_DIM, (first + head + 1) * HEAD_DIM)
        blocks = [(ref, columns) for ref in refs[:count]] + [(ref, cells) for ref in refs[count:]]
        blocks.append((text_ref, columns))
        work.append((head, [(fresh_ref, columns), (stale_ref, columns)], same_patch))
        odd = len(blocks) % 2
        if odd:
            work.append((head, blocks[:1], None))
        for start in range(odd, len(blocks), 2):
            last = start + 2 == len(blocks)
            work.append((head, blocks[start : start + 2], keep if last else None))

    upcoming = scores_of(*work[0][:2])
    num = den = None
    for index, (head, group, kept) in enumerate(work):
        scores = upcoming
        if index + 1 < len(work):
            upcoming = scores_of(*work[index + 1][:2])
        weights = jnp.exp2(scores * FACTOR)
        if kept is not None:
            weights = weights * kept
        part, total = times(weights, both(group, 1)), lanes(weights)
        num = part if num is None else num + part
        den = total if den is None else den + total
        if index + 1 == len(work) or work[index + 1][0] != head:
            cells = slice(head * HEAD_DIM, (head + 1) * HEAD_DIM)
            own_ref[:, cells] = num[:video]
            msg_ref[:, cells] = num[video:]
            packed = jnp.where(lane == first + head, jnp.sum(den, axis=1, keepdims=True), packed)
            num = den = None
    own_den_ref[...] = packed[:video]
    msg_ref[:, width:] = packed[video:]
    if copy_out:
        cache_copy.wait()


def merge_kernel(first, own_ref, den_ref, msg_ref, att_ref):
    width = att_ref.shape[1]
    for head in range(width // HEAD_DIM):
        columns = slice(head * HEAD_DIM, (head + 1) * HEAD_DIM)
        lane = first + head
        num = own_ref[:, columns] + msg_ref[:, columns]
        den = den_ref[:, lane : lane + 1] + msg_ref[:, width + lane : width + lane + 1]
        att_ref[:, columns] = (num / den).astype(BF16)


def part_kernel(place_ref, weight_ref, first_ref, second_ref, out_ref, w_other_ref, w_ref, sems):
    depth = w_ref.shape[0]
    half = first_ref.shape[1]
    copies = []
    for index, (group, target) in enumerate(
        ((place_ref[0], w_ref), (1 - place_ref[0], w_other_ref))
    ):
        rows = pl.ds(pl.multiple_of(group * depth, depth), depth)
        copies.append(pltpu.make_async_copy(weight_ref.at[rows], target, sems.at[index]))
        copies[-1].start()
    copies[0].wait()
    out_ref[...] = jnp.dot(
        first_ref[...], w_ref[:half, :], preferred_element_type=F32
    ) + jnp.dot(second_ref[...], w_ref[half:, :], preferred_element_type=F32)
    copies[1].wait()


def more_kernel(part_ref, att_ref, w_ref, out_ref):
    half = att_ref.shape[1]
    out_ref[...] = part_ref[...] + jnp.dot(
        att_ref[...], w_ref[:half, :], preferred_element_type=F32
    )


def final_kernel(part_ref, att_ref, w_ref, hidden_ref, gate_ref, out_ref, buffer_ref, sems):
    half = att_ref.shape[1]
    gate = gate_ref[...].reshape(1, part_ref.shape[1])
    count = sems.shape[0]
    step = part_ref.shape[1] // count
    copies = []
    for index in range(count):
        cells = slice(index * step, (index + 1) * step)
        total = part_ref[:, cells] + jnp.dot(
            att_ref[...], w_ref[half:, cells], preferred_element_type=F32
        )
        mixed = hidden_ref[:, cells].astype(F32) + gate[:, cells] * total
        buffer_ref[:, cells] = mixed.astype(BF16)
        copies.append(
            pltpu.make_async_copy(buffer_ref.at[:, cells], out_ref.at[:, cells], sems.at[index])
        )
        copies[-1].start()
    for copy in copies:
        copy.wait()


def params(megabytes):
    return pltpu.CompilerParams(vmem_limit_bytes=megabytes * 1024 * 1024)


def in_hbm(array):
    return pltpu.with_memory_space_constraint(array, pltpu.HBM)


def cost(flops, nbytes, transcendentals=0):
    return pl.CostEstimate(
        flops=int(flops), bytes_accessed=int(nbytes), transcendentals=int(transcendentals)
    )


def plain_call(kernel, outs, name, estimate, *operands):
    return pl.pallas_call(
        kernel,
        in_specs=[pl.BlockSpec(memory_space=pltpu.VMEM)] * len(operands),
        out_specs=[pl.BlockSpec(memory_space=pltpu.VMEM)] * len(outs),
        out_shape=[jax.ShapeDtypeStruct(shape, dtype) for shape, dtype in outs],
        compiler_params=params(24),
        cost_estimate=estimate,
        name=name,
    )(*operands)


def ring_moves(sections):
    chips = sections // 2
    order = list(range(0, chips, 2)) + list(range(chips - 1, 0, -2))
    moves = [], []
    for here, there in zip(order, order[1:] + order[:1]):
        for core in range(2):
            moves[core].append((2 * here + core, 2 * there + core))
            moves[1 - core].append((2 * there + core, 2 * here + core))
    return sorted(moves[0]), sorted(moves[1])


def per_device(
    sections, hidden, text_hidden, text_mask, stale_cache, qkv_weight, out_weight, query_gain,
    key_gain, norm_shift, norm_scale, branch_gate,
):
    video, features = hidden.shape
    text = text_hidden.shape[0] // 2
    width = stale_cache.shape[2]
    heads = width // HEAD_DIM
    group_columns = heads * TRIPLE
    chips = sections // 2
    out_features = out_weight.shape[1]
    top = video + EXTRA
    rows = top + text

    group = lax.axis_index("head")
    core = lax.axis_index("section") % 2
    place = jnp.stack([group, core]).astype(jnp.int32)
    swap_core = [(s, s ^ 1) for s in range(sections)]
    swap_head = [(0, 1), (1, 0)]
    ways = ring_moves(sections)
    half_way = chips // 2

    def ring_step(blocks):
        return [lax.ppermute(block, "section", way) for block, way in zip(blocks, ways)]

    vmem = pl.BlockSpec(memory_space=pltpu.VMEM)
    hbm = pl.BlockSpec(memory_space=pltpu.HBM)
    smem = pl.BlockSpec(memory_space=pltpu.SMEM)
    whole = ring_step((stale_cache, stale_cache))

    columns = 2 * TRIPLE
    blocks = group_columns // columns
    per_head = head_rows(video, text)

    def project_cost(share):
        share = 8 * rows * features * group_columns * share
        return cost(share, share // (4 * rows))

    a_rows, message, stats, ahead = pl.pallas_call(
        send_kernel,
        in_specs=[smem] + [hbm] * 5,
        out_specs=[vmem] * 4,
        out_shape=[
            jax.ShapeDtypeStruct((rows, features), BF16),
            jax.ShapeDtypeStruct((per_head + 2 * EXTRA, HEAD_DIM), BF16),
            jax.ShapeDtypeStruct((rows, HEAD_DIM), F32),
            jax.ShapeDtypeStruct((features, columns), BF16),
        ],
        scratch_shapes=[
            pltpu.VMEM((video, features), BF16),
            pltpu.VMEM((text, features), BF16),
            pltpu.VMEM((features,), F32),
            pltpu.VMEM((features,), F32),
            pltpu.VMEM((features, TRIPLE), BF16),
            pltpu.SemaphoreType.DMA((6,)),
        ],
        compiler_params=params(40),
        cost_estimate=project_cost(0.4),
        name="project_send",
    )(place, *map(in_hbm, (hidden, text_hidden, norm_scale, norm_shift, qkv_weight)))
    received = lax.ppermute(message, "head", swap_head)

    message_more, own_ahead = pl.pallas_call(
        functools.partial(send_more_kernel, video),
        in_specs=[smem, vmem, vmem, hbm],
        out_specs=[vmem] * 2,
        out_shape=[
            jax.ShapeDtypeStruct(((heads - 1) * per_head, HEAD_DIM), BF16),
            jax.ShapeDtypeStruct((features, columns), BF16),
        ],
        scratch_shapes=[
            pltpu.VMEM((features, group_columns - columns - 2 * TRIPLE), BF16),
            pltpu.VMEM((features, TRIPLE), BF16),
            pltpu.SemaphoreType.DMA((3,)),
        ],
        compiler_params=params(40),
        cost_estimate=project_cost(0.6),
        name="project_send_more",
    )(place, a_rows, ahead, in_hbm(qkv_weight))
    received_more = lax.ppermute(message_more, "head", swap_head)

    split = plain_call(
        split_kernel, [((2, video, width // 2), BF16)] * 4, "split_heads", cost(0, 8 * video * width),
        *lax.optimization_barrier((*whole, message_more, received))[:2],
    )
    chains = [[ring_step((split[0], split[2]))], [ring_step((split[1], split[3]))]]

    small = (query_gain, key_gain, text_mask, branch_gate, hidden, stale_cache)
    outs = pl.pallas_call(
        own_kernel,
        in_specs=[smem, vmem, vmem, hbm] + [hbm] * len(small),
        out_specs=[vmem] * (2 + len(small)),
        out_shape=[
            jax.ShapeDtypeStruct((top, group_columns), F32),
            jax.ShapeDtypeStruct((text, 2 * width), F32),
        ]
        + [jax.ShapeDtypeStruct(array.shape, array.dtype) for array in small],
        scratch_shapes=[
            pltpu.VMEM((blocks - 1, features, columns), BF16),
            pltpu.SemaphoreType.DMA((blocks - 1 + len(small),)),
        ],
        compiler_params=params(40),
        cost_estimate=project_cost(1),
        name="project_own",
    )(place, a_rows, own_ahead, *map(in_hbm, (qkv_weight,) + small))
    own, own_text = outs[:2]
    query_gain, key_gain, text_mask, branch_gate, hidden, stale = outs[2:]

    for _ in range(half_way - 3):
        for chain in chains:
            chain.append(ring_step(lax.optimization_barrier((*chain[-1], own))[:2]))
    far = [lax.ppermute(chain[-1][0], "section", ways[0]) for chain in chains]

    received_more = lax.optimization_barrier((received_more, *chains[0][0], *chains[1][0]))[0]
    *queries, fresh = plain_call(
        functools.partial(norm_kernel, features * 2, text),
        [((video, width // 2), BF16)] * 2 + [((2, video, width), BF16)],
        "norm_video",
        cost(1000 * top * group_columns, 8 * top * group_columns),
        own, received, received_more, stats, query_gain, key_gain,
    )
    other_queries = [lax.ppermute(half, "section", swap_core) for half in queries]
    (text_kv,) = plain_call(
        functools.partial(text_kernel, features * 2),
        [((2, text, width), BF16)],
        "norm_text",
        cost(text * group_columns, text * group_columns),
        own_text, received, received_more, stats, own, key_gain,
    )

    context = chips * video + video + text
    attended, other_attended = [], []
    for index, chain in enumerate(chains):
        first = index * heads // 2
        halves = [block for step in chain for block in step] + [far[index]]
        copy_out = index == 1
        own_queries = queries[index]
        if copy_out:
            own_queries = lax.optimization_barrier((own_queries, num_own))[0]
        num_own, den_own, num_message, *copied = pl.pallas_call(
            functools.partial(attend_kernel, first, len(whole)),
            in_specs=[smem] + [vmem] * (6 + len(whole) + len(halves)),
            out_specs=[vmem] * 3 + [hbm] * copy_out,
            out_shape=[
                jax.ShapeDtypeStruct((video, width // 2), F32),
                jax.ShapeDtypeStruct((video, HEAD_DIM), F32),
                jax.ShapeDtypeStruct((video, width // 2 + HEAD_DIM), F32),
            ]
            + [jax.ShapeDtypeStruct(fresh.shape, BF16)] * copy_out,
            scratch_shapes=[pltpu.SemaphoreType.DMA] * copy_out,
            compiler_params=params(24),
            cost_estimate=cost(video * context, context * width, video * heads),
            name="attend",
        )(
            place, own_queries, other_queries[index], fresh, stale, text_kv, text_mask,
            *whole, *halves,
        )
        num_received = lax.ppermute(num_message, "section", swap_core)
        attended += plain_call(
            functools.partial(merge_kernel, first),
            [((video, width // 2), BF16)],
            "merge",
            cost(2 * video * width, 5 * video * width),
            num_own, den_own, num_received,
        )
        other_attended.append(lax.ppermute(attended[-1], "head", swap_head))

    out_cost = cost(4 * video * width * out_features, 2 * width * out_features)
    part, w_other = pl.pallas_call(
        part_kernel,
        in_specs=[smem, hbm, vmem, vmem],
        out_specs=[vmem] * 2,
        out_shape=[
            jax.ShapeDtypeStruct((video, out_features), F32),
            jax.ShapeDtypeStruct((width, out_features), BF16),
        ],
        scratch_shapes=[
            pltpu.VMEM((width, out_features), BF16),
            pltpu.SemaphoreType.DMA((2,)),
        ],
        compiler_params=params(24),
        cost_estimate=out_cost,
        name="part_out",
    )(place, in_hbm(out_weight), *attended)
    (part,) = plain_call(
        more_kernel, [((video, out_features), F32)], "more_out", out_cost,
        part, other_attended[0], w_other,
    )
    mixed = pl.pallas_call(
        final_kernel,
        in_specs=[vmem] * 5,
        out_specs=hbm,
        out_shape=jax.ShapeDtypeStruct((video, out_features), BF16),
        scratch_shapes=[
            pltpu.VMEM((video, out_features), BF16),
            pltpu.SemaphoreType.DMA((out_features // 512,)),
        ],
        compiler_params=params(24),
        cost_estimate=out_cost,
        name="final_out",
    )(part, other_attended[1], w_other, hidden, branch_gate)
    return (mixed, copied[0])


def solution(mesh):
    in_specs = (
        P("section", "head"),
        P(None, "head"),
        P(),
        P(None, "section", "head"),
        P("head", None),
        P(None, "head"),
        P(),
        P(),
        P("head"),
        P("head"),
        P("head"),
    )
    out_specs = (P("section", "head"), P(None, "section", "head"))
    return jax.shard_map(
        functools.partial(per_device, mesh.shape["section"]),
        mesh=mesh, in_specs=in_specs, out_specs=out_specs, check_vma=False,
    )
```

```python
import functools
import math

import jax
import jax.numpy as jnp
from jax import lax
from jax.experimental import pallas as pl
from jax.experimental.pallas import tpu as pltpu
from jax.sharding import PartitionSpec as P

HEAD_DIM = 128
TRIPLE = 3 * HEAD_DIM
EXTRA = 16
PIECE = 2 * HEAD_DIM
LOOK_AHEAD = 2
EPS = 1e-06
F32 = jnp.float32
BF16 = jnp.bfloat16


def split_bf16(value, parts):
    pieces = []
    rest = value
    for _ in range(parts):
        piece = rest.astype(BF16)
        pieces.append(piece)
        rest = rest - piece.astype(F32)
    return pieces


def head_rows(video, text):
    return 3 * video + 2 * text + EXTRA


def column_copy(w_ref, first, target, sem):
    columns = target.shape[1]
    start = pl.multiple_of(first, HEAD_DIM)
    return pltpu.make_async_copy(w_ref.at[:, pl.ds(start, columns)], target, sem)


def partial_sums(a_ref, w_ref, video, text, msg_ref, first):
    band = lax.broadcasted_iota(jnp.int32, (EXTRA, HEAD_DIM), 0) // 4
    top = video + EXTRA
    terms = None
    for start in range(0, w_ref.shape[1], PIECE):
        stop = min(start + PIECE, w_ref.shape[1])
        product = jnp.dot(a_ref[...], w_ref[:, start:stop], preferred_element_type=F32)
        for local in range(0, stop - start, HEAD_DIM):
            part = product[:, local : local + HEAD_DIM]
            head, kind = divmod((start + local) // HEAD_DIM, 3)
            base = (first + head) * head_rows(video, text)
            msg_ref[base + kind * video : base + (kind + 1) * video, :] = part[:video].astype(BF16)
            terms = part[video:top] if kind == 0 else jnp.where(band == kind, part[video:top], terms)
            base += 3 * video
            if kind:
                rows = slice(base + (kind - 1) * text, base + kind * text)
                msg_ref[rows, :] = part[top:].astype(BF16)
            if kind == 2:
                base += 2 * text
                msg_ref[base : base + EXTRA, :] = terms.astype(BF16)


def send_kernel(
    place_ref, x_ref, t_ref, scale_ref, shift_ref, w_ref,
    a_ref, msg_ref, stat_ref, ahead_ref,
    x_buffer, t_buffer, scale_buffer, shift_buffer, w_buffer, sems,
):
    video, features = x_buffer.shape
    text = t_buffer.shape[0]
    top = video + EXTRA
    columns = w_buffer.shape[1]
    base = (1 - place_ref[0]) * (w_ref.shape[1] // 2)
    copies = [
        pltpu.make_async_copy(scale_ref, scale_buffer, sems.at[0]),
        pltpu.make_async_copy(shift_ref, shift_buffer, sems.at[1]),
        pltpu.make_async_copy(x_ref, x_buffer, sems.at[2]),
        pltpu.make_async_copy(
            t_ref.at[pl.ds(pl.multiple_of(place_ref[1] * text, text), text)], t_buffer, sems.at[3]
        ),
        column_copy(w_ref, base, w_buffer, sems.at[4]),
        column_copy(w_ref, base + columns, ahead_ref, sems.at[5]),
    ]
    for copy in copies[:5]:
        copy.start()

    copies[0].wait()
    copies[1].wait()
    gain = 1.0 + scale_buffer[...].reshape(1, features)
    pieces = split_bf16(gain, 2) + split_bf16(shift_buffer[...].reshape(1, features), 2)
    row = lax.broadcasted_iota(jnp.int32, (EXTRA, features), 0)
    extra = jnp.zeros((EXTRA, features), F32)
    for index, piece in enumerate(pieces):
        extra = jnp.where(row % 4 == index, piece.astype(F32), extra)
    a_ref[video:top, :] = extra.astype(BF16)

    def prepare(rows_ref, start):
        rows = rows_ref[...].astype(F32)
        count = rows.shape[0]
        mean = jnp.sum(rows, axis=1, keepdims=True) * (1.0 / features)
        centered = rows - mean
        second = jnp.sum(centered * centered, axis=1, keepdims=True)
        a_ref[start : start + count, :] = (centered * gain).astype(BF16)
        lane = lax.broadcasted_iota(jnp.int32, (count, HEAD_DIM), 1)
        packed = jnp.zeros((count, HEAD_DIM), F32)
        for index, piece in enumerate(split_bf16(mean, 3) + split_bf16(second, 3)):
            packed = jnp.where(lane == index, piece.astype(F32), packed)
        stat_ref[start : start + count, :] = jnp.where(
            lane == 0, mean, jnp.where(lane == 1, second, 0.0)
        )
        return jnp.transpose(packed)[:EXTRA]

    copies[2].wait()
    copies[5].start()
    stats = [prepare(x_buffer, 0)]
    copies[3].wait()
    stats.append(prepare(t_buffer, top))
    stat_ref[video:top, :] = jnp.zeros((EXTRA, HEAD_DIM), F32)
    start = head_rows(video, text) * columns // TRIPLE
    msg_ref[start : start + 2 * EXTRA, :] = jnp.concatenate(stats, axis=0).astype(BF16)
    copies[4].wait()
    partial_sums(a_ref, w_buffer, video, text, msg_ref, 0)
    copies[5].wait()


def send_more_kernel(
    video, place_ref, a_ref, ahead_ref, w_ref, msg_ref, own_ahead_ref, w_buffer, last_buffer, sems,
):
    text = a_ref.shape[0] - video - EXTRA
    width = w_ref.shape[1] // 2
    other, own = (1 - place_ref[0]) * width, place_ref[0] * width
    first = width - last_buffer.shape[1]
    copies = [
        column_copy(w_ref, other + first - w_buffer.shape[1], w_buffer, sems.at[0]),
        column_copy(w_ref, other + first, last_buffer, sems.at[1]),
        column_copy(w_ref, own, own_ahead_ref, sems.at[2]),
    ]
    copies[0].start()
    copies[1].start()
    partial_sums(a_ref, ahead_ref, video, text, msg_ref, 0)
    copies[0].wait()
    copies[2].start()
    head = ahead_ref.shape[1] // TRIPLE
    partial_sums(a_ref, w_buffer, video, text, msg_ref, head)
    copies[1].wait()
    head += w_buffer.shape[1] // TRIPLE
    partial_sums(a_ref, last_buffer, video, text, msg_ref, head)
    copies[2].wait()


def own_kernel(place_ref, a_ref, ahead_ref, w_ref, *refs):
    small = (len(refs) - 4) // 2
    out_ref, text_ref = refs[small : small + 2]
    w_buffer, sems = refs[-2:]
    top = out_ref.shape[0]
    later, _, columns = w_buffer.shape
    base = place_ref[0] * (w_ref.shape[1] // 2) + columns
    copies = [
        column_copy(w_ref, base + index * columns, w_buffer.at[index], sems.at[index])
        for index in range(later)
    ]
    for source, target in zip(refs[:small], refs[small + 2 : -2]):
        copies.append(pltpu.make_async_copy(source, target, sems.at[len(copies)]))
    copies[0].start()

    for block in range(later + 1):
        if block:
            copies[block - 1].wait()
        if block == 1:
            for copy in copies[later:]:
                copy.start()
        for start in range(0, columns, PIECE):
            cells = slice(start, start + PIECE)
            part = w_buffer[block - 1, :, cells] if block else ahead_ref[:, cells]
            product = jnp.dot(a_ref[...], part, preferred_element_type=F32)
            first = block * columns + start
            out_ref[:, first : first + PIECE] = product[:top]
            for local in range(0, PIECE, HEAD_DIM):
                head, kind = divmod((first + local) // HEAD_DIM, 3)
                if kind:
                    target = (2 * head + kind - 1) * HEAD_DIM
                    text_ref[:, target : target + HEAD_DIM] = product[
                        top:, local : local + HEAD_DIM
                    ]
            if block == 0 and start == 0:
                for copy in copies[1:later]:
                    copy.start()
    for copy in copies[later:]:
        copy.wait()


def row_stats(total_features, own, received):
    count = own.shape[0]
    received = received.astype(F32)
    padding = jnp.zeros((HEAD_DIM - received.shape[0], count), F32)
    received = jnp.transpose(jnp.concatenate([received, padding], axis=0))
    parts = [received[:, index : index + 1] for index in range(6)]
    gap = 0.5 * (own[:, 0:1] - (parts[0] + parts[1] + parts[2]))
    second = own[:, 1:2] + (parts[3] + parts[4] + parts[5])
    var = second * (1.0 / total_features) + gap * gap
    return gap, lax.rsqrt(var + EPS)


def column_terms(own_ref, msg_ref, video, base, part):
    other = msg_ref[base : base + EXTRA, :].astype(F32)
    other = other[4 * (part % 3) : 4 * (part % 3) + 4]
    own = own_ref[video : video + 8, part * HEAD_DIM : (part + 1) * HEAD_DIM]
    scale = (own[0:1] + own[1:2]) - (other[0:1] + other[1:2])
    shift = (own[2:3] + own[3:4]) + (other[2:3] + other[3:4])
    return scale, shift


def head_place(head, rows, first_ref, more_ref):
    early = first_ref.shape[0] // rows
    return (first_ref, head * rows) if head < early else (more_ref, (head - early) * rows)


def head_norm(part, gain):
    square = jnp.sum(part * part, axis=1, keepdims=True) * (1.0 / HEAD_DIM)
    return part * lax.rsqrt(square + EPS) * gain


def norm_kernel(
    total_features, text, own_ref, first_ref, more_ref, stat_ref, qg_ref, kg_ref,
    qa_ref, qb_ref, kv_ref,
):
    video = qa_ref.shape[0]
    half = qa_ref.shape[1] // HEAD_DIM
    rows = head_rows(video, text)
    query_gain = qg_ref[...].reshape(1, HEAD_DIM)
    key_gain = kg_ref[...].reshape(1, HEAD_DIM)
    start = first_ref.shape[0] - 2 * EXTRA
    gap, inverse = row_stats(
        total_features, stat_ref[:video, :], first_ref[start : start + EXTRA, :video]
    )
    for head in range(2 * half):
        msg_ref, base = head_place(head, rows, first_ref, more_ref)

        def total(kind):
            part = 3 * head + kind
            scale, shift = column_terms(own_ref, msg_ref, video, base + rows - EXTRA, part)
            other = msg_ref[base + kind * video : base + (kind + 1) * video, :].astype(F32)
            both = own_ref[:video, part * HEAD_DIM : (part + 1) * HEAD_DIM] + other
            return (both + gap * scale) * inverse + shift

        columns = slice(head * HEAD_DIM, (head + 1) * HEAD_DIM)
        cells = slice(head % half * HEAD_DIM, (head % half + 1) * HEAD_DIM)
        q_ref = qa_ref if head < half else qb_ref
        q_ref[:, cells] = head_norm(total(0), query_gain).astype(BF16)
        kv_ref[0, :, columns] = head_norm(total(1), key_gain).astype(BF16)
        kv_ref[1, :, columns] = total(2).astype(BF16)


def text_kernel(
    total_features, own_ref, first_ref, more_ref, stat_ref, top_ref, kg_ref, kv_ref
):
    text = kv_ref.shape[1]
    heads = kv_ref.shape[2] // HEAD_DIM
    video = top_ref.shape[0] - EXTRA
    rows = head_rows(video, text)
    key_gain = kg_ref[...].reshape(1, HEAD_DIM)
    start = first_ref.shape[0] - EXTRA
    gap, inverse = row_stats(
        total_features, stat_ref[video + EXTRA :, :], first_ref[start : start + EXTRA, :text]
    )
    for head in range(heads):
        msg_ref, base = head_place(head, rows, first_ref, more_ref)

        def total(kind):
            scale, shift = column_terms(
                top_ref, msg_ref, video, base + rows - EXTRA, 3 * head + 1 + kind
            )
            start = base + 3 * video + kind * text
            other = msg_ref[start : start + text, :].astype(F32)
            first = (2 * head + kind) * HEAD_DIM
            return (own_ref[:, first : first + HEAD_DIM] + other + gap * scale) * inverse + shift

        columns = slice(head * HEAD_DIM, (head + 1) * HEAD_DIM)
        kv_ref[0, :, columns] = head_norm(total(0), key_gain).astype(BF16)
        kv_ref[1, :, columns] = total(1).astype(BF16)


FACTOR = math.log2(math.e) / math.sqrt(HEAD_DIM)


def split_kernel(*refs):
    count = len(refs) // 3
    for index in range(count):
        half = refs[index].shape[2] // 2
        refs[count + 2 * index][...] = refs[index][:, :, :half]
        refs[count + 2 * index + 1][...] = refs[index][:, :, half:]


def weigh(rows, keys):
    scores = lax.dot_general(rows, keys, (((1,), (1,)), ((), ())), preferred_element_type=F32)
    return jnp.exp2(scores * FACTOR)


def lanes(weights):
    total = weights[:, :HEAD_DIM]
    for start in range(HEAD_DIM, weights.shape[1], HEAD_DIM):
        total = total + weights[:, start : start + HEAD_DIM]
    return total


def times(weights, values):
    return jnp.dot(weights.astype(BF16), values, preferred_element_type=F32)


def both(group, index):
    return jnp.concatenate([ref[index, :, part] for ref, part in group], axis=0)


def attend_kernel(
    first, count, place_ref, qo_ref, qp_ref, fresh_ref, stale_ref, text_ref, mask_ref, *refs,
):
    copy_out = len(refs[-1].shape) == 0
    if copy_out:
        *refs, cache_ref, sem = refs
        cache_copy = pltpu.make_async_copy(fresh_ref, cache_ref, sem)
        cache_copy.start()
    *refs, own_ref, own_den_ref, msg_ref = refs
    video, width = qo_ref.shape
    text = text_ref.shape[1]
    lane = lax.broadcasted_iota(jnp.int32, (2 * video, HEAD_DIM), 1)
    mask = mask_ref[...].reshape(1, 2 * text).astype(F32)
    mask = jnp.where(place_ref[1] == 0, mask[:, :text], mask[:, text:])
    keep = jnp.concatenate([jnp.ones((1, video), F32), mask], axis=1)
    same_patch = (
        (lax.broadcasted_iota(jnp.int32, (2 * video, 2 * video), 0) < video)
        == (lax.broadcasted_iota(jnp.int32, (2 * video, 2 * video), 1) < video)
    ).astype(F32)
    packed = jnp.zeros((2 * video, HEAD_DIM), F32)

    def scores_of(head, group):
        cells = slice(head * HEAD_DIM, (head + 1) * HEAD_DIM)
        queries = jnp.concatenate([qo_ref[:, cells], qp_ref[:, cells]], axis=0)
        return lax.dot_general(
            queries, both(group, 0), (((1,), (1,)), ((), ())), preferred_element_type=F32
        )

    work = []
    for head in range(width // HEAD_DIM):
        cells = slice(head * HEAD_DIM, (head + 1) * HEAD_DIM)
        columns = slice((first + head) * HEAD_DIM, (first + head + 1) * HEAD_DIM)
        blocks = [(ref, columns) for ref in refs[:count]] + [(ref, cells) for ref in refs[count:]]
        blocks.append((text_ref, columns))
        work.append((head, [(fresh_ref, columns), (stale_ref, columns)], same_patch))
        odd = len(blocks) % 2
        if odd:
            work.append((head, blocks[:1], None))
        for start in range(odd, len(blocks), 2):
            last = start + 2 == len(blocks)
            work.append((head, blocks[start : start + 2], keep if last else None))

    upcoming = [scores_of(*item[:2]) for item in work[:LOOK_AHEAD]]
    num = den = None
    for index, (head, group, kept) in enumerate(work):
        scores = upcoming.pop(0)
        if index + LOOK_AHEAD < len(work):
            upcoming.append(scores_of(*work[index + LOOK_AHEAD][:2]))
        weights = jnp.exp2(scores * FACTOR)
        if kept is not None:
            weights = weights * kept
        part, total = times(weights, both(group, 1)), lanes(weights)
        num = part if num is None else num + part
        den = total if den is None else den + total
        if index + 1 == len(work) or work[index + 1][0] != head:
            cells = slice(head * HEAD_DIM, (head + 1) * HEAD_DIM)
            own_ref[:, cells] = num[:video]
            msg_ref[:, cells] = num[video:]
            packed = jnp.where(lane == first + head, jnp.sum(den, axis=1, keepdims=True), packed)
            num = den = None
    own_den_ref[...] = packed[:video]
    msg_ref[:, width:] = packed[video:]
    if copy_out:
        cache_copy.wait()


def merge_kernel(first, own_ref, den_ref, msg_ref, att_ref):
    width = att_ref.shape[1]
    for head in range(width // HEAD_DIM):
        columns = slice(head * HEAD_DIM, (head + 1) * HEAD_DIM)
        lane = first + head
        num = own_ref[:, columns] + msg_ref[:, columns]
        den = den_ref[:, lane : lane + 1] + msg_ref[:, width + lane : width + lane + 1]
        att_ref[:, columns] = (num / den).astype(BF16)


def part_kernel(
    place_ref, weight_ref, hidden_ref, first_ref, second_ref, out_ref, w_other_ref, hidden_copy_ref,
    w_ref, sems,
):
    depth = w_ref.shape[0]
    half = first_ref.shape[1]
    copies = []
    for index, (group, target) in enumerate(
        ((place_ref[0], w_ref), (1 - place_ref[0], w_other_ref))
    ):
        rows = pl.ds(pl.multiple_of(group * depth, depth), depth)
        copies.append(pltpu.make_async_copy(weight_ref.at[rows], target, sems.at[index]))
    copies.append(pltpu.make_async_copy(hidden_ref, hidden_copy_ref, sems.at[2]))
    for copy in copies:
        copy.start()
    copies[0].wait()
    out_ref[...] = jnp.dot(
        first_ref[...], w_ref[:half, :], preferred_element_type=F32
    ) + jnp.dot(second_ref[...], w_ref[half:, :], preferred_element_type=F32)
    for copy in copies[1:]:
        copy.wait()


def more_kernel(part_ref, att_ref, w_ref, out_ref):
    half = att_ref.shape[1]
    out_ref[...] = part_ref[...] + jnp.dot(
        att_ref[...], w_ref[:half, :], preferred_element_type=F32
    )


def final_kernel(part_ref, att_ref, w_ref, hidden_ref, gate_ref, out_ref, buffer_ref, sems):
    half = att_ref.shape[1]
    gate = gate_ref[...].reshape(1, part_ref.shape[1])
    count = sems.shape[0]
    step = part_ref.shape[1] // count
    copies = []
    for index in range(count):
        cells = slice(index * step, (index + 1) * step)
        total = part_ref[:, cells] + jnp.dot(
            att_ref[...], w_ref[half:, cells], preferred_element_type=F32
        )
        mixed = hidden_ref[:, cells].astype(F32) + gate[:, cells] * total
        buffer_ref[:, cells] = mixed.astype(BF16)
        copies.append(
            pltpu.make_async_copy(buffer_ref.at[:, cells], out_ref.at[:, cells], sems.at[index])
        )
        copies[-1].start()
    for copy in copies:
        copy.wait()


def params(megabytes):
    return pltpu.CompilerParams(vmem_limit_bytes=megabytes * 1024 * 1024)


def in_hbm(array):
    return pltpu.with_memory_space_constraint(array, pltpu.HBM)


def cost(flops, nbytes, transcendentals=0):
    return pl.CostEstimate(
        flops=int(flops), bytes_accessed=int(nbytes), transcendentals=int(transcendentals)
    )


def plain_call(kernel, outs, name, estimate, *operands):
    return pl.pallas_call(
        kernel,
        in_specs=[pl.BlockSpec(memory_space=pltpu.VMEM)] * len(operands),
        out_specs=[pl.BlockSpec(memory_space=pltpu.VMEM)] * len(outs),
        out_shape=[jax.ShapeDtypeStruct(shape, dtype) for shape, dtype in outs],
        compiler_params=params(24),
        cost_estimate=estimate,
        name=name,
    )(*operands)


def ring_moves(sections):
    chips = sections // 2
    order = list(range(0, chips, 2)) + list(range(chips - 1, 0, -2))
    moves = [], []
    for here, there in zip(order, order[1:] + order[:1]):
        for core in range(2):
            moves[core].append((2 * here + core, 2 * there + core))
            moves[1 - core].append((2 * there + core, 2 * here + core))
    return sorted(moves[0]), sorted(moves[1])


def per_device(
    sections, hidden, text_hidden, text_mask, stale_cache, qkv_weight, out_weight, query_gain,
    key_gain, norm_shift, norm_scale, branch_gate,
):
    video, features = hidden.shape
    text = text_hidden.shape[0] // 2
    width = stale_cache.shape[2]
    heads = width // HEAD_DIM
    group_columns = heads * TRIPLE
    chips = sections // 2
    out_features = out_weight.shape[1]
    top = video + EXTRA
    rows = top + text

    group = lax.axis_index("head")
    core = lax.axis_index("section") % 2
    place = jnp.stack([group, core]).astype(jnp.int32)
    swap_core = [(s, s ^ 1) for s in range(sections)]
    swap_head = [(0, 1), (1, 0)]
    ways = ring_moves(sections)
    half_way = chips // 2

    def ring_step(blocks):
        return [lax.ppermute(block, "section", way) for block, way in zip(blocks, ways)]

    vmem = pl.BlockSpec(memory_space=pltpu.VMEM)
    hbm = pl.BlockSpec(memory_space=pltpu.HBM)
    smem = pl.BlockSpec(memory_space=pltpu.SMEM)
    whole = ring_step((stale_cache, stale_cache))

    columns = 2 * TRIPLE
    blocks = group_columns // columns
    per_head = head_rows(video, text)

    def project_cost(share):
        share = 8 * rows * features * group_columns * share
        return cost(share, share // (4 * rows))

    a_rows, message, stats, ahead = pl.pallas_call(
        send_kernel,
        in_specs=[smem] + [hbm] * 5,
        out_specs=[vmem] * 4,
        out_shape=[
            jax.ShapeDtypeStruct((rows, features), BF16),
            jax.ShapeDtypeStruct((per_head + 2 * EXTRA, HEAD_DIM), BF16),
            jax.ShapeDtypeStruct((rows, HEAD_DIM), F32),
            jax.ShapeDtypeStruct((features, columns), BF16),
        ],
        scratch_shapes=[
            pltpu.VMEM((video, features), BF16),
            pltpu.VMEM((text, features), BF16),
            pltpu.VMEM((features,), F32),
            pltpu.VMEM((features,), F32),
            pltpu.VMEM((features, TRIPLE), BF16),
            pltpu.SemaphoreType.DMA((6,)),
        ],
        compiler_params=params(40),
        cost_estimate=project_cost(0.4),
        name="project_send",
    )(place, *map(in_hbm, (hidden, text_hidden, norm_scale, norm_shift, qkv_weight)))
    received = lax.ppermute(message, "head", swap_head)

    message_more, own_ahead = pl.pallas_call(
        functools.partial(send_more_kernel, video),
        in_specs=[smem, vmem, vmem, hbm],
        out_specs=[vmem] * 2,
        out_shape=[
            jax.ShapeDtypeStruct(((heads - 1) * per_head, HEAD_DIM), BF16),
            jax.ShapeDtypeStruct((features, columns), BF16),
        ],
        scratch_shapes=[
            pltpu.VMEM((features, group_columns - columns - 2 * TRIPLE), BF16),
            pltpu.VMEM((features, TRIPLE), BF16),
            pltpu.SemaphoreType.DMA((3,)),
        ],
        compiler_params=params(40),
        cost_estimate=project_cost(0.6),
        name="project_send_more",
    )(place, a_rows, ahead, in_hbm(qkv_weight))
    received_more = lax.ppermute(message_more, "head", swap_head)

    split = plain_call(
        split_kernel, [((2, video, width // 2), BF16)] * 4, "split_heads", cost(0, 8 * video * width),
        *lax.optimization_barrier((*whole, message_more, received))[:2],
    )
    chains = [[ring_step((split[0], split[2]))], [ring_step((split[1], split[3]))]]

    small = (query_gain, key_gain, text_mask, branch_gate, stale_cache)
    outs = pl.pallas_call(
        own_kernel,
        in_specs=[smem, vmem, vmem, hbm] + [hbm] * len(small),
        out_specs=[vmem] * (2 + len(small)),
        out_shape=[
            jax.ShapeDtypeStruct((top, group_columns), F32),
            jax.ShapeDtypeStruct((text, 2 * width), F32),
        ]
        + [jax.ShapeDtypeStruct(array.shape, array.dtype) for array in small],
        scratch_shapes=[
            pltpu.VMEM((blocks - 1, features, columns), BF16),
            pltpu.SemaphoreType.DMA((blocks - 1 + len(small),)),
        ],
        compiler_params=params(40),
        cost_estimate=project_cost(1),
        name="project_own",
    )(place, a_rows, own_ahead, *map(in_hbm, (qkv_weight,) + small))
    own, own_text = outs[:2]
    query_gain, key_gain, text_mask, branch_gate, stale = outs[2:]

    for _ in range(half_way - 3):
        for chain in chains:
            chain.append(ring_step(lax.optimization_barrier((*chain[-1], own))[:2]))
    far = [lax.ppermute(chain[-1][0], "section", ways[0]) for chain in chains]

    received_more = lax.optimization_barrier((received_more, *chains[0][0], *chains[1][0]))[0]
    *queries, fresh = plain_call(
        functools.partial(norm_kernel, features * 2, text),
        [((video, width // 2), BF16)] * 2 + [((2, video, width), BF16)],
        "norm_video",
        cost(1000 * top * group_columns, 8 * top * group_columns),
        own, received, received_more, stats, query_gain, key_gain,
    )
    other_queries = [lax.ppermute(half, "section", swap_core) for half in queries]
    (text_kv,) = plain_call(
        functools.partial(text_kernel, features * 2),
        [((2, text, width), BF16)],
        "norm_text",
        cost(text * group_columns, text * group_columns),
        own_text, received, received_more, stats, own, key_gain,
    )

    context = chips * video + video + text
    attended, other_attended = [], []
    for index, chain in enumerate(chains):
        first = index * heads // 2
        halves = [block for step in chain for block in step] + [far[index]]
        copy_out = index == 1
        own_queries = queries[index]
        if copy_out:
            own_queries = lax.optimization_barrier((own_queries, num_own))[0]
        num_own, den_own, num_message, *copied = pl.pallas_call(
            functools.partial(attend_kernel, first, len(whole)),
            in_specs=[smem] + [vmem] * (6 + len(whole) + len(halves)),
            out_specs=[vmem] * 3 + [hbm] * copy_out,
            out_shape=[
                jax.ShapeDtypeStruct((video, width // 2), F32),
                jax.ShapeDtypeStruct((video, HEAD_DIM), F32),
                jax.ShapeDtypeStruct((video, width // 2 + HEAD_DIM), F32),
            ]
            + [jax.ShapeDtypeStruct(fresh.shape, BF16)] * copy_out,
            scratch_shapes=[pltpu.SemaphoreType.DMA] * copy_out,
            compiler_params=params(24),
            cost_estimate=cost(video * context, context * width, video * heads),
            name="attend",
        )(
            place, own_queries, other_queries[index], fresh, stale, text_kv, text_mask,
            *whole, *halves,
        )
        num_received = lax.ppermute(num_message, "section", swap_core)
        attended += plain_call(
            functools.partial(merge_kernel, first),
            [((video, width // 2), BF16)],
            "merge",
            cost(2 * video * width, 5 * video * width),
            num_own, den_own, num_received,
        )
        other_attended.append(lax.ppermute(attended[-1], "head", swap_head))

    out_cost = cost(4 * video * width * out_features, 2 * width * out_features)
    part, w_other, hidden = pl.pallas_call(
        part_kernel,
        in_specs=[smem, hbm, hbm, vmem, vmem],
        out_specs=[vmem] * 3,
        out_shape=[
            jax.ShapeDtypeStruct((video, out_features), F32),
            jax.ShapeDtypeStruct((width, out_features), BF16),
            jax.ShapeDtypeStruct(hidden.shape, BF16),
        ],
        scratch_shapes=[
            pltpu.VMEM((width, out_features), BF16),
            pltpu.SemaphoreType.DMA((3,)),
        ],
        compiler_params=params(24),
        cost_estimate=out_cost,
        name="part_out",
    )(place, in_hbm(out_weight), in_hbm(hidden), *attended)
    (part,) = plain_call(
        more_kernel, [((video, out_features), F32)], "more_out", out_cost,
        part, other_attended[0], w_other,
    )
    mixed = pl.pallas_call(
        final_kernel,
        in_specs=[vmem] * 5,
        out_specs=hbm,
        out_shape=jax.ShapeDtypeStruct((video, out_features), BF16),
        scratch_shapes=[
            pltpu.VMEM((video, out_features), BF16),
            pltpu.SemaphoreType.DMA((out_features // 512,)),
        ],
        compiler_params=params(24),
        cost_estimate=out_cost,
        name="final_out",
    )(part, other_attended[1], w_other, hidden, branch_gate)
    return (mixed, copied[0])


def solution(mesh):
    in_specs = (
        P("section", "head"),
        P(None, "head"),
        P(),
        P(None, "section", "head"),
        P("head", None),
        P(None, "head"),
        P(),
        P(),
        P("head"),
        P("head"),
        P("head"),
    )
    out_specs = (P("section", "head"), P(None, "section", "head"))
    return jax.shard_map(
        functools.partial(per_device, mesh.shape["section"]),
        mesh=mesh, in_specs=in_specs, out_specs=out_specs, check_vma=False,
    )
```

```python
import functools
import math

import jax
import jax.numpy as jnp
from jax import lax
from jax.experimental import pallas as pl
from jax.experimental.pallas import tpu as pltpu
from jax.sharding import PartitionSpec as P

HEAD_DIM = 128
TRIPLE = 3 * HEAD_DIM
EXTRA = 16
PIECE = 2 * HEAD_DIM
LOOK_AHEAD = 2
EPS = 1e-06
F32 = jnp.float32
BF16 = jnp.bfloat16


def split_bf16(value, parts):
    pieces = []
    rest = value
    for _ in range(parts):
        piece = rest.astype(BF16)
        pieces.append(piece)
        rest = rest - piece.astype(F32)
    return pieces


def head_rows(video, text):
    return 3 * video + 2 * text + EXTRA


def column_copy(w_ref, first, target, sem):
    columns = target.shape[1]
    start = pl.multiple_of(first, HEAD_DIM)
    return pltpu.make_async_copy(w_ref.at[:, pl.ds(start, columns)], target, sem)


def partial_sums(a_ref, w_ref, video, text, msg_ref, first):
    band = lax.broadcasted_iota(jnp.int32, (EXTRA, HEAD_DIM), 0) // 4
    top = video + EXTRA
    terms = None
    for start in range(0, w_ref.shape[1], PIECE):
        stop = min(start + PIECE, w_ref.shape[1])
        product = jnp.dot(a_ref[...], w_ref[:, start:stop], preferred_element_type=F32)
        for local in range(0, stop - start, HEAD_DIM):
            part = product[:, local : local + HEAD_DIM]
            head, kind = divmod((start + local) // HEAD_DIM, 3)
            base = (first + head) * head_rows(video, text)
            msg_ref[base + kind * video : base + (kind + 1) * video, :] = part[:video].astype(BF16)
            terms = part[video:top] if kind == 0 else jnp.where(band == kind, part[video:top], terms)
            base += 3 * video
            if kind:
                rows = slice(base + (kind - 1) * text, base + kind * text)
                msg_ref[rows, :] = part[top:].astype(BF16)
            if kind == 2:
                base += 2 * text
                msg_ref[base : base + EXTRA, :] = terms.astype(BF16)


def send_kernel(
    place_ref, x_ref, t_ref, scale_ref, shift_ref, w_ref,
    a_ref, msg_ref, stat_ref, ahead_ref,
    x_buffer, t_buffer, scale_buffer, shift_buffer, w_buffer, sems,
):
    video, features = x_buffer.shape
    text = t_buffer.shape[0]
    top = video + EXTRA
    columns = w_buffer.shape[1]
    base = (1 - place_ref[0]) * (w_ref.shape[1] // 2)
    copies = [
        pltpu.make_async_copy(scale_ref, scale_buffer, sems.at[0]),
        pltpu.make_async_copy(shift_ref, shift_buffer, sems.at[1]),
        pltpu.make_async_copy(x_ref, x_buffer, sems.at[2]),
        pltpu.make_async_copy(
            t_ref.at[pl.ds(pl.multiple_of(place_ref[1] * text, text), text)], t_buffer, sems.at[3]
        ),
        column_copy(w_ref, base, w_buffer, sems.at[4]),
        column_copy(w_ref, base + columns, ahead_ref, sems.at[5]),
    ]
    for copy in copies[:5]:
        copy.start()

    copies[0].wait()
    copies[1].wait()
    gain = 1.0 + scale_buffer[...].reshape(1, features)
    pieces = split_bf16(gain, 2) + split_bf16(shift_buffer[...].reshape(1, features), 2)
    row = lax.broadcasted_iota(jnp.int32, (EXTRA, features), 0)
    extra = jnp.zeros((EXTRA, features), F32)
    for index, piece in enumerate(pieces):
        extra = jnp.where(row % 4 == index, piece.astype(F32), extra)
    a_ref[video:top, :] = extra.astype(BF16)

    def prepare(rows_ref, start):
        rows = rows_ref[...].astype(F32)
        count = rows.shape[0]
        mean = jnp.sum(rows, axis=1, keepdims=True) * (1.0 / features)
        centered = rows - mean
        second = jnp.sum(centered * centered, axis=1, keepdims=True)
        a_ref[start : start + count, :] = (centered * gain).astype(BF16)
        lane = lax.broadcasted_iota(jnp.int32, (count, HEAD_DIM), 1)
        packed = jnp.zeros((count, HEAD_DIM), F32)
        for index, piece in enumerate(split_bf16(mean, 3) + split_bf16(second, 3)):
            packed = jnp.where(lane == index, piece.astype(F32), packed)
        stat_ref[start : start + count, :] = jnp.where(
            lane == 0, mean, jnp.where(lane == 1, second, 0.0)
        )
        return jnp.transpose(packed)[:EXTRA]

    copies[2].wait()
    copies[5].start()
    stats = [prepare(x_buffer, 0)]
    copies[3].wait()
    stats.append(prepare(t_buffer, top))
    stat_ref[video:top, :] = jnp.zeros((EXTRA, HEAD_DIM), F32)
    start = head_rows(video, text) * columns // TRIPLE
    msg_ref[start : start + 2 * EXTRA, :] = jnp.concatenate(stats, axis=0).astype(BF16)
    copies[4].wait()
    partial_sums(a_ref, w_buffer, video, text, msg_ref, 0)
    copies[5].wait()


def send_more_kernel(
    video, place_ref, a_ref, ahead_ref, w_ref, msg_ref, own_ahead_ref, w_buffer, last_buffer, sems,
):
    text = a_ref.shape[0] - video - EXTRA
    width = w_ref.shape[1] // 2
    other, own = (1 - place_ref[0]) * width, place_ref[0] * width
    first = width - last_buffer.shape[1]
    copies = [
        column_copy(w_ref, other + first - w_buffer.shape[1], w_buffer, sems.at[0]),
        column_copy(w_ref, other + first, last_buffer, sems.at[1]),
        column_copy(w_ref, own, own_ahead_ref, sems.at[2]),
    ]
    copies[0].start()
    copies[1].start()
    partial_sums(a_ref, ahead_ref, video, text, msg_ref, 0)
    copies[0].wait()
    copies[2].start()
    head = ahead_ref.shape[1] // TRIPLE
    partial_sums(a_ref, w_buffer, video, text, msg_ref, head)
    copies[1].wait()
    head += w_buffer.shape[1] // TRIPLE
    partial_sums(a_ref, last_buffer, video, text, msg_ref, head)
    copies[2].wait()


def own_kernel(place_ref, a_ref, ahead_ref, w_ref, *refs):
    small = (len(refs) - 4) // 2
    out_ref, text_ref = refs[small : small + 2]
    w_buffer, sems = refs[-2:]
    top = out_ref.shape[0]
    later, _, columns = w_buffer.shape
    base = place_ref[0] * (w_ref.shape[1] // 2) + columns
    copies = [
        column_copy(w_ref, base + index * columns, w_buffer.at[index], sems.at[index])
        for index in range(later)
    ]
    for source, target in zip(refs[:small], refs[small + 2 : -2]):
        copies.append(pltpu.make_async_copy(source, target, sems.at[len(copies)]))
    copies[0].start()

    for block in range(later + 1):
        if block:
            copies[block - 1].wait()
        if block == 1:
            for copy in copies[later:]:
                copy.start()
        for start in range(0, columns, PIECE):
            cells = slice(start, start + PIECE)
            part = w_buffer[block - 1, :, cells] if block else ahead_ref[:, cells]
            product = jnp.dot(a_ref[...], part, preferred_element_type=F32)
            first = block * columns + start
            out_ref[:, first : first + PIECE] = product[:top]
            for local in range(0, PIECE, HEAD_DIM):
                head, kind = divmod((first + local) // HEAD_DIM, 3)
                if kind:
                    target = (2 * head + kind - 1) * HEAD_DIM
                    text_ref[:, target : target + HEAD_DIM] = product[
                        top:, local : local + HEAD_DIM
                    ]
            if block == 0 and start == 0:
                for copy in copies[1:later]:
                    copy.start()
    for copy in copies[later:]:
        copy.wait()


def row_stats(total_features, own, received):
    count = own.shape[0]
    received = received.astype(F32)
    padding = jnp.zeros((HEAD_DIM - received.shape[0], count), F32)
    received = jnp.transpose(jnp.concatenate([received, padding], axis=0))
    parts = [received[:, index : index + 1] for index in range(6)]
    gap = 0.5 * (own[:, 0:1] - (parts[0] + parts[1] + parts[2]))
    second = own[:, 1:2] + (parts[3] + parts[4] + parts[5])
    var = second * (1.0 / total_features) + gap * gap
    return gap, lax.rsqrt(var + EPS)


def column_terms(own_ref, msg_ref, video, base, part):
    other = msg_ref[base : base + EXTRA, :].astype(F32)
    other = other[4 * (part % 3) : 4 * (part % 3) + 4]
    own = own_ref[video : video + 8, part * HEAD_DIM : (part + 1) * HEAD_DIM]
    scale = (own[0:1] + own[1:2]) - (other[0:1] + other[1:2])
    shift = (own[2:3] + own[3:4]) + (other[2:3] + other[3:4])
    return scale, shift


def head_place(head, rows, first_ref, more_ref):
    early = first_ref.shape[0] // rows
    return (first_ref, head * rows) if head < early else (more_ref, (head - early) * rows)


def head_norm(part, gain):
    square = jnp.sum(part * part, axis=1, keepdims=True) * (1.0 / HEAD_DIM)
    return part * lax.rsqrt(square + EPS) * gain


def norm_kernel(
    total_features, text, own_ref, first_ref, more_ref, stat_ref, qg_ref, kg_ref,
    qa_ref, qb_ref, kv_ref,
):
    video = qa_ref.shape[0]
    half = qa_ref.shape[1] // HEAD_DIM
    rows = head_rows(video, text)
    query_gain = qg_ref[...].reshape(1, HEAD_DIM)
    key_gain = kg_ref[...].reshape(1, HEAD_DIM)
    start = first_ref.shape[0] - 2 * EXTRA
    gap, inverse = row_stats(
        total_features, stat_ref[:video, :], first_ref[start : start + EXTRA, :video]
    )
    for head in range(2 * half):
        msg_ref, base = head_place(head, rows, first_ref, more_ref)

        def total(kind):
            part = 3 * head + kind
            scale, shift = column_terms(own_ref, msg_ref, video, base + rows - EXTRA, part)
            other = msg_ref[base + kind * video : base + (kind + 1) * video, :].astype(F32)
            both = own_ref[:video, part * HEAD_DIM : (part + 1) * HEAD_DIM] + other
            return (both + gap * scale) * inverse + shift

        columns = slice(head * HEAD_DIM, (head + 1) * HEAD_DIM)
        cells = slice(head % half * HEAD_DIM, (head % half + 1) * HEAD_DIM)
        q_ref = qa_ref if head < half else qb_ref
        q_ref[:, cells] = head_norm(total(0), query_gain).astype(BF16)
        kv_ref[0, :, columns] = head_norm(total(1), key_gain).astype(BF16)
        kv_ref[1, :, columns] = total(2).astype(BF16)


def text_kernel(
    total_features, own_ref, first_ref, more_ref, stat_ref, top_ref, kg_ref, kv_ref
):
    text = kv_ref.shape[1]
    heads = kv_ref.shape[2] // HEAD_DIM
    video = top_ref.shape[0] - EXTRA
    rows = head_rows(video, text)
    key_gain = kg_ref[...].reshape(1, HEAD_DIM)
    start = first_ref.shape[0] - EXTRA
    gap, inverse = row_stats(
        total_features, stat_ref[video + EXTRA :, :], first_ref[start : start + EXTRA, :text]
    )
    for head in range(heads):
        msg_ref, base = head_place(head, rows, first_ref, more_ref)

        def total(kind):
            scale, shift = column_terms(
                top_ref, msg_ref, video, base + rows - EXTRA, 3 * head + 1 + kind
            )
            start = base + 3 * video + kind * text
            other = msg_ref[start : start + text, :].astype(F32)
            first = (2 * head + kind) * HEAD_DIM
            return (own_ref[:, first : first + HEAD_DIM] + other + gap * scale) * inverse + shift

        columns = slice(head * HEAD_DIM, (head + 1) * HEAD_DIM)
        kv_ref[0, :, columns] = head_norm(total(0), key_gain).astype(BF16)
        kv_ref[1, :, columns] = total(1).astype(BF16)


FACTOR = math.log2(math.e) / math.sqrt(HEAD_DIM)


def split_kernel(*refs):
    count = len(refs) // 3
    for index in range(count):
        half = refs[index].shape[2] // 2
        refs[count + 2 * index][...] = refs[index][:, :, :half]
        refs[count + 2 * index + 1][...] = refs[index][:, :, half:]


def weigh(rows, keys):
    scores = lax.dot_general(rows, keys, (((1,), (1,)), ((), ())), preferred_element_type=F32)
    return jnp.exp2(scores * FACTOR)


def lanes(weights):
    total = weights[:, :HEAD_DIM]
    for start in range(HEAD_DIM, weights.shape[1], HEAD_DIM):
        total = total + weights[:, start : start + HEAD_DIM]
    return total


def times(weights, values):
    return jnp.dot(weights.astype(BF16), values, preferred_element_type=F32)


def both(group, index):
    return jnp.concatenate([ref[index, :, part] for ref, part in group], axis=0)


def attend_kernel(
    first, count, finish, place_ref, qo_ref, qp_ref, fresh_ref, stale_ref, text_ref, mask_ref, *refs,
):
    *refs, num_ref, den_ref = refs
    if finish:
        *refs, own_ref = refs
        own_den_ref, msg_ref = num_ref, den_ref
    video, width = qo_ref.shape
    text = text_ref.shape[1]
    lane = lax.broadcasted_iota(jnp.int32, (2 * video, HEAD_DIM), 1)
    mask = mask_ref[...].reshape(1, 2 * text).astype(F32)
    mask = jnp.where(place_ref[1] == 0, mask[:, :text], mask[:, text:])
    keep = jnp.concatenate([jnp.ones((1, video), F32), mask], axis=1)
    same_patch = (
        (lax.broadcasted_iota(jnp.int32, (2 * video, 2 * video), 0) < video)
        == (lax.broadcasted_iota(jnp.int32, (2 * video, 2 * video), 1) < video)
    ).astype(F32)
    packed = jnp.zeros((2 * video, HEAD_DIM), F32)

    def scores_of(head, group):
        cells = slice(head * HEAD_DIM, (head + 1) * HEAD_DIM)
        queries = jnp.concatenate([qo_ref[:, cells], qp_ref[:, cells]], axis=0)
        return lax.dot_general(
            queries, both(group, 0), (((1,), (1,)), ((), ())), preferred_element_type=F32
        )

    work = []
    for head in range(width // HEAD_DIM):
        cells = slice(head * HEAD_DIM, (head + 1) * HEAD_DIM)
        columns = slice((first + head) * HEAD_DIM, (first + head + 1) * HEAD_DIM)
        blocks = [(ref, columns) for ref in refs[:count]] + [(ref, cells) for ref in refs[count:]]
        blocks.append((text_ref, columns))
        work.append((head, [(fresh_ref, columns), (stale_ref, columns)], same_patch))
        odd = len(blocks) % 2
        if odd:
            work.append((head, blocks[:1], None))
        for start in range(odd, len(blocks), 2):
            last = start + 2 == len(blocks)
            work.append((head, blocks[start : start + 2], keep if last else None))

    upcoming = [scores_of(*item[:2]) for item in work[:LOOK_AHEAD]]
    num = den = None
    for index, (head, group, kept) in enumerate(work):
        scores = upcoming.pop(0)
        if index + LOOK_AHEAD < len(work):
            upcoming.append(scores_of(*work[index + LOOK_AHEAD][:2]))
        weights = jnp.exp2(scores * FACTOR)
        if kept is not None:
            weights = weights * kept
        part, total = times(weights, both(group, 1)), lanes(weights)
        num = part if num is None else num + part
        den = total if den is None else den + total
        if index + 1 == len(work) or work[index + 1][0] != head:
            cells = slice(head * HEAD_DIM, (head + 1) * HEAD_DIM)
            if finish:
                own_ref[:, cells] = num[:video]
                msg_ref[:, cells] = num[video:]
            else:
                num_ref[:, cells] = num
            packed = jnp.where(lane == first + head, jnp.sum(den, axis=1, keepdims=True), packed)
            num = den = None
    if finish:
        own_den_ref[...] = packed[:video]
        msg_ref[:, width:] = packed[video:]
    else:
        den_ref[...] = packed


def last_kernel(first, qo_ref, qp_ref, num_ref, den_ref, far_ref, own_ref, own_den_ref, msg_ref):
    video, width = qo_ref.shape
    lane = lax.broadcasted_iota(jnp.int32, (2 * video, HEAD_DIM), 1)
    packed = den_ref[...]
    for head in range(width // HEAD_DIM):
        cells = slice(head * HEAD_DIM, (head + 1) * HEAD_DIM)
        queries = jnp.concatenate([qo_ref[:, cells], qp_ref[:, cells]], axis=0)
        weights = weigh(queries, far_ref[0, :, cells])
        num = num_ref[:, cells] + times(weights, far_ref[1, :, cells])
        own_ref[:, cells] = num[:video]
        msg_ref[:, cells] = num[video:]
        total = jnp.sum(lanes(weights), axis=1, keepdims=True)
        packed = packed + jnp.where(lane == first + head, total, 0.0)
    own_den_ref[...] = packed[:video]
    msg_ref[:, width:] = packed[video:]


def merge_kernel(first, own_ref, den_ref, msg_ref, att_ref):
    width = att_ref.shape[1]
    for head in range(width // HEAD_DIM):
        columns = slice(head * HEAD_DIM, (head + 1) * HEAD_DIM)
        lane = first + head
        num = own_ref[:, columns] + msg_ref[:, columns]
        den = den_ref[:, lane : lane + 1] + msg_ref[:, width + lane : width + lane + 1]
        att_ref[:, columns] = (num / den).astype(BF16)


def part_kernel(
    place_ref, weight_ref, hidden_ref, fresh_ref, first_ref, second_ref,
    out_ref, w_other_ref, hidden_copy_ref, cache_ref, w_ref, sems,
):
    depth = w_ref.shape[0]
    half = first_ref.shape[1]
    copies = []
    for index, (group, target) in enumerate(
        ((place_ref[0], w_ref), (1 - place_ref[0], w_other_ref))
    ):
        rows = pl.ds(pl.multiple_of(group * depth, depth), depth)
        copies.append(pltpu.make_async_copy(weight_ref.at[rows], target, sems.at[index]))
    copies.append(pltpu.make_async_copy(hidden_ref, hidden_copy_ref, sems.at[2]))
    copies.append(pltpu.make_async_copy(fresh_ref, cache_ref, sems.at[3]))
    for copy in copies:
        copy.start()
    copies[0].wait()
    out_ref[...] = jnp.dot(
        first_ref[...], w_ref[:half, :], preferred_element_type=F32
    ) + jnp.dot(second_ref[...], w_ref[half:, :], preferred_element_type=F32)
    for copy in copies[1:]:
        copy.wait()


def more_kernel(part_ref, att_ref, w_ref, out_ref):
    half = att_ref.shape[1]
    out_ref[...] = part_ref[...] + jnp.dot(
        att_ref[...], w_ref[:half, :], preferred_element_type=F32
    )


def final_kernel(part_ref, att_ref, w_ref, hidden_ref, gate_ref, out_ref, buffer_ref, sems):
    half = att_ref.shape[1]
    gate = gate_ref[...].reshape(1, part_ref.shape[1])
    count = sems.shape[0]
    step = part_ref.shape[1] // count
    copies = []
    for index in range(count):
        cells = slice(index * step, (index + 1) * step)
        total = part_ref[:, cells] + jnp.dot(
            att_ref[...], w_ref[half:, cells], preferred_element_type=F32
        )
        mixed = hidden_ref[:, cells].astype(F32) + gate[:, cells] * total
        buffer_ref[:, cells] = mixed.astype(BF16)
        copies.append(
            pltpu.make_async_copy(buffer_ref.at[:, cells], out_ref.at[:, cells], sems.at[index])
        )
        copies[-1].start()
    for copy in copies:
        copy.wait()


def params(megabytes):
    return pltpu.CompilerParams(vmem_limit_bytes=megabytes * 1024 * 1024)


def in_hbm(array):
    return pltpu.with_memory_space_constraint(array, pltpu.HBM)


def cost(flops, nbytes, transcendentals=0):
    return pl.CostEstimate(
        flops=int(flops), bytes_accessed=int(nbytes), transcendentals=int(transcendentals)
    )


def plain_call(kernel, outs, name, estimate, *operands):
    return pl.pallas_call(
        kernel,
        in_specs=[pl.BlockSpec(memory_space=pltpu.VMEM)] * len(operands),
        out_specs=[pl.BlockSpec(memory_space=pltpu.VMEM)] * len(outs),
        out_shape=[jax.ShapeDtypeStruct(shape, dtype) for shape, dtype in outs],
        compiler_params=params(24),
        cost_estimate=estimate,
        name=name,
    )(*operands)


def ring_moves(sections):
    chips = sections // 2
    order = list(range(0, chips, 2)) + list(range(chips - 1, 0, -2))
    moves = [], []
    for here, there in zip(order, order[1:] + order[:1]):
        for core in range(2):
            moves[core].append((2 * here + core, 2 * there + core))
            moves[1 - core].append((2 * there + core, 2 * here + core))
    return sorted(moves[0]), sorted(moves[1])


def per_device(
    sections, hidden, text_hidden, text_mask, stale_cache, qkv_weight, out_weight, query_gain,
    key_gain, norm_shift, norm_scale, branch_gate,
):
    video, features = hidden.shape
    text = text_hidden.shape[0] // 2
    width = stale_cache.shape[2]
    heads = width // HEAD_DIM
    group_columns = heads * TRIPLE
    chips = sections // 2
    out_features = out_weight.shape[1]
    top = video + EXTRA
    rows = top + text

    group = lax.axis_index("head")
    core = lax.axis_index("section") % 2
    place = jnp.stack([group, core]).astype(jnp.int32)
    swap_core = [(s, s ^ 1) for s in range(sections)]
    swap_head = [(0, 1), (1, 0)]
    ways = ring_moves(sections)
    half_way = chips // 2

    def ring_step(blocks):
        return [lax.ppermute(block, "section", way) for block, way in zip(blocks, ways)]

    vmem = pl.BlockSpec(memory_space=pltpu.VMEM)
    hbm = pl.BlockSpec(memory_space=pltpu.HBM)
    smem = pl.BlockSpec(memory_space=pltpu.SMEM)
    whole = ring_step((stale_cache, stale_cache))

    columns = 2 * TRIPLE
    blocks = group_columns // columns
    per_head = head_rows(video, text)

    def project_cost(share):
        share = 8 * rows * features * group_columns * share
        return cost(share, share // (4 * rows))

    a_rows, message, stats, ahead = pl.pallas_call(
        send_kernel,
        in_specs=[smem] + [hbm] * 5,
        out_specs=[vmem] * 4,
        out_shape=[
            jax.ShapeDtypeStruct((rows, features), BF16),
            jax.ShapeDtypeStruct((per_head + 2 * EXTRA, HEAD_DIM), BF16),
            jax.ShapeDtypeStruct((rows, HEAD_DIM), F32),
            jax.ShapeDtypeStruct((features, columns), BF16),
        ],
        scratch_shapes=[
            pltpu.VMEM((video, features), BF16),
            pltpu.VMEM((text, features), BF16),
            pltpu.VMEM((features,), F32),
            pltpu.VMEM((features,), F32),
            pltpu.VMEM((features, TRIPLE), BF16),
            pltpu.SemaphoreType.DMA((6,)),
        ],
        compiler_params=params(40),
        cost_estimate=project_cost(0.4),
        name="project_send",
    )(place, *map(in_hbm, (hidden, text_hidden, norm_scale, norm_shift, qkv_weight)))
    received = lax.ppermute(message, "head", swap_head)

    message_more, own_ahead = pl.pallas_call(
        functools.partial(send_more_kernel, video),
        in_specs=[smem, vmem, vmem, hbm],
        out_specs=[vmem] * 2,
        out_shape=[
            jax.ShapeDtypeStruct(((heads - 1) * per_head, HEAD_DIM), BF16),
            jax.ShapeDtypeStruct((features, columns), BF16),
        ],
        scratch_shapes=[
            pltpu.VMEM((features, group_columns - columns - 2 * TRIPLE), BF16),
            pltpu.VMEM((features, TRIPLE), BF16),
            pltpu.SemaphoreType.DMA((3,)),
        ],
        compiler_params=params(40),
        cost_estimate=project_cost(0.6),
        name="project_send_more",
    )(place, a_rows, ahead, in_hbm(qkv_weight))
    received_more = lax.ppermute(message_more, "head", swap_head)

    split = plain_call(
        split_kernel, [((2, video, width // 2), BF16)] * 4, "split_heads", cost(0, 8 * video * width),
        *lax.optimization_barrier((*whole, message_more, received))[:2],
    )
    chains = [[ring_step((split[0], split[2]))], [ring_step((split[1], split[3]))]]

    small = (query_gain, key_gain, text_mask, branch_gate, stale_cache)
    outs = pl.pallas_call(
        own_kernel,
        in_specs=[smem, vmem, vmem, hbm] + [hbm] * len(small),
        out_specs=[vmem] * (2 + len(small)),
        out_shape=[
            jax.ShapeDtypeStruct((top, group_columns), F32),
            jax.ShapeDtypeStruct((text, 2 * width), F32),
        ]
        + [jax.ShapeDtypeStruct(array.shape, array.dtype) for array in small],
        scratch_shapes=[
            pltpu.VMEM((blocks - 1, features, columns), BF16),
            pltpu.SemaphoreType.DMA((blocks - 1 + len(small),)),
        ],
        compiler_params=params(40),
        cost_estimate=project_cost(1),
        name="project_own",
    )(place, a_rows, own_ahead, *map(in_hbm, (qkv_weight,) + small))
    own, own_text = outs[:2]
    query_gain, key_gain, text_mask, branch_gate, stale = outs[2:]

    for _ in range(half_way - 3):
        for chain in chains:
            chain.append(ring_step(lax.optimization_barrier((*chain[-1], own))[:2]))
    far = [lax.ppermute(chain[-1][0], "section", ways[0]) for chain in chains]

    received_more = lax.optimization_barrier((received_more, *chains[0][0], *chains[1][0]))[0]
    *queries, fresh = plain_call(
        functools.partial(norm_kernel, features * 2, text),
        [((video, width // 2), BF16)] * 2 + [((2, video, width), BF16)],
        "norm_video",
        cost(1000 * top * group_columns, 8 * top * group_columns),
        own, received, received_more, stats, query_gain, key_gain,
    )
    other_queries = [lax.ppermute(half, "section", swap_core) for half in queries]
    (text_kv,) = plain_call(
        functools.partial(text_kernel, features * 2),
        [((2, text, width), BF16)],
        "norm_text",
        cost(text * group_columns, text * group_columns),
        own_text, received, received_more, stats, own, key_gain,
    )

    context = chips * video + video + text
    finished = [
        jax.ShapeDtypeStruct((video, width // 2), F32),
        jax.ShapeDtypeStruct((video, HEAD_DIM), F32),
        jax.ShapeDtypeStruct((video, width // 2 + HEAD_DIM), F32),
    ]
    attended, other_attended = [], []
    for index, chain in enumerate(chains):
        first = index * heads // 2
        halves = [block for step in chain for block in step]
        finish = index == 0
        own_queries = queries[index]
        if finish:
            halves.append(far[index])
            outs = finished
        else:
            own_queries = lax.optimization_barrier((own_queries, num_own))[0]
            outs = [
                jax.ShapeDtypeStruct((2 * video, width // 2), F32),
                jax.ShapeDtypeStruct((2 * video, HEAD_DIM), F32),
            ]
        outs = pl.pallas_call(
            functools.partial(attend_kernel, first, len(whole), finish),
            in_specs=[smem] + [vmem] * (6 + len(whole) + len(halves)),
            out_specs=[vmem] * len(outs),
            out_shape=outs,
            compiler_params=params(24),
            cost_estimate=cost(video * context, context * width, video * heads),
            name="attend",
        )(
            place, own_queries, other_queries[index], fresh, stale, text_kv, text_mask,
            *whole, *halves,
        )
        if not finish:
            outs = plain_call(
                functools.partial(last_kernel, first),
                [(out.shape, out.dtype) for out in finished],
                "attend_last",
                cost(video * video, video * width),
                own_queries, other_queries[index], *outs, far[index],
            )
        num_own, den_own, num_message = outs
        num_received = lax.ppermute(num_message, "section", swap_core)
        attended += plain_call(
            functools.partial(merge_kernel, first),
            [((video, width // 2), BF16)],
            "merge",
            cost(2 * video * width, 5 * video * width),
            num_own, den_own, num_received,
        )
        other_attended.append(lax.ppermute(attended[-1], "head", swap_head))

    out_cost = cost(4 * video * width * out_features, 2 * width * out_features)
    part, w_other, hidden, new_cache = pl.pallas_call(
        part_kernel,
        in_specs=[smem, hbm, hbm] + [vmem] * 3,
        out_specs=[vmem] * 3 + [hbm],
        out_shape=[
            jax.ShapeDtypeStruct((video, out_features), F32),
            jax.ShapeDtypeStruct((width, out_features), BF16),
            jax.ShapeDtypeStruct(hidden.shape, BF16),
            jax.ShapeDtypeStruct(fresh.shape, BF16),
        ],
        scratch_shapes=[
            pltpu.VMEM((width, out_features), BF16),
            pltpu.SemaphoreType.DMA((4,)),
        ],
        compiler_params=params(24),
        cost_estimate=out_cost,
        name="part_out",
    )(place, in_hbm(out_weight), in_hbm(hidden), fresh, *attended)
    (part,) = plain_call(
        more_kernel, [((video, out_features), F32)], "more_out", out_cost,
        part, other_attended[0], w_other,
    )
    mixed = pl.pallas_call(
        final_kernel,
        in_specs=[vmem] * 5,
        out_specs=hbm,
        out_shape=jax.ShapeDtypeStruct((video, out_features), BF16),
        scratch_shapes=[
            pltpu.VMEM((video, out_features), BF16),
            pltpu.SemaphoreType.DMA((out_features // 512,)),
        ],
        compiler_params=params(24),
        cost_estimate=out_cost,
        name="final_out",
    )(part, other_attended[1], w_other, hidden, branch_gate)
    return (mixed, new_cache)


def solution(mesh):
    in_specs = (
        P("section", "head"),
        P(None, "head"),
        P(),
        P(None, "section", "head"),
        P("head", None),
        P(None, "head"),
        P(),
        P(),
        P("head"),
        P("head"),
        P("head"),
    )
    out_specs = (P("section", "head"), P(None, "section", "head"))
    return jax.shard_map(
        functools.partial(per_device, mesh.shape["section"]),
        mesh=mesh, in_specs=in_specs, out_specs=out_specs, check_vma=False,
    )
```

```python
import functools
import math

import jax
import jax.numpy as jnp
from jax import lax
from jax.experimental import pallas as pl
from jax.experimental.pallas import tpu as pltpu
from jax.sharding import PartitionSpec as P

HEAD_DIM = 128
TRIPLE = 3 * HEAD_DIM
EXTRA = 16
PIECE = 2 * HEAD_DIM
LOOK_AHEAD = 3
EPS = 1e-06
F32 = jnp.float32
BF16 = jnp.bfloat16


def split_bf16(value, parts):
    pieces = []
    rest = value
    for _ in range(parts):
        piece = rest.astype(BF16)
        pieces.append(piece)
        rest = rest - piece.astype(F32)
    return pieces


def head_rows(video, text):
    return 3 * video + 2 * text + EXTRA


def column_copy(w_ref, first, target, sem):
    columns = target.shape[1]
    start = pl.multiple_of(first, HEAD_DIM)
    return pltpu.make_async_copy(w_ref.at[:, pl.ds(start, columns)], target, sem)


def partial_sums(a_ref, w_ref, video, text, msg_ref, first):
    band = lax.broadcasted_iota(jnp.int32, (EXTRA, HEAD_DIM), 0) // 4
    top = video + EXTRA
    terms = None
    for start in range(0, w_ref.shape[1], PIECE):
        stop = min(start + PIECE, w_ref.shape[1])
        product = jnp.dot(a_ref[...], w_ref[:, start:stop], preferred_element_type=F32)
        for local in range(0, stop - start, HEAD_DIM):
            part = product[:, local : local + HEAD_DIM]
            head, kind = divmod((start + local) // HEAD_DIM, 3)
            base = (first + head) * head_rows(video, text)
            msg_ref[base + kind * video : base + (kind + 1) * video, :] = part[:video].astype(BF16)
            terms = part[video:top] if kind == 0 else jnp.where(band == kind, part[video:top], terms)
            base += 3 * video
            if kind:
                rows = slice(base + (kind - 1) * text, base + kind * text)
                msg_ref[rows, :] = part[top:].astype(BF16)
            if kind == 2:
                base += 2 * text
                msg_ref[base : base + EXTRA, :] = terms.astype(BF16)


def send_kernel(
    place_ref, x_ref, t_ref, scale_ref, shift_ref, w_ref,
    a_ref, msg_ref, stat_ref, ahead_ref,
    x_buffer, t_buffer, scale_buffer, shift_buffer, w_buffer, sems,
):
    video, features = x_buffer.shape
    text = t_buffer.shape[0]
    top = video + EXTRA
    columns = w_buffer.shape[1]
    base = (1 - place_ref[0]) * (w_ref.shape[1] // 2)
    copies = [
        pltpu.make_async_copy(scale_ref, scale_buffer, sems.at[0]),
        pltpu.make_async_copy(shift_ref, shift_buffer, sems.at[1]),
        pltpu.make_async_copy(x_ref, x_buffer, sems.at[2]),
        pltpu.make_async_copy(
            t_ref.at[pl.ds(pl.multiple_of(place_ref[1] * text, text), text)], t_buffer, sems.at[3]
        ),
        column_copy(w_ref, base, w_buffer, sems.at[4]),
        column_copy(w_ref, base + columns, ahead_ref, sems.at[5]),
    ]
    for copy in copies[:5]:
        copy.start()

    copies[0].wait()
    copies[1].wait()
    gain = 1.0 + scale_buffer[...].reshape(1, features)
    pieces = split_bf16(gain, 2) + split_bf16(shift_buffer[...].reshape(1, features), 2)
    row = lax.broadcasted_iota(jnp.int32, (EXTRA, features), 0)
    extra = jnp.zeros((EXTRA, features), F32)
    for index, piece in enumerate(pieces):
        extra = jnp.where(row % 4 == index, piece.astype(F32), extra)
    a_ref[video:top, :] = extra.astype(BF16)

    def prepare(rows_ref, start):
        rows = rows_ref[...].astype(F32)
        count = rows.shape[0]
        mean = jnp.sum(rows, axis=1, keepdims=True) * (1.0 / features)
        centered = rows - mean
        second = jnp.sum(centered * centered, axis=1, keepdims=True)
        a_ref[start : start + count, :] = (centered * gain).astype(BF16)
        lane = lax.broadcasted_iota(jnp.int32, (count, HEAD_DIM), 1)
        packed = jnp.zeros((count, HEAD_DIM), F32)
        for index, piece in enumerate(split_bf16(mean, 3) + split_bf16(second, 3)):
            packed = jnp.where(lane == index, piece.astype(F32), packed)
        stat_ref[start : start + count, :] = jnp.where(
            lane == 0, mean, jnp.where(lane == 1, second, 0.0)
        )
        return jnp.transpose(packed)[:EXTRA]

    copies[2].wait()
    copies[5].start()
    stats = [prepare(x_buffer, 0)]
    copies[3].wait()
    stats.append(prepare(t_buffer, top))
    stat_ref[video:top, :] = jnp.zeros((EXTRA, HEAD_DIM), F32)
    start = head_rows(video, text) * columns // TRIPLE
    msg_ref[start : start + 2 * EXTRA, :] = jnp.concatenate(stats, axis=0).astype(BF16)
    copies[4].wait()
    partial_sums(a_ref, w_buffer, video, text, msg_ref, 0)
    copies[5].wait()


def send_more_kernel(
    video, place_ref, a_ref, ahead_ref, w_ref, msg_ref, own_ahead_ref, w_buffer, last_buffer, sems,
):
    text = a_ref.shape[0] - video - EXTRA
    width = w_ref.shape[1] // 2
    other, own = (1 - place_ref[0]) * width, place_ref[0] * width
    first = width - last_buffer.shape[1]
    copies = [
        column_copy(w_ref, other + first - w_buffer.shape[1], w_buffer, sems.at[0]),
        column_copy(w_ref, other + first, last_buffer, sems.at[1]),
        column_copy(w_ref, own, own_ahead_ref, sems.at[2]),
    ]
    copies[0].start()
    copies[1].start()
    partial_sums(a_ref, ahead_ref, video, text, msg_ref, 0)
    copies[0].wait()
    copies[2].start()
    head = ahead_ref.shape[1] // TRIPLE
    partial_sums(a_ref, w_buffer, video, text, msg_ref, head)
    copies[1].wait()
    head += w_buffer.shape[1] // TRIPLE
    partial_sums(a_ref, last_buffer, video, text, msg_ref, head)
    copies[2].wait()


def own_kernel(place_ref, a_ref, ahead_ref, w_ref, *refs):
    small = (len(refs) - 4) // 2
    out_ref, text_ref = refs[small : small + 2]
    w_buffer, sems = refs[-2:]
    top = out_ref.shape[0]
    later, _, columns = w_buffer.shape
    base = place_ref[0] * (w_ref.shape[1] // 2) + columns
    copies = [
        column_copy(w_ref, base + index * columns, w_buffer.at[index], sems.at[index])
        for index in range(later)
    ]
    for source, target in zip(refs[:small], refs[small + 2 : -2]):
        copies.append(pltpu.make_async_copy(source, target, sems.at[len(copies)]))
    copies[0].start()

    for block in range(later + 1):
        if block:
            copies[block - 1].wait()
        if block == 1:
            for copy in copies[later:]:
                copy.start()
        for start in range(0, columns, PIECE):
            cells = slice(start, start + PIECE)
            part = w_buffer[block - 1, :, cells] if block else ahead_ref[:, cells]
            product = jnp.dot(a_ref[...], part, preferred_element_type=F32)
            first = block * columns + start
            out_ref[:, first : first + PIECE] = product[:top]
            for local in range(0, PIECE, HEAD_DIM):
                head, kind = divmod((first + local) // HEAD_DIM, 3)
                if kind:
                    target = (2 * head + kind - 1) * HEAD_DIM
                    text_ref[:, target : target + HEAD_DIM] = product[
                        top:, local : local + HEAD_DIM
                    ]
            if block == 0 and start == 0:
                for copy in copies[1:later]:
                    copy.start()
    for copy in copies[later:]:
        copy.wait()


def row_stats(total_features, own, received):
    count = own.shape[0]
    received = received.astype(F32)
    padding = jnp.zeros((HEAD_DIM - received.shape[0], count), F32)
    received = jnp.transpose(jnp.concatenate([received, padding], axis=0))
    parts = [received[:, index : index + 1] for index in range(6)]
    gap = 0.5 * (own[:, 0:1] - (parts[0] + parts[1] + parts[2]))
    second = own[:, 1:2] + (parts[3] + parts[4] + parts[5])
    var = second * (1.0 / total_features) + gap * gap
    return gap, lax.rsqrt(var + EPS)


def column_terms(own_ref, msg_ref, video, base, part):
    other = msg_ref[base : base + EXTRA, :].astype(F32)
    other = other[4 * (part % 3) : 4 * (part % 3) + 4]
    own = own_ref[video : video + 8, part * HEAD_DIM : (part + 1) * HEAD_DIM]
    scale = (own[0:1] + own[1:2]) - (other[0:1] + other[1:2])
    shift = (own[2:3] + own[3:4]) + (other[2:3] + other[3:4])
    return scale, shift


def head_place(head, rows, first_ref, more_ref):
    early = first_ref.shape[0] // rows
    return (first_ref, head * rows) if head < early else (more_ref, (head - early) * rows)


def head_norm(part, gain):
    square = jnp.sum(part * part, axis=1, keepdims=True) * (1.0 / HEAD_DIM)
    return part * lax.rsqrt(square + EPS) * gain


def norm_kernel(
    total_features, text, own_ref, first_ref, more_ref, stat_ref, qg_ref, kg_ref,
    qa_ref, qb_ref, kv_ref,
):
    video = qa_ref.shape[0]
    half = qa_ref.shape[1] // HEAD_DIM
    rows = head_rows(video, text)
    query_gain = qg_ref[...].reshape(1, HEAD_DIM)
    key_gain = kg_ref[...].reshape(1, HEAD_DIM)
    start = first_ref.shape[0] - 2 * EXTRA
    gap, inverse = row_stats(
        total_features, stat_ref[:video, :], first_ref[start : start + EXTRA, :video]
    )
    for head in range(2 * half):
        msg_ref, base = head_place(head, rows, first_ref, more_ref)

        def total(kind):
            part = 3 * head + kind
            scale, shift = column_terms(own_ref, msg_ref, video, base + rows - EXTRA, part)
            other = msg_ref[base + kind * video : base + (kind + 1) * video, :].astype(F32)
            both = own_ref[:video, part * HEAD_DIM : (part + 1) * HEAD_DIM] + other
            return (both + gap * scale) * inverse + shift

        columns = slice(head * HEAD_DIM, (head + 1) * HEAD_DIM)
        cells = slice(head % half * HEAD_DIM, (head % half + 1) * HEAD_DIM)
        q_ref = qa_ref if head < half else qb_ref
        q_ref[:, cells] = head_norm(total(0), query_gain).astype(BF16)
        kv_ref[0, :, columns] = head_norm(total(1), key_gain).astype(BF16)
        kv_ref[1, :, columns] = total(2).astype(BF16)


def text_kernel(
    total_features, own_ref, first_ref, more_ref, stat_ref, top_ref, kg_ref, kv_ref
):
    text = kv_ref.shape[1]
    heads = kv_ref.shape[2] // HEAD_DIM
    video = top_ref.shape[0] - EXTRA
    rows = head_rows(video, text)
    key_gain = kg_ref[...].reshape(1, HEAD_DIM)
    start = first_ref.shape[0] - EXTRA
    gap, inverse = row_stats(
        total_features, stat_ref[video + EXTRA :, :], first_ref[start : start + EXTRA, :text]
    )
    for head in range(heads):
        msg_ref, base = head_place(head, rows, first_ref, more_ref)

        def total(kind):
            scale, shift = column_terms(
                top_ref, msg_ref, video, base + rows - EXTRA, 3 * head + 1 + kind
            )
            start = base + 3 * video + kind * text
            other = msg_ref[start : start + text, :].astype(F32)
            first = (2 * head + kind) * HEAD_DIM
            return (own_ref[:, first : first + HEAD_DIM] + other + gap * scale) * inverse + shift

        columns = slice(head * HEAD_DIM, (head + 1) * HEAD_DIM)
        kv_ref[0, :, columns] = head_norm(total(0), key_gain).astype(BF16)
        kv_ref[1, :, columns] = total(1).astype(BF16)


FACTOR = math.log2(math.e) / math.sqrt(HEAD_DIM)


def split_kernel(*refs):
    count = len(refs) // 3
    for index in range(count):
        half = refs[index].shape[2] // 2
        refs[count + 2 * index][...] = refs[index][:, :, :half]
        refs[count + 2 * index + 1][...] = refs[index][:, :, half:]


def weigh(rows, keys):
    scores = lax.dot_general(rows, keys, (((1,), (1,)), ((), ())), preferred_element_type=F32)
    return jnp.exp2(scores * FACTOR)


def lanes(weights):
    total = weights[:, :HEAD_DIM]
    for start in range(HEAD_DIM, weights.shape[1], HEAD_DIM):
        total = total + weights[:, start : start + HEAD_DIM]
    return total


def times(weights, values):
    return jnp.dot(weights.astype(BF16), values, preferred_element_type=F32)


def both(group, index):
    return jnp.concatenate([ref[index, :, part] for ref, part in group], axis=0)


def attend_kernel(
    first, count, finish, place_ref, qo_ref, qp_ref, fresh_ref, stale_ref, text_ref, mask_ref, *refs,
):
    *refs, num_ref, den_ref = refs
    if finish:
        *refs, own_ref = refs
        own_den_ref, msg_ref = num_ref, den_ref
    video, width = qo_ref.shape
    text = text_ref.shape[1]
    lane = lax.broadcasted_iota(jnp.int32, (2 * video, HEAD_DIM), 1)
    mask = mask_ref[...].reshape(1, 2 * text).astype(F32)
    mask = jnp.where(place_ref[1] == 0, mask[:, :text], mask[:, text:])
    keep = jnp.concatenate([jnp.ones((1, video), F32), mask], axis=1)
    same_patch = (
        (lax.broadcasted_iota(jnp.int32, (2 * video, 2 * video), 0) < video)
        == (lax.broadcasted_iota(jnp.int32, (2 * video, 2 * video), 1) < video)
    ).astype(F32)
    packed = jnp.zeros((2 * video, HEAD_DIM), F32)

    def scores_of(head, group):
        cells = slice(head * HEAD_DIM, (head + 1) * HEAD_DIM)
        queries = jnp.concatenate([qo_ref[:, cells], qp_ref[:, cells]], axis=0)
        return lax.dot_general(
            queries, both(group, 0), (((1,), (1,)), ((), ())), preferred_element_type=F32
        )

    work = []
    for head in range(width // HEAD_DIM):
        cells = slice(head * HEAD_DIM, (head + 1) * HEAD_DIM)
        columns = slice((first + head) * HEAD_DIM, (first + head + 1) * HEAD_DIM)
        blocks = [(ref, columns) for ref in refs[:count]] + [(ref, cells) for ref in refs[count:]]
        blocks.append((text_ref, columns))
        work.append((head, [(fresh_ref, columns), (stale_ref, columns)], same_patch))
        odd = len(blocks) % 2
        if odd:
            work.append((head, blocks[:1], None))
        for start in range(odd, len(blocks), 2):
            last = start + 2 == len(blocks)
            work.append((head, blocks[start : start + 2], keep if last else None))

    upcoming = [scores_of(*item[:2]) for item in work[:LOOK_AHEAD]]
    num = den = None
    for index, (head, group, kept) in enumerate(work):
        scores = upcoming.pop(0)
        if index + LOOK_AHEAD < len(work):
            upcoming.append(scores_of(*work[index + LOOK_AHEAD][:2]))
        weights = jnp.exp2(scores * FACTOR)
        if kept is not None:
            weights = weights * kept
        part, total = times(weights, both(group, 1)), lanes(weights)
        num = part if num is None else num + part
        den = total if den is None else den + total
        if index + 1 == len(work) or work[index + 1][0] != head:
            cells = slice(head * HEAD_DIM, (head + 1) * HEAD_DIM)
            if finish:
                own_ref[:, cells] = num[:video]
                msg_ref[:, cells] = num[video:]
            else:
                num_ref[:, cells] = num
            packed = jnp.where(lane == first + head, jnp.sum(den, axis=1, keepdims=True), packed)
            num = den = None
    if finish:
        own_den_ref[...] = packed[:video]
        msg_ref[:, width:] = packed[video:]
    else:
        den_ref[...] = packed


def last_kernel(first, qo_ref, qp_ref, num_ref, den_ref, far_ref, own_ref, own_den_ref, msg_ref):
    video, width = qo_ref.shape
    lane = lax.broadcasted_iota(jnp.int32, (2 * video, HEAD_DIM), 1)
    packed = den_ref[...]
    for head in range(width // HEAD_DIM):
        cells = slice(head * HEAD_DIM, (head + 1) * HEAD_DIM)
        queries = jnp.concatenate([qo_ref[:, cells], qp_ref[:, cells]], axis=0)
        weights = weigh(queries, far_ref[0, :, cells])
        num = num_ref[:, cells] + times(weights, far_ref[1, :, cells])
        own_ref[:, cells] = num[:video]
        msg_ref[:, cells] = num[video:]
        total = jnp.sum(lanes(weights), axis=1, keepdims=True)
        packed = packed + jnp.where(lane == first + head, total, 0.0)
    own_den_ref[...] = packed[:video]
    msg_ref[:, width:] = packed[video:]


def merge_kernel(first, own_ref, den_ref, msg_ref, att_ref):
    width = att_ref.shape[1]
    for head in range(width // HEAD_DIM):
        columns = slice(head * HEAD_DIM, (head + 1) * HEAD_DIM)
        lane = first + head
        num = own_ref[:, columns] + msg_ref[:, columns]
        den = den_ref[:, lane : lane + 1] + msg_ref[:, width + lane : width + lane + 1]
        att_ref[:, columns] = (num / den).astype(BF16)


def part_kernel(
    place_ref, weight_ref, hidden_ref, fresh_ref, first_ref, second_ref,
    out_ref, w_other_ref, hidden_copy_ref, cache_ref, w_ref, sems,
):
    depth = w_ref.shape[0]
    half = first_ref.shape[1]
    copies = []
    for index, (group, target) in enumerate(
        ((place_ref[0], w_ref), (1 - place_ref[0], w_other_ref))
    ):
        rows = pl.ds(pl.multiple_of(group * depth, depth), depth)
        copies.append(pltpu.make_async_copy(weight_ref.at[rows], target, sems.at[index]))
    copies.append(pltpu.make_async_copy(hidden_ref, hidden_copy_ref, sems.at[2]))
    copies.append(pltpu.make_async_copy(fresh_ref, cache_ref, sems.at[3]))
    for copy in copies:
        copy.start()
    copies[0].wait()
    out_ref[...] = jnp.dot(
        first_ref[...], w_ref[:half, :], preferred_element_type=F32
    ) + jnp.dot(second_ref[...], w_ref[half:, :], preferred_element_type=F32)
    for copy in copies[1:]:
        copy.wait()


def more_kernel(part_ref, att_ref, w_ref, out_ref):
    half = att_ref.shape[1]
    out_ref[...] = part_ref[...] + jnp.dot(
        att_ref[...], w_ref[:half, :], preferred_element_type=F32
    )


def final_kernel(part_ref, att_ref, w_ref, hidden_ref, gate_ref, out_ref, buffer_ref, sems):
    half = att_ref.shape[1]
    gate = gate_ref[...].reshape(1, part_ref.shape[1])
    count = sems.shape[0]
    step = part_ref.shape[1] // count
    copies = []
    for index in range(count):
        cells = slice(index * step, (index + 1) * step)
        total = part_ref[:, cells] + jnp.dot(
            att_ref[...], w_ref[half:, cells], preferred_element_type=F32
        )
        mixed = hidden_ref[:, cells].astype(F32) + gate[:, cells] * total
        buffer_ref[:, cells] = mixed.astype(BF16)
        copies.append(
            pltpu.make_async_copy(buffer_ref.at[:, cells], out_ref.at[:, cells], sems.at[index])
        )
        copies[-1].start()
    for copy in copies:
        copy.wait()


def params(megabytes):
    return pltpu.CompilerParams(vmem_limit_bytes=megabytes * 1024 * 1024)


def in_hbm(array):
    return pltpu.with_memory_space_constraint(array, pltpu.HBM)


def cost(flops, nbytes, transcendentals=0):
    return pl.CostEstimate(
        flops=int(flops), bytes_accessed=int(nbytes), transcendentals=int(transcendentals)
    )


def plain_call(kernel, outs, name, estimate, *operands):
    return pl.pallas_call(
        kernel,
        in_specs=[pl.BlockSpec(memory_space=pltpu.VMEM)] * len(operands),
        out_specs=[pl.BlockSpec(memory_space=pltpu.VMEM)] * len(outs),
        out_shape=[jax.ShapeDtypeStruct(shape, dtype) for shape, dtype in outs],
        compiler_params=params(24),
        cost_estimate=estimate,
        name=name,
    )(*operands)


def ring_moves(sections):
    chips = sections // 2
    order = list(range(0, chips, 2)) + list(range(chips - 1, 0, -2))
    moves = [], []
    for here, there in zip(order, order[1:] + order[:1]):
        for core in range(2):
            moves[core].append((2 * here + core, 2 * there + core))
            moves[1 - core].append((2 * there + core, 2 * here + core))
    return sorted(moves[0]), sorted(moves[1])


def per_device(
    sections, hidden, text_hidden, text_mask, stale_cache, qkv_weight, out_weight, query_gain,
    key_gain, norm_shift, norm_scale, branch_gate,
):
    video, features = hidden.shape
    text = text_hidden.shape[0] // 2
    width = stale_cache.shape[2]
    heads = width // HEAD_DIM
    group_columns = heads * TRIPLE
    chips = sections // 2
    out_features = out_weight.shape[1]
    top = video + EXTRA
    rows = top + text

    group = lax.axis_index("head")
    core = lax.axis_index("section") % 2
    place = jnp.stack([group, core]).astype(jnp.int32)
    swap_core = [(s, s ^ 1) for s in range(sections)]
    swap_head = [(0, 1), (1, 0)]
    ways = ring_moves(sections)
    half_way = chips // 2

    def ring_step(blocks):
        return [lax.ppermute(block, "section", way) for block, way in zip(blocks, ways)]

    vmem = pl.BlockSpec(memory_space=pltpu.VMEM)
    hbm = pl.BlockSpec(memory_space=pltpu.HBM)
    smem = pl.BlockSpec(memory_space=pltpu.SMEM)
    whole = ring_step((stale_cache, stale_cache))

    columns = 2 * TRIPLE
    blocks = group_columns // columns
    per_head = head_rows(video, text)

    def project_cost(share):
        share = 8 * rows * features * group_columns * share
        return cost(share, share // (4 * rows))

    a_rows, message, stats, ahead = pl.pallas_call(
        send_kernel,
        in_specs=[smem] + [hbm] * 5,
        out_specs=[vmem] * 4,
        out_shape=[
            jax.ShapeDtypeStruct((rows, features), BF16),
            jax.ShapeDtypeStruct((per_head + 2 * EXTRA, HEAD_DIM), BF16),
            jax.ShapeDtypeStruct((rows, HEAD_DIM), F32),
            jax.ShapeDtypeStruct((features, columns), BF16),
        ],
        scratch_shapes=[
            pltpu.VMEM((video, features), BF16),
            pltpu.VMEM((text, features), BF16),
            pltpu.VMEM((features,), F32),
            pltpu.VMEM((features,), F32),
            pltpu.VMEM((features, TRIPLE), BF16),
            pltpu.SemaphoreType.DMA((6,)),
        ],
        compiler_params=params(40),
        cost_estimate=project_cost(0.4),
        name="project_send",
    )(place, *map(in_hbm, (hidden, text_hidden, norm_scale, norm_shift, qkv_weight)))
    received = lax.ppermute(message, "head", swap_head)

    message_more, own_ahead = pl.pallas_call(
        functools.partial(send_more_kernel, video),
        in_specs=[smem, vmem, vmem, hbm],
        out_specs=[vmem] * 2,
        out_shape=[
            jax.ShapeDtypeStruct(((heads - 1) * per_head, HEAD_DIM), BF16),
            jax.ShapeDtypeStruct((features, columns), BF16),
        ],
        scratch_shapes=[
            pltpu.VMEM((features, group_columns - columns - 2 * TRIPLE), BF16),
            pltpu.VMEM((features, TRIPLE), BF16),
            pltpu.SemaphoreType.DMA((3,)),
        ],
        compiler_params=params(40),
        cost_estimate=project_cost(0.6),
        name="project_send_more",
    )(place, a_rows, ahead, in_hbm(qkv_weight))
    received_more = lax.ppermute(message_more, "head", swap_head)

    split = plain_call(
        split_kernel, [((2, video, width // 2), BF16)] * 4, "split_heads", cost(0, 8 * video * width),
        *lax.optimization_barrier((*whole, message_more, received))[:2],
    )
    chains = [[ring_step((split[0], split[2]))], [ring_step((split[1], split[3]))]]

    small = (query_gain, key_gain, text_mask, branch_gate, stale_cache)
    outs = pl.pallas_call(
        own_kernel,
        in_specs=[smem, vmem, vmem, hbm] + [hbm] * len(small),
        out_specs=[vmem] * (2 + len(small)),
        out_shape=[
            jax.ShapeDtypeStruct((top, group_columns), F32),
            jax.ShapeDtypeStruct((text, 2 * width), F32),
        ]
        + [jax.ShapeDtypeStruct(array.shape, array.dtype) for array in small],
        scratch_shapes=[
            pltpu.VMEM((blocks - 1, features, columns), BF16),
            pltpu.SemaphoreType.DMA((blocks - 1 + len(small),)),
        ],
        compiler_params=params(40),
        cost_estimate=project_cost(1),
        name="project_own",
    )(place, a_rows, own_ahead, *map(in_hbm, (qkv_weight,) + small))
    own, own_text = outs[:2]
    query_gain, key_gain, text_mask, branch_gate, stale = outs[2:]

    for _ in range(half_way - 3):
        for chain in chains:
            chain.append(ring_step(lax.optimization_barrier((*chain[-1], own))[:2]))
    far = [lax.ppermute(chain[-1][0], "section", ways[0]) for chain in chains]

    received_more = lax.optimization_barrier((received_more, *chains[0][0], *chains[1][0]))[0]
    *queries, fresh = plain_call(
        functools.partial(norm_kernel, features * 2, text),
        [((video, width // 2), BF16)] * 2 + [((2, video, width), BF16)],
        "norm_video",
        cost(1000 * top * group_columns, 8 * top * group_columns),
        own, received, received_more, stats, query_gain, key_gain,
    )
    other_queries = [lax.ppermute(half, "section", swap_core) for half in queries]
    (text_kv,) = plain_call(
        functools.partial(text_kernel, features * 2),
        [((2, text, width), BF16)],
        "norm_text",
        cost(text * group_columns, text * group_columns),
        own_text, received, received_more, stats, own, key_gain,
    )

    context = chips * video + video + text
    finished = [
        jax.ShapeDtypeStruct((video, width // 2), F32),
        jax.ShapeDtypeStruct((video, HEAD_DIM), F32),
        jax.ShapeDtypeStruct((video, width // 2 + HEAD_DIM), F32),
    ]
    attended, other_attended = [], []
    for index, chain in enumerate(chains):
        first = index * heads // 2
        halves = [block for step in chain for block in step]
        finish = index == 0
        own_queries = queries[index]
        if finish:
            halves.append(far[index])
            outs = finished
        else:
            own_queries = lax.optimization_barrier((own_queries, num_own))[0]
            outs = [
                jax.ShapeDtypeStruct((2 * video, width // 2), F32),
                jax.ShapeDtypeStruct((2 * video, HEAD_DIM), F32),
            ]
        outs = pl.pallas_call(
            functools.partial(attend_kernel, first, len(whole), finish),
            in_specs=[smem] + [vmem] * (6 + len(whole) + len(halves)),
            out_specs=[vmem] * len(outs),
            out_shape=outs,
            compiler_params=params(24),
            cost_estimate=cost(video * context, context * width, video * heads),
            name="attend",
        )(
            place, own_queries, other_queries[index], fresh, stale, text_kv, text_mask,
            *whole, *halves,
        )
        if not finish:
            outs = plain_call(
                functools.partial(last_kernel, first),
                [(out.shape, out.dtype) for out in finished],
                "attend_last",
                cost(video * video, video * width),
                own_queries, other_queries[index], *outs, far[index],
            )
        num_own, den_own, num_message = outs
        num_received = lax.ppermute(num_message, "section", swap_core)
        attended += plain_call(
            functools.partial(merge_kernel, first),
            [((video, width // 2), BF16)],
            "merge",
            cost(2 * video * width, 5 * video * width),
            num_own, den_own, num_received,
        )
        other_attended.append(lax.ppermute(attended[-1], "head", swap_head))

    out_cost = cost(4 * video * width * out_features, 2 * width * out_features)
    part, w_other, hidden, new_cache = pl.pallas_call(
        part_kernel,
        in_specs=[smem, hbm, hbm] + [vmem] * 3,
        out_specs=[vmem] * 3 + [hbm],
        out_shape=[
            jax.ShapeDtypeStruct((video, out_features), F32),
            jax.ShapeDtypeStruct((width, out_features), BF16),
            jax.ShapeDtypeStruct(hidden.shape, BF16),
            jax.ShapeDtypeStruct(fresh.shape, BF16),
        ],
        scratch_shapes=[
            pltpu.VMEM((width, out_features), BF16),
            pltpu.SemaphoreType.DMA((4,)),
        ],
        compiler_params=params(24),
        cost_estimate=out_cost,
        name="part_out",
    )(place, in_hbm(out_weight), in_hbm(hidden), fresh, *attended)
    (part,) = plain_call(
        more_kernel, [((video, out_features), F32)], "more_out", out_cost,
        part, other_attended[0], w_other,
    )
    mixed = pl.pallas_call(
        final_kernel,
        in_specs=[vmem] * 5,
        out_specs=hbm,
        out_shape=jax.ShapeDtypeStruct((video, out_features), BF16),
        scratch_shapes=[
            pltpu.VMEM((video, out_features), BF16),
            pltpu.SemaphoreType.DMA((out_features // 512,)),
        ],
        compiler_params=params(24),
        cost_estimate=out_cost,
        name="final_out",
    )(part, other_attended[1], w_other, hidden, branch_gate)
    return (mixed, new_cache)


def solution(mesh):
    in_specs = (
        P("section", "head"),
        P(None, "head"),
        P(),
        P(None, "section", "head"),
        P("head", None),
        P(None, "head"),
        P(),
        P(),
        P("head"),
        P("head"),
        P("head"),
    )
    out_specs = (P("section", "head"), P(None, "section", "head"))
    return jax.shard_map(
        functools.partial(per_device, mesh.shape["section"]),
        mesh=mesh, in_specs=in_specs, out_specs=out_specs, check_vma=False,
    )
```

```python
import functools
import math

import jax
import jax.numpy as jnp
from jax import lax
from jax.experimental import pallas as pl
from jax.experimental.pallas import tpu as pltpu
from jax.sharding import PartitionSpec as P

HEAD_DIM = 128
TRIPLE = 3 * HEAD_DIM
EXTRA = 16
PIECE = 2 * HEAD_DIM
LOOK_AHEAD = 3
EPS = 1e-06
F32 = jnp.float32
BF16 = jnp.bfloat16


def split_bf16(value, parts):
    pieces = []
    rest = value
    for _ in range(parts):
        piece = rest.astype(BF16)
        pieces.append(piece)
        rest = rest - piece.astype(F32)
    return pieces


def head_rows(video, text):
    return 3 * video + 2 * text + EXTRA


def column_copy(w_ref, first, target, sem):
    columns = target.shape[1]
    start = pl.multiple_of(first, HEAD_DIM)
    return pltpu.make_async_copy(w_ref.at[:, pl.ds(start, columns)], target, sem)


def partial_sums(a_ref, w_ref, video, text, msg_ref, first):
    row = lax.broadcasted_iota(jnp.int32, (EXTRA, HEAD_DIM), 0)
    band, member = row // 4, row % 4
    top = video + EXTRA
    terms = None
    for start in range(0, w_ref.shape[1], PIECE):
        stop = min(start + PIECE, w_ref.shape[1])
        product = jnp.dot(a_ref[...], w_ref[:, start:stop], preferred_element_type=F32)
        for local in range(0, stop - start, HEAD_DIM):
            part = product[:, local : local + HEAD_DIM]
            head, kind = divmod((start + local) // HEAD_DIM, 3)
            base = (first + head) * head_rows(video, text)
            msg_ref[base + kind * video : base + (kind + 1) * video, :] = part[:video].astype(BF16)
            extra = part[video:top]
            pieces = split_bf16(extra[0:1] + extra[1:2], 2) + split_bf16(extra[2:3] + extra[3:4], 2)
            split = pieces[3].astype(F32)
            for index in range(3):
                split = jnp.where(member == index, pieces[index].astype(F32), split)
            terms = split if kind == 0 else jnp.where(band == kind, split, terms)
            base += 3 * video
            if kind:
                rows = slice(base + (kind - 1) * text, base + kind * text)
                msg_ref[rows, :] = part[top:].astype(BF16)
            if kind == 2:
                base += 2 * text
                msg_ref[base : base + EXTRA, :] = terms.astype(BF16)


def send_kernel(
    place_ref, x_ref, t_ref, scale_ref, shift_ref, w_ref,
    a_ref, msg_ref, stat_ref, ahead_ref,
    x_buffer, t_buffer, scale_buffer, shift_buffer, w_buffer, sems,
):
    video, features = x_buffer.shape
    text = t_buffer.shape[0]
    top = video + EXTRA
    columns = w_buffer.shape[1]
    base = (1 - place_ref[0]) * (w_ref.shape[1] // 2)
    copies = [
        pltpu.make_async_copy(scale_ref, scale_buffer, sems.at[0]),
        pltpu.make_async_copy(shift_ref, shift_buffer, sems.at[1]),
        pltpu.make_async_copy(x_ref, x_buffer, sems.at[2]),
        pltpu.make_async_copy(
            t_ref.at[pl.ds(pl.multiple_of(place_ref[1] * text, text), text)], t_buffer, sems.at[3]
        ),
        column_copy(w_ref, base, w_buffer, sems.at[4]),
        column_copy(w_ref, base + columns, ahead_ref, sems.at[5]),
    ]
    for copy in copies[:5]:
        copy.start()

    copies[0].wait()
    copies[1].wait()
    gain = 1.0 + scale_buffer[...].reshape(1, features)
    pieces = split_bf16(gain, 2) + split_bf16(shift_buffer[...].reshape(1, features), 2)
    row = lax.broadcasted_iota(jnp.int32, (EXTRA, features), 0)
    extra = jnp.zeros((EXTRA, features), F32)
    for index, piece in enumerate(pieces):
        extra = jnp.where(row % 4 == index, piece.astype(F32), extra)
    a_ref[video:top, :] = extra.astype(BF16)

    def prepare(rows_ref, start):
        rows = rows_ref[...].astype(F32)
        count = rows.shape[0]
        mean = jnp.sum(rows, axis=1, keepdims=True) * (1.0 / features)
        centered = rows - mean
        second = jnp.sum(centered * centered, axis=1, keepdims=True)
        a_ref[start : start + count, :] = (centered * gain).astype(BF16)
        lane = lax.broadcasted_iota(jnp.int32, (count, HEAD_DIM), 1)
        packed = jnp.zeros((count, HEAD_DIM), F32)
        for index, piece in enumerate(split_bf16(mean, 3) + split_bf16(second, 3)):
            packed = jnp.where(lane == index, piece.astype(F32), packed)
        stat_ref[start : start + count, :] = jnp.where(
            lane == 0, mean, jnp.where(lane == 1, second, 0.0)
        )
        return jnp.transpose(packed)[:EXTRA]

    copies[2].wait()
    copies[5].start()
    stats = [prepare(x_buffer, 0)]
    copies[3].wait()
    stats.append(prepare(t_buffer, top))
    stat_ref[video:top, :] = jnp.zeros((EXTRA, HEAD_DIM), F32)
    start = head_rows(video, text) * columns // TRIPLE
    msg_ref[start : start + 2 * EXTRA, :] = jnp.concatenate(stats, axis=0).astype(BF16)
    copies[4].wait()
    partial_sums(a_ref, w_buffer, video, text, msg_ref, 0)
    copies[5].wait()


def send_more_kernel(
    video, place_ref, a_ref, ahead_ref, w_ref, msg_ref, own_ahead_ref, w_buffer, last_buffer, sems,
):
    text = a_ref.shape[0] - video - EXTRA
    width = w_ref.shape[1] // 2
    other, own = (1 - place_ref[0]) * width, place_ref[0] * width
    first = width - last_buffer.shape[1]
    copies = [
        column_copy(w_ref, other + first - w_buffer.shape[1], w_buffer, sems.at[0]),
        column_copy(w_ref, other + first, last_buffer, sems.at[1]),
        column_copy(w_ref, own, own_ahead_ref, sems.at[2]),
    ]
    copies[0].start()
    copies[1].start()
    partial_sums(a_ref, ahead_ref, video, text, msg_ref, 0)
    copies[0].wait()
    copies[2].start()
    head = ahead_ref.shape[1] // TRIPLE
    partial_sums(a_ref, w_buffer, video, text, msg_ref, head)
    copies[1].wait()
    head += w_buffer.shape[1] // TRIPLE
    partial_sums(a_ref, last_buffer, video, text, msg_ref, head)
    copies[2].wait()


def own_kernel(place_ref, a_ref, ahead_ref, w_ref, *refs):
    small = (len(refs) - 4) // 2
    out_ref, text_ref = refs[small : small + 2]
    w_buffer, sems = refs[-2:]
    top = out_ref.shape[0]
    later, _, columns = w_buffer.shape
    base = place_ref[0] * (w_ref.shape[1] // 2) + columns
    copies = [
        column_copy(w_ref, base + index * columns, w_buffer.at[index], sems.at[index])
        for index in range(later)
    ]
    for source, target in zip(refs[:small], refs[small + 2 : -2]):
        copies.append(pltpu.make_async_copy(source, target, sems.at[len(copies)]))
    copies[0].start()

    for block in range(later + 1):
        if block:
            copies[block - 1].wait()
        if block == 1:
            for copy in copies[later:]:
                copy.start()
        for start in range(0, columns, PIECE):
            cells = slice(start, start + PIECE)
            part = w_buffer[block - 1, :, cells] if block else ahead_ref[:, cells]
            product = jnp.dot(a_ref[...], part, preferred_element_type=F32)
            first = block * columns + start
            out_ref[:, first : first + PIECE] = product[:top]
            for local in range(0, PIECE, HEAD_DIM):
                head, kind = divmod((first + local) // HEAD_DIM, 3)
                if kind:
                    target = (2 * head + kind - 1) * HEAD_DIM
                    text_ref[:, target : target + HEAD_DIM] = product[
                        top:, local : local + HEAD_DIM
                    ]
            if block == 0 and start == 0:
                for copy in copies[1:later]:
                    copy.start()
    for copy in copies[later:]:
        copy.wait()


def row_stats(total_features, own, received):
    count = own.shape[0]
    received = received.astype(F32)
    padding = jnp.zeros((HEAD_DIM - received.shape[0], count), F32)
    received = jnp.transpose(jnp.concatenate([received, padding], axis=0))
    parts = [received[:, index : index + 1] for index in range(6)]
    gap = 0.5 * (own[:, 0:1] - (parts[0] + parts[1] + parts[2]))
    second = own[:, 1:2] + (parts[3] + parts[4] + parts[5])
    var = second * (1.0 / total_features) + gap * gap
    return gap, lax.rsqrt(var + EPS)


def column_terms(own_ref, msg_ref, video, base, part):
    other = msg_ref[base : base + EXTRA, :].astype(F32)
    other = other[4 * (part % 3) : 4 * (part % 3) + 4]
    own = own_ref[video : video + 8, part * HEAD_DIM : (part + 1) * HEAD_DIM]
    scale = (own[0:1] + own[1:2]) - (other[0:1] + other[1:2])
    shift = (own[2:3] + own[3:4]) + (other[2:3] + other[3:4])
    return scale, shift


def head_place(head, rows, first_ref, more_ref):
    early = first_ref.shape[0] // rows
    return (first_ref, head * rows) if head < early else (more_ref, (head - early) * rows)


def head_norm(part, gain):
    square = jnp.sum(part * part, axis=1, keepdims=True) * (1.0 / HEAD_DIM)
    return part * lax.rsqrt(square + EPS) * gain


def norm_kernel(
    total_features, text, own_ref, first_ref, more_ref, stat_ref, qg_ref, kg_ref,
    qa_ref, qb_ref, kv_ref,
):
    video = qa_ref.shape[0]
    half = qa_ref.shape[1] // HEAD_DIM
    rows = head_rows(video, text)
    query_gain = qg_ref[...].reshape(1, HEAD_DIM)
    key_gain = kg_ref[...].reshape(1, HEAD_DIM)
    start = first_ref.shape[0] - 2 * EXTRA
    gap, inverse = row_stats(
        total_features, stat_ref[:video, :], first_ref[start : start + EXTRA, :video]
    )
    for head in range(2 * half):
        msg_ref, base = head_place(head, rows, first_ref, more_ref)

        def total(kind):
            part = 3 * head + kind
            scale, shift = column_terms(own_ref, msg_ref, video, base + rows - EXTRA, part)
            other = msg_ref[base + kind * video : base + (kind + 1) * video, :].astype(F32)
            both = own_ref[:video, part * HEAD_DIM : (part + 1) * HEAD_DIM] + other
            return (both + gap * scale) * inverse + shift

        columns = slice(head * HEAD_DIM, (head + 1) * HEAD_DIM)
        cells = slice(head % half * HEAD_DIM, (head % half + 1) * HEAD_DIM)
        q_ref = qa_ref if head < half else qb_ref
        q_ref[:, cells] = head_norm(total(0), query_gain).astype(BF16)
        kv_ref[0, :, columns] = head_norm(total(1), key_gain).astype(BF16)
        kv_ref[1, :, columns] = total(2).astype(BF16)


def text_kernel(
    total_features, own_ref, first_ref, more_ref, stat_ref, top_ref, kg_ref, kv_ref
):
    text = kv_ref.shape[1]
    heads = kv_ref.shape[2] // HEAD_DIM
    video = top_ref.shape[0] - EXTRA
    rows = head_rows(video, text)
    key_gain = kg_ref[...].reshape(1, HEAD_DIM)
    start = first_ref.shape[0] - EXTRA
    gap, inverse = row_stats(
        total_features, stat_ref[video + EXTRA :, :], first_ref[start : start + EXTRA, :text]
    )
    for head in range(heads):
        msg_ref, base = head_place(head, rows, first_ref, more_ref)

        def total(kind):
            scale, shift = column_terms(
                top_ref, msg_ref, video, base + rows - EXTRA, 3 * head + 1 + kind
            )
            start = base + 3 * video + kind * text
            other = msg_ref[start : start + text, :].astype(F32)
            first = (2 * head + kind) * HEAD_DIM
            return (own_ref[:, first : first + HEAD_DIM] + other + gap * scale) * inverse + shift

        columns = slice(head * HEAD_DIM, (head + 1) * HEAD_DIM)
        kv_ref[0, :, columns] = head_norm(total(0), key_gain).astype(BF16)
        kv_ref[1, :, columns] = total(1).astype(BF16)


FACTOR = math.log2(math.e) / math.sqrt(HEAD_DIM)


def split_kernel(*refs):
    count = len(refs) // 3
    for index in range(count):
        half = refs[index].shape[2] // 2
        refs[count + 2 * index][...] = refs[index][:, :, :half]
        refs[count + 2 * index + 1][...] = refs[index][:, :, half:]


def weigh(rows, keys):
    scores = lax.dot_general(rows, keys, (((1,), (1,)), ((), ())), preferred_element_type=F32)
    return jnp.exp2(scores * FACTOR)


def lanes(weights):
    total = weights[:, :HEAD_DIM]
    for start in range(HEAD_DIM, weights.shape[1], HEAD_DIM):
        total = total + weights[:, start : start + HEAD_DIM]
    return total


def times(weights, values):
    return jnp.dot(weights.astype(BF16), values, preferred_element_type=F32)


def both(group, index):
    return jnp.concatenate([ref[index, :, part] for ref, part in group], axis=0)


def attend_kernel(
    first, count, finish, place_ref, qo_ref, qp_ref, fresh_ref, stale_ref, text_ref, mask_ref, *refs,
):
    *refs, num_ref, den_ref = refs
    if finish:
        *refs, own_ref = refs
        own_den_ref, msg_ref = num_ref, den_ref
    video, width = qo_ref.shape
    text = text_ref.shape[1]
    lane = lax.broadcasted_iota(jnp.int32, (2 * video, HEAD_DIM), 1)
    mask = mask_ref[...].reshape(1, 2 * text).astype(F32)
    mask = jnp.where(place_ref[1] == 0, mask[:, :text], mask[:, text:])
    keep = jnp.concatenate([jnp.ones((1, video), F32), mask], axis=1)
    same_patch = (
        (lax.broadcasted_iota(jnp.int32, (2 * video, 2 * video), 0) < video)
        == (lax.broadcasted_iota(jnp.int32, (2 * video, 2 * video), 1) < video)
    ).astype(F32)
    packed = jnp.zeros((2 * video, HEAD_DIM), F32)

    def scores_of(head, group):
        cells = slice(head * HEAD_DIM, (head + 1) * HEAD_DIM)
        queries = jnp.concatenate([qo_ref[:, cells], qp_ref[:, cells]], axis=0)
        return lax.dot_general(
            queries, both(group, 0), (((1,), (1,)), ((), ())), preferred_element_type=F32
        )

    work = []
    for head in range(width // HEAD_DIM):
        cells = slice(head * HEAD_DIM, (head + 1) * HEAD_DIM)
        columns = slice((first + head) * HEAD_DIM, (first + head + 1) * HEAD_DIM)
        blocks = [(ref, columns) for ref in refs[:count]] + [(ref, cells) for ref in refs[count:]]
        blocks.append((text_ref, columns))
        work.append((head, [(fresh_ref, columns), (stale_ref, columns)], same_patch))
        odd = len(blocks) % 2
        if odd:
            work.append((head, blocks[:1], None))
        for start in range(odd, len(blocks), 2):
            last = start + 2 == len(blocks)
            work.append((head, blocks[start : start + 2], keep if last else None))

    upcoming = [scores_of(*item[:2]) for item in work[:LOOK_AHEAD]]
    num = den = None
    for index, (head, group, kept) in enumerate(work):
        scores = upcoming.pop(0)
        if index + LOOK_AHEAD < len(work):
            upcoming.append(scores_of(*work[index + LOOK_AHEAD][:2]))
        weights = jnp.exp2(scores * FACTOR)
        if kept is not None:
            weights = weights * kept
        part, total = times(weights, both(group, 1)), lanes(weights)
        num = part if num is None else num + part
        den = total if den is None else den + total
        if index + 1 == len(work) or work[index + 1][0] != head:
            cells = slice(head * HEAD_DIM, (head + 1) * HEAD_DIM)
            if finish:
                own_ref[:, cells] = num[:video]
                msg_ref[:, cells] = num[video:]
            else:
                num_ref[:, cells] = num
            packed = jnp.where(lane == first + head, jnp.sum(den, axis=1, keepdims=True), packed)
            num = den = None
    if finish:
        own_den_ref[...] = packed[:video]
        msg_ref[:, width:] = packed[video:]
    else:
        den_ref[...] = packed


def last_kernel(first, qo_ref, qp_ref, num_ref, den_ref, far_ref, own_ref, own_den_ref, msg_ref):
    video, width = qo_ref.shape
    lane = lax.broadcasted_iota(jnp.int32, (2 * video, HEAD_DIM), 1)
    packed = den_ref[...]
    for head in range(width // HEAD_DIM):
        cells = slice(head * HEAD_DIM, (head + 1) * HEAD_DIM)
        queries = jnp.concatenate([qo_ref[:, cells], qp_ref[:, cells]], axis=0)
        weights = weigh(queries, far_ref[0, :, cells])
        num = num_ref[:, cells] + times(weights, far_ref[1, :, cells])
        own_ref[:, cells] = num[:video]
        msg_ref[:, cells] = num[video:]
        total = jnp.sum(lanes(weights), axis=1, keepdims=True)
        packed = packed + jnp.where(lane == first + head, total, 0.0)
    own_den_ref[...] = packed[:video]
    msg_ref[:, width:] = packed[video:]


def merge_kernel(first, own_ref, den_ref, msg_ref, att_ref):
    width = att_ref.shape[1]
    for head in range(width // HEAD_DIM):
        columns = slice(head * HEAD_DIM, (head + 1) * HEAD_DIM)
        lane = first + head
        num = own_ref[:, columns] + msg_ref[:, columns]
        den = den_ref[:, lane : lane + 1] + msg_ref[:, width + lane : width + lane + 1]
        att_ref[:, columns] = (num / den).astype(BF16)


def part_kernel(
    place_ref, weight_ref, hidden_ref, fresh_ref, first_ref, second_ref,
    out_ref, w_other_ref, hidden_copy_ref, cache_ref, w_ref, sems,
):
    depth = w_ref.shape[0]
    half = first_ref.shape[1]
    copies = []
    for index, (group, target) in enumerate(
        ((place_ref[0], w_ref), (1 - place_ref[0], w_other_ref))
    ):
        rows = pl.ds(pl.multiple_of(group * depth, depth), depth)
        copies.append(pltpu.make_async_copy(weight_ref.at[rows], target, sems.at[index]))
    copies.append(pltpu.make_async_copy(hidden_ref, hidden_copy_ref, sems.at[2]))
    copies.append(pltpu.make_async_copy(fresh_ref, cache_ref, sems.at[3]))
    for copy in copies:
        copy.start()
    copies[0].wait()
    out_ref[...] = jnp.dot(
        first_ref[...], w_ref[:half, :], preferred_element_type=F32
    ) + jnp.dot(second_ref[...], w_ref[half:, :], preferred_element_type=F32)
    for copy in copies[1:]:
        copy.wait()


def more_kernel(part_ref, att_ref, w_ref, out_ref):
    half = att_ref.shape[1]
    out_ref[...] = part_ref[...] + jnp.dot(
        att_ref[...], w_ref[:half, :], preferred_element_type=F32
    )


def final_kernel(part_ref, att_ref, w_ref, hidden_ref, gate_ref, out_ref, buffer_ref, sems):
    half = att_ref.shape[1]
    gate = gate_ref[...].reshape(1, part_ref.shape[1])
    count = sems.shape[0]
    step = part_ref.shape[1] // count
    copies = []
    for index in range(count):
        cells = slice(index * step, (index + 1) * step)
        total = part_ref[:, cells] + jnp.dot(
            att_ref[...], w_ref[half:, cells], preferred_element_type=F32
        )
        mixed = hidden_ref[:, cells].astype(F32) + gate[:, cells] * total
        buffer_ref[:, cells] = mixed.astype(BF16)
        copies.append(
            pltpu.make_async_copy(buffer_ref.at[:, cells], out_ref.at[:, cells], sems.at[index])
        )
        copies[-1].start()
    for copy in copies:
        copy.wait()


def params(megabytes):
    return pltpu.CompilerParams(vmem_limit_bytes=megabytes * 1024 * 1024)


def in_hbm(array):
    return pltpu.with_memory_space_constraint(array, pltpu.HBM)


def cost(flops, nbytes, transcendentals=0):
    return pl.CostEstimate(
        flops=int(flops), bytes_accessed=int(nbytes), transcendentals=int(transcendentals)
    )


def plain_call(kernel, outs, name, estimate, *operands):
    return pl.pallas_call(
        kernel,
        in_specs=[pl.BlockSpec(memory_space=pltpu.VMEM)] * len(operands),
        out_specs=[pl.BlockSpec(memory_space=pltpu.VMEM)] * len(outs),
        out_shape=[jax.ShapeDtypeStruct(shape, dtype) for shape, dtype in outs],
        compiler_params=params(24),
        cost_estimate=estimate,
        name=name,
    )(*operands)


def ring_moves(sections):
    chips = sections // 2
    order = list(range(0, chips, 2)) + list(range(chips - 1, 0, -2))
    moves = [], []
    for here, there in zip(order, order[1:] + order[:1]):
        for core in range(2):
            moves[core].append((2 * here + core, 2 * there + core))
            moves[1 - core].append((2 * there + core, 2 * here + core))
    return sorted(moves[0]), sorted(moves[1])


def per_device(
    sections, hidden, text_hidden, text_mask, stale_cache, qkv_weight, out_weight, query_gain,
    key_gain, norm_shift, norm_scale, branch_gate,
):
    video, features = hidden.shape
    text = text_hidden.shape[0] // 2
    width = stale_cache.shape[2]
    heads = width // HEAD_DIM
    group_columns = heads * TRIPLE
    chips = sections // 2
    out_features = out_weight.shape[1]
    top = video + EXTRA
    rows = top + text

    group = lax.axis_index("head")
    core = lax.axis_index("section") % 2
    place = jnp.stack([group, core]).astype(jnp.int32)
    swap_core = [(s, s ^ 1) for s in range(sections)]
    swap_head = [(0, 1), (1, 0)]
    ways = ring_moves(sections)
    half_way = chips // 2

    def ring_step(blocks):
        return [lax.ppermute(block, "section", way) for block, way in zip(blocks, ways)]

    vmem = pl.BlockSpec(memory_space=pltpu.VMEM)
    hbm = pl.BlockSpec(memory_space=pltpu.HBM)
    smem = pl.BlockSpec(memory_space=pltpu.SMEM)
    whole = ring_step((stale_cache, stale_cache))

    columns = 2 * TRIPLE
    blocks = group_columns // columns
    per_head = head_rows(video, text)

    def project_cost(share):
        share = 8 * rows * features * group_columns * share
        return cost(share, share // (4 * rows))

    a_rows, message, stats, ahead = pl.pallas_call(
        send_kernel,
        in_specs=[smem] + [hbm] * 5,
        out_specs=[vmem] * 4,
        out_shape=[
            jax.ShapeDtypeStruct((rows, features), BF16),
            jax.ShapeDtypeStruct((per_head + 2 * EXTRA, HEAD_DIM), BF16),
            jax.ShapeDtypeStruct((rows, HEAD_DIM), F32),
            jax.ShapeDtypeStruct((features, columns), BF16),
        ],
        scratch_shapes=[
            pltpu.VMEM((video, features), BF16),
            pltpu.VMEM((text, features), BF16),
            pltpu.VMEM((features,), F32),
            pltpu.VMEM((features,), F32),
            pltpu.VMEM((features, TRIPLE), BF16),
            pltpu.SemaphoreType.DMA((6,)),
        ],
        compiler_params=params(40),
        cost_estimate=project_cost(0.4),
        name="project_send",
    )(place, *map(in_hbm, (hidden, text_hidden, norm_scale, norm_shift, qkv_weight)))
    received = lax.ppermute(message, "head", swap_head)

    message_more, own_ahead = pl.pallas_call(
        functools.partial(send_more_kernel, video),
        in_specs=[smem, vmem, vmem, hbm],
        out_specs=[vmem] * 2,
        out_shape=[
            jax.ShapeDtypeStruct(((heads - 1) * per_head, HEAD_DIM), BF16),
            jax.ShapeDtypeStruct((features, columns), BF16),
        ],
        scratch_shapes=[
            pltpu.VMEM((features, group_columns - columns - 2 * TRIPLE), BF16),
            pltpu.VMEM((features, TRIPLE), BF16),
            pltpu.SemaphoreType.DMA((3,)),
        ],
        compiler_params=params(40),
        cost_estimate=project_cost(0.6),
        name="project_send_more",
    )(place, a_rows, ahead, in_hbm(qkv_weight))
    received_more = lax.ppermute(message_more, "head", swap_head)

    split = plain_call(
        split_kernel, [((2, video, width // 2), BF16)] * 4, "split_heads", cost(0, 8 * video * width),
        *lax.optimization_barrier((*whole, message_more, received))[:2],
    )
    chains = [[ring_step((split[0], split[2]))], [ring_step((split[1], split[3]))]]

    small = (query_gain, key_gain, text_mask, branch_gate, stale_cache)
    outs = pl.pallas_call(
        own_kernel,
        in_specs=[smem, vmem, vmem, hbm] + [hbm] * len(small),
        out_specs=[vmem] * (2 + len(small)),
        out_shape=[
            jax.ShapeDtypeStruct((top, group_columns), F32),
            jax.ShapeDtypeStruct((text, 2 * width), F32),
        ]
        + [jax.ShapeDtypeStruct(array.shape, array.dtype) for array in small],
        scratch_shapes=[
            pltpu.VMEM((blocks - 1, features, columns), BF16),
            pltpu.SemaphoreType.DMA((blocks - 1 + len(small),)),
        ],
        compiler_params=params(40),
        cost_estimate=project_cost(1),
        name="project_own",
    )(place, a_rows, own_ahead, *map(in_hbm, (qkv_weight,) + small))
    own, own_text = outs[:2]
    query_gain, key_gain, text_mask, branch_gate, stale = outs[2:]

    for _ in range(half_way - 3):
        for chain in chains:
            chain.append(ring_step(lax.optimization_barrier((*chain[-1], own))[:2]))
    far = [lax.ppermute(chain[-1][0], "section", ways[0]) for chain in chains]

    received_more = lax.optimization_barrier((received_more, *chains[0][0], *chains[1][0]))[0]
    *queries, fresh = plain_call(
        functools.partial(norm_kernel, features * 2, text),
        [((video, width // 2), BF16)] * 2 + [((2, video, width), BF16)],
        "norm_video",
        cost(1000 * top * group_columns, 8 * top * group_columns),
        own, received, received_more, stats, query_gain, key_gain,
    )
    other_queries = [lax.ppermute(half, "section", swap_core) for half in queries]
    (text_kv,) = plain_call(
        functools.partial(text_kernel, features * 2),
        [((2, text, width), BF16)],
        "norm_text",
        cost(text * group_columns, text * group_columns),
        own_text, received, received_more, stats, own, key_gain,
    )

    context = chips * video + video + text
    finished = [
        jax.ShapeDtypeStruct((video, width // 2), F32),
        jax.ShapeDtypeStruct((video, HEAD_DIM), F32),
        jax.ShapeDtypeStruct((video, width // 2 + HEAD_DIM), F32),
    ]
    attended, other_attended = [], []
    for index, chain in enumerate(chains):
        first = index * heads // 2
        halves = [block for step in chain for block in step]
        finish = index == 0
        own_queries = queries[index]
        if finish:
            halves.append(far[index])
            outs = finished
        else:
            own_queries = lax.optimization_barrier((own_queries, num_own))[0]
            outs = [
                jax.ShapeDtypeStruct((2 * video, width // 2), F32),
                jax.ShapeDtypeStruct((2 * video, HEAD_DIM), F32),
            ]
        outs = pl.pallas_call(
            functools.partial(attend_kernel, first, len(whole), finish),
            in_specs=[smem] + [vmem] * (6 + len(whole) + len(halves)),
            out_specs=[vmem] * len(outs),
            out_shape=outs,
            compiler_params=params(24),
            cost_estimate=cost(video * context, context * width, video * heads),
            name="attend",
        )(
            place, own_queries, other_queries[index], fresh, stale, text_kv, text_mask,
            *whole, *halves,
        )
        if not finish:
            outs = plain_call(
                functools.partial(last_kernel, first),
                [(out.shape, out.dtype) for out in finished],
                "attend_last",
                cost(video * video, video * width),
                own_queries, other_queries[index], *outs, far[index],
            )
        num_own, den_own, num_message = outs
        num_received = lax.ppermute(num_message, "section", swap_core)
        attended += plain_call(
            functools.partial(merge_kernel, first),
            [((video, width // 2), BF16)],
            "merge",
            cost(2 * video * width, 5 * video * width),
            num_own, den_own, num_received,
        )
        other_attended.append(lax.ppermute(attended[-1], "head", swap_head))

    out_cost = cost(4 * video * width * out_features, 2 * width * out_features)
    part, w_other, hidden, new_cache = pl.pallas_call(
        part_kernel,
        in_specs=[smem, hbm, hbm] + [vmem] * 3,
        out_specs=[vmem] * 3 + [hbm],
        out_shape=[
            jax.ShapeDtypeStruct((video, out_features), F32),
            jax.ShapeDtypeStruct((width, out_features), BF16),
            jax.ShapeDtypeStruct(hidden.shape, BF16),
            jax.ShapeDtypeStruct(fresh.shape, BF16),
        ],
        scratch_shapes=[
            pltpu.VMEM((width, out_features), BF16),
            pltpu.SemaphoreType.DMA((4,)),
        ],
        compiler_params=params(24),
        cost_estimate=out_cost,
        name="part_out",
    )(place, in_hbm(out_weight), in_hbm(hidden), fresh, *attended)
    (part,) = plain_call(
        more_kernel, [((video, out_features), F32)], "more_out", out_cost,
        part, other_attended[0], w_other,
    )
    mixed = pl.pallas_call(
        final_kernel,
        in_specs=[vmem] * 5,
        out_specs=hbm,
        out_shape=jax.ShapeDtypeStruct((video, out_features), BF16),
        scratch_shapes=[
            pltpu.VMEM((video, out_features), BF16),
            pltpu.SemaphoreType.DMA((out_features // 512,)),
        ],
        compiler_params=params(24),
        cost_estimate=out_cost,
        name="final_out",
    )(part, other_attended[1], w_other, hidden, branch_gate)
    return (mixed, new_cache)


def solution(mesh):
    in_specs = (
        P("section", "head"),
        P(None, "head"),
        P(),
        P(None, "section", "head"),
        P("head", None),
        P(None, "head"),
        P(),
        P(),
        P("head"),
        P("head"),
        P("head"),
    )
    out_specs = (P("section", "head"), P(None, "section", "head"))
    return jax.shard_map(
        functools.partial(per_device, mesh.shape["section"]),
        mesh=mesh, in_specs=in_specs, out_specs=out_specs, check_vma=False,
    )
```
